32 devices in a mesh: blk: 4 (over z), dp: 2 (over x), head: 4 (over y, core).
Axes of the slice: x: 2, y: 2, z: 4, core: 2. Of those that a mesh axis runs over, the one named last changes fastest.
Arguments:
- tokens: bfloat16 [2, 2, 4, 196608], P(None, 'dp', 'head', 'blk'), may hold values from -6 to 6
- doc_lengths: int32 [2, 2, 4], P(None, 'dp'), may hold values from 0 to 1024, as said below
- cotangent: bfloat16 [2, 2, 4, 196608], P(None, 'dp', 'head', 'blk'), may hold values from -6 to 6
- query_weight: bfloat16 [4, 192, 192], P('head', ('blk', 'dp')), may hold values from -0.4375 to 0.4375
- query_bias: bfloat16 [4, 192], P('head', ('blk', 'dp')), may hold values from -1.75 to 1.75
- key_weight: bfloat16 [4, 192, 192], P('head', ('blk', 'dp')), may hold values from -0.4375 to 0.4375
- value_weight: bfloat16 [4, 192, 192], P('head', ('blk', 'dp')), may hold values from -0.4375 to 0.4375
- value_bias: bfloat16 [4, 192], P('head', ('blk', 'dp')), may hold values from -1.75 to 1.75
- out_weight: bfloat16 [768, 768], P(('blk', 'dp'), 'head'), may hold values from -3.5 to 3.5
- out_bias: bfloat16 [4, 192], P('head', ('blk', 'dp')), may hold values from -1.75 to 1.75
- first_gain: bfloat16 [4, 192], P('head', ('blk', 'dp')), may hold values from 0.5 to 1.5
- first_shift: bfloat16 [4, 192], P('head', ('blk', 'dp')), may hold values from -1.75 to 1.75
- up_weight: bfloat16 [4, 192, 768], P('head', ('blk', 'dp')), may hold values from -0.4375 to 0.4375
- up_bias: bfloat16 [4, 768], P('head', ('blk', 'dp')), may hold values from -1.75 to 1.75
- down_weight: bfloat16 [4, 768, 192], P('head', ('blk', 'dp')), may hold values from -0.21875 to 0.21875
- down_bias: bfloat16 [4, 192], P('head', ('blk', 'dp')), may hold values from -1.75 to 1.75
- second_gain: bfloat16 [4, 192], P('head', ('blk', 'dp')), may hold values from 0.5 to 1.5
- second_shift: bfloat16 [4, 192], P('head', ('blk', 'dp')), may hold values from -1.75 to 1.75
Outputs:
- mixed_out: bfloat16 [2, 2, 4, 196608], P(None, 'dp', 'head', 'blk')
- tokens_grad: float32 [2, 2, 4, 196608], P(None, 'dp', 'head', 'blk')
- query_weight_grad: float32 [4, 192, 192], P('head', ('blk', 'dp'))
- query_bias_grad: float32 [4, 192], P('head', ('blk', 'dp'))
- key_weight_grad: float32 [4, 192, 192], P('head', ('blk', 'dp'))
- value_weight_grad: float32 [4, 192, 192], P('head', ('blk', 'dp'))
- value_bias_grad: float32 [4, 192], P('head', ('blk', 'dp'))
- out_weight_grad: float32 [768, 768], P(('blk', 'dp'), 'head')
- out_bias_grad: float32 [4, 192], P('head', ('blk', 'dp'))
- first_gain_grad: float32 [4, 192], P('head', ('blk', 'dp'))
- first_shift_grad: float32 [4, 192], P('head', ('blk', 'dp'))
- up_weight_grad: float32 [4, 192, 768], P('head', ('blk', 'dp'))
- up_bias_grad: float32 [4, 768], P('head', ('blk', 'dp'))
- down_weight_grad: float32 [4, 768, 192], P('head', ('blk', 'dp'))
- down_bias_grad: float32 [4, 192], P('head', ('blk', 'dp'))
- second_gain_grad: float32 [4, 192], P('head', ('blk', 'dp'))
- second_shift_grad: float32 [4, 192], P('head', ('blk', 'dp'))
The draws below stay inside these ranges and needn't reach their ends.
Inputs may be any that keep to these rules, and one draw needn't show every extreme that they name: `doc_lengths`: each row sums to 1024. In every micro-batch one group, drawn from the seed, holds one sequence of all 1024 tokens (its other entries 0); every other group holds 4 sequences, each of 128 to 384 tokens.
All inputs are finite; a program needn't handle non-finite values.
Results may differ from the reference program's by a relative error of at most 0.025.
Values may be sent and summed in bfloat16 or wider, within the bound.
A program may use at most 128 MiB of HBM per device.

```python
import math
import jax
import jax.numpy as jnp
from jax import lax

D = 768
HEAD_DIM = 64
GROUPS = 4
MB = 2
NDOC = 4
GT = 1024
SEQ_GROUPS = 2
GW = 192
FFG = 768


def draw_doc_lengths(key, part):
    key = jax.random.fold_in(key, 7)
    first_key, second_key = jax.random.split(key)
    quarter = GT // 4
    reach = GT // 8
    shifts = jax.random.randint(first_key, (MB, SEQ_GROUPS, 2), -reach, reach + 1)
    short_rows = jnp.stack([quarter + shifts[:, :, 0], quarter - shifts[:, :, 0], quarter + shifts[:, :, 1], GT - 3 * quarter - shifts[:, :, 1]], axis=2)
    long_row = jnp.concatenate([jnp.full((MB, SEQ_GROUPS, 1), GT, jnp.int32), jnp.zeros((MB, SEQ_GROUPS, NDOC - 1), jnp.int32)], axis=2)
    chosen = jax.random.randint(second_key, (MB, 1, 1), 0, SEQ_GROUPS)
    group_ids = jnp.arange(SEQ_GROUPS, dtype=jnp.int32)[None, :, None]
    return jnp.where(group_ids == chosen, long_row, short_rows.astype(jnp.int32)).astype(jnp.int32)


def levels(rng, extent, cuts, least, high):
    def one(position, parts):
        heights = jax.random.uniform(jax.random.fold_in(jax.random.fold_in(rng, 6), position), (parts,), jnp.float32, least / len(cuts), high / len(cuts))
        return jnp.repeat(jnp.exp(heights), extent[position] // parts).reshape((-1,) + (1,) * (len(extent) - position - 1))

    level = one(*cuts[0])
    for cut in cuts[1:]:
        level = level * one(*cut)
    return level


def scatter_about(key, extent, scale, limit, pieces=(), kind=jnp.bfloat16):
    values = scale * jax.random.normal(key, extent, jnp.float32)
    if pieces:
        values = values * levels(key, extent, pieces, -0.22, 0.18)
    return jnp.clip(values, -limit, limit).astype(kind)


def setup_inputs(seed: int = 0) -> dict:
    keys = jax.random.split(jax.random.key(seed), 19)
    tokens = scatter_about(keys[0], (MB, SEQ_GROUPS, GROUPS, GT * GW), 1.0, 6.0, ((1, 2), (2, 4), (3, 4)))
    doc_lengths = draw_doc_lengths(jax.random.fold_in(keys[18], 71), 0)
    cotangent = scatter_about(keys[2], (MB, SEQ_GROUPS, GROUPS, GT * GW), 1.0, 6.0, ((1, 2), (2, 4), (3, 4)))
    query_weight = scatter_about(keys[3], (GROUPS, GW, GW), GW ** -0.5, 0.4375, ((0, 4), (1, 8)))
    query_bias = scatter_about(keys[4], (GROUPS, GW), 0.3, 1.75, ((0, 4), (1, 8)))
    key_weight = scatter_about(keys[5], (GROUPS, GW, GW), GW ** -0.5, 0.4375, ((0, 4), (1, 8)))
    value_weight = scatter_about(keys[6], (GROUPS, GW, GW), GW ** -0.5, 0.4375, ((0, 4), (1, 8)))
    value_bias = scatter_about(keys[7], (GROUPS, GW), 0.3, 1.75, ((0, 4), (1, 8)))
    out_weight = scatter_about(keys[8], (D, D), ((GT * (4 * D) ** -1) ** 0.5), 3.5, ((0, 8), (1, 4)))
    out_bias = scatter_about(keys[9], (GROUPS, GW), 0.3, 1.75, ((0, 4), (1, 8)))
    first_gain = jnp.clip(1.0 + 0.1 * jax.random.normal(keys[10], (GROUPS, GW), jnp.float32), 0.5, 1.5).astype(jnp.bfloat16)
    first_shift = scatter_about(keys[11], (GROUPS, GW), 0.3, 1.75, ((0, 4), (1, 8)))
    up_weight = scatter_about(keys[12], (GROUPS, GW, FFG), GW ** -0.5, 0.4375, ((0, 4), (1, 8)))
    up_bias = scatter_about(keys[13], (GROUPS, FFG), 0.3, 1.75, ((0, 4), (1, 8)))
    down_weight = scatter_about(keys[14], (GROUPS, FFG, GW), FFG ** -0.5, 0.21875, ((0, 4), (1, 8)))
    down_bias = scatter_about(keys[15], (GROUPS, GW), 0.3, 1.75, ((0, 4), (1, 8)))
    second_gain = jnp.clip(1.0 + 0.1 * jax.random.normal(keys[16], (GROUPS, GW), jnp.float32), 0.5, 1.5).astype(jnp.bfloat16)
    second_shift = scatter_about(keys[17], (GROUPS, GW), 0.3, 1.75, ((0, 4), (1, 8)))
    return {"tokens": tokens, "doc_lengths": doc_lengths, "cotangent": cotangent, "query_weight": query_weight, "query_bias": query_bias, "key_weight": key_weight, "value_weight": value_weight, "value_bias": value_bias, "out_weight": out_weight, "out_bias": out_bias, "first_gain": first_gain, "first_shift": first_shift, "up_weight": up_weight, "up_bias": up_bias, "down_weight": down_weight, "down_bias": down_bias, "second_gain": second_gain, "second_shift": second_shift}


EPS = 1e-05
HIGH = lax.Precision.HIGHEST

@jax.custom_vjp
def low(v):
    return lax.optimization_barrier(v.astype(jnp.bfloat16)).astype(jnp.float32)

@jax.custom_vjp
def low_back(v):
    return v

def low_keep(v):
    return (low(v), None)

def low_pass(kept, grad):
    return (grad,)

def back_keep(v):
    return (v, None)

def back_low(kept, grad):
    return (low(grad),)
low.defvjp(low_keep, low_pass)
low_back.defvjp(back_keep, back_low)

def doc_index(positions, lengths):
    ends = jnp.cumsum(lengths)
    return lax.optimization_barrier(jnp.sum((positions[:, None] >= ends[None, :]).astype(jnp.int32), axis=1))

def grouped(values, weight):
    token_count = values.shape[0]
    split = values.reshape(token_count, weight.shape[0], weight.shape[1])
    return jnp.einsum('tgi,gio->tgo', split, weight, precision=HIGH).reshape(token_count, -1)

def layer_norm(hidden, gain, shift):
    mean_val = lax.optimization_barrier(jnp.mean(hidden, axis=1, keepdims=True))
    var_val = lax.optimization_barrier(jnp.mean(hidden * hidden, axis=1, keepdims=True)) - mean_val * mean_val
    return (hidden - mean_val) * lax.rsqrt(var_val + EPS) * gain.reshape(-1) + shift.reshape(-1)

def attention(queries, keys_all, values_all, docs):
    token_count = queries.shape[0]
    head_count = queries.shape[1] // HEAD_DIM
    query_heads = queries.reshape(token_count, head_count, HEAD_DIM)
    key_heads = keys_all.reshape(token_count, head_count, HEAD_DIM)
    value_heads = values_all.reshape(token_count, head_count, HEAD_DIM)
    block_rows = math.gcd(token_count, 1024)

    def block(pair):
        query_rows, query_docs = pair
        scores = low_back(jnp.einsum('qhd,khd->hqk', query_rows, key_heads, precision=HIGH) * HEAD_DIM ** (-0.5))
        scores = jnp.where((query_docs[:, None] == docs[None, :])[None], scores, -1e+30)
        weights = jax.nn.softmax(scores, axis=2)
        return jnp.einsum('hqk,khd->qhd', low(weights), value_heads, precision=HIGH)
    outputs = lax.map(jax.checkpoint(block), (query_heads.reshape(token_count // block_rows, block_rows, head_count, HEAD_DIM), docs.reshape(token_count // block_rows, block_rows)))
    return outputs.reshape(token_count, head_count * HEAD_DIM)

def layer(source, lengths, query_weight, query_bias, key_weight, value_weight, value_bias, out_weight, out_bias, first_gain, first_shift, up_weight, up_bias, down_weight, down_bias, second_gain, second_shift):
    token_count = source.shape[0]
    docs = doc_index(jnp.arange(token_count, dtype=jnp.int32), lengths)
    queries = low(low_back(grouped(source, query_weight) + query_bias.reshape(-1)))
    keys_all = low(low_back(grouped(source, key_weight)))
    values_all = low(low_back(grouped(source, value_weight) + value_bias.reshape(-1)))
    attended = low(low_back(attention(queries, keys_all, values_all, docs)))
    projected = low_back(jnp.dot(attended, out_weight, precision=HIGH) + out_bias.reshape(-1))
    first_out = layer_norm(source + projected, first_gain, first_shift)
    pre_up = low_back(grouped(low(first_out), up_weight) + up_bias.reshape(-1))
    activated = low(jax.nn.gelu(pre_up, approximate=False))
    down_out = low_back(grouped(activated, down_weight) + down_bias.reshape(-1))
    return layer_norm(first_out + down_out, second_gain, second_shift)

def to_rows(array, group_count, group_width):
    group_tokens = array.shape[3] // group_width
    split = array.reshape(-1, group_count, group_tokens, group_width)
    return jnp.transpose(split, (0, 2, 1, 3)).reshape(-1, group_tokens, group_count * group_width)

def from_rows(array, group_count, group_width, shape):
    split = array.reshape(-1, array.shape[1], group_count, group_width)
    return jnp.transpose(split, (0, 2, 1, 3)).reshape(shape)

def reference(tokens, doc_lengths, cotangent, query_weight, query_bias, key_weight, value_weight, value_bias, out_weight, out_bias, first_gain, first_shift, up_weight, up_bias, down_weight, down_bias, second_gain, second_shift):
    params = tuple((member.astype(jnp.float32) for member in (query_weight, query_bias, key_weight, value_weight, value_bias, out_weight, out_bias, first_gain, first_shift, up_weight, up_bias, down_weight, down_bias, second_gain, second_shift)))
    group_count = query_weight.shape[0]
    group_width = query_weight.shape[2]
    flat_tokens = to_rows(tokens, group_count, group_width).astype(jnp.float32)
    flat_cot = to_rows(cotangent, group_count, group_width).astype(jnp.float32)
    flat_lengths = doc_lengths.reshape(-1, doc_lengths.shape[2]).astype(jnp.int32)

    def step(totals, batch_item):
        source, lengths, grad_out = batch_item

        def apply_layer(source_in, *weights):
            return layer(source_in, lengths, *weights)
        result, pullback = jax.vjp(apply_layer, source, *params)
        grads = pullback(grad_out)
        new_totals = tuple((left + right for left, right in zip(totals, grads[1:])))
        return (new_totals, (result.astype(jnp.bfloat16), grads[0]))
    start_totals = tuple((jnp.zeros(member.shape, jnp.float32) for member in params))
    totals, (results, input_grads) = lax.scan(step, start_totals, (flat_tokens, flat_lengths, flat_cot))
    return (from_rows(results, group_count, group_width, tokens.shape), from_rows(input_grads, group_count, group_width, tokens.shape), totals[0], totals[1], totals[2], totals[3], totals[4], totals[5], totals[6], totals[7], totals[8], totals[9], totals[10], totals[11], totals[12], totals[13], totals[14])
```

```python
import types

import jax
import jax.numpy as jnp
from jax import lax
from jax.experimental import pallas as pl
from jax.experimental.pallas import tpu as pltpu
from jax.sharding import PartitionSpec as P

HEAD_DIM = 64
EPS = 1e-05
BIG = 1e30
MESH = pl.DeviceIdType.MESH
F32 = jnp.float32
BF16 = jnp.bfloat16
V_BQ, V_BV, V_BO, V_G1, V_S1, V_BD, V_G2, V_S2, V_BU = range(9)
VROWS = 16


def up_to(n, m):
    return (n + m - 1) // m * m


def mm(a, b):
    return lax.dot_general(a, b, (((1,), (0,)), ((), ())), preferred_element_type=F32)


def mm_nt(a, b):
    return lax.dot_general(a, b, (((1,), (1,)), ((), ())), preferred_element_type=F32)


def loop(n, fn):
    if n <= 8:
        for i in range(n):
            fn(i)
    else:
        lax.fori_loop(0, n, lambda i, c: (fn(i), c)[1], 0)


def rcopy(src, dst, ss, rs, dev):
    return pltpu.make_async_remote_copy(
        src_ref=src, dst_ref=dst, send_sem=ss, recv_sem=rs, device_id=dev, device_id_type=MESH
    )


class Sizes:
    def __init__(self, mesh, tokens, query_weight, up_weight, doc_lengths):
        self.nb, self.nd, self.nh = mesh.shape["blk"], mesh.shape["dp"], mesh.shape["head"]
        self.W = self.nb * self.nd
        self.C, self.F = query_weight.shape[2], up_weight.shape[2]
        self.MB = tokens.shape[0]
        self.R = tokens.shape[3] // self.C
        self.S = self.nb // self.MB
        self.tb = self.nb // (self.MB * self.nd)
        self.Q = self.MB * self.R
        self.H = self.C // HEAD_DIM
        self.ND = doc_lengths.shape[2]
        self.r = query_weight.shape[1]
        self.rs = up_to(self.r, 8)
        self.rA = up_to(2 * self.rs, 16)
        self.rC = up_to(4 * self.r, 16)
        self.L = 2 * self.C
        self.XR = self.C + 16
        self.keep = self.nb * self.R * self.Q * self.H * 2 <= (8 << 20)
        assert self.F == 4 * self.C and self.F == self.nh * self.C


def main_scratch(z):
    dma = pltpu.SemaphoreType.DMA
    v = pltpu.VMEM
    nb, W, L, R, C, F, Q, H = z.nb, z.W, z.L, z.R, z.C, z.F, z.Q, z.H
    dd = max(z.nd - 1, 1)
    return dict(
        xs=v((z.MB, z.XR, R), BF16),
        xb=v((nb, z.XR, R), BF16),
        cs=v((z.MB, C, R), BF16),
        cb=v((z.MB, C, R), BF16),
        bufA=v((W, z.rA, L), BF16),
        bufB=v((W, z.rA, L), BF16),
        bufC=v((W, z.rC, L), BF16),
        bufV=v((W, VROWS, 128), BF16),
        fst=v((max(z.rA, z.rC), L), F32),
        vst=v((VROWS, 128), F32),
        fkv=v((C + 8, L), F32),
        fq=v((C + 8, L), F32),
        fup=v((C + 8, F), F32),
        fod=v((F + 16, L), F32),
        vcol=v((C + 8, 16), F32),
        ucol=v((F + 16, 16), F32),
        wkv=v((C, L), BF16),
        wkvt=v((L, C), BF16),
        wq=v((C, C), BF16),
        wqt=v((C, C), BF16),
        wup=v((C, F), BF16),
        wupt=v((F, C), BF16),
        wo=v((z.nh, C, C), BF16),
        wor=v((z.nh, C, C), BF16),
        wot=v((C, F), BF16),
        wdn=v((F, C), BF16),
        wdnt=v((C, F), BF16),
        xq=v((C, Q), BF16),
        qx=v((H, 128, Q), BF16),
        qt=v((H, Q, 128), BF16),
        kx=v((nb, H, HEAD_DIM, R), BF16),
        vx=v((nb, H, HEAD_DIM + 16, R), BF16),
        kt=v((nb, H, R, 128), BF16),
        vt=v((nb, H, R, 128), BF16),
        sbuf=v((nb if z.keep else 1, R, Q), F32),
        pbuf=v((H, nb if z.keep else 1, R, Q), BF16),
        mrow=v((H, 8, Q), F32),
        oall=v((z.nh, C, Q), BF16),
        pall=v((z.nh, C, Q), BF16),
        stats=v((3, z.nh, 8, Q), F32),
        u=v((F, Q), F32),
        act=v((F, Q), BF16),
        du=v((F, Q), BF16),
        mo=v((z.MB, C, R), BF16),
        dox=v((H, 128, Q), BF16),
        dot=v((H, Q, 128), BF16),
        dqacc=v((H, HEAD_DIM, Q), F32),
        dkv=v((L, R), BF16),
        dq=v((C, Q), BF16),
        tgs=v((nb, C, R), BF16),
        gkv=v((C + 8, L), F32),
        gq=v((C + 8, L), F32),
        gup=v((C + 8, F), F32),
        god=v((F + 16, L), F32),
        vg=v((VROWS, C), F32),
        vgu=v((VROWS, F), F32),
        pA=v((W, z.rA, L), BF16),
        pB=v((W, z.rA, L), BF16),
        pC=v((W, z.rC, L), BF16),
        pV=v((W, VROWS, 128), BF16),
        r1A=v((dd, nb, z.rA, L), BF16),
        r1B=v((dd, nb, z.rA, L), BF16),
        r1C=v((dd, nb, z.rC, L), BF16),
        r1V=v((dd, nb, VROWS, 128), BF16),
        s2A=v((nb, z.rA, L), BF16),
        s2B=v((nb, z.rA, L), BF16),
        s2C=v((nb, z.rC, L), BF16),
        s2V=v((nb, VROWS, 128), BF16),
        r2A=v((nb, z.rA, L), BF16),
        r2B=v((nb, z.rA, L), BF16),
        r2C=v((nb, z.rC, L), BF16),
        r2V=v((nb, VROWS, 128), BF16),
        x_ss=dma((z.MB * z.S,)),
        x_rs=dma((nb,)),
        c_ss=dma((z.MB,)),
        c_rs=dma((z.MB,)),
        g1_ss=dma((4, nb)),
        g1_rs=dma((4, nb)),
        g2_ss=dma((4, dd, nb)),
        g2_rs=dma((4, dd, nb)),
        o_ss=dma((z.nh, H)),
        o_rs=dma((z.nh, H)),
        w_ss=dma((z.nh,)),
        w_rs=dma((z.nh,)),
        st_ss=dma((3, z.nh)),
        st_rs=dma((3, z.nh)),
        p_ss=dma((z.nh,)),
        p_rs=dma((z.nh,)),
        mo_ss=dma((z.MB,)),
        mo_rs=dma((z.MB,)),
        t_ss=dma((nb,)),
        t_rs=dma((z.MB * z.S,)),
        s1_ss=dma((4, dd, nb)),
        s1_rs=dma((4, dd, nb)),
        s2_ss=dma((4, nb)),
        s2_rs=dma((4, nb)),
    )


INPUTS = [
    "lens", "tok", "cot", "wq_in", "bq", "wk_in", "wv_in", "bv", "wo_in", "bo", "g1", "s1", "wup_in", "bu",
    "wdn_in", "bd", "g2", "s2",
]
OUTPUTS = ["o_mo", "o_tg", "o_A", "o_B", "o_C", "o_V"]


def main_kernel(z, names, *refs):
    k = types.SimpleNamespace(**dict(zip(names, refs)))
    nb, nd, nh, W, MB, R, C, F, Q, H, L, S = (
        z.nb, z.nd, z.nh, z.W, z.MB, z.R, z.C, z.F, z.Q, z.H, z.L, z.S,
    )
    b, d, h = lax.axis_index("blk"), lax.axis_index("dp"), lax.axis_index("head")
    w_me = b * nd + d
    team = b // z.tb
    m_t, d_t = team // nd, team % nd
    s_me = (b - team * z.tb) * nd + d
    D = nh * C
    hpeer = [lax.rem(h + i, nh) for i in range(nh)]
    hsrc = [lax.rem(h + nh - i, nh) for i in range(nh)]

    bar = pltpu.get_barrier_semaphore()
    for i in range(1, W):
        w = lax.rem(w_me + i, W)
        pl.semaphore_signal(bar, inc=1, device_id=(w // nd, w % nd, h), device_id_type=MESH)
    for i in range(1, nh):
        pl.semaphore_signal(bar, inc=1, device_id=(b, d, hpeer[i]), device_id_type=MESH)

    k.fst[...] = jnp.zeros_like(k.fst)
    k.fst[0 : z.r, 0:C] = k.wk_in[0].astype(F32)
    k.fst[0 : z.r, C:L] = k.wv_in[0].astype(F32)
    k.fst[z.rs : z.rs + z.r, 0:C] = k.wq_in[0].astype(F32)
    k.bufA[w_me] = k.fst[0 : z.rA].astype(BF16)
    k.fst[0 : z.r] = k.wup_in[0, :, 0:L].astype(F32)
    k.fst[z.rs : z.rs + z.r] = k.wup_in[0, :, L : 2 * L].astype(F32)
    k.bufB[w_me] = k.fst[0 : z.rA].astype(BF16)
    k.fst[0 : 4 * z.r, 0:C] = k.wo_in[...].astype(F32)
    k.fst[0 : 4 * z.r, C:L] = k.wdn_in[0].astype(F32)
    k.bufC[w_me] = k.fst[0 : z.rC].astype(BF16)
    k.vst[...] = jnp.zeros_like(k.vst)
    for j, ref in enumerate((k.bq, k.bv, k.bo, k.g1, k.s1, k.bd, k.g2, k.s2)):
        k.vst[j : j + 1, 0 : z.r] = ref[...].astype(F32)
    k.vst[V_BU : V_BU + 1, 0 : 4 * z.r] = k.bu[...].astype(F32)
    k.bufV[w_me] = k.vst[...].astype(BF16)

    pos = b * R + lax.broadcasted_iota(jnp.int32, (16, R), 1)
    row16 = lax.broadcasted_iota(jnp.int32, (16, R), 0)
    for m in range(MB):
        doc = jnp.zeros((16, R), jnp.int32)
        end = k.lens[m, 0, 0]
        for j in range(z.ND):
            if j > 0:
                end = end + k.lens[m, 0, j]
            doc = doc + (pos >= end).astype(jnp.int32)
        onehot = jnp.where(row16 == doc, 1.0, 0.0).astype(BF16)
        k.xs[m, 0:C] = k.tok[m].T
        k.xs[m, C : z.XR] = onehot
        k.cs[m] = k.cot[m].T

    pl.semaphore_wait(bar, W - 1 + nh - 1)

    def member(m, s):
        return (m * nd + d) * z.tb + s // nd, s % nd

    def x_send(m, s):
        bt, dt = member(m, s)
        return rcopy(k.xs.at[m], k.xb.at[b], k.x_ss.at[m * S + s], k.x_rs.at[b], (bt, dt, h))

    def not_me(pos):
        return jnp.logical_or(pos[0] != b, pos[1] != d)

    def is_me(pos):
        return jnp.logical_and(pos[0] == b, pos[1] == d)

    def start_x(i):
        m, s = i // S, i % S

        @pl.when(not_me(member(m, s)))
        def _():
            x_send(m, s).start()

        @pl.when(is_me(member(m, s)))
        def _():
            k.xb[b] = k.xs[m]

    loop(MB * S, start_x)

    bufs = (k.bufA, k.bufV, k.bufB, k.bufC)

    def g1(q, i):
        bt = lax.rem(b + i, nb)
        return rcopy(bufs[q].at[w_me], bufs[q].at[w_me], k.g1_ss.at[q, i], k.g1_rs.at[q, i], (bt, d, h))

    def g1_wait(q, i):
        src = lax.rem(b + nb - i, nb) * nd + d
        rcopy(bufs[q].at[src], bufs[q].at[src], k.g1_ss.at[q, i], k.g1_rs.at[q, i], (b, d, h)).wait_recv()

    def g2(q, e, i):
        src = lax.rem(b + nb - i, nb) * nd + d
        dt = lax.rem(d + e, nd)
        return rcopy(
            bufs[q].at[src], bufs[q].at[src], k.g2_ss.at[q, e - 1, i], k.g2_rs.at[q, e - 1, i], (b, dt, h)
        )

    def g2_wait(q, e, i):
        src = lax.rem(b + nb - i, nb) * nd + lax.rem(d + nd - e, nd)
        rcopy(
            bufs[q].at[src], bufs[q].at[src], k.g2_ss.at[q, e - 1, i], k.g2_rs.at[q, e - 1, i], (b, d, h)
        ).wait_recv()

    def gather_start(q):
        for e in range(1, nd):
            g2(q, e, 0).start()
        loop(nb - 1, lambda i: g1(q, i + 1).start())

    def gather_forward(q):
        def one(i):
            g1_wait(q, i + 1)
            for e in range(1, nd):
                g2(q, e, i + 1).start()

        loop(nb - 1, one)

    def gather_wait(q):
        for e in range(1, nd):
            loop(nb, lambda i: g2_wait(q, e, i))

    def gather_drain(q):
        loop(nb - 1, lambda i: g1(q, i + 1).wait_send())
        for e in range(1, nd):
            loop(nb, lambda i: g2(q, e, i).wait_send())

    gather_start(0)
    gather_start(1)

    own_s = b // MB

    def c_send(m):
        return rcopy(
            k.cs.at[m], k.cb.at[b % MB], k.c_ss.at[m], k.c_rs.at[b % MB], (*member(m, own_s), h)
        )

    for m in range(MB):

        @pl.when(not_me(member(m, own_s)))
        def _():
            c_send(m).start()

        @pl.when(is_me(member(m, own_s)))
        def _():
            k.cb[b % MB] = k.cs[m]

    gather_start(2)
    gather_start(3)
    gather_forward(0)
    gather_forward(1)
    gather_wait(0)
    gather_wait(1)

    for w in range(W):
        slab = k.bufA[w].astype(F32)
        k.fkv[w * z.r : w * z.r + z.rs] = slab[0 : z.rs]
        k.fq[w * z.r : w * z.r + z.rs] = slab[z.rs : 2 * z.rs]
    k.wkv[...] = k.fkv[0:C].astype(BF16)
    k.wkvt[...] = k.fkv[0:C].T.astype(BF16)
    k.wq[...] = k.fq[0:C, 0:C].astype(BF16)
    k.wqt[...] = k.fq[0:C, 0:C].T.astype(BF16)
    eye = (
        lax.broadcasted_iota(jnp.int32, (128, 128), 0) == lax.broadcasted_iota(jnp.int32, (128, 128), 1)
    ).astype(F32).astype(BF16)
    for w in range(W):
        col = mm_nt(eye, k.bufV[w])
        k.vcol[w * z.r : w * z.r + z.rs] = col[0 : z.rs]
        k.ucol[w * 4 * z.r : w * 4 * z.r + z.rC] = col[0 : z.rC]

    def vec(j):
        return k.vcol[0:C, j : j + 1]

    x_src_self = d == d_t
    feat_row = lax.broadcasted_iota(jnp.int32, (16, R), 0)

    def x_wait(j):
        @pl.when(jnp.logical_not(jnp.logical_and(x_src_self, j == b)))
        def _():
            rcopy(k.xb.at[j], k.xb.at[j], k.x_ss.at[0], k.x_rs.at[j], (b, d, h)).wait_recv()

    one_rows = jnp.where(feat_row < 2, 1.0, 0.0).astype(BF16)

    def kv_block(j):
        x_wait(j)
        kv = mm(k.wkvt[...], k.xb[j, 0:C])
        kb = kv[0:C].astype(BF16)
        vb = (kv[C:L] + vec(V_BV)).astype(BF16)
        hot = k.xb[j, C : z.XR].astype(F32)
        kf = jnp.where(feat_row < z.ND, (hot - 1.0) * BIG, 0.0).astype(BF16)
        pad = jnp.zeros((48, R), BF16)
        for a in range(H):
            kh, vh = kb[a * HEAD_DIM : (a + 1) * HEAD_DIM], vb[a * HEAD_DIM : (a + 1) * HEAD_DIM]
            k.kx[j, a] = kh
            k.vx[j, a, 0:HEAD_DIM] = vh
            k.vx[j, a, HEAD_DIM:] = one_rows
            k.kt[j, a] = jnp.concatenate([kh, kf, pad], axis=0).T
            k.vt[j, a] = jnp.concatenate([vh, one_rows, pad], axis=0).T

    loop(nb, kv_block)

    for i in range(MB):
        xi = k.xb[s_me * MB + i]
        k.xq[:, i * R : (i + 1) * R] = xi[0:C]
        qi = ((mm(k.wqt[...], xi[0:C]) + vec(V_BQ)).astype(BF16).astype(F32) * HEAD_DIM**-0.5).astype(BF16)
        pad = jnp.zeros((48, R), BF16)
        for a in range(H):
            full = jnp.concatenate([qi[a * HEAD_DIM : (a + 1) * HEAD_DIM], xi[C : z.XR], pad], axis=0)
            k.qx[a, :, i * R : (i + 1) * R] = full
            k.qt[a, i * R : (i + 1) * R, :] = full.T

    def o_send(i, a):
        part = pl.ds(a * HEAD_DIM, HEAD_DIM)
        return rcopy(
            k.oall.at[h, part], k.oall.at[h, part], k.o_ss.at[i, a], k.o_rs.at[i, a], (b, d, hpeer[i])
        )

    def o_wait(i, a):
        part = pl.ds(a * HEAD_DIM, HEAD_DIM)
        rcopy(
            k.oall.at[hsrc[i], part], k.oall.at[hsrc[i], part], k.o_ss.at[i, a], k.o_rs.at[i, a], (b, d, h)
        ).wait_recv()

    def scores(a, j):
        return mm(k.kt[j, a], k.qx[a])

    def prob(a, j):
        if z.keep:
            return k.pbuf[a, j]
        return jnp.exp(scores(a, j) - k.mrow[a, 0:1]).astype(BF16)

    for a in range(H):
        k.mrow[a] = jnp.full((8, Q), -3e38, F32)

        def top(j):
            s = scores(a, j)
            if z.keep:
                k.sbuf[j] = s
            k.mrow[a, 0:1] = jnp.maximum(k.mrow[a, 0:1], jnp.max(s, axis=0, keepdims=True))

        loop(nb, top)
        acc_ref = k.dqacc
        k.mrow[a, 1:2] = jnp.zeros((1, Q), F32)
        acc_ref[a] = jnp.zeros((HEAD_DIM, Q), F32)

        def weigh(j):
            if z.keep:
                k.pbuf[a, j] = jnp.exp(k.sbuf[j] - k.mrow[a, 0:1]).astype(BF16)
            o = mm(k.vx[j, a], prob(a, j))
            acc_ref[a] += o[0:HEAD_DIM]
            k.mrow[a, 1:2] += o[HEAD_DIM : HEAD_DIM + 1]

        loop(nb, weigh)
        inv = 1.0 / k.mrow[a, 1:2]
        k.mrow[a, 2:3] = inv
        k.oall[h, a * HEAD_DIM : (a + 1) * HEAD_DIM] = (acc_ref[a] * inv).astype(BF16)
        for i in range(1, nh):
            o_send(i, a).start()
        if a == 0:
            gather_forward(2)
        if a == 1:
            gather_forward(3)

    gather_wait(3)
    for w in range(W):
        k.fod[w * 4 * z.r : w * 4 * z.r + z.rC] = k.bufC[w].astype(F32)
    for j in range(nh):
        k.wo[j] = k.fod[j * C : (j + 1) * C, 0:C].astype(BF16)
    k.wot[...] = k.fod[0:F, 0:C].T.astype(BF16)
    k.wdn[...] = k.fod[0:F, C:L].astype(BF16)
    k.wdnt[...] = k.fod[0:F, C:L].T.astype(BF16)

    def w_send(i):
        return rcopy(k.wo.at[hpeer[i]], k.wor.at[h], k.w_ss.at[i], k.w_rs.at[i], (b, d, hpeer[i]))

    for i in range(1, nh):
        w_send(i).start()
    k.wor[h] = k.wo[h]
    gather_wait(2)
    for w in range(W):
        slab = k.bufB[w].astype(F32)
        k.fup[w * z.r : w * z.r + z.rs, 0:L] = slab[0 : z.rs]
        k.fup[w * z.r : w * z.r + z.rs, L:F] = slab[z.rs : 2 * z.rs]
    k.wup[...] = k.fup[0:C].astype(BF16)
    k.wupt[...] = k.fup[0:C].T.astype(BF16)

    for i in range(1, nh):
        for a in range(H):
            o_wait(i, a)
    o_full = k.oall[...].reshape(D, Q)
    h1 = k.xq[...].astype(F32) + mm(k.wot[...], o_full) + vec(V_BO)

    def st_send(e, i):
        return rcopy(
            k.stats.at[e, h], k.stats.at[e, h], k.st_ss.at[e, i], k.st_rs.at[e, i], (b, d, hpeer[i])
        )

    def reduce_start(e, rows):
        k.stats[e, h] = jnp.zeros((8, Q), F32)
        for j, v in enumerate(rows):
            k.stats[e, h, j : j + 1] = jnp.sum(v, axis=0, keepdims=True)
        for i in range(1, nh):
            st_send(e, i).start()

    def reduce_end(e):
        for i in range(1, nh):
            src = hsrc[i]
            rcopy(
                k.stats.at[e, src], k.stats.at[e, src], k.st_ss.at[e, i], k.st_rs.at[e, i], (b, d, h)
            ).wait_recv()
        total = k.stats[e, 0]
        for j in range(1, nh):
            total = total + k.stats[e, j]
        return total / D

    reduce_start(0, (h1, h1 * h1))
    tot = reduce_end(0)
    mu1 = tot[0:1]
    r1 = lax.rsqrt(tot[1:2] - mu1 * mu1 + EPS)
    n1 = (h1 - mu1) * r1
    y1 = n1 * vec(V_G1) + vec(V_S1)
    y1b = y1.astype(BF16)

    ub = k.ucol[0:F, V_BU : V_BU + 1]
    u = mm(k.wupt[...], y1b) + ub
    k.u[...] = u
    act = (0.5 * u * (1.0 + lax.erf(u * (0.5**0.5)))).astype(BF16)
    k.act[...] = act
    h2 = y1 + mm(k.wdnt[...], act) + vec(V_BD)

    for i in range(MB):

        @pl.when(jnp.logical_not(jnp.logical_and(x_src_self, s_me * MB + i == b)))
        def _():
            rcopy(k.cb.at[i], k.cb.at[i], k.c_ss.at[i], k.c_rs.at[i], (b, d, h)).wait_recv()

    g = jnp.concatenate([k.cb[i] for i in range(MB)], axis=1).astype(F32)
    dn2 = g * vec(V_G2)
    reduce_start(1, (h2, h2 * h2, dn2, dn2 * h2))
    uu = k.u[...]
    k.u[...] = 0.5 * (1.0 + lax.erf(uu * (0.5**0.5))) + uu * jnp.exp(-0.5 * uu * uu) * ((2 * jnp.pi) ** -0.5)
    tot = reduce_end(1)
    mu2 = tot[0:1]
    r2 = lax.rsqrt(tot[1:2] - mu2 * mu2 + EPS)
    n2 = (h2 - mu2) * r2
    out = (n2 * vec(V_G2) + vec(V_S2)).astype(BF16)
    for i in range(MB):
        k.mo[i] = out[:, i * R : (i + 1) * R]

    def mo_dst(i):
        return s_me * MB + i, d_t

    def mo_send(i):
        return rcopy(k.mo.at[i], k.o_mo.at[m_t], k.mo_ss.at[i], k.mo_rs.at[m_t], (*mo_dst(i), h))

    for i in range(MB):

        @pl.when(not_me(mo_dst(i)))
        def _():
            mo_send(i).start()

        @pl.when(is_me(mo_dst(i)))
        def _():
            k.o_mo[m_t] = k.mo[i]

    dh2 = r2 * (dn2 - tot[2:3] - n2 * (r2 * (tot[3:4] - mu2 * tot[2:3])))
    dz = dh2.astype(BF16)
    ones = jnp.ones((16, Q), BF16)

    def vec_grad(j, x):
        k.vg[j : j + 1] = mm_nt(ones, x)[0:1]

    k.vg[...] = jnp.zeros_like(k.vg)
    k.vgu[...] = jnp.zeros_like(k.vgu)
    vec_grad(V_G2, (g * n2).astype(BF16))
    vec_grad(V_S2, g.astype(BF16))
    vec_grad(V_BD, dz)

    du = (mm(k.wdn[...], dz) * k.u[...]).astype(BF16)
    k.du[...] = du
    dy1 = dh2 + mm(k.wup[...], du)
    dn1 = dy1 * vec(V_G1)
    reduce_start(2, (dn1, dn1 * n1))
    k.god[0:F, C:L] = mm_nt(k.act[...], dz)
    k.gup[0:C] = mm_nt(y1b, k.du[...])
    k.vgu[V_BU : V_BU + 1] = mm_nt(ones, k.du[...])[0:1]
    vec_grad(V_G1, (dy1 * n1).astype(BF16))
    vec_grad(V_S1, dy1.astype(BF16))
    tot = reduce_end(2)
    dh1 = r1 * (dn1 - tot[0:1] - n1 * tot[1:2])
    dp = dh1.astype(BF16)
    k.pall[h] = dp

    def p_send(i):
        return rcopy(k.pall.at[h], k.pall.at[h], k.p_ss.at[i], k.p_rs.at[i], (b, d, hpeer[i]))

    for i in range(1, nh):
        p_send(i).start()

    k.god[0:F, 0:C] = mm_nt(o_full, dp)
    vec_grad(V_BO, dp)
    for w in range(W):
        k.pB[w] = jnp.concatenate(
            [k.gup[w * z.r : w * z.r + z.rs, 0:L], k.gup[w * z.r : w * z.r + z.rs, L:F]]
            + ([jnp.zeros((z.rA - 2 * z.rs, L), F32)] if z.rA > 2 * z.rs else []),
            axis=0,
        ).astype(BF16)
        k.pC[w] = k.god[w * 4 * z.r : w * 4 * z.r + z.rC].astype(BF16)

    packs = (k.pA, k.pV, k.pB, k.pC)
    firsts = (k.r1A, k.r1V, k.r1B, k.r1C)
    seconds = (k.s2A, k.s2V, k.s2B, k.s2C)
    lasts = (k.r2A, k.r2V, k.r2B, k.r2C)
    sums = (k.o_A, k.o_V, k.o_B, k.o_C)

    def s1_send(q, e, i):
        dt = lax.rem(d + e, nd)
        return rcopy(
            packs[q].at[i * nd + dt], firsts[q].at[e - 1, i], k.s1_ss.at[q, e - 1, i], k.s1_rs.at[q, e - 1, i],
            (b, dt, h),
        )

    def s2_send(q, i):
        bt = lax.rem(b + i, nb)
        return rcopy(
            seconds[q].at[bt], lasts[q].at[b], k.s2_ss.at[q, i], k.s2_rs.at[q, i], (bt, d, h)
        )

    def scatter_start(q):
        for e in range(1, nd):
            loop(nb, lambda i: s1_send(q, e, i).start())

    def scatter_forward(q):
        def one(i):
            bt = lax.rem(b + i, nb)
            part = packs[q][bt * nd + d].astype(F32)
            for e in range(1, nd):
                rcopy(
                    firsts[q].at[e - 1, bt], firsts[q].at[e - 1, bt], k.s1_ss.at[q, e - 1, bt],
                    k.s1_rs.at[q, e - 1, bt], (b, d, h),
                ).wait_recv()
                part = part + firsts[q][e - 1, bt].astype(F32)
            return bt, part

        def send(i):
            bt, part = one(i)
            seconds[q][bt] = part.astype(BF16)
            s2_send(q, i).start()

        loop(nb - 1, lambda i: send(i + 1))
        sums[q][...] = one(0)[1]

    def scatter_end(q):
        def one(i):
            src = lax.rem(b + nb - i, nb)
            rcopy(
                lasts[q].at[src], lasts[q].at[src], k.s2_ss.at[q, i], k.s2_rs.at[q, i], (b, d, h)
            ).wait_recv()
            sums[q][...] += lasts[q][src].astype(F32)

        loop(nb - 1, lambda i: one(i + 1))
        loop(nb - 1, lambda i: s2_send(q, i + 1).wait_send())
        for e in range(1, nd):
            loop(nb, lambda i: s1_send(q, e, i).wait_send())

    scatter_start(2)
    scatter_start(3)

    for i in range(1, nh):
        src = hsrc[i]
        rcopy(k.wor.at[src], k.wor.at[src], k.w_ss.at[i], k.w_rs.at[i], (b, d, h)).wait_recv()
        rcopy(k.pall.at[src], k.pall.at[src], k.p_ss.at[i], k.p_rs.at[i], (b, d, h)).wait_recv()
    do = mm(k.wor[0], k.pall[0])
    for j in range(1, nh):
        do = do + mm(k.wor[j], k.pall[j])
    do = do.astype(BF16).astype(F32)
    row16q = lax.broadcasted_iota(jnp.int32, (16, Q), 0)
    for a in range(H):
        part = do[a * HEAD_DIM : (a + 1) * HEAD_DIM] * k.mrow[a, 2:3]
        own = k.oall[h, a * HEAD_DIM : (a + 1) * HEAD_DIM].astype(F32)
        delta = jnp.sum(part * own, axis=0, keepdims=True)
        hi = delta.astype(BF16).astype(F32)
        tail = jnp.where(row16q == 0, -hi, jnp.where(row16q == 1, hi - delta, 0.0))
        full = jnp.concatenate([part.astype(BF16), tail.astype(BF16), jnp.zeros((48, Q), BF16)], axis=0)
        k.dox[a] = full
        k.dot[a] = full.T
        k.dqacc[a] = jnp.zeros((HEAD_DIM, Q), F32)

    k.gkv[...] = jnp.zeros_like(k.gkv)
    k.gq[...] = jnp.zeros_like(k.gq)

    def back_block(j):
        for a in range(H):
            p = prob(a, j)
            ds = (p.astype(F32) * mm(k.vt[j, a], k.dox[a])).astype(BF16)
            k.dqacc[a] += mm(k.kx[j, a], ds)
            dk = mm(ds, k.qt[a])
            dv = mm(p, k.dot[a])
            k.dkv[a * HEAD_DIM : (a + 1) * HEAD_DIM] = dk.T[0:HEAD_DIM].astype(BF16)
            k.dkv[C + a * HEAD_DIM : C + (a + 1) * HEAD_DIM] = dv.T[0:HEAD_DIM].astype(BF16)
        dkv = k.dkv[...]
        k.gkv[0:C] += mm_nt(k.xb[j, 0:C], dkv)
        k.tgs[j] = mm(k.wkv[...], dkv).astype(BF16)
        k.vg[V_BV : V_BV + 1] += mm_nt(ones[:, 0:R], dkv[C:L])[0:1]

    loop(nb, back_block)
    scatter_forward(2)
    scatter_forward(3)

    for a in range(H):
        k.dq[a * HEAD_DIM : (a + 1) * HEAD_DIM] = (k.dqacc[a] * HEAD_DIM**-0.5).astype(BF16)
    dq = k.dq[...]
    k.gq[0:C, 0:C] = mm_nt(k.xq[...], dq)
    vec_grad(V_BQ, dq)
    own = dh1 + mm(k.wq[...], dq)
    for i in range(MB):
        j = s_me * MB + i
        k.tgs[j] = (k.tgs[j].astype(F32) + own[:, i * R : (i + 1) * R]).astype(BF16)

    def t_send(j):
        return rcopy(
            k.tgs.at[j], k.o_tg.at[m_t * S + s_me], k.t_ss.at[j], k.t_rs.at[m_t * S + s_me], (j, d_t, h)
        )

    def t_start(j):
        @pl.when(not_me((j, d_t)))
        def _():
            t_send(j).start()

        @pl.when(is_me((j, d_t)))
        def _():
            k.o_tg[m_t * S + s_me] = k.tgs[j]

    loop(nb, t_start)

    for w in range(W):
        k.pA[w] = jnp.concatenate(
            [k.gkv[w * z.r : w * z.r + z.rs], k.gq[w * z.r : w * z.r + z.rs]]
            + ([jnp.zeros((z.rA - 2 * z.rs, L), F32)] if z.rA > 2 * z.rs else []),
            axis=0,
        ).astype(BF16)
    vgb, vgub = k.vg[...].astype(BF16), k.vgu[...].astype(BF16)

    def pack_v(w):
        def pick(n, per):
            i = lax.broadcasted_iota(jnp.int32, (n, 128), 0)
            j = lax.broadcasted_iota(jnp.int32, (n, 128), 1)
            return jnp.where(jnp.logical_and(i == w * per + j, j < per), 1.0, 0.0).astype(BF16)

        k.pV[w] = (mm(vgb, pick(C, z.r)) + mm(vgub, pick(F, 4 * z.r))).astype(BF16)

    loop(W, pack_v)
    scatter_start(0)
    scatter_start(1)
    scatter_forward(0)
    scatter_forward(1)

    for q in (2, 3, 0, 1):
        scatter_end(q)

    def t_wait(i):
        m, s = i // S, i % S

        @pl.when(not_me(member(m, s)))
        def _():
            rcopy(k.o_tg.at[i], k.o_tg.at[i], k.t_ss.at[0], k.t_rs.at[i], (b, d, h)).wait_recv()

    loop(MB * S, t_wait)

    def t_drain(j):
        @pl.when(not_me((j, d_t)))
        def _():
            t_send(j).wait_send()

    loop(nb, t_drain)
    for m in range(MB):

        @pl.when(not_me(member(m, own_s)))
        def _():
            rcopy(k.o_mo.at[m], k.o_mo.at[m], k.mo_ss.at[m], k.mo_rs.at[m], (b, d, h)).wait_recv()
            c_send(m).wait_send()

    for i in range(MB):

        @pl.when(not_me(mo_dst(i)))
        def _():
            mo_send(i).wait_send()

    def x_drain(i):
        m, s = i // S, i % S

        @pl.when(not_me(member(m, s)))
        def _():
            x_send(m, s).wait_send()

    loop(MB * S, x_drain)
    for q in range(4):
        gather_drain(q)
    for i in range(1, nh):
        for a in range(H):
            o_send(i, a).wait_send()
        w_send(i).wait_send()
        p_send(i).wait_send()
        for e in range(3):
            st_send(e, i).wait_send()


def finish_kernel(z, mo, tg, gA, gB, gC, gV, *outs):
    (mixed, dtok, dwq, dbq, dwk, dwv, dbv, dwo, dbo, dg1, ds1, dwup, dbu, dwdn, dbd, dg2, ds2) = outs
    r, rs, C, L, S = z.r, z.rs, z.C, z.L, z.S
    for m in range(z.MB):
        mixed[m] = mo[m].T
        total = tg[m * S].astype(F32)
        for s in range(1, S):
            total = total + tg[m * S + s].astype(F32)
        dtok[m] = total.T
    dwk[0] = gA[0:r, 0:C]
    dwv[0] = gA[0:r, C:L]
    dwq[0] = gA[rs : rs + r, 0:C]
    dwup[0, :, 0:L] = gB[0:r]
    dwup[0, :, L : 2 * L] = gB[rs : rs + r]
    dwo[...] = gC[0 : 4 * r, 0:C]
    dwdn[0] = gC[0 : 4 * r, C:L]
    for j, ref in enumerate((dbq, dbv, dbo, dg1, ds1, dbd, dg2, ds2)):
        ref[...] = gV[j : j + 1, 0:r]
    dbu[...] = gV[V_BU : V_BU + 1, 0 : 4 * r]


def solution(mesh):
    vec_spec = P("head", ("blk", "dp"))
    mat_spec = P("head", ("blk", "dp"), None)
    tok_spec = P(None, "dp", "head", "blk")
    out_spec = P(("blk", "dp"), "head")

    def body(
        tokens, doc_lengths, cotangent, query_weight, query_bias, key_weight, value_weight, value_bias,
        out_weight, out_bias, first_gain, first_shift, up_weight, up_bias, down_weight, down_bias,
        second_gain, second_shift,
    ):
        z = Sizes(mesh, tokens, query_weight, up_weight, doc_lengths)
        scratch = main_scratch(z)
        vmem = pl.BlockSpec(memory_space=pltpu.VMEM)
        smem = pl.BlockSpec(memory_space=pltpu.SMEM)
        names = INPUTS + OUTPUTS + list(scratch)
        sds = jax.ShapeDtypeStruct
        parts = pl.pallas_call(
            lambda *refs: main_kernel(z, names, *refs),
            out_shape=[
                sds((z.MB, z.C, z.R), BF16),
                sds((z.MB * z.S, z.C, z.R), BF16),
                sds((z.rA, z.L), F32),
                sds((z.rA, z.L), F32),
                sds((z.rC, z.L), F32),
                sds((VROWS, 128), F32),
            ],
            in_specs=[smem] + [vmem] * (len(INPUTS) - 1),
            out_specs=[vmem] * len(OUTPUTS),
            scratch_shapes=list(scratch.values()),
            compiler_params=pltpu.CompilerParams(
                collective_id=0, has_side_effects=True, vmem_limit_bytes=63 << 20
            ),
            name="layer",
        )(
            doc_lengths, tokens.reshape(z.MB, z.R, z.C), cotangent.reshape(z.MB, z.R, z.C), query_weight,
            query_bias, key_weight, value_weight, value_bias, out_weight, out_bias, first_gain, first_shift,
            up_weight, up_bias, down_weight, down_bias, second_gain, second_shift,
        )
        mat, vec = sds((1, z.r, z.C), F32), sds((1, z.r), F32)
        outs = pl.pallas_call(
            lambda *refs: finish_kernel(z, *refs),
            out_shape=[
                sds((z.MB, z.R, z.C), BF16), sds((z.MB, z.R, z.C), F32), mat, vec, mat, mat, vec,
                sds((4 * z.r, z.C), F32), vec, vec, vec, sds((1, z.r, z.F), F32), sds((1, 4 * z.r), F32),
                sds((1, 4 * z.r, z.C), F32), vec, vec, vec,
            ],
            in_specs=[vmem] * len(OUTPUTS),
            out_specs=[vmem] * 17,
            name="finish",
        )(*parts)
        shape = tokens.shape
        return (outs[0].reshape(shape), outs[1].reshape(shape), *outs[2:])

    return jax.shard_map(
        body,
        mesh=mesh,
        in_specs=(
            tok_spec, P(None, "dp", None), tok_spec, mat_spec, vec_spec, mat_spec, mat_spec, vec_spec,
            out_spec, vec_spec, vec_spec, vec_spec, mat_spec, vec_spec, mat_spec, vec_spec, vec_spec, vec_spec,
        ),
        out_specs=(
            tok_spec, tok_spec, mat_spec, vec_spec, mat_spec, mat_spec, vec_spec, out_spec, vec_spec, vec_spec,
            vec_spec, mat_spec, vec_spec, mat_spec, vec_spec, vec_spec, vec_spec,
        ),
        check_vma=False,
    )
```

```python
import types

import jax
import jax.numpy as jnp
from jax import lax
from jax.experimental import pallas as pl
from jax.experimental.pallas import tpu as pltpu
from jax.sharding import PartitionSpec as P

HEAD_DIM = 64
EPS = 1e-05
BIG = 1e30
MESH = pl.DeviceIdType.MESH
F32 = jnp.float32
BF16 = jnp.bfloat16
V_BQ, V_BV, V_BO, V_G1, V_S1, V_BD, V_G2, V_S2, V_BU = range(9)
VROWS = 16


def up_to(n, m):
    return (n + m - 1) // m * m


def mm(a, b):
    return lax.dot_general(a, b, (((1,), (0,)), ((), ())), preferred_element_type=F32)


def mm_nt(a, b):
    return lax.dot_general(a, b, (((1,), (1,)), ((), ())), preferred_element_type=F32)


def loop(n, fn):
    if n <= 8:
        for i in range(n):
            fn(i)
    else:
        lax.fori_loop(0, n, lambda i, c: (fn(i), c)[1], 0)


def rcopy(src, dst, ss, rs, dev):
    return pltpu.make_async_remote_copy(
        src_ref=src, dst_ref=dst, send_sem=ss, recv_sem=rs, device_id=dev, device_id_type=MESH
    )


class Sizes:
    def __init__(self, mesh, tokens, query_weight, up_weight, doc_lengths):
        self.nb, self.nd, self.nh = mesh.shape["blk"], mesh.shape["dp"], mesh.shape["head"]
        self.W = self.nb * self.nd
        self.C, self.F = query_weight.shape[2], up_weight.shape[2]
        self.MB = tokens.shape[0]
        self.R = tokens.shape[3] // self.C
        self.S = self.nb // self.MB
        self.tb = self.nb // (self.MB * self.nd)
        self.Q = self.MB * self.R
        self.H = self.C // HEAD_DIM
        self.ND = doc_lengths.shape[2]
        self.r = query_weight.shape[1]
        self.rs = up_to(self.r, 8)
        self.rA = up_to(2 * self.rs, 16)
        self.rC = up_to(4 * self.r, 16)
        self.L = 2 * self.C
        self.XR = self.C + 16
        self.keep = self.nb * self.R * self.Q * self.H * 2 <= (8 << 20)
        assert self.F == 4 * self.C and self.F == self.nh * self.C


def main_scratch(z):
    dma = pltpu.SemaphoreType.DMA
    v = pltpu.VMEM
    nb, W, L, R, C, F, Q, H = z.nb, z.W, z.L, z.R, z.C, z.F, z.Q, z.H
    dd = max(z.nd - 1, 1)
    return dict(
        xs=v((z.MB, z.XR, R), BF16),
        xb=v((nb, z.XR, R), BF16),
        cs=v((z.MB, C, R), BF16),
        cb=v((z.MB, C, R), BF16),
        bufA=v((W, z.rA, L), BF16),
        bufB=v((W, z.rA, L), BF16),
        bufC=v((W, z.rC, L), BF16),
        bufV=v((W, VROWS, 128), BF16),
        fst=v((max(z.rA, z.rC), L), F32),
        vst=v((VROWS, 128), F32),
        fkv=v((C + 8, L), F32),
        fq=v((C + 8, L), F32),
        fup=v((C + 8, F), F32),
        fod=v((F + 16, L), F32),
        vcol=v((C + 8, 16), F32),
        ucol=v((F + 16, 16), F32),
        wkv=v((C, L), BF16),
        wkvt=v((L, C), BF16),
        wq=v((C, C), BF16),
        wqt=v((C, C), BF16),
        wup=v((C, F), BF16),
        wupt=v((F, C), BF16),
        wo=v((z.nh, C, C), BF16),
        wor=v((z.nh, C, C), BF16),
        wot=v((C, F), BF16),
        wdn=v((F, C), BF16),
        wdnt=v((C, F), BF16),
        xq=v((C, Q), BF16),
        qx=v((H, 128, Q), BF16),
        qt=v((H, Q, 128), BF16),
        kx=v((nb, H, HEAD_DIM, R), BF16),
        vx=v((nb, H, HEAD_DIM + 16, R), BF16),
        kt=v((nb, H, R, 128), BF16),
        vt=v((nb, H, R, 128), BF16),
        sbuf=v((nb if z.keep else 1, R, Q), F32),
        pbuf=v((H, nb if z.keep else 1, R, Q), BF16),
        mrow=v((H, 8, Q), F32),
        oall=v((z.nh, C, Q), BF16),
        pall=v((z.nh, C, Q), BF16),
        stats=v((3, z.nh, 4 * Q // 128, 128), F32),
        u=v((F, Q), F32),
        act=v((F, Q), BF16),
        du=v((F, Q), BF16),
        mo=v((z.MB, C, R), BF16),
        dox=v((H, 128, Q), BF16),
        dot=v((H, Q, 128), BF16),
        dqacc=v((H, HEAD_DIM, Q), F32),
        dkv=v((L, R), BF16),
        dq=v((C, Q), BF16),
        tgs=v((nb, C, R), BF16),
        tgo=v((z.MB, C, R), F32),
        tgr=v((z.MB, z.S, C, R), BF16),
        tgx=v((z.MB, C, R), BF16),
        gkv=v((C + 8, L), F32),
        gq=v((C + 8, L), F32),
        gup=v((C + 8, F), F32),
        god=v((F + 16, L), F32),
        vg=v((VROWS, C), F32),
        vgu=v((VROWS, F), F32),
        pA=v((W, z.rA, L), BF16),
        pB=v((W, z.rA, L), BF16),
        pC=v((W, z.rC, L), BF16),
        pV=v((W, VROWS, 128), BF16),
        r1A=v((dd, nb, z.rA, L), BF16),
        r1B=v((dd, nb, z.rA, L), BF16),
        r1C=v((dd, nb, z.rC, L), BF16),
        r1V=v((dd, nb, VROWS, 128), BF16),
        s2A=v((nb, z.rA, L), BF16),
        s2B=v((nb, z.rA, L), BF16),
        s2C=v((nb, z.rC, L), BF16),
        s2V=v((nb, VROWS, 128), BF16),
        r2A=v((nb, z.rA, L), BF16),
        r2B=v((nb, z.rA, L), BF16),
        r2C=v((nb, z.rC, L), BF16),
        r2V=v((nb, VROWS, 128), BF16),
        x_ss=dma((z.MB,)),
        xf_ss=dma((z.MB, z.S)),
        x_rs=dma((nb,)),
        c_ss=dma((z.MB,)),
        c_rs=dma((z.MB,)),
        g1_ss=dma((4, nb)),
        g1_rs=dma((4, nb)),
        g2_ss=dma((4, dd, nb)),
        g2_rs=dma((4, dd, nb)),
        o_ss=dma((z.nh, H)),
        o_rs=dma((z.nh, H)),
        w_ss=dma((z.nh,)),
        w_rs=dma((z.nh,)),
        st_ss=dma((3, z.nh)),
        st_rs=dma((3, z.nh)),
        p_ss=dma((z.nh, H)),
        p_rs=dma((z.nh, H)),
        mo_ss=dma((z.MB,)),
        mo_rs=dma((z.MB,)),
        tp_ss=dma((nb,)),
        tp_rs=dma((z.MB, z.S)),
        t_ss=dma((z.MB,)),
        t_rs=dma((z.MB,)),
        s1_ss=dma((4, dd, nb)),
        s1_rs=dma((4, dd, nb)),
        s2_ss=dma((4, nb)),
        s2_rs=dma((4, nb)),
    )


INPUTS = [
    "lens", "tok", "cot", "wq_in", "bq", "wk_in", "wv_in", "bv", "wo_in", "bo", "g1", "s1", "wup_in", "bu",
    "wdn_in", "bd", "g2", "s2",
]
OUTPUTS = ["o_mo", "o_tg", "o_A", "o_B", "o_C", "o_V"]


def main_kernel(z, names, *refs):
    k = types.SimpleNamespace(**dict(zip(names, refs)))
    nb, nd, nh, W, MB, R, C, F, Q, H, L, S = (
        z.nb, z.nd, z.nh, z.W, z.MB, z.R, z.C, z.F, z.Q, z.H, z.L, z.S,
    )
    b, d, h = lax.axis_index("blk"), lax.axis_index("dp"), lax.axis_index("head")
    w_me = b * nd + d
    team = b // z.tb
    m_t, d_t = team // nd, team % nd
    s_me = (b - team * z.tb) * nd + d
    D = nh * C
    hpeer = [lax.rem(h + i, nh) for i in range(nh)]
    hsrc = [lax.rem(h + nh - i, nh) for i in range(nh)]

    bar = pltpu.get_barrier_semaphore()
    for i in range(1, W):
        w = lax.rem(w_me + i, W)
        pl.semaphore_signal(bar, inc=1, device_id=(w // nd, w % nd, h), device_id_type=MESH)
    for i in range(1, nh):
        pl.semaphore_signal(bar, inc=1, device_id=(b, d, hpeer[i]), device_id_type=MESH)

    k.fst[...] = jnp.zeros_like(k.fst)
    k.fst[0 : z.r, 0:C] = k.wk_in[0].astype(F32)
    k.fst[0 : z.r, C:L] = k.wv_in[0].astype(F32)
    k.fst[z.rs : z.rs + z.r, 0:C] = k.wq_in[0].astype(F32)
    k.bufA[w_me] = k.fst[0 : z.rA].astype(BF16)
    k.fst[0 : z.r] = k.wup_in[0, :, 0:L].astype(F32)
    k.fst[z.rs : z.rs + z.r] = k.wup_in[0, :, L : 2 * L].astype(F32)
    k.bufB[w_me] = k.fst[0 : z.rA].astype(BF16)
    k.fst[0 : 4 * z.r, 0:C] = k.wo_in[...].astype(F32)
    k.fst[0 : 4 * z.r, C:L] = k.wdn_in[0].astype(F32)
    k.bufC[w_me] = k.fst[0 : z.rC].astype(BF16)
    k.vst[...] = jnp.zeros_like(k.vst)
    for j, ref in enumerate((k.bq, k.bv, k.bo, k.g1, k.s1, k.bd, k.g2, k.s2)):
        k.vst[j : j + 1, 0 : z.r] = ref[...].astype(F32)
    k.vst[V_BU : V_BU + 1, 0 : 4 * z.r] = k.bu[...].astype(F32)
    k.bufV[w_me] = k.vst[...].astype(BF16)

    pos = b * R + lax.broadcasted_iota(jnp.int32, (16, R), 1)
    row16 = lax.broadcasted_iota(jnp.int32, (16, R), 0)
    for m in range(MB):
        doc = jnp.zeros((16, R), jnp.int32)
        end = k.lens[m, 0, 0]
        for j in range(z.ND):
            if j > 0:
                end = end + k.lens[m, 0, j]
            doc = doc + (pos >= end).astype(jnp.int32)
        onehot = jnp.where(row16 == doc, 1.0, 0.0).astype(BF16)
        k.xs[m, 0:C] = k.tok[m].T
        k.xs[m, C : z.XR] = onehot
        k.cs[m] = k.cot[m].T

    pl.semaphore_wait(bar, W - 1 + nh - 1)

    def member(m, s):
        return (m * nd + d) * z.tb + s // nd, s % nd

    def mate(s):
        return team * z.tb + s // nd, s % nd

    def not_me(pos):
        return jnp.logical_or(pos[0] != b, pos[1] != d)

    def is_me(pos):
        return jnp.logical_and(pos[0] == b, pos[1] == d)

    own_s, own_i = b % S, b // S
    mine = [i * S + s_me for i in range(MB)]

    def x_send(m):
        return rcopy(k.xs.at[m], k.xb.at[b], k.x_ss.at[m], k.x_rs.at[b], (*member(m, own_s), h))

    def x_pass(i, e):
        to = mate(lax.rem(s_me + e, S))
        return rcopy(k.xb.at[mine[i]], k.xb.at[mine[i]], k.xf_ss.at[i, e], k.x_rs.at[mine[i]], (*to, h))

    def x_wait(j):
        rcopy(k.xb.at[j], k.xb.at[j], k.x_ss.at[0], k.x_rs.at[j], (b, d, h)).wait_recv()

    def from_me(i):
        return jnp.logical_and(d == d_t, mine[i] == b)

    for m in range(MB):

        @pl.when(not_me(member(m, own_s)))
        def _():
            x_send(m).start()

        @pl.when(is_me(member(m, own_s)))
        def _():
            k.xb[b] = k.xs[m]

    bufs = (k.bufA, k.bufV, k.bufB, k.bufC)

    def g1(q, i):
        bt = lax.rem(b + i, nb)
        return rcopy(bufs[q].at[w_me], bufs[q].at[w_me], k.g1_ss.at[q, i], k.g1_rs.at[q, i], (bt, d, h))

    def g1_wait(q, i):
        src = lax.rem(b + nb - i, nb) * nd + d
        rcopy(bufs[q].at[src], bufs[q].at[src], k.g1_ss.at[q, i], k.g1_rs.at[q, i], (b, d, h)).wait_recv()

    def g2(q, e, i):
        src = lax.rem(b + nb - i, nb) * nd + d
        dt = lax.rem(d + e, nd)
        return rcopy(
            bufs[q].at[src], bufs[q].at[src], k.g2_ss.at[q, e - 1, i], k.g2_rs.at[q, e - 1, i], (b, dt, h)
        )

    def g2_wait(q, e, i):
        src = lax.rem(b + nb - i, nb) * nd + lax.rem(d + nd - e, nd)
        rcopy(
            bufs[q].at[src], bufs[q].at[src], k.g2_ss.at[q, e - 1, i], k.g2_rs.at[q, e - 1, i], (b, d, h)
        ).wait_recv()

    def gather_start(q):
        for e in range(1, nd):
            g2(q, e, 0).start()
        loop(nb - 1, lambda i: g1(q, i + 1).start())

    def gather_forward(q):
        def one(i):
            g1_wait(q, i + 1)
            for e in range(1, nd):
                g2(q, e, i + 1).start()

        loop(nb - 1, one)

    def gather_wait(q):
        for e in range(1, nd):
            loop(nb, lambda i: g2_wait(q, e, i))

    def gather_drain(q):
        loop(nb - 1, lambda i: g1(q, i + 1).wait_send())
        for e in range(1, nd):
            loop(nb, lambda i: g2(q, e, i).wait_send())

    gather_start(0)
    gather_start(1)

    for i in range(MB):

        @pl.when(jnp.logical_not(from_me(i)))
        def _():
            x_wait(mine[i])

        loop(S - 1, lambda e: x_pass(i, e + 1).start())

    gather_forward(0)
    gather_forward(1)
    gather_start(3)

    gather_wait(0)
    gather_wait(1)

    for w in range(W):
        slab = k.bufA[w].astype(F32)
        k.fkv[w * z.r : w * z.r + z.rs] = slab[0 : z.rs]
        k.fq[w * z.r : w * z.r + z.rs] = slab[z.rs : 2 * z.rs]
    k.wkv[...] = k.fkv[0:C].astype(BF16)
    k.wkvt[...] = k.fkv[0:C].T.astype(BF16)
    k.wq[...] = k.fq[0:C, 0:C].astype(BF16)
    k.wqt[...] = k.fq[0:C, 0:C].T.astype(BF16)
    eye = (
        lax.broadcasted_iota(jnp.int32, (128, 128), 0) == lax.broadcasted_iota(jnp.int32, (128, 128), 1)
    ).astype(F32).astype(BF16)
    for w in range(W):
        col = mm_nt(eye, k.bufV[w])
        k.vcol[w * z.r : w * z.r + z.rs] = col[0 : z.rs]
        k.ucol[w * 4 * z.r : w * 4 * z.r + z.rC] = col[0 : z.rC]

    def vec(j):
        return k.vcol[0:C, j : j + 1]

    feat_row = lax.broadcasted_iota(jnp.int32, (16, R), 0)
    one_rows = jnp.where(feat_row < 2, 1.0, 0.0).astype(BF16)

    def kv_block(j):
        kv = mm(k.wkvt[...], k.xb[j, 0:C])
        kb = kv[0:C].astype(BF16)
        vb = (kv[C:L] + vec(V_BV)).astype(BF16)
        hot = k.xb[j, C : z.XR].astype(F32)
        kf = jnp.where(feat_row < z.ND, (hot - 1.0) * BIG, 0.0).astype(BF16)
        pad = jnp.zeros((48, R), BF16)
        for a in range(H):
            kh, vh = kb[a * HEAD_DIM : (a + 1) * HEAD_DIM], vb[a * HEAD_DIM : (a + 1) * HEAD_DIM]
            k.kx[j, a] = kh
            k.vx[j, a, 0:HEAD_DIM] = vh
            k.vx[j, a, HEAD_DIM:] = one_rows
            k.kt[j, a] = jnp.concatenate([kh, kf, pad], axis=0).T
            k.vt[j, a] = jnp.concatenate([vh, one_rows, pad], axis=0).T

    def kv_other(n):
        j = lax.rem(s_me + 1 + n // MB, S) + (n % MB) * S
        x_wait(j)
        kv_block(j)

    for i in range(MB):
        kv_block(mine[i])
    loop(nb - MB, kv_other)

    for i in range(MB):
        xi = k.xb[mine[i]]
        k.xq[:, i * R : (i + 1) * R] = xi[0:C]
        qi = ((mm(k.wqt[...], xi[0:C]) + vec(V_BQ)).astype(BF16).astype(F32) * HEAD_DIM**-0.5).astype(BF16)
        pad = jnp.zeros((48, R), BF16)
        for a in range(H):
            full = jnp.concatenate([qi[a * HEAD_DIM : (a + 1) * HEAD_DIM], xi[C : z.XR], pad], axis=0)
            k.qx[a, :, i * R : (i + 1) * R] = full
            k.qt[a, i * R : (i + 1) * R, :] = full.T

    def c_send(m):
        return rcopy(k.cs.at[m], k.cb.at[own_i], k.c_ss.at[m], k.c_rs.at[own_i], (*member(m, own_s), h))

    def c_start():
        for m in range(MB):

            @pl.when(not_me(member(m, own_s)))
            def _():
                c_send(m).start()

            @pl.when(is_me(member(m, own_s)))
            def _():
                k.cb[own_i] = k.cs[m]

    half = nh // 2

    def xor(i):
        return lax.bitwise_xor(h, i)

    def head_send(buf, ss, rs, i, a):
        part = pl.ds(a * HEAD_DIM, HEAD_DIM)
        src, to = (h, xor(i)) if i <= half else (xor(half), xor(i - half))
        return rcopy(buf.at[src, part], buf.at[src, part], ss.at[i, a], rs.at[i, a], (b, d, to))

    def head_wait(buf, ss, rs, i, a):
        part = pl.ds(a * HEAD_DIM, HEAD_DIM)
        rcopy(buf.at[xor(i), part], buf.at[xor(i), part], ss.at[i, a], rs.at[i, a], (b, d, h)).wait_recv()

    def head_start(buf, ss, rs, a):
        for i in range(half, 0, -1):
            head_send(buf, ss, rs, i, a).start()

    def head_pass(buf, ss, rs, a):
        head_wait(buf, ss, rs, half, a)
        for i in range(half + 1, nh):
            head_send(buf, ss, rs, i, a).start()

    def head_end(buf, ss, rs, a):
        for i in range(1, nh):
            if i != half:
                head_wait(buf, ss, rs, i, a)

    o_net = (k.oall, k.o_ss, k.o_rs)
    p_net = (k.pall, k.p_ss, k.p_rs)

    def scores(a, j):
        return mm(k.kt[j, a], k.qx[a])

    def prob(a, j):
        if z.keep:
            return k.pbuf[a, j]
        return jnp.exp(scores(a, j) - k.mrow[a, 0:1]).astype(BF16)

    for a in range(H):
        k.mrow[a] = jnp.full((8, Q), -3e38, F32)

        def top(j):
            s = scores(a, j)
            if z.keep:
                k.sbuf[j] = s
            k.mrow[a, 0:1] = jnp.maximum(k.mrow[a, 0:1], jnp.max(s, axis=0, keepdims=True))

        loop(nb, top)
        acc_ref = k.dqacc
        k.mrow[a, 1:2] = jnp.zeros((1, Q), F32)
        acc_ref[a] = jnp.zeros((HEAD_DIM, Q), F32)

        def weigh(j):
            if z.keep:
                k.pbuf[a, j] = jnp.exp(k.sbuf[j] - k.mrow[a, 0:1]).astype(BF16)
            o = mm(k.vx[j, a], prob(a, j))
            acc_ref[a] += o[0:HEAD_DIM]
            k.mrow[a, 1:2] += o[HEAD_DIM : HEAD_DIM + 1]

        loop(nb, weigh)
        inv = 1.0 / k.mrow[a, 1:2]
        k.mrow[a, 2:3] = inv
        k.oall[h, a * HEAD_DIM : (a + 1) * HEAD_DIM] = (acc_ref[a] * inv).astype(BF16)
        head_start(*o_net, a)
        if a == 0:
            gather_start(2)

    gather_forward(3)
    for a in range(H):
        head_pass(*o_net, a)
    c_start()

    gather_wait(3)
    for w in range(W):
        k.fod[w * 4 * z.r : w * 4 * z.r + z.rC] = k.bufC[w].astype(F32)
    for j in range(nh):
        k.wo[j] = k.fod[j * C : (j + 1) * C, 0:C].astype(BF16)
    k.wot[...] = k.fod[0:F, 0:C].T.astype(BF16)
    k.wdn[...] = k.fod[0:F, C:L].astype(BF16)
    k.wdnt[...] = k.fod[0:F, C:L].T.astype(BF16)

    def w_send(i):
        return rcopy(k.wo.at[hpeer[i]], k.wor.at[h], k.w_ss.at[i], k.w_rs.at[i], (b, d, hpeer[i]))

    for a in range(H):
        head_end(*o_net, a)
    o_full = k.oall[...].reshape(D, Q)
    h1 = k.xq[...].astype(F32) + mm(k.wot[...], o_full) + vec(V_BO)

    lane_rows = Q // 128
    stat_rows = [pl.ds(0, n * lane_rows) for n in (2, 4, 2)]

    def st_send(e, i):
        mine_ = k.stats.at[e, h, stat_rows[e]]
        return rcopy(mine_, mine_, k.st_ss.at[e, i], k.st_rs.at[e, i], (b, d, hpeer[i]))

    def reduce_start(e, rows):
        for j, v in enumerate(rows):
            row = jnp.sum(v, axis=0, keepdims=True)
            for c in range(lane_rows):
                k.stats[e, h, pl.ds(j * lane_rows + c, 1)] = row[:, c * 128 : (c + 1) * 128]
        for i in range(1, nh):
            st_send(e, i).start()

    def reduce_end(e):
        for i in range(1, nh):
            src = k.stats.at[e, hsrc[i], stat_rows[e]]
            rcopy(src, src, k.st_ss.at[e, i], k.st_rs.at[e, i], (b, d, h)).wait_recv()
        total = k.stats[e, 0, stat_rows[e]]
        for j in range(1, nh):
            total = total + k.stats[e, j, stat_rows[e]]
        total = total / D
        return [
            jnp.concatenate([total[j * lane_rows + c :][0:1] for c in range(lane_rows)], axis=1)
            for j in range(stat_rows[e].size // lane_rows)
        ]

    reduce_start(0, (h1, h1 * h1))

    gather_forward(2)
    gather_wait(2)
    for w in range(W):
        slab = k.bufB[w].astype(F32)
        k.fup[w * z.r : w * z.r + z.rs, 0:L] = slab[0 : z.rs]
        k.fup[w * z.r : w * z.r + z.rs, L:F] = slab[z.rs : 2 * z.rs]
    k.wup[...] = k.fup[0:C].astype(BF16)
    k.wupt[...] = k.fup[0:C].T.astype(BF16)

    tot = reduce_end(0)
    for i in range(1, nh):
        w_send(i).start()
    k.wor[h] = k.wo[h]
    mu1 = tot[0]
    r1 = lax.rsqrt(tot[1] - mu1 * mu1 + EPS)
    n1 = (h1 - mu1) * r1
    y1 = n1 * vec(V_G1) + vec(V_S1)
    y1b = y1.astype(BF16)

    ub = k.ucol[0:F, V_BU : V_BU + 1]
    u = mm(k.wupt[...], y1b) + ub
    k.u[...] = u
    act = (0.5 * u * (1.0 + lax.erf(u * (0.5**0.5)))).astype(BF16)
    k.act[...] = act
    h2 = y1 + mm(k.wdnt[...], act) + vec(V_BD)

    for i in range(MB):

        @pl.when(jnp.logical_not(from_me(i)))
        def _():
            rcopy(k.cb.at[i], k.cb.at[i], k.c_ss.at[i], k.c_rs.at[i], (b, d, h)).wait_recv()

    g = jnp.concatenate([k.cb[i] for i in range(MB)], axis=1).astype(F32)
    dn2 = g * vec(V_G2)
    reduce_start(1, (h2, h2 * h2, dn2, dn2 * h2))
    uu = k.u[...]
    k.u[...] = 0.5 * (1.0 + lax.erf(uu * (0.5**0.5))) + uu * jnp.exp(-0.5 * uu * uu) * ((2 * jnp.pi) ** -0.5)
    tot = reduce_end(1)
    mu2 = tot[0]
    r2 = lax.rsqrt(tot[1] - mu2 * mu2 + EPS)
    n2 = (h2 - mu2) * r2
    out = (n2 * vec(V_G2) + vec(V_S2)).astype(BF16)
    for i in range(MB):
        k.mo[i] = out[:, i * R : (i + 1) * R]

    def mo_dst(i):
        return mine[i], d_t

    def mo_send(i):
        return rcopy(k.mo.at[i], k.o_mo.at[m_t], k.mo_ss.at[i], k.mo_rs.at[m_t], (*mo_dst(i), h))

    for i in range(MB):

        @pl.when(not_me(mo_dst(i)))
        def _():
            mo_send(i).start()

        @pl.when(is_me(mo_dst(i)))
        def _():
            k.o_mo[m_t] = k.mo[i]

    dh2 = r2 * (dn2 - tot[2] - n2 * (r2 * (tot[3] - mu2 * tot[2])))
    dz = dh2.astype(BF16)
    ones = jnp.ones((16, Q), BF16)

    def vec_grad(j, x):
        k.vg[j : j + 1] = mm_nt(ones, x)[0:1]

    k.vg[...] = jnp.zeros_like(k.vg)
    k.vgu[...] = jnp.zeros_like(k.vgu)
    vec_grad(V_G2, (g * n2).astype(BF16))
    vec_grad(V_S2, g.astype(BF16))
    vec_grad(V_BD, dz)

    packs = (k.pA, k.pV, k.pB, k.pC)
    firsts = (k.r1A, k.r1V, k.r1B, k.r1C)
    seconds = (k.s2A, k.s2V, k.s2B, k.s2C)
    lasts = (k.r2A, k.r2V, k.r2B, k.r2C)
    sums = (k.o_A, k.o_V, k.o_B, k.o_C)

    def s1_send(q, e, i):
        dt = lax.rem(d + e, nd)
        return rcopy(
            packs[q].at[i * nd + dt], firsts[q].at[e - 1, i], k.s1_ss.at[q, e - 1, i], k.s1_rs.at[q, e - 1, i],
            (b, dt, h),
        )

    def s2_send(q, i):
        bt = lax.rem(b + i, nb)
        return rcopy(
            seconds[q].at[bt], lasts[q].at[b], k.s2_ss.at[q, i], k.s2_rs.at[q, i], (bt, d, h)
        )

    def scatter_start(q):
        for e in range(1, nd):
            loop(nb, lambda i: s1_send(q, e, i).start())

    def scatter_sum(q, bt):
        part = packs[q][bt * nd + d].astype(F32)
        for e in range(1, nd):
            rcopy(
                firsts[q].at[e - 1, bt], firsts[q].at[e - 1, bt], k.s1_ss.at[q, e - 1, bt],
                k.s1_rs.at[q, e - 1, bt], (b, d, h),
            ).wait_recv()
            part = part + firsts[q][e - 1, bt].astype(F32)
        return part

    def scatter_pass(q, i):
        bt = lax.rem(b + i, nb)
        seconds[q][bt] = scatter_sum(q, bt).astype(BF16)
        s2_send(q, i).start()

    def scatter_own(q):
        sums[q][...] = scatter_sum(q, b)

    def scatter_forward(q):
        loop(nb - 1, lambda i: scatter_pass(q, i + 1))
        scatter_own(q)

    def scatter_end(q):
        def one(i):
            src = lax.rem(b + nb - i, nb)
            rcopy(
                lasts[q].at[src], lasts[q].at[src], k.s2_ss.at[q, i], k.s2_rs.at[q, i], (b, d, h)
            ).wait_recv()
            sums[q][...] += lasts[q][src].astype(F32)

        loop(nb - 1, lambda i: one(i + 1))
        loop(nb - 1, lambda i: s2_send(q, i + 1).wait_send())
        for e in range(1, nd):
            loop(nb, lambda i: s1_send(q, e, i).wait_send())

    du = (mm(k.wdn[...], dz) * k.u[...]).astype(BF16)
    k.du[...] = du
    dy1 = dh2 + mm(k.wup[...], du)
    dn1 = dy1 * vec(V_G1)
    reduce_start(2, (dn1, dn1 * n1))
    k.gup[0:C] = mm_nt(y1b, k.du[...])
    for w in range(W):
        k.pB[w] = jnp.concatenate(
            [k.gup[w * z.r : w * z.r + z.rs, 0:L], k.gup[w * z.r : w * z.r + z.rs, L:F]]
            + ([jnp.zeros((z.rA - 2 * z.rs, L), F32)] if z.rA > 2 * z.rs else []),
            axis=0,
        ).astype(BF16)
    scatter_start(2)
    k.god[0:F, C:L] = mm_nt(k.act[...], dz)
    k.vgu[V_BU : V_BU + 1] = mm_nt(ones, k.du[...])[0:1]
    vec_grad(V_G1, (dy1 * n1).astype(BF16))
    vec_grad(V_S1, dy1.astype(BF16))
    tot = reduce_end(2)
    dh1 = r1 * (dn1 - tot[0] - n1 * tot[1])
    dp = dh1.astype(BF16)
    k.pall[h] = dp

    for a in range(H):
        head_start(*p_net, a)

    k.god[0:F, 0:C] = mm_nt(o_full, dp)
    vec_grad(V_BO, dp)
    for w in range(W):
        k.pC[w] = k.god[w * 4 * z.r : w * 4 * z.r + z.rC].astype(BF16)
    scatter_start(3)
    for a in range(H):
        head_pass(*p_net, a)
    scatter_forward(2)

    for a in range(H):
        head_end(*p_net, a)
    for i in range(1, nh):
        src = hsrc[i]
        rcopy(k.wor.at[src], k.wor.at[src], k.w_ss.at[i], k.w_rs.at[i], (b, d, h)).wait_recv()
    do = mm(k.wor[0], k.pall[0])
    for j in range(1, nh):
        do = do + mm(k.wor[j], k.pall[j])
    do = do.astype(BF16).astype(F32)
    row16q = lax.broadcasted_iota(jnp.int32, (16, Q), 0)
    for a in range(H):
        part = do[a * HEAD_DIM : (a + 1) * HEAD_DIM] * k.mrow[a, 2:3]
        own = k.oall[h, a * HEAD_DIM : (a + 1) * HEAD_DIM].astype(F32)
        delta = jnp.sum(part * own, axis=0, keepdims=True)
        hi = delta.astype(BF16).astype(F32)
        tail = jnp.where(row16q == 0, -hi, jnp.where(row16q == 1, hi - delta, 0.0))
        full = jnp.concatenate([part.astype(BF16), tail.astype(BF16), jnp.zeros((48, Q), BF16)], axis=0)
        k.dox[a] = full
        k.dot[a] = full.T
        k.dqacc[a] = jnp.zeros((HEAD_DIM, Q), F32)

    k.gkv[...] = jnp.zeros_like(k.gkv)
    k.gq[...] = jnp.zeros_like(k.gq)

    def tp_send(j):
        to = j % S
        dst = k.tgr.at[j // S, s_me]
        return rcopy(k.tgs.at[j], dst, k.tp_ss.at[j], k.tp_rs.at[j // S, s_me], (*mate(to), h))

    def back_block(j):
        for a in range(H):
            p = prob(a, j)
            ds = (p.astype(F32) * mm(k.vt[j, a], k.dox[a])).astype(BF16)
            k.dqacc[a] += mm(k.kx[j, a], ds)
            dk = mm(ds, k.qt[a])
            dv = mm(p, k.dot[a])
            k.dkv[a * HEAD_DIM : (a + 1) * HEAD_DIM] = dk.T[0:HEAD_DIM].astype(BF16)
            k.dkv[C + a * HEAD_DIM : C + (a + 1) * HEAD_DIM] = dv.T[0:HEAD_DIM].astype(BF16)
        dkv = k.dkv[...]
        k.gkv[0:C] += mm_nt(k.xb[j, 0:C], dkv)
        k.vg[V_BV : V_BV + 1] += mm_nt(ones[:, 0:R], dkv[C:L])[0:1]
        return mm(k.wkv[...], dkv)

    def back_other(n):
        j = lax.rem(s_me + 1 + n // MB, S) + (n % MB) * S
        k.tgs[j] = back_block(j).astype(BF16)
        tp_send(j).start()

    loop(nb - MB, back_other)
    scatter_forward(3)
    for i in range(MB):
        k.tgo[i] = back_block(mine[i])

    for a in range(H):
        k.dq[a * HEAD_DIM : (a + 1) * HEAD_DIM] = (k.dqacc[a] * HEAD_DIM**-0.5).astype(BF16)
    dq = k.dq[...]
    k.gq[0:C, 0:C] = mm_nt(k.xq[...], dq)
    vec_grad(V_BQ, dq)

    for w in range(W):
        k.pA[w] = jnp.concatenate(
            [k.gkv[w * z.r : w * z.r + z.rs], k.gq[w * z.r : w * z.r + z.rs]]
            + ([jnp.zeros((z.rA - 2 * z.rs, L), F32)] if z.rA > 2 * z.rs else []),
            axis=0,
        ).astype(BF16)
    vgb, vgub = k.vg[...].astype(BF16), k.vgu[...].astype(BF16)

    def pack_v(w):
        def pick(n, per):
            i = lax.broadcasted_iota(jnp.int32, (n, 128), 0)
            j = lax.broadcasted_iota(jnp.int32, (n, 128), 1)
            return jnp.where(jnp.logical_and(i == w * per + j, j < per), 1.0, 0.0).astype(BF16)

        k.pV[w] = (mm(vgb, pick(C, z.r)) + mm(vgub, pick(F, 4 * z.r))).astype(BF16)

    loop(W, pack_v)
    scatter_start(0)
    scatter_start(1)

    def t_send(i):
        return rcopy(k.tgx.at[i], k.o_tg.at[m_t], k.t_ss.at[i], k.t_rs.at[m_t], (*mo_dst(i), h))

    own = dh1 + mm(k.wq[...], dq)
    for i in range(MB):
        k.tgo[i] += own[:, i * R : (i + 1) * R]

        def add(e):
            s = lax.rem(s_me + e + 1, S)
            rcopy(k.tgr.at[i, s], k.tgr.at[i, s], k.tp_ss.at[0], k.tp_rs.at[i, s], (b, d, h)).wait_recv()
            k.tgo[i] += k.tgr[i, s].astype(F32)

        loop(S - 1, add)
        k.tgx[i] = k.tgo[i].astype(BF16)

        @pl.when(not_me(mo_dst(i)))
        def _():
            t_send(i).start()

        @pl.when(is_me(mo_dst(i)))
        def _():
            k.o_tg[m_t] = k.tgx[i]

    scatter_forward(0)
    scatter_forward(1)

    for q in (2, 3, 0, 1):
        scatter_end(q)

    for m in range(MB):

        @pl.when(not_me(member(m, own_s)))
        def _():
            rcopy(k.o_tg.at[m], k.o_tg.at[m], k.t_ss.at[m], k.t_rs.at[m], (b, d, h)).wait_recv()
            rcopy(k.o_mo.at[m], k.o_mo.at[m], k.mo_ss.at[m], k.mo_rs.at[m], (b, d, h)).wait_recv()
            c_send(m).wait_send()
            x_send(m).wait_send()

    for i in range(MB):

        @pl.when(not_me(mo_dst(i)))
        def _():
            mo_send(i).wait_send()
            t_send(i).wait_send()

        loop(S - 1, lambda e: x_pass(i, e + 1).wait_send())

    def tp_drain(n):
        tp_send(lax.rem(s_me + 1 + n // MB, S) + (n % MB) * S).wait_send()

    loop(nb - MB, tp_drain)
    for q in range(4):
        gather_drain(q)
    for i in range(1, nh):
        for a in range(H):
            head_send(*o_net, i, a).wait_send()
            head_send(*p_net, i, a).wait_send()
        w_send(i).wait_send()
        for e in range(3):
            st_send(e, i).wait_send()


def finish_kernel(z, mo, tg, gA, gB, gC, gV, *outs):
    (mixed, dtok, dwq, dbq, dwk, dwv, dbv, dwo, dbo, dg1, ds1, dwup, dbu, dwdn, dbd, dg2, ds2) = outs
    r, rs, C, L = z.r, z.rs, z.C, z.L
    for m in range(z.MB):
        mixed[m] = mo[m].T
        dtok[m] = tg[m].astype(F32).T
    dwk[0] = gA[0:r, 0:C]
    dwv[0] = gA[0:r, C:L]
    dwq[0] = gA[rs : rs + r, 0:C]
    dwup[0, :, 0:L] = gB[0:r]
    dwup[0, :, L : 2 * L] = gB[rs : rs + r]
    dwo[...] = gC[0 : 4 * r, 0:C]
    dwdn[0] = gC[0 : 4 * r, C:L]
    for j, ref in enumerate((dbq, dbv, dbo, dg1, ds1, dbd, dg2, ds2)):
        ref[...] = gV[j : j + 1, 0:r]
    dbu[...] = gV[V_BU : V_BU + 1, 0 : 4 * r]


def solution(mesh):
    vec_spec = P("head", ("blk", "dp"))
    mat_spec = P("head", ("blk", "dp"), None)
    tok_spec = P(None, "dp", "head", "blk")
    out_spec = P(("blk", "dp"), "head")

    def body(
        tokens, doc_lengths, cotangent, query_weight, query_bias, key_weight, value_weight, value_bias,
        out_weight, out_bias, first_gain, first_shift, up_weight, up_bias, down_weight, down_bias,
        second_gain, second_shift,
    ):
        z = Sizes(mesh, tokens, query_weight, up_weight, doc_lengths)
        scratch = main_scratch(z)
        vmem = pl.BlockSpec(memory_space=pltpu.VMEM)
        smem = pl.BlockSpec(memory_space=pltpu.SMEM)
        names = INPUTS + OUTPUTS + list(scratch)
        sds = jax.ShapeDtypeStruct
        parts = pl.pallas_call(
            lambda *refs: main_kernel(z, names, *refs),
            out_shape=[
                sds((z.MB, z.C, z.R), BF16),
                sds((z.MB, z.C, z.R), BF16),
                sds((z.rA, z.L), F32),
                sds((z.rA, z.L), F32),
                sds((z.rC, z.L), F32),
                sds((VROWS, 128), F32),
            ],
            in_specs=[smem] + [vmem] * (len(INPUTS) - 1),
            out_specs=[vmem] * len(OUTPUTS),
            scratch_shapes=list(scratch.values()),
            compiler_params=pltpu.CompilerParams(
                collective_id=0, has_side_effects=True, vmem_limit_bytes=63 << 20
            ),
            name="layer",
        )(
            doc_lengths, tokens.reshape(z.MB, z.R, z.C), cotangent.reshape(z.MB, z.R, z.C), query_weight,
            query_bias, key_weight, value_weight, value_bias, out_weight, out_bias, first_gain, first_shift,
            up_weight, up_bias, down_weight, down_bias, second_gain, second_shift,
        )
        mat, vec = sds((1, z.r, z.C), F32), sds((1, z.r), F32)
        outs = pl.pallas_call(
            lambda *refs: finish_kernel(z, *refs),
            out_shape=[
                sds((z.MB, z.R, z.C), BF16), sds((z.MB, z.R, z.C), F32), mat, vec, mat, mat, vec,
                sds((4 * z.r, z.C), F32), vec, vec, vec, sds((1, z.r, z.F), F32), sds((1, 4 * z.r), F32),
                sds((1, 4 * z.r, z.C), F32), vec, vec, vec,
            ],
            in_specs=[vmem] * len(OUTPUTS),
            out_specs=[vmem] * 17,
            name="finish",
        )(*parts)
        shape = tokens.shape
        return (outs[0].reshape(shape), outs[1].reshape(shape), *outs[2:])

    return jax.shard_map(
        body,
        mesh=mesh,
        in_specs=(
            tok_spec, P(None, "dp", None), tok_spec, mat_spec, vec_spec, mat_spec, mat_spec, vec_spec,
            out_spec, vec_spec, vec_spec, vec_spec, mat_spec, vec_spec, mat_spec, vec_spec, vec_spec, vec_spec,
        ),
        out_specs=(
            tok_spec, tok_spec, mat_spec, vec_spec, mat_spec, mat_spec, vec_spec, out_spec, vec_spec, vec_spec,
            vec_spec, mat_spec, vec_spec, mat_spec, vec_spec, vec_spec, vec_spec,
        ),
        check_vma=False,
    )
```

```python
import types

import jax
import jax.numpy as jnp
from jax import lax
from jax.experimental import pallas as pl
from jax.experimental.pallas import tpu as pltpu
from jax.sharding import PartitionSpec as P

HEAD_DIM = 64
EPS = 1e-05
BIG = 1e30
MESH = pl.DeviceIdType.MESH
F32 = jnp.float32
BF16 = jnp.bfloat16
V_BQ, V_BV, V_BO, V_G1, V_S1, V_BD, V_G2, V_S2 = range(8)
VECS = 16
M_QKV, M_OUT, M_UP, M_DOWN = range(4)


def up_to(n, m):
    return (n + m - 1) // m * m


def mm(a, b):
    return lax.dot_general(a, b, (((1,), (0,)), ((), ())), preferred_element_type=F32)


def mm_nt(a, b):
    return lax.dot_general(a, b, (((1,), (1,)), ((), ())), preferred_element_type=F32)


def loop(n, fn):
    if n <= 8:
        for i in range(n):
            fn(i)
    else:
        lax.fori_loop(0, n, lambda i, c: (fn(i), c)[1], 0)


def rcopy(src, dst, ss, rs, dev):
    return pltpu.make_async_remote_copy(
        src_ref=src, dst_ref=dst, send_sem=ss, recv_sem=rs, device_id=dev, device_id_type=MESH
    )


class Sizes:
    def __init__(self, mesh, tokens, query_weight, up_weight, doc_lengths):
        self.nb, self.nd, self.nh = mesh.shape["blk"], mesh.shape["dp"], mesh.shape["head"]
        self.W = self.nb * self.nd
        self.C, self.F = query_weight.shape[2], up_weight.shape[2]
        self.MB = tokens.shape[0]
        self.R = tokens.shape[3] // self.C
        self.S = self.nb // self.MB
        self.Q = self.MB * self.R
        self.H = self.C // HEAD_DIM
        self.ND = doc_lengths.shape[2]
        self.r = query_weight.shape[1]
        self.rs = up_to(self.r, 8)
        self.r2 = up_to(2 * self.r, 8)
        self.rA = up_to(2 * self.rs, 16)
        self.L = 2 * self.C
        self.keep = self.nb * self.R * self.Q * self.H * 2 <= (8 << 20)
        assert self.F == 4 * self.C and self.F == self.nh * self.C and self.W % self.nh == 0


def main_scratch(z):
    dma = pltpu.SemaphoreType.DMA
    v = pltpu.VMEM
    nb, W, L, R, C, F, Q, H, MB, rA, nh = z.nb, z.W, z.L, z.R, z.C, z.F, z.Q, z.H, z.MB, z.rA, z.nh
    dd = max(z.nd - 1, 1)
    return dict(
        xs=v((MB, C, R), BF16),
        xb=v((nb, C, R), BF16),
        cs=v((MB, C, R), BF16),
        cb=v((MB, C, R), BF16),
        buf=v((4, W, rA, L), BF16),
        wob=v((nh, W // nh, rA, L), BF16),
        fst=v((rA, L), F32),
        vst=v((VECS, 128), F32),
        fkv=v((C + 8, L), F32),
        fq=v((C + 8, L), F32),
        fup=v((C + 16, F), F32),
        fod=v((F + 16, C), F32),
        wkv=v((C, L), BF16),
        wkvt=v((L, C), BF16),
        wq=v((C, C), BF16),
        wqt=v((C, C), BF16),
        wup=v((C, F), BF16),
        wupt=v((F, C + 16), BF16),
        wor=v((C, F), BF16),
        wot=v((C, F), BF16),
        wdn=v((F, C), BF16),
        wdnt=v((C, F), BF16),
        xq=v((C, Q), BF16),
        qx=v((MB, H, 128, R), BF16),
        kx=v((nb, H, HEAD_DIM, R), BF16),
        vx=v((nb, H, HEAD_DIM + 16, R), BF16),
        kt=v((nb, H, R, 128), BF16),
        vt=v((nb, H, R, 128), BF16),
        pbuf=v((MB, H, nb, R, R) if z.keep else (1, 1, 1, 16, 128), BF16),
        mrow=v((MB, H, 8, R), F32),
        oall=v((MB, nh, C, R), BF16),
        pall=v((MB, nh, C, R), BF16),
        stats=v((3, MB, nh, 8, 128), F32),
        n1=v((MB, C, R), F32),
        y1=v((MB, C, R), F32),
        h2=v((MB, C, R), F32),
        gel=v((MB, F, R), F32),
        dh1=v((MB, C, R), F32),
        y1b=v((C, Q), BF16),
        act=v((F, Q), BF16),
        dz=v((C, Q), BF16),
        du=v((F, Q), BF16),
        mo=v((MB, C, R), BF16),
        dox=v((MB, H, 128, R), BF16),
        dqacc=v((MB, H, HEAD_DIM, R), F32),
        dkacc=v((nb - MB if z.keep else 1, L, R), F32),
        dkv=v((L, R), F32),
        dq=v((C, Q), BF16),
        tgs=v((nb, C, R), BF16),
        tgo=v((MB, C, R), F32),
        tgr=v((MB, z.S, C, R), BF16),
        tgx=v((MB, C, R), BF16),
        gkv=v((C + 8, L), F32),
        gq=v((C + 8, L), F32),
        gup=v((C + 8, F), F32),
        gout=v((F + 16, C), F32),
        gdn=v((F + 16, C), F32),
        vg=v((VECS, C), F32),
        ug=v((8, F), F32),
        pk=v((4, W, rA, L), BF16),
        got1=v((4, dd, nb, rA, L), BF16),
        sent2=v((4, nb, rA, L), BF16),
        got2=v((4, nb, rA, L), BF16),
        x_ss=dma((MB,)),
        xf_ss=dma((MB, z.S)),
        x_rs=dma((nb,)),
        c_ss=dma((MB,)),
        c_rs=dma((MB,)),
        g1_ss=dma((4, nb)),
        g1_rs=dma((4, nb)),
        g2_ss=dma((4, dd, nb)),
        g2_rs=dma((4, dd, nb)),
        o_ss=dma((MB, nh)),
        o_rs=dma((MB, nh)),
        p_ss=dma((MB, nh)),
        p_rs=dma((MB, nh)),
        w_ss=dma((nh,)),
        w_rs=dma((nh,)),
        st_ss=dma((3, MB, nh)),
        st_rs=dma((3, MB, nh)),
        mo_ss=dma((MB,)),
        mo_rs=dma((MB,)),
        tp_ss=dma((nb,)),
        tp_rs=dma((MB, z.S)),
        t_ss=dma((MB,)),
        t_rs=dma((MB,)),
        s1_ss=dma((4, dd, nb)),
        s1_rs=dma((4, dd, nb)),
        s2_ss=dma((4, nb)),
        s2_rs=dma((4, nb)),
    )


INPUTS = [
    "lens", "tok", "cot", "wq_in", "bq", "wk_in", "wv_in", "bv", "wo_in", "bo", "g1", "s1", "wup_in", "bu",
    "wdn_in", "bd", "g2", "s2",
]
OUTPUTS = ["o_mo", "o_tg", "o_G"]


def main_kernel(z, names, *refs):
    k = types.SimpleNamespace(**dict(zip(names, refs)))
    nb, nd, nh, W, MB, R, C, F, H, L, S, r, rs, rA = (
        z.nb, z.nd, z.nh, z.W, z.MB, z.R, z.C, z.F, z.H, z.L, z.S, z.r, z.rs, z.rA,
    )
    b, d, h = lax.axis_index("blk"), lax.axis_index("dp"), lax.axis_index("head")
    w_me = b * nd + d
    m_t, s_me = b // S, b % S
    mine = [i * S + s_me for i in range(MB)]
    D = nh * C
    half = nh // 2

    def xor(i):
        return lax.bitwise_xor(h, i)

    def later(e):
        return lax.rem(m_t + e, MB)

    def mate(e):
        return lax.rem(s_me + e, S)

    bar = pltpu.get_barrier_semaphore()
    peers = [(lax.rem(b + i, nb), d, h) for i in range(1, nb)]
    peers += [(b, lax.rem(d + i, nd), h) for i in range(1, nd)]
    peers += [(b, d, xor(i)) for i in range(1, nh)]
    for peer in peers:
        pl.semaphore_signal(bar, inc=1, device_id=peer, device_id_type=MESH)

    def pack(q):
        k.buf[q, w_me] = k.fst[...].astype(BF16)

    k.vst[...] = jnp.zeros_like(k.vst)
    for j, ref in enumerate((k.bq, k.bv, k.bo, k.g1, k.s1, k.bd, k.g2, k.s2)):
        k.vst[j : j + 1, 0:r] = ref[...].astype(F32)
    k.fst[...] = jnp.zeros_like(k.fst)
    k.fst[0:r, 0:C] = k.wk_in[0].astype(F32)
    k.fst[0:r, C:L] = k.wv_in[0].astype(F32)
    k.fst[rs : rs + r, 0:C] = k.wq_in[0].astype(F32)
    k.fst[rs : rs + r, C : C + VECS] = k.vst[...].T[0:r]
    k.fst[rs : rs + 1, C + VECS : C + VECS + 4 * r] = k.bu[...].astype(F32)
    pack(M_QKV)
    for q, src in ((M_OUT, k.wo_in[...]), (M_DOWN, k.wdn_in[0])):
        src = src.astype(F32)
        k.fst[0 : 2 * r, 0:C] = src[0 : 2 * r]
        k.fst[0 : 2 * r, C:L] = src[2 * r : 4 * r]
        pack(q)
    k.fst[0:r] = k.wup_in[0, :, 0:L].astype(F32)
    k.fst[rs : rs + r] = k.wup_in[0, :, L : 2 * L].astype(F32)
    pack(M_UP)

    for m in range(MB):
        k.xs[m] = k.tok[m].T
        k.cs[m] = k.cot[m].T
    k.xb[b] = k.xs[m_t]
    k.cb[m_t] = k.cs[m_t]

    pl.semaphore_wait(bar, len(peers))

    def g1(q, i):
        own = k.buf.at[q, w_me]
        return rcopy(own, own, k.g1_ss.at[q, i], k.g1_rs.at[q, i], (lax.rem(b + i, nb), d, h))

    def g1_wait(q, i):
        src = k.buf.at[q, lax.rem(b + nb - i, nb) * nd + d]
        rcopy(src, src, k.g1_ss.at[q, i], k.g1_rs.at[q, i], (b, d, h)).wait_recv()

    def g2(q, e, i):
        src = k.buf.at[q, lax.rem(b + nb - i, nb) * nd + d]
        return rcopy(src, src, k.g2_ss.at[q, e - 1, i], k.g2_rs.at[q, e - 1, i], (b, lax.rem(d + e, nd), h))

    def g2_wait(q, e, i):
        src = k.buf.at[q, lax.rem(b + nb - i, nb) * nd + lax.rem(d + nd - e, nd)]
        rcopy(src, src, k.g2_ss.at[q, e - 1, i], k.g2_rs.at[q, e - 1, i], (b, d, h)).wait_recv()

    def gather_start(q):
        for e in range(1, nd):
            g2(q, e, 0).start()
        loop(nb - 1, lambda i: g1(q, i + 1).start())

    def gather_forward(q):
        def one(i):
            g1_wait(q, i + 1)
            for e in range(1, nd):
                g2(q, e, i + 1).start()

        loop(nb - 1, one)

    def gather_wait(q):
        for e in range(1, nd):
            loop(nb, lambda i: g2_wait(q, e, i))

    def gather_drain(q):
        loop(nb - 1, lambda i: g1(q, i + 1).wait_send())
        for e in range(1, nd):
            loop(nb, lambda i: g2(q, e, i).wait_send())

    gather_start(M_QKV)

    def x_send(e):
        m = later(e)
        return rcopy(k.xs.at[m], k.xb.at[b], k.x_ss.at[e], k.x_rs.at[b], (m * S + s_me, d, h))

    def x_pass(e, f):
        src = k.xb.at[later(e) * S + s_me]
        return rcopy(src, src, k.xf_ss.at[e, f], k.x_rs.at[later(e) * S + s_me], (m_t * S + mate(f), d, h))

    def x_wait(j):
        rcopy(k.xb.at[j], k.xb.at[j], k.x_ss.at[0], k.x_rs.at[j], (b, d, h)).wait_recv()

    for e in range(1, MB):
        x_send(e).start()
    loop(S - 1, lambda f: x_pass(0, f + 1).start())

    gather_forward(M_QKV)

    for e in range(1, MB):
        x_wait(later(e) * S + s_me)
        loop(S - 1, lambda f: x_pass(e, f + 1).start())
    gather_start(M_OUT)

    gather_wait(M_QKV)

    for w in range(W):
        slab = k.buf[M_QKV, w].astype(F32)
        k.fkv[w * r : w * r + rs] = slab[0:rs]
        k.fq[w * r : w * r + rs] = slab[rs : 2 * rs]
    k.wkv[...] = k.fkv[0:C].astype(BF16)
    k.wkvt[...] = k.fkv[0:C].T.astype(BF16)
    k.wq[...] = k.fq[0:C, 0:C].astype(BF16)
    k.wqt[...] = k.fq[0:C, 0:C].T.astype(BF16)

    def vec(j):
        return k.fq[0:C, C + j : C + j + 1]

    row16 = lax.broadcasted_iota(jnp.int32, (16, R), 0)
    lane = lax.broadcasted_iota(jnp.int32, (16, R), 1)
    pad = jnp.zeros((48, R), BF16)
    one_rows = jnp.where(row16 < 2, 1.0, 0.0).astype(BF16)

    def in_doc(j):
        doc = jnp.zeros((16, R), jnp.int32)
        end = jnp.int32(0)
        for n in range(z.ND):
            end = end + k.lens[m_t, 0, n]
            doc = doc + (j * R + lane >= end).astype(jnp.int32)
        return row16 == doc

    def kv_block(j):
        kv = mm(k.wkvt[...], k.xb[j])
        kb = kv[0:C].astype(BF16)
        vb = (kv[C:L] + vec(V_BV)).astype(BF16)
        barred = jnp.logical_and(row16 < z.ND, jnp.logical_not(in_doc(j)))
        kf = jnp.where(barred, -BIG, 0.0).astype(BF16)
        for a in range(H):
            kh, vh = kb[a * HEAD_DIM : (a + 1) * HEAD_DIM], vb[a * HEAD_DIM : (a + 1) * HEAD_DIM]
            k.kx[j, a] = kh
            k.vx[j, a, 0:HEAD_DIM] = vh
            k.vx[j, a, HEAD_DIM:] = one_rows
            k.kt[j, a] = jnp.concatenate([kh, kf, pad], axis=0).T
            k.vt[j, a] = jnp.concatenate([vh, one_rows, pad], axis=0).T

    def other(n):
        return lax.rem(s_me + 1 + n // MB, S) + lax.rem(m_t + n, MB) * S

    def kv_other(n):
        x_wait(other(n))
        kv_block(other(n))

    for i in range(MB):
        kv_block(mine[i])

    for i in range(MB):
        xi = k.xb[mine[i]]
        k.xq[:, i * R : (i + 1) * R] = xi
        qi = ((mm(k.wqt[...], xi) + vec(V_BQ)).astype(BF16).astype(F32) * HEAD_DIM**-0.5).astype(BF16)
        hot = jnp.where(in_doc(mine[i]), 1.0, 0.0).astype(BF16)
        for a in range(H):
            full = jnp.concatenate([qi[a * HEAD_DIM : (a + 1) * HEAD_DIM], hot, pad], axis=0)
            k.qx[i, a] = full

    loop(nb - MB, kv_other)
    gather_start(M_UP)

    def head_send(net, i, p):
        buf, ss, rs_ = net
        src, to = (h, xor(p)) if p <= half else (xor(half), xor(p - half))
        return rcopy(buf.at[i, src], buf.at[i, src], ss.at[i, p], rs_.at[i, p], (b, d, to))

    def head_wait(net, i, p):
        buf, ss, rs_ = net
        rcopy(buf.at[i, xor(p)], buf.at[i, xor(p)], ss.at[i, p], rs_.at[i, p], (b, d, h)).wait_recv()

    def head_start(net, i):
        for p in range(half, 0, -1):
            head_send(net, i, p).start()

    def head_pass(net, i):
        head_wait(net, i, half)
        for p in range(half + 1, nh):
            head_send(net, i, p).start()

    def head_end(net, i):
        for p in range(1, nh):
            if p != half:
                head_wait(net, i, p)

    o_net = (k.oall, k.o_ss, k.o_rs)
    p_net = (k.pall, k.p_ss, k.p_rs)

    def scores(i, a, j):
        return mm(k.kt[j, a], k.qx[i, a])

    def prob(i, a, j):
        if z.keep:
            return k.pbuf[i, a, j]
        return jnp.exp(scores(i, a, j) - k.mrow[i, a, 0:1]).astype(BF16)

    def attend(i, a):
        if z.keep:
            s = [scores(i, a, j) for j in range(nb)]
            top = jnp.max(s[0], axis=0, keepdims=True)
            for j in range(1, nb):
                top = jnp.maximum(top, jnp.max(s[j], axis=0, keepdims=True))
            o = None
            for j in range(nb):
                e = jnp.exp(s[j] - top).astype(BF16)
                k.pbuf[i, a, j] = e
                o = mm(k.vx[j, a], e) if o is None else o + mm(k.vx[j, a], e)
        else:
            k.mrow[i, a, 0:1] = jnp.full((1, R), -3e38, F32)

            def see(j):
                best = jnp.max(scores(i, a, j), axis=0, keepdims=True)
                k.mrow[i, a, 0:1] = jnp.maximum(k.mrow[i, a, 0:1], best)

            loop(nb, see)
            acc = k.tgo.at[0, 0 : HEAD_DIM + 16]
            acc[...] = jnp.zeros((HEAD_DIM + 16, R), F32)

            def add(j):
                acc[...] += mm(k.vx[j, a], prob(i, a, j))

            loop(nb, add)
            o = acc[...]
        inv = 1.0 / o[HEAD_DIM : HEAD_DIM + 1]
        k.mrow[i, a, 2:3] = inv
        k.oall[i, h, a * HEAD_DIM : (a + 1) * HEAD_DIM] = (o[0:HEAD_DIM] * inv).astype(BF16)

    for i in range(MB):
        for a in range(H):
            attend(i, a)
        head_start(o_net, i)
    gather_start(M_DOWN)

    def c_send(e):
        m = later(e)
        return rcopy(k.cs.at[m], k.cb.at[m_t], k.c_ss.at[e], k.c_rs.at[m_t], (m * S + s_me, d, h))

    for e in range(1, MB):
        c_send(e).start()

    gather_forward(M_OUT)
    gather_forward(M_UP)
    for i in range(MB):
        head_pass(o_net, i)
    gather_wait(M_OUT)

    per = W // nh

    def w_send(p):
        src = k.buf.at[M_OUT, pl.ds(xor(p) * per, per)]
        return rcopy(src, k.wob.at[h], k.w_ss.at[p], k.w_rs.at[p], (b, d, xor(p)))

    for p in range(1, nh):
        w_send(p).start()

    def spread(dst, slab, row):
        slab = slab.astype(F32)
        dst[row : row + z.r2] = slab[0 : z.r2, 0:C]
        dst[row + 2 * r : row + 2 * r + z.r2] = slab[0 : z.r2, C:L]

    for w in range(W):
        spread(k.fod, k.buf[M_OUT, w], 4 * r * w)
    k.wot[...] = k.fod[0:F].T.astype(BF16)

    gather_forward(M_DOWN)

    lane_rows = R // 128

    def st_send(e, i, p):
        own = k.stats.at[e, i, h]
        return rcopy(own, own, k.st_ss.at[e, i, p], k.st_rs.at[e, i, p], (b, d, xor(p)))

    def reduce_start(e, i, rows):
        for j, v in enumerate(rows):
            row = jnp.sum(v, axis=0, keepdims=True)
            for c in range(lane_rows):
                k.stats[e, i, h, pl.ds(j * lane_rows + c, 1)] = row[:, c * 128 : (c + 1) * 128]
        if len(rows) * lane_rows < 8:
            rest = 8 - len(rows) * lane_rows
            k.stats[e, i, h, pl.ds(8 - rest, rest)] = jnp.zeros((rest, 128), F32)
        for p in range(nh - 1, 0, -1):
            st_send(e, i, p).start()

    def reduce_end(e, i, n):
        for p in range(1, nh):
            src = k.stats.at[e, i, xor(p)]
            rcopy(src, src, k.st_ss.at[e, i, p], k.st_rs.at[e, i, p], (b, d, h)).wait_recv()
        total = k.stats[e, i, 0]
        for j in range(1, nh):
            total = total + k.stats[e, i, j]
        total = total / D
        return [
            jnp.concatenate([total[j * lane_rows + c :][0:1] for c in range(lane_rows)], axis=1)
            for j in range(n)
        ]

    def cols(ref, i):
        return ref[:, i * R : (i + 1) * R]

    for i in range(MB):
        head_end(o_net, i)
        h1 = cols(k.xq, i).astype(F32) + mm(k.wot[...], k.oall[i].reshape(D, R)) + vec(V_BO)
        k.n1[i] = h1
        reduce_start(0, i, (h1, h1 * h1))

    gather_wait(M_UP)
    for w in range(W):
        slab = k.buf[M_UP, w].astype(F32)
        k.fup[w * r : w * r + rs, 0:L] = slab[0:rs]
        k.fup[w * r : w * r + rs, L:F] = slab[rs : 2 * rs]
    k.fup[C : C + 16] = jnp.zeros((16, F), F32)
    for w in range(W):
        row = k.buf[M_QKV, w].astype(F32)[rs : rs + 1, C + VECS : C + VECS + 4 * r]
        k.fup[C : C + 1, 4 * r * w : 4 * r * (w + 1)] = row
    k.wup[...] = k.fup[0:C].astype(BF16)
    k.wupt[...] = k.fup[...].T.astype(BF16)
    gather_wait(M_DOWN)
    for w in range(W):
        spread(k.fod, k.buf[M_DOWN, w], 4 * r * w)
    k.wdn[...] = k.fod[0:F].astype(BF16)
    k.wdnt[...] = k.fod[0:F].T.astype(BF16)

    first_one = jnp.where(row16 < 1, 1.0, 0.0).astype(BF16)
    r1 = [None] * MB
    gdn = [None] * MB
    for i in range(MB):
        mean, square = reduce_end(0, i, 2)
        r1[i] = lax.rsqrt(square - mean * mean + EPS)
        n1 = (k.n1[i] - mean) * r1[i]
        k.n1[i] = n1
        y1 = n1 * vec(V_G1) + vec(V_S1)
        k.y1[i] = y1
        y1b = y1.astype(BF16)
        k.y1b[:, i * R : (i + 1) * R] = y1b
        u = mm(k.wupt[...], jnp.concatenate([y1b, first_one], axis=0))
        cdf = 0.5 * (1.0 + lax.erf(u * (0.5**0.5)))
        act = (u * cdf).astype(BF16)
        k.act[:, i * R : (i + 1) * R] = act
        h2 = y1 + mm(k.wdnt[...], act) + vec(V_BD)
        k.h2[i] = h2

        @pl.when(m_t != i)
        def _():
            rcopy(k.cb.at[i], k.cb.at[i], k.c_ss.at[0], k.c_rs.at[i], (b, d, h)).wait_recv()

        dn2 = k.cb[i].astype(F32) * vec(V_G2)
        reduce_start(1, i, (h2, h2 * h2, dn2, dn2 * h2))
        k.gel[i] = cdf + u * jnp.exp(-0.5 * u * u) * ((2 * jnp.pi) ** -0.5)
    k.vg[...] = jnp.zeros_like(k.vg)
    ones = jnp.ones((16, R), BF16)

    def vec_grad(j, x):
        k.vg[j : j + 1] += mm_nt(ones, x)[0:1]

    def mo_send(i):
        return rcopy(k.mo.at[i], k.o_mo.at[m_t], k.mo_ss.at[i], k.mo_rs.at[m_t], (mine[i], d, h))

    for i in range(MB):
        mean, square, dmean, dsquare = reduce_end(1, i, 4)
        r2 = lax.rsqrt(square - mean * mean + EPS)
        g = k.cb[i].astype(F32)
        dn2 = g * vec(V_G2)
        n2 = (k.h2[i] - mean) * r2
        dh2 = r2 * (dn2 - dmean - n2 * (r2 * (dsquare - mean * dmean)))
        dz = dh2.astype(BF16)
        k.dz[:, i * R : (i + 1) * R] = dz
        du = (mm(k.wdn[...], dz) * k.gel[i]).astype(BF16)
        k.du[:, i * R : (i + 1) * R] = du
        dy1 = dh2 + mm(k.wup[...], du)
        dn1 = dy1 * vec(V_G1)
        k.dh1[i] = dn1
        n1 = k.n1[i]
        reduce_start(2, i, (dn1, dn1 * n1))
        k.mo[i] = (n2 * vec(V_G2) + vec(V_S2)).astype(BF16)

        @pl.when(m_t != i)
        def _():
            mo_send(i).start()

        @pl.when(m_t == i)
        def _():
            k.o_mo[m_t] = k.mo[i]

        vec_grad(V_G2, (g * n2).astype(BF16))
        vec_grad(V_S2, k.cb[i])
        vec_grad(V_BD, dz)
        vec_grad(V_G1, (dy1 * n1).astype(BF16))
        vec_grad(V_S1, dy1.astype(BF16))

    def s1_send(q, e, i):
        dt = lax.rem(d + e, nd)
        return rcopy(
            k.pk.at[q, i * nd + dt], k.got1.at[q, e - 1, i], k.s1_ss.at[q, e - 1, i], k.s1_rs.at[q, e - 1, i],
            (b, dt, h),
        )

    def s2_send(q, i):
        bt = lax.rem(b + i, nb)
        return rcopy(k.sent2.at[q, bt], k.got2.at[q, b], k.s2_ss.at[q, i], k.s2_rs.at[q, i], (bt, d, h))

    def scatter_start(q):
        for e in range(1, nd):
            loop(nb, lambda i: s1_send(q, e, i).start())

    def scatter_sum(q, bt):
        part = k.pk[q, bt * nd + d].astype(F32)
        for e in range(1, nd):
            src = k.got1.at[q, e - 1, bt]
            rcopy(src, src, k.s1_ss.at[q, e - 1, bt], k.s1_rs.at[q, e - 1, bt], (b, d, h)).wait_recv()
            part = part + src[...].astype(F32)
        return part

    def scatter_forward(q):
        def one(i):
            bt = lax.rem(b + i + 1, nb)
            k.sent2[q, bt] = scatter_sum(q, bt).astype(BF16)
            s2_send(q, i + 1).start()

        loop(nb - 1, one)
        k.o_G[q] = scatter_sum(q, b)

    def scatter_end(q):
        def one(i):
            src = k.got2.at[q, lax.rem(b + nb - i - 1, nb)]
            rcopy(src, src, k.s2_ss.at[q, i + 1], k.s2_rs.at[q, i + 1], (b, d, h)).wait_recv()
            k.o_G[q] += src[...].astype(F32)

        loop(nb - 1, one)
        loop(nb - 1, lambda i: s2_send(q, i + 1).wait_send())
        for e in range(1, nd):
            loop(nb, lambda i: s1_send(q, e, i).wait_send())

    def rows_of(parts):
        rows = jnp.concatenate(parts, axis=0)
        if rows.shape[0] < rA:
            rows = jnp.concatenate([rows, jnp.zeros((rA - rows.shape[0], L), F32)], axis=0)
        return rows.astype(BF16)

    def pack_halves(q, g):
        for w in range(W):
            at = 4 * r * w
            pair = jnp.concatenate([g[at : at + z.r2], g[at + 2 * r : at + 2 * r + z.r2]], axis=1)
            k.pk[q, w] = rows_of([pair])
        scatter_start(q)

    k.gdn[0:F] = mm_nt(k.act[...], k.dz[...])
    pack_halves(M_DOWN, k.gdn)
    k.gup[0:C] = mm_nt(k.y1b[...], k.du[...])
    for w in range(W):
        k.pk[M_UP, w] = rows_of([k.gup[w * r : w * r + rs, 0:L], k.gup[w * r : w * r + rs, L:F]])
    scatter_start(M_UP)

    for i in range(MB):
        dmean, dsquare = reduce_end(2, i, 2)
        dh1 = r1[i] * (k.dh1[i] - dmean - k.n1[i] * dsquare)
        k.dh1[i] = dh1
        dp = dh1.astype(BF16)
        k.pall[i, h] = dp
        head_start(p_net, i)

    g = None
    for i in range(MB):
        dp = k.pall[i, h]
        part = mm_nt(k.oall[i].reshape(D, R), dp)
        g = part if g is None else g + part
        vec_grad(V_BO, dp)
    k.gout[0:F] = g
    pack_halves(M_OUT, k.gout)
    ug = mm_nt(jnp.ones((16, z.Q), BF16), k.du[...])
    k.gq[...] = jnp.zeros_like(k.gq)
    for w in range(W):
        k.gq[w * r : w * r + 1, C + VECS : C + VECS + 4 * r] = ug[0:1, 4 * r * w : 4 * r * (w + 1)]
    k.gkv[...] = jnp.zeros_like(k.gkv)

    for p in range(1, nh):
        src = k.wob.at[xor(p)]
        rcopy(src, src, k.w_ss.at[p], k.w_rs.at[p], (b, d, h)).wait_recv()
    k.wob[h] = k.buf[M_OUT, pl.ds(h * per, per)]
    for j in range(nh):
        for n in range(per):
            spread(k.fod, k.wob[j, n], j * C + 4 * r * n)
    for j in range(nh):
        k.wor[:, j * C : (j + 1) * C] = k.fod[j * C : (j + 1) * C].astype(BF16)

    head_pass(p_net, 0)
    scatter_forward(M_DOWN)
    for i in range(1, MB):
        head_pass(p_net, i)

    def grad_in(i):
        head_end(p_net, i)
        do = mm(k.wor[...], k.pall[i].reshape(D, R)).astype(BF16).astype(F32)
        for a in range(H):
            part = do[a * HEAD_DIM : (a + 1) * HEAD_DIM] * k.mrow[i, a, 2:3]
            own = k.oall[i, h, a * HEAD_DIM : (a + 1) * HEAD_DIM].astype(F32)
            delta = jnp.sum(part * own, axis=0, keepdims=True)
            hi = delta.astype(BF16).astype(F32)
            rest = jnp.where(row16 == 0, -hi, jnp.where(row16 == 1, hi - delta, 0.0))
            full = jnp.concatenate([part.astype(BF16), rest.astype(BF16), pad], axis=0)
            k.dox[i, a] = full
            k.dqacc[i, a] = jnp.zeros((HEAD_DIM, R), F32)

    def back(j, queries, into):
        for a in range(H):
            dk = dv = None
            for i in queries:
                p = prob(i, a, j)
                ds = (p.astype(F32) * mm(k.vt[j, a], k.dox[i, a])).astype(BF16)
                k.dqacc[i, a] += mm(k.kx[j, a], ds)
                dk_i, dv_i = mm_nt(k.qx[i, a, 0:HEAD_DIM], ds), mm_nt(k.dox[i, a, 0:HEAD_DIM], p)
                dk = dk_i if dk is None else dk + dk_i
                dv = dv_i if dv is None else dv + dv_i
            into(slice(a * HEAD_DIM, (a + 1) * HEAD_DIM), dk)
            into(slice(C + a * HEAD_DIM, C + (a + 1) * HEAD_DIM), dv)

    def tokens_part(j, dkv):
        k.gkv[0:C] += mm_nt(k.xb[j], dkv)
        vec_grad(V_BV, dkv[C:L])
        return mm(k.wkv[...], dkv)

    def tp_send(n):
        j = other(n)
        slot = j // S
        return rcopy(k.tgs.at[j], k.tgr.at[slot, s_me], k.tp_ss.at[j], k.tp_rs.at[slot, s_me], (m_t * S + j % S, d, h))

    def back_other(n, queries):
        slot = n if z.keep else 0

        def into(rows, v):
            if queries[0] == 0:
                k.dkacc[slot, rows] = v
            else:
                k.dkacc[slot, rows] += v

        back(other(n), queries, into)
        if queries[-1] == MB - 1:
            k.tgs[other(n)] = tokens_part(other(n), k.dkacc[slot].astype(BF16)).astype(BF16)
            tp_send(n).start()

    for i in range(MB):
        grad_in(i)
        if z.keep:
            loop(nb - MB, lambda n: back_other(n, [i]))
        if i == 0:
            scatter_forward(M_UP)
    if not z.keep:
        loop(nb - MB, lambda n: back_other(n, list(range(MB))))

    for i in range(MB):

        def into(rows, v):
            k.dkv[rows] = v

        back(mine[i], range(MB), into)
        k.tgo[i] = tokens_part(mine[i], k.dkv[...].astype(BF16))
        if i == 0:
            scatter_forward(M_OUT)

    for i in range(MB):
        for a in range(H):
            rows = slice(a * HEAD_DIM, (a + 1) * HEAD_DIM)
            k.dq[rows, i * R : (i + 1) * R] = (k.dqacc[i, a] * HEAD_DIM**-0.5).astype(BF16)
        vec_grad(V_BQ, cols(k.dq, i))
    k.gq[0:C, 0:C] = mm_nt(k.xq[...], k.dq[...])
    k.gq[0:C, C : C + VECS] = k.vg[...].T

    for w in range(W):
        k.pk[M_QKV, w] = rows_of([k.gkv[w * r : w * r + rs], k.gq[w * r : w * r + rs]])
    scatter_start(M_QKV)

    def t_send(i):
        return rcopy(k.tgx.at[i], k.o_tg.at[m_t], k.t_ss.at[i], k.t_rs.at[m_t], (mine[i], d, h))

    for i in range(MB):
        k.tgo[i] += k.dh1[i] + mm(k.wq[...], cols(k.dq, i))

        def add(f):
            src = k.tgr.at[i, mate(f + 1)]
            rcopy(src, src, k.tp_ss.at[0], k.tp_rs.at[i, mate(f + 1)], (b, d, h)).wait_recv()
            k.tgo[i] += src[...].astype(F32)

        loop(S - 1, add)
        k.tgx[i] = k.tgo[i].astype(BF16)

        @pl.when(m_t != i)
        def _():
            t_send(i).start()

        @pl.when(m_t == i)
        def _():
            k.o_tg[m_t] = k.tgx[i]

    scatter_forward(M_QKV)

    for q in (M_DOWN, M_UP, M_OUT, M_QKV):
        scatter_end(q)
    for e in range(1, MB):
        m = later(e)
        for out, ss, rs_ in ((k.o_tg, k.t_ss, k.t_rs), (k.o_mo, k.mo_ss, k.mo_rs)):
            rcopy(out.at[m], out.at[m], ss.at[m], rs_.at[m], (b, d, h)).wait_recv()
        c_send(e).wait_send()
        x_send(e).wait_send()
        mo_send_e = rcopy(k.mo.at[m], k.o_mo.at[m_t], k.mo_ss.at[m], k.mo_rs.at[m_t], (b, d, h))
        mo_send_e.wait_send()
        t_send_e = rcopy(k.tgx.at[m], k.o_tg.at[m_t], k.t_ss.at[m], k.t_rs.at[m_t], (b, d, h))
        t_send_e.wait_send()
    for e in range(MB):
        loop(S - 1, lambda f: x_pass(e, f + 1).wait_send())
    loop(nb - MB, lambda n: tp_send(n).wait_send())
    for q in range(4):
        gather_drain(q)
    for p in range(1, nh):
        w_send(p).wait_send()
        for i in range(MB):
            head_send(o_net, i, p).wait_send()
            head_send(p_net, i, p).wait_send()
            for e in range(3):
                st_send(e, i, p).wait_send()


def finish_kernel(z, mo, tg, G, *outs):
    (mixed, dtok, dwq, dbq, dwk, dwv, dbv, dwo, dbo, dg1, ds1, dwup, dbu, dwdn, dbd, dg2, ds2) = outs
    r, rs, C, L = z.r, z.rs, z.C, z.L
    for m in range(z.MB):
        mixed[m] = mo[m].T
        dtok[m] = tg[m].astype(F32).T
    dwk[0] = G[M_QKV, 0:r, 0:C]
    dwv[0] = G[M_QKV, 0:r, C:L]
    dwq[0] = G[M_QKV, rs : rs + r, 0:C]
    dwup[0, :, 0:L] = G[M_UP, 0:r]
    dwup[0, :, L : 2 * L] = G[M_UP, rs : rs + r]
    for q, ref in ((M_OUT, dwo), (M_DOWN, dwdn.at[0])):
        ref[0 : 2 * r] = G[q, 0 : 2 * r, 0:C]
        ref[2 * r : 4 * r] = G[q, 0 : 2 * r, C:L]
    vecs = G[M_QKV, rs : 2 * rs, C : C + VECS].T
    for j, ref in enumerate((dbq, dbv, dbo, dg1, ds1, dbd, dg2, ds2)):
        ref[...] = vecs[j : j + 1, 0:r]
    dbu[...] = G[M_QKV, rs : rs + 1, C + VECS : C + VECS + 4 * r]


def solution(mesh):
    vec_spec = P("head", ("blk", "dp"))
    mat_spec = P("head", ("blk", "dp"), None)
    tok_spec = P(None, "dp", "head", "blk")
    out_spec = P(("blk", "dp"), "head")

    def body(
        tokens, doc_lengths, cotangent, query_weight, query_bias, key_weight, value_weight, value_bias,
        out_weight, out_bias, first_gain, first_shift, up_weight, up_bias, down_weight, down_bias,
        second_gain, second_shift,
    ):
        z = Sizes(mesh, tokens, query_weight, up_weight, doc_lengths)
        scratch = main_scratch(z)
        vmem = pl.BlockSpec(memory_space=pltpu.VMEM)
        smem = pl.BlockSpec(memory_space=pltpu.SMEM)
        names = INPUTS + OUTPUTS + list(scratch)
        sds = jax.ShapeDtypeStruct
        parts = pl.pallas_call(
            lambda *refs: main_kernel(z, names, *refs),
            out_shape=[
                sds((z.MB, z.C, z.R), BF16),
                sds((z.MB, z.C, z.R), BF16),
                sds((4, z.rA, z.L), F32),
            ],
            in_specs=[smem] + [vmem] * (len(INPUTS) - 1),
            out_specs=[vmem] * len(OUTPUTS),
            scratch_shapes=list(scratch.values()),
            compiler_params=pltpu.CompilerParams(
                collective_id=0, has_side_effects=True, vmem_limit_bytes=63 << 20
            ),
            name="layer",
        )(
            doc_lengths, tokens.reshape(z.MB, z.R, z.C), cotangent.reshape(z.MB, z.R, z.C), query_weight,
            query_bias, key_weight, value_weight, value_bias, out_weight, out_bias, first_gain, first_shift,
            up_weight, up_bias, down_weight, down_bias, second_gain, second_shift,
        )
        mat, vec = sds((1, z.r, z.C), F32), sds((1, z.r), F32)
        outs = pl.pallas_call(
            lambda *refs: finish_kernel(z, *refs),
            out_shape=[
                sds((z.MB, z.R, z.C), BF16), sds((z.MB, z.R, z.C), F32), mat, vec, mat, mat, vec,
                sds((4 * z.r, z.C), F32), vec, vec, vec, sds((1, z.r, z.F), F32), sds((1, 4 * z.r), F32),
                sds((1, 4 * z.r, z.C), F32), vec, vec, vec,
            ],
            in_specs=[vmem] * len(OUTPUTS),
            out_specs=[vmem] * 17,
            name="finish",
        )(*parts)
        shape = tokens.shape
        return (outs[0].reshape(shape), outs[1].reshape(shape), *outs[2:])

    return jax.shard_map(
        body,
        mesh=mesh,
        in_specs=(
            tok_spec, P(None, "dp", None), tok_spec, mat_spec, vec_spec, mat_spec, mat_spec, vec_spec,
            out_spec, vec_spec, vec_spec, vec_spec, mat_spec, vec_spec, mat_spec, vec_spec, vec_spec, vec_spec,
        ),
        out_specs=(
            tok_spec, tok_spec, mat_spec, vec_spec, mat_spec, mat_spec, vec_spec, out_spec, vec_spec, vec_spec,
            vec_spec, mat_spec, vec_spec, mat_spec, vec_spec, vec_spec, vec_spec,
        ),
        check_vma=False,
    )
```

```python
import math
import types

import jax
import jax.numpy as jnp
from jax import lax
from jax.experimental import pallas as pl
from jax.experimental.pallas import tpu as pltpu
from jax.sharding import PartitionSpec as P

HEAD_DIM = 64
EPS = 1e-05
BIG = 1e30
MESH = pl.DeviceIdType.MESH
F32 = jnp.float32
BF16 = jnp.bfloat16
V_BQ, V_BV, V_BO, V_G1, V_S1, V_BD, V_G2, V_S2 = range(8)
VECS = 16
M_QKV, M_OUT, M_UP, M_DOWN = range(4)


def up_to(n, m):
    return (n + m - 1) // m * m


def mm(a, b):
    return lax.dot_general(a, b, (((1,), (0,)), ((), ())), preferred_element_type=F32)


def mm_nt(a, b):
    return lax.dot_general(a, b, (((1,), (1,)), ((), ())), preferred_element_type=F32)


def loop(n, fn):
    if n <= 8:
        for i in range(n):
            fn(i)
    else:
        lax.fori_loop(0, n, lambda i, c: (fn(i), c)[1], 0)


def rcopy(src, dst, ss, rs, dev):
    return pltpu.make_async_remote_copy(
        src_ref=src, dst_ref=dst, send_sem=ss, recv_sem=rs, device_id=dev, device_id_type=MESH
    )


def pieces(c, u):
    at, end = u * c, (u + 1) * c
    found = []
    while at < end:
        size = min(128 - at % 128, end - at)
        found.append((at // 128, at % 128, size))
        at += size
    return found


def columns_of(z, flat):
    rows = [flat[pl.ds(i, z.R // z.per, stride=z.span)].T for i in range(z.span)]
    tokens = []
    for u in range(z.per):
        tokens.append(jnp.concatenate([rows[i][at : at + n] for i, at, n in pieces(z.C, u)], axis=0))
    return jnp.concatenate(tokens, axis=1)


def put_rows(z, value, put):
    n = z.R // z.per
    parts = [[] for _ in range(z.span)]
    for u in range(z.per):
        c = 0
        for i, _, size in pieces(z.C, u):
            parts[i].append(value[c : c + size, u * n : (u + 1) * n])
            c += size
    for i in range(z.span):
        put(i, jnp.concatenate(parts[i], axis=0).T)


class Sizes:
    def __init__(self, mesh, tokens, query_weight, up_weight, doc_lengths):
        self.nb, self.nd, self.nh = mesh.shape["blk"], mesh.shape["dp"], mesh.shape["head"]
        self.W = self.nb * self.nd
        self.C, self.F = query_weight.shape[2], up_weight.shape[2]
        self.MB = tokens.shape[0]
        self.R = tokens.shape[3] // self.C
        self.S = self.nb // self.MB
        self.Q = self.MB * self.R
        self.N = self.R * self.C // 128
        self.per = 128 // math.gcd(self.C, 128)
        self.span = self.per * self.C // 128
        self.H = self.C // HEAD_DIM
        self.ND = doc_lengths.shape[2]
        self.r = query_weight.shape[1]
        self.rs = up_to(self.r, 8)
        self.r2 = up_to(2 * self.r, 8)
        self.rA = up_to(2 * self.rs, 16)
        self.L = 2 * self.C
        self.keep = self.nb * self.R * self.Q * self.H * 2 <= (8 << 20)
        assert self.F == 4 * self.C and self.F == self.nh * self.C and self.W % self.nh == 0


def main_scratch(z):
    dma = pltpu.SemaphoreType.DMA
    v = pltpu.VMEM
    nb, W, L, R, C, F, Q, H, MB, rA, nh = z.nb, z.W, z.L, z.R, z.C, z.F, z.Q, z.H, z.MB, z.rA, z.nh
    dd = max(z.nd - 1, 1)
    return dict(
        flat=v((2 * MB, z.N, 128), F32),
        xs=v((MB, C, R), BF16),
        xb=v((nb, C, R), BF16),
        cs=v((MB, C, R), BF16),
        cb=v((MB, C, R), BF16),
        buf=v((4, W, rA, L), BF16),
        wob=v((nh, W // nh, rA, L), BF16),
        fst=v((rA, L), F32),
        vst=v((VECS, 128), F32),
        fkv=v((C + 8, L), F32),
        fq=v((C + 8, L), F32),
        fup=v((C + 16, F), F32),
        fod=v((F + 16, C), F32),
        wkv=v((C, L), BF16),
        wkvt=v((L, C), BF16),
        wq=v((C, C), BF16),
        wqt=v((C, C), BF16),
        wup=v((C, F), BF16),
        wupt=v((F, C + 16), BF16),
        wor=v((C, F), BF16),
        wot=v((C, F), BF16),
        wdn=v((F, C), BF16),
        wdnt=v((C, F), BF16),
        xq=v((C, Q), BF16),
        qx=v((MB, H, 128, R), BF16),
        kx=v((nb, H, HEAD_DIM, R), BF16),
        vx=v((nb, H, HEAD_DIM + 16, R), BF16),
        kt=v((nb, H, R, 128), BF16),
        vt=v((nb, H, R, 128), BF16),
        pbuf=v((MB, H, nb, R, R) if z.keep else (1, 1, 1, 16, 128), BF16),
        mrow=v((MB, H, 8, R), F32),
        oall=v((MB, nh, C, R), BF16),
        pall=v((MB, nh, C, R), BF16),
        stats=v((3, MB, nh, 8, 128), F32),
        n1=v((MB, C, R), F32),
        y1=v((MB, C, R), F32),
        h2=v((MB, C, R), F32),
        gel=v((MB, F, R), F32),
        dh1=v((MB, C, R), F32),
        y1b=v((C, Q), BF16),
        act=v((F, Q), BF16),
        dz=v((C, Q), BF16),
        du=v((F, Q), BF16),
        mo=v((MB, C, R), BF16),
        dox=v((MB, H, 128, R), BF16),
        dqacc=v((MB, H, HEAD_DIM, R), F32),
        dkacc=v((nb - MB if z.keep else 1, L, R), F32),
        dkv=v((L, R), F32),
        dq=v((C, Q), BF16),
        tgs=v((nb, C, R), BF16),
        tgo=v((MB, C, R), F32),
        tgr=v((MB, z.S, C, R), BF16),
        tgx=v((MB, C, R), BF16),
        gkv=v((C + 8, L), F32),
        gq=v((C + 8, L), F32),
        gup=v((C + 8, F), F32),
        gout=v((F + 16, C), F32),
        gdn=v((F + 16, C), F32),
        vg=v((VECS, C), F32),
        ug=v((8, F), F32),
        pk=v((4, W, rA, L), BF16),
        got1=v((4, dd, nb, rA, L), BF16),
        sent2=v((4, nb, rA, L), BF16),
        got2=v((4, nb, rA, L), BF16),
        x_ss=dma((MB,)),
        xf_ss=dma((MB, z.S)),
        x_rs=dma((nb,)),
        c_ss=dma((MB,)),
        c_rs=dma((MB,)),
        g1_ss=dma((4, nb)),
        g1_rs=dma((4, nb)),
        g2_ss=dma((4, dd, nb)),
        g2_rs=dma((4, dd, nb)),
        o_ss=dma((MB, nh)),
        o_rs=dma((MB, nh)),
        p_ss=dma((MB, nh)),
        p_rs=dma((MB, nh)),
        w_ss=dma((nh,)),
        w_rs=dma((nh,)),
        st_ss=dma((3, MB, nh)),
        st_rs=dma((3, MB, nh)),
        mo_ss=dma((MB,)),
        mo_rs=dma((MB,)),
        tp_ss=dma((nb,)),
        tp_rs=dma((MB, z.S)),
        t_ss=dma((MB,)),
        t_rs=dma((MB,)),
        s1_ss=dma((4, dd, nb)),
        s1_rs=dma((4, dd, nb)),
        s2_ss=dma((4, nb)),
        s2_rs=dma((4, nb)),
    )


INPUTS = [
    "lens", "tok", "cot", "wq_in", "bq", "wk_in", "wv_in", "bv", "wo_in", "bo", "g1", "s1", "wup_in", "bu",
    "wdn_in", "bd", "g2", "s2",
]
OUTPUTS = ["o_mo", "o_tg", "o_G"]


def main_kernel(z, names, *refs):
    k = types.SimpleNamespace(**dict(zip(names, refs)))
    nb, nd, nh, W, MB, R, C, F, H, L, S, r, rs, rA = (
        z.nb, z.nd, z.nh, z.W, z.MB, z.R, z.C, z.F, z.H, z.L, z.S, z.r, z.rs, z.rA,
    )
    b, d, h = lax.axis_index("blk"), lax.axis_index("dp"), lax.axis_index("head")
    w_me = b * nd + d
    m_t, s_me = b // S, b % S
    mine = [i * S + s_me for i in range(MB)]
    D = nh * C
    half = nh // 2

    def xor(i):
        return lax.bitwise_xor(h, i)

    def later(e):
        return lax.rem(m_t + e, MB)

    def mate(e):
        return lax.rem(s_me + e, S)

    bar = pltpu.get_barrier_semaphore()
    peers = [(lax.rem(b + i, nb), d, h) for i in range(1, nb)]
    peers += [(b, lax.rem(d + i, nd), h) for i in range(1, nd)]
    peers += [(b, d, xor(i)) for i in range(1, nh)]
    for peer in peers:
        pl.semaphore_signal(bar, inc=1, device_id=peer, device_id_type=MESH)

    def pack(q):
        k.buf[q, w_me] = k.fst[...].astype(BF16)

    k.vst[...] = jnp.zeros_like(k.vst)
    for j, ref in enumerate((k.bq, k.bv, k.bo, k.g1, k.s1, k.bd, k.g2, k.s2)):
        k.vst[j : j + 1, 0:r] = ref[...].astype(F32)
    k.fst[...] = jnp.zeros_like(k.fst)
    k.fst[0:r, 0:C] = k.wk_in[0].astype(F32)
    k.fst[0:r, C:L] = k.wv_in[0].astype(F32)
    k.fst[rs : rs + r, 0:C] = k.wq_in[0].astype(F32)
    k.fst[rs : rs + r, C : C + VECS] = k.vst[...].T[0:r]
    k.fst[rs : rs + 1, C + VECS : C + VECS + 4 * r] = k.bu[...].astype(F32)
    pack(M_QKV)
    for q, src in ((M_OUT, k.wo_in[...]), (M_DOWN, k.wdn_in[0])):
        src = src.astype(F32)
        k.fst[0 : 2 * r, 0:C] = src[0 : 2 * r]
        k.fst[0 : 2 * r, C:L] = src[2 * r : 4 * r]
        pack(q)
    k.fst[0:r] = k.wup_in[0, :, 0:L].astype(F32)
    k.fst[rs : rs + r] = k.wup_in[0, :, L : 2 * L].astype(F32)
    pack(M_UP)

    for n, (src, dst) in enumerate(((k.tok, k.xs), (k.cot, k.cs))):
        both = src[...].astype(F32)
        for m in range(MB):
            k.flat[n * MB + m] = both[:, m]
            dst[m] = columns_of(z, k.flat.at[n * MB + m]).astype(BF16)
    k.xb[b] = k.xs[m_t]
    k.cb[m_t] = k.cs[m_t]

    pl.semaphore_wait(bar, len(peers))

    def g1(q, i):
        own = k.buf.at[q, w_me]
        return rcopy(own, own, k.g1_ss.at[q, i], k.g1_rs.at[q, i], (lax.rem(b + i, nb), d, h))

    def g1_wait(q, i):
        src = k.buf.at[q, lax.rem(b + nb - i, nb) * nd + d]
        rcopy(src, src, k.g1_ss.at[q, i], k.g1_rs.at[q, i], (b, d, h)).wait_recv()

    def g2(q, e, i):
        src = k.buf.at[q, lax.rem(b + nb - i, nb) * nd + d]
        return rcopy(src, src, k.g2_ss.at[q, e - 1, i], k.g2_rs.at[q, e - 1, i], (b, lax.rem(d + e, nd), h))

    def g2_wait(q, e, i):
        src = k.buf.at[q, lax.rem(b + nb - i, nb) * nd + lax.rem(d + nd - e, nd)]
        rcopy(src, src, k.g2_ss.at[q, e - 1, i], k.g2_rs.at[q, e - 1, i], (b, d, h)).wait_recv()

    def gather_start(q):
        for e in range(1, nd):
            g2(q, e, 0).start()
        loop(nb - 1, lambda i: g1(q, i + 1).start())

    def gather_forward(q):
        def one(i):
            g1_wait(q, i + 1)
            for e in range(1, nd):
                g2(q, e, i + 1).start()

        loop(nb - 1, one)

    def gather_wait(q):
        for e in range(1, nd):
            loop(nb, lambda i: g2_wait(q, e, i))

    def gather_drain(q):
        loop(nb - 1, lambda i: g1(q, i + 1).wait_send())
        for e in range(1, nd):
            loop(nb, lambda i: g2(q, e, i).wait_send())

    gather_start(M_QKV)

    def x_send(e):
        m = later(e)
        return rcopy(k.xs.at[m], k.xb.at[b], k.x_ss.at[e], k.x_rs.at[b], (m * S + s_me, d, h))

    def x_pass(e, f):
        src = k.xb.at[later(e) * S + s_me]
        return rcopy(src, src, k.xf_ss.at[e, f], k.x_rs.at[later(e) * S + s_me], (m_t * S + mate(f), d, h))

    def x_wait(j):
        rcopy(k.xb.at[j], k.xb.at[j], k.x_ss.at[0], k.x_rs.at[j], (b, d, h)).wait_recv()

    for e in range(1, MB):
        x_send(e).start()
    loop(S - 1, lambda f: x_pass(0, f + 1).start())

    gather_forward(M_QKV)

    for e in range(1, MB):
        x_wait(later(e) * S + s_me)
        loop(S - 1, lambda f: x_pass(e, f + 1).start())
    gather_start(M_OUT)

    gather_wait(M_QKV)

    for w in range(W):
        slab = k.buf[M_QKV, w].astype(F32)
        k.fkv[w * r : w * r + rs] = slab[0:rs]
        k.fq[w * r : w * r + rs] = slab[rs : 2 * rs]
    k.wkv[...] = k.fkv[0:C].astype(BF16)
    k.wkvt[...] = k.fkv[0:C].T.astype(BF16)
    k.wq[...] = k.fq[0:C, 0:C].astype(BF16)
    k.wqt[...] = k.fq[0:C, 0:C].T.astype(BF16)

    def vec(j):
        return k.fq[0:C, C + j : C + j + 1]

    row16 = lax.broadcasted_iota(jnp.int32, (16, R), 0)
    column = lax.broadcasted_iota(jnp.int32, (16, R), 1)
    step = R // z.per
    token = z.per * (column % step) + column // step
    pad = jnp.zeros((48, R), BF16)
    one_rows = jnp.where(row16 < 2, 1.0, 0.0).astype(BF16)

    def in_doc(j):
        doc = jnp.zeros((16, R), jnp.int32)
        end = jnp.int32(0)
        for n in range(z.ND):
            end = end + k.lens[m_t, 0, n]
            doc = doc + (j * R + token >= end).astype(jnp.int32)
        return row16 == doc

    def kv_block(j):
        kv = mm(k.wkvt[...], k.xb[j])
        kb = kv[0:C].astype(BF16)
        vb = (kv[C:L] + vec(V_BV)).astype(BF16)
        barred = jnp.logical_and(row16 < z.ND, jnp.logical_not(in_doc(j)))
        kf = jnp.where(barred, -BIG, 0.0).astype(BF16)
        for a in range(H):
            kh, vh = kb[a * HEAD_DIM : (a + 1) * HEAD_DIM], vb[a * HEAD_DIM : (a + 1) * HEAD_DIM]
            k.kx[j, a] = kh
            k.vx[j, a, 0:HEAD_DIM] = vh
            k.vx[j, a, HEAD_DIM:] = one_rows
            k.kt[j, a] = jnp.concatenate([kh, kf, pad], axis=0).T
            k.vt[j, a] = jnp.concatenate([vh, one_rows, pad], axis=0).T

    def other(n):
        return lax.rem(s_me + 1 + n // MB, S) + lax.rem(m_t + n, MB) * S

    def kv_other(n):
        x_wait(other(n))
        kv_block(other(n))

    for i in range(MB):
        kv_block(mine[i])

    for i in range(MB):
        xi = k.xb[mine[i]]
        k.xq[:, i * R : (i + 1) * R] = xi
        qi = ((mm(k.wqt[...], xi) + vec(V_BQ)).astype(BF16).astype(F32) * HEAD_DIM**-0.5).astype(BF16)
        hot = jnp.where(in_doc(mine[i]), 1.0, 0.0).astype(BF16)
        for a in range(H):
            full = jnp.concatenate([qi[a * HEAD_DIM : (a + 1) * HEAD_DIM], hot, pad], axis=0)
            k.qx[i, a] = full

    loop(nb - MB, kv_other)
    gather_start(M_UP)

    def head_send(net, i, p):
        buf, ss, rs_ = net
        src, to = (h, xor(p)) if p <= half else (xor(half), xor(p - half))
        return rcopy(buf.at[i, src], buf.at[i, src], ss.at[i, p], rs_.at[i, p], (b, d, to))

    def head_wait(net, i, p):
        buf, ss, rs_ = net
        rcopy(buf.at[i, xor(p)], buf.at[i, xor(p)], ss.at[i, p], rs_.at[i, p], (b, d, h)).wait_recv()

    def head_start(net, i):
        for p in range(half, 0, -1):
            head_send(net, i, p).start()

    def head_pass(net, i):
        head_wait(net, i, half)
        for p in range(half + 1, nh):
            head_send(net, i, p).start()

    def head_end(net, i):
        for p in range(1, nh):
            if p != half:
                head_wait(net, i, p)

    o_net = (k.oall, k.o_ss, k.o_rs)
    p_net = (k.pall, k.p_ss, k.p_rs)

    def scores(i, a, j):
        return mm(k.kt[j, a], k.qx[i, a])

    def prob(i, a, j):
        if z.keep:
            return k.pbuf[i, a, j]
        return jnp.exp(scores(i, a, j) - k.mrow[i, a, 0:1]).astype(BF16)

    def attend(i, a):
        if z.keep:
            s = [scores(i, a, j) for j in range(nb)]
            top = jnp.max(s[0], axis=0, keepdims=True)
            for j in range(1, nb):
                top = jnp.maximum(top, jnp.max(s[j], axis=0, keepdims=True))
            o = None
            for j in range(nb):
                e = jnp.exp(s[j] - top).astype(BF16)
                k.pbuf[i, a, j] = e
                o = mm(k.vx[j, a], e) if o is None else o + mm(k.vx[j, a], e)
        else:
            k.mrow[i, a, 0:1] = jnp.full((1, R), -3e38, F32)

            def see(j):
                best = jnp.max(scores(i, a, j), axis=0, keepdims=True)
                k.mrow[i, a, 0:1] = jnp.maximum(k.mrow[i, a, 0:1], best)

            loop(nb, see)
            acc = k.tgo.at[0, 0 : HEAD_DIM + 16]
            acc[...] = jnp.zeros((HEAD_DIM + 16, R), F32)

            def add(j):
                acc[...] += mm(k.vx[j, a], prob(i, a, j))

            loop(nb, add)
            o = acc[...]
        inv = 1.0 / o[HEAD_DIM : HEAD_DIM + 1]
        k.mrow[i, a, 2:3] = inv
        k.oall[i, h, a * HEAD_DIM : (a + 1) * HEAD_DIM] = (o[0:HEAD_DIM] * inv).astype(BF16)

    for i in range(MB):
        for a in range(H):
            attend(i, a)
        head_start(o_net, i)
    gather_start(M_DOWN)

    def c_send(e):
        m = later(e)
        return rcopy(k.cs.at[m], k.cb.at[m_t], k.c_ss.at[e], k.c_rs.at[m_t], (m * S + s_me, d, h))

    for e in range(1, MB):
        c_send(e).start()

    gather_forward(M_OUT)
    gather_forward(M_UP)
    for i in range(MB):
        head_pass(o_net, i)
    gather_wait(M_OUT)

    per = W // nh

    def w_send(p):
        src = k.buf.at[M_OUT, pl.ds(xor(p) * per, per)]
        return rcopy(src, k.wob.at[h], k.w_ss.at[p], k.w_rs.at[p], (b, d, xor(p)))

    for p in range(1, nh):
        w_send(p).start()

    def spread(dst, slab, row):
        slab = slab.astype(F32)
        dst[row : row + z.r2] = slab[0 : z.r2, 0:C]
        dst[row + 2 * r : row + 2 * r + z.r2] = slab[0 : z.r2, C:L]

    for w in range(W):
        spread(k.fod, k.buf[M_OUT, w], 4 * r * w)
    k.wot[...] = k.fod[0:F].T.astype(BF16)

    gather_forward(M_DOWN)

    lane_rows = R // 128

    def st_send(e, i, p):
        own = k.stats.at[e, i, h]
        return rcopy(own, own, k.st_ss.at[e, i, p], k.st_rs.at[e, i, p], (b, d, xor(p)))

    def reduce_start(e, i, rows):
        for j, v in enumerate(rows):
            row = jnp.sum(v, axis=0, keepdims=True)
            for c in range(lane_rows):
                k.stats[e, i, h, pl.ds(j * lane_rows + c, 1)] = row[:, c * 128 : (c + 1) * 128]
        if len(rows) * lane_rows < 8:
            rest = 8 - len(rows) * lane_rows
            k.stats[e, i, h, pl.ds(8 - rest, rest)] = jnp.zeros((rest, 128), F32)
        for p in range(nh - 1, 0, -1):
            st_send(e, i, p).start()

    def reduce_end(e, i, n):
        for p in range(1, nh):
            src = k.stats.at[e, i, xor(p)]
            rcopy(src, src, k.st_ss.at[e, i, p], k.st_rs.at[e, i, p], (b, d, h)).wait_recv()
        total = k.stats[e, i, 0]
        for j in range(1, nh):
            total = total + k.stats[e, i, j]
        total = total / D
        return [
            jnp.concatenate([total[j * lane_rows + c :][0:1] for c in range(lane_rows)], axis=1)
            for j in range(n)
        ]

    def cols(ref, i):
        return ref[:, i * R : (i + 1) * R]

    for i in range(MB):
        head_end(o_net, i)
        h1 = cols(k.xq, i).astype(F32) + mm(k.wot[...], k.oall[i].reshape(D, R)) + vec(V_BO)
        k.n1[i] = h1
        reduce_start(0, i, (h1, h1 * h1))

    gather_wait(M_UP)
    for w in range(W):
        slab = k.buf[M_UP, w].astype(F32)
        k.fup[w * r : w * r + rs, 0:L] = slab[0:rs]
        k.fup[w * r : w * r + rs, L:F] = slab[rs : 2 * rs]
    k.fup[C : C + 16] = jnp.zeros((16, F), F32)
    for w in range(W):
        row = k.buf[M_QKV, w].astype(F32)[rs : rs + 1, C + VECS : C + VECS + 4 * r]
        k.fup[C : C + 1, 4 * r * w : 4 * r * (w + 1)] = row
    k.wup[...] = k.fup[0:C].astype(BF16)
    k.wupt[...] = k.fup[...].T.astype(BF16)
    gather_wait(M_DOWN)
    for w in range(W):
        spread(k.fod, k.buf[M_DOWN, w], 4 * r * w)
    k.wdn[...] = k.fod[0:F].astype(BF16)
    k.wdnt[...] = k.fod[0:F].T.astype(BF16)

    first_one = jnp.where(row16 < 1, 1.0, 0.0).astype(BF16)
    r1 = [None] * MB
    gdn = [None] * MB
    for i in range(MB):
        mean, square = reduce_end(0, i, 2)
        r1[i] = lax.rsqrt(square - mean * mean + EPS)
        n1 = (k.n1[i] - mean) * r1[i]
        k.n1[i] = n1
        y1 = n1 * vec(V_G1) + vec(V_S1)
        k.y1[i] = y1
        y1b = y1.astype(BF16)
        k.y1b[:, i * R : (i + 1) * R] = y1b
        u = mm(k.wupt[...], jnp.concatenate([y1b, first_one], axis=0))
        cdf = 0.5 * (1.0 + lax.erf(u * (0.5**0.5)))
        act = (u * cdf).astype(BF16)
        k.act[:, i * R : (i + 1) * R] = act
        h2 = y1 + mm(k.wdnt[...], act) + vec(V_BD)
        k.h2[i] = h2

        @pl.when(m_t != i)
        def _():
            rcopy(k.cb.at[i], k.cb.at[i], k.c_ss.at[0], k.c_rs.at[i], (b, d, h)).wait_recv()

        dn2 = k.cb[i].astype(F32) * vec(V_G2)
        reduce_start(1, i, (h2, h2 * h2, dn2, dn2 * h2))
        k.gel[i] = cdf + u * jnp.exp(-0.5 * u * u) * ((2 * jnp.pi) ** -0.5)
    k.vg[...] = jnp.zeros_like(k.vg)
    ones = jnp.ones((16, R), BF16)

    def vec_grad(j, x):
        k.vg[j : j + 1] += mm_nt(ones, x)[0:1]

    def mo_send(i):
        return rcopy(k.mo.at[i], k.o_mo.at[m_t], k.mo_ss.at[i], k.mo_rs.at[m_t], (mine[i], d, h))

    for i in range(MB):
        mean, square, dmean, dsquare = reduce_end(1, i, 4)
        r2 = lax.rsqrt(square - mean * mean + EPS)
        g = k.cb[i].astype(F32)
        dn2 = g * vec(V_G2)
        n2 = (k.h2[i] - mean) * r2
        dh2 = r2 * (dn2 - dmean - n2 * (r2 * (dsquare - mean * dmean)))
        dz = dh2.astype(BF16)
        k.dz[:, i * R : (i + 1) * R] = dz
        du = (mm(k.wdn[...], dz) * k.gel[i]).astype(BF16)
        k.du[:, i * R : (i + 1) * R] = du
        dy1 = dh2 + mm(k.wup[...], du)
        dn1 = dy1 * vec(V_G1)
        k.dh1[i] = dn1
        n1 = k.n1[i]
        reduce_start(2, i, (dn1, dn1 * n1))
        k.mo[i] = (n2 * vec(V_G2) + vec(V_S2)).astype(BF16)

        @pl.when(m_t != i)
        def _():
            mo_send(i).start()

        @pl.when(m_t == i)
        def _():
            k.o_mo[m_t] = k.mo[i]

        vec_grad(V_G2, (g * n2).astype(BF16))
        vec_grad(V_S2, k.cb[i])
        vec_grad(V_BD, dz)
        vec_grad(V_G1, (dy1 * n1).astype(BF16))
        vec_grad(V_S1, dy1.astype(BF16))

    def s1_send(q, e, i):
        dt = lax.rem(d + e, nd)
        return rcopy(
            k.pk.at[q, i * nd + dt], k.got1.at[q, e - 1, i], k.s1_ss.at[q, e - 1, i], k.s1_rs.at[q, e - 1, i],
            (b, dt, h),
        )

    def s2_send(q, i):
        bt = lax.rem(b + i, nb)
        return rcopy(k.sent2.at[q, bt], k.got2.at[q, b], k.s2_ss.at[q, i], k.s2_rs.at[q, i], (bt, d, h))

    def scatter_start(q):
        for e in range(1, nd):
            loop(nb, lambda i: s1_send(q, e, i).start())

    def scatter_sum(q, bt):
        part = k.pk[q, bt * nd + d].astype(F32)
        for e in range(1, nd):
            src = k.got1.at[q, e - 1, bt]
            rcopy(src, src, k.s1_ss.at[q, e - 1, bt], k.s1_rs.at[q, e - 1, bt], (b, d, h)).wait_recv()
            part = part + src[...].astype(F32)
        return part

    def scatter_forward(q):
        def one(i):
            bt = lax.rem(b + i + 1, nb)
            k.sent2[q, bt] = scatter_sum(q, bt).astype(BF16)
            s2_send(q, i + 1).start()

        loop(nb - 1, one)
        k.o_G[q] = scatter_sum(q, b)

    def scatter_end(q):
        def one(i):
            src = k.got2.at[q, lax.rem(b + nb - i - 1, nb)]
            rcopy(src, src, k.s2_ss.at[q, i + 1], k.s2_rs.at[q, i + 1], (b, d, h)).wait_recv()
            k.o_G[q] += src[...].astype(F32)

        loop(nb - 1, one)
        loop(nb - 1, lambda i: s2_send(q, i + 1).wait_send())
        for e in range(1, nd):
            loop(nb, lambda i: s1_send(q, e, i).wait_send())

    def rows_of(parts):
        rows = jnp.concatenate(parts, axis=0)
        if rows.shape[0] < rA:
            rows = jnp.concatenate([rows, jnp.zeros((rA - rows.shape[0], L), F32)], axis=0)
        return rows.astype(BF16)

    def pack_halves(q, g):
        for w in range(W):
            at = 4 * r * w
            pair = jnp.concatenate([g[at : at + z.r2], g[at + 2 * r : at + 2 * r + z.r2]], axis=1)
            k.pk[q, w] = rows_of([pair])
        scatter_start(q)

    k.gdn[0:F] = mm_nt(k.act[...], k.dz[...])
    pack_halves(M_DOWN, k.gdn)
    k.gup[0:C] = mm_nt(k.y1b[...], k.du[...])
    for w in range(W):
        k.pk[M_UP, w] = rows_of([k.gup[w * r : w * r + rs, 0:L], k.gup[w * r : w * r + rs, L:F]])
    scatter_start(M_UP)

    for i in range(MB):
        dmean, dsquare = reduce_end(2, i, 2)
        dh1 = r1[i] * (k.dh1[i] - dmean - k.n1[i] * dsquare)
        k.dh1[i] = dh1
        dp = dh1.astype(BF16)
        k.pall[i, h] = dp
        head_start(p_net, i)

    g = None
    for i in range(MB):
        dp = k.pall[i, h]
        part = mm_nt(k.oall[i].reshape(D, R), dp)
        g = part if g is None else g + part
        vec_grad(V_BO, dp)
    k.gout[0:F] = g
    pack_halves(M_OUT, k.gout)
    ug = mm_nt(jnp.ones((16, z.Q), BF16), k.du[...])
    k.gq[...] = jnp.zeros_like(k.gq)
    for w in range(W):
        k.gq[w * r : w * r + 1, C + VECS : C + VECS + 4 * r] = ug[0:1, 4 * r * w : 4 * r * (w + 1)]
    k.gkv[...] = jnp.zeros_like(k.gkv)

    for p in range(1, nh):
        src = k.wob.at[xor(p)]
        rcopy(src, src, k.w_ss.at[p], k.w_rs.at[p], (b, d, h)).wait_recv()
    k.wob[h] = k.buf[M_OUT, pl.ds(h * per, per)]
    for j in range(nh):
        for n in range(per):
            spread(k.fod, k.wob[j, n], j * C + 4 * r * n)
    for j in range(nh):
        k.wor[:, j * C : (j + 1) * C] = k.fod[j * C : (j + 1) * C].astype(BF16)

    head_pass(p_net, 0)
    scatter_forward(M_DOWN)
    for i in range(1, MB):
        head_pass(p_net, i)

    def grad_in(i):
        head_end(p_net, i)
        do = mm(k.wor[...], k.pall[i].reshape(D, R)).astype(BF16).astype(F32)
        for a in range(H):
            part = do[a * HEAD_DIM : (a + 1) * HEAD_DIM] * k.mrow[i, a, 2:3]
            own = k.oall[i, h, a * HEAD_DIM : (a + 1) * HEAD_DIM].astype(F32)
            delta = jnp.sum(part * own, axis=0, keepdims=True)
            hi = delta.astype(BF16).astype(F32)
            rest = jnp.where(row16 == 0, -hi, jnp.where(row16 == 1, hi - delta, 0.0))
            full = jnp.concatenate([part.astype(BF16), rest.astype(BF16), pad], axis=0)
            k.dox[i, a] = full
            k.dqacc[i, a] = jnp.zeros((HEAD_DIM, R), F32)

    def back(j, queries, into):
        for a in range(H):
            dk = dv = None
            for i in queries:
                p = prob(i, a, j)
                ds = (p.astype(F32) * mm(k.vt[j, a], k.dox[i, a])).astype(BF16)
                k.dqacc[i, a] += mm(k.kx[j, a], ds)
                dk_i, dv_i = mm_nt(k.qx[i, a, 0:HEAD_DIM], ds), mm_nt(k.dox[i, a, 0:HEAD_DIM], p)
                dk = dk_i if dk is None else dk + dk_i
                dv = dv_i if dv is None else dv + dv_i
            into(slice(a * HEAD_DIM, (a + 1) * HEAD_DIM), dk)
            into(slice(C + a * HEAD_DIM, C + (a + 1) * HEAD_DIM), dv)

    def tokens_part(j, dkv):
        k.gkv[0:C] += mm_nt(k.xb[j], dkv)
        vec_grad(V_BV, dkv[C:L])
        return mm(k.wkv[...], dkv)

    def tp_send(n):
        j = other(n)
        slot = j // S
        return rcopy(k.tgs.at[j], k.tgr.at[slot, s_me], k.tp_ss.at[j], k.tp_rs.at[slot, s_me], (m_t * S + j % S, d, h))

    def back_other(n, queries):
        slot = n if z.keep else 0

        def into(rows, v):
            if queries[0] == 0:
                k.dkacc[slot, rows] = v
            else:
                k.dkacc[slot, rows] += v

        back(other(n), queries, into)
        if queries[-1] == MB - 1:
            k.tgs[other(n)] = tokens_part(other(n), k.dkacc[slot].astype(BF16)).astype(BF16)
            tp_send(n).start()

    for i in range(MB):
        grad_in(i)
        if z.keep:
            loop(nb - MB, lambda n: back_other(n, [i]))
        if i == 0:
            scatter_forward(M_UP)
    if not z.keep:
        loop(nb - MB, lambda n: back_other(n, list(range(MB))))

    for i in range(MB):

        def into(rows, v):
            k.dkv[rows] = v

        back(mine[i], range(MB), into)
        k.tgo[i] = tokens_part(mine[i], k.dkv[...].astype(BF16))
        if i == 0:
            scatter_forward(M_OUT)

    for i in range(MB):
        for a in range(H):
            rows = slice(a * HEAD_DIM, (a + 1) * HEAD_DIM)
            k.dq[rows, i * R : (i + 1) * R] = (k.dqacc[i, a] * HEAD_DIM**-0.5).astype(BF16)
        vec_grad(V_BQ, cols(k.dq, i))
    k.gq[0:C, 0:C] = mm_nt(k.xq[...], k.dq[...])
    k.gq[0:C, C : C + VECS] = k.vg[...].T

    for w in range(W):
        k.pk[M_QKV, w] = rows_of([k.gkv[w * r : w * r + rs], k.gq[w * r : w * r + rs]])
    scatter_start(M_QKV)

    def t_send(i):
        return rcopy(k.tgx.at[i], k.o_tg.at[m_t], k.t_ss.at[i], k.t_rs.at[m_t], (mine[i], d, h))

    for i in range(MB):
        k.tgo[i] += k.dh1[i] + mm(k.wq[...], cols(k.dq, i))

        def add(f):
            src = k.tgr.at[i, mate(f + 1)]
            rcopy(src, src, k.tp_ss.at[0], k.tp_rs.at[i, mate(f + 1)], (b, d, h)).wait_recv()
            k.tgo[i] += src[...].astype(F32)

        loop(S - 1, add)
        k.tgx[i] = k.tgo[i].astype(BF16)

        @pl.when(m_t != i)
        def _():
            t_send(i).start()

        @pl.when(m_t == i)
        def _():
            k.o_tg[m_t] = k.tgx[i]

    scatter_forward(M_QKV)

    for q in (M_DOWN, M_UP, M_OUT, M_QKV):
        scatter_end(q)
    for e in range(1, MB):
        m = later(e)
        for out, ss, rs_ in ((k.o_tg, k.t_ss, k.t_rs), (k.o_mo, k.mo_ss, k.mo_rs)):
            rcopy(out.at[m], out.at[m], ss.at[m], rs_.at[m], (b, d, h)).wait_recv()
        c_send(e).wait_send()
        x_send(e).wait_send()
        mo_send_e = rcopy(k.mo.at[m], k.o_mo.at[m_t], k.mo_ss.at[m], k.mo_rs.at[m_t], (b, d, h))
        mo_send_e.wait_send()
        t_send_e = rcopy(k.tgx.at[m], k.o_tg.at[m_t], k.t_ss.at[m], k.t_rs.at[m_t], (b, d, h))
        t_send_e.wait_send()
    for e in range(MB):
        loop(S - 1, lambda f: x_pass(e, f + 1).wait_send())
    loop(nb - MB, lambda n: tp_send(n).wait_send())
    for q in range(4):
        gather_drain(q)
    for p in range(1, nh):
        w_send(p).wait_send()
        for i in range(MB):
            head_send(o_net, i, p).wait_send()
            head_send(p_net, i, p).wait_send()
            for e in range(3):
                st_send(e, i, p).wait_send()


def finish_kernel(z, mo, tg, G, *outs):
    (mixed, dtok, dwq, dbq, dwk, dwv, dbv, dwo, dbo, dg1, ds1, dwup, dbu, dwdn, dbd, dg2, ds2, both) = outs
    r, rs, C, L = z.r, z.rs, z.C, z.L
    for m in range(z.MB):


        def put_mixed(i, rows):
            both[pl.ds(i, z.R // z.per, stride=z.span), m] = rows

        def put_grad(i, rows):
            dtok[m, pl.ds(i, z.R // z.per, stride=z.span)] = rows

        put_rows(z, mo[m].astype(F32), put_mixed)
        put_rows(z, tg[m].astype(F32), put_grad)
    mixed[...] = both[...].astype(BF16)
    dwk[0] = G[M_QKV, 0:r, 0:C]
    dwv[0] = G[M_QKV, 0:r, C:L]
    dwq[0] = G[M_QKV, rs : rs + r, 0:C]
    dwup[0, :, 0:L] = G[M_UP, 0:r]
    dwup[0, :, L : 2 * L] = G[M_UP, rs : rs + r]
    for q, ref in ((M_OUT, dwo), (M_DOWN, dwdn.at[0])):
        ref[0 : 2 * r] = G[q, 0 : 2 * r, 0:C]
        ref[2 * r : 4 * r] = G[q, 0 : 2 * r, C:L]
    vecs = G[M_QKV, rs : 2 * rs, C : C + VECS].T
    for j, ref in enumerate((dbq, dbv, dbo, dg1, ds1, dbd, dg2, ds2)):
        ref[...] = vecs[j : j + 1, 0:r]
    dbu[...] = G[M_QKV, rs : rs + 1, C + VECS : C + VECS + 4 * r]


def solution(mesh):
    vec_spec = P("head", ("blk", "dp"))
    mat_spec = P("head", ("blk", "dp"), None)
    tok_spec = P(None, "dp", "head", "blk")
    out_spec = P(("blk", "dp"), "head")

    def body(
        tokens, doc_lengths, cotangent, query_weight, query_bias, key_weight, value_weight, value_bias,
        out_weight, out_bias, first_gain, first_shift, up_weight, up_bias, down_weight, down_bias,
        second_gain, second_shift,
    ):
        z = Sizes(mesh, tokens, query_weight, up_weight, doc_lengths)

        def as_rows(a):
            return a.reshape(z.MB, z.N, 128).transpose(1, 0, 2)

        scratch = main_scratch(z)
        vmem = pl.BlockSpec(memory_space=pltpu.VMEM)
        smem = pl.BlockSpec(memory_space=pltpu.SMEM)
        names = INPUTS + OUTPUTS + list(scratch)
        sds = jax.ShapeDtypeStruct
        parts = pl.pallas_call(
            lambda *refs: main_kernel(z, names, *refs),
            out_shape=[
                sds((z.MB, z.C, z.R), BF16),
                sds((z.MB, z.C, z.R), BF16),
                sds((4, z.rA, z.L), F32),
            ],
            in_specs=[smem] + [vmem] * (len(INPUTS) - 1),
            out_specs=[vmem] * len(OUTPUTS),
            scratch_shapes=list(scratch.values()),
            compiler_params=pltpu.CompilerParams(
                collective_id=0, has_side_effects=True, vmem_limit_bytes=63 << 20
            ),
            name="layer",
        )(
            doc_lengths, as_rows(tokens), as_rows(cotangent), query_weight,
            query_bias, key_weight, value_weight, value_bias, out_weight, out_bias, first_gain, first_shift,
            up_weight, up_bias, down_weight, down_bias, second_gain, second_shift,
        )
        mat, vec = sds((1, z.r, z.C), F32), sds((1, z.r), F32)
        outs = pl.pallas_call(
            lambda *refs: finish_kernel(z, *refs),
            out_shape=[
                sds((z.N, z.MB, 128), BF16), sds((z.MB, z.N, 128), F32), mat, vec, mat, mat, vec,
                sds((4 * z.r, z.C), F32), vec, vec, vec, sds((1, z.r, z.F), F32), sds((1, 4 * z.r), F32),
                sds((1, 4 * z.r, z.C), F32), vec, vec, vec,
            ],
            in_specs=[vmem] * len(OUTPUTS),
            out_specs=[vmem] * 17,
            scratch_shapes=[pltpu.VMEM((z.N, z.MB, 128), F32)],
            name="finish",
        )(*parts)
        shape = tokens.shape
        return (outs[0].transpose(1, 0, 2).reshape(shape), outs[1].reshape(shape), *outs[2:])

    return jax.shard_map(
        body,
        mesh=mesh,
        in_specs=(
            tok_spec, P(None, "dp", None), tok_spec, mat_spec, vec_spec, mat_spec, mat_spec, vec_spec,
            out_spec, vec_spec, vec_spec, vec_spec, mat_spec, vec_spec, mat_spec, vec_spec, vec_spec, vec_spec,
        ),
        out_specs=(
            tok_spec, tok_spec, mat_spec, vec_spec, mat_spec, mat_spec, vec_spec, out_spec, vec_spec, vec_spec,
            vec_spec, mat_spec, vec_spec, mat_spec, vec_spec, vec_spec, vec_spec,
        ),
        check_vma=False,
    )
```

```python
import math
import types

import jax
import jax.numpy as jnp
from jax import lax
from jax.experimental import pallas as pl
from jax.experimental.pallas import tpu as pltpu
from jax.sharding import PartitionSpec as P

HEAD_DIM = 64
EPS = 1e-05
BIG = 1e30
MESH = pl.DeviceIdType.MESH
F32 = jnp.float32
BF16 = jnp.bfloat16
V_BQ, V_BV, V_BO, V_G1, V_S1, V_BD, V_G2, V_S2 = range(8)
VECS = 16
M_QKV, M_OUT, M_UP, M_DOWN = range(4)


def up_to(n, m):
    return (n + m - 1) // m * m


def mm(a, b):
    return lax.dot_general(a, b, (((1,), (0,)), ((), ())), preferred_element_type=F32)


def mm_nt(a, b):
    return lax.dot_general(a, b, (((1,), (1,)), ((), ())), preferred_element_type=F32)


def loop(n, fn):
    if n <= 8:
        for i in range(n):
            fn(i)
    else:
        lax.fori_loop(0, n, lambda i, c: (fn(i), c)[1], 0)


def rcopy(src, dst, ss, rs, dev):
    return pltpu.make_async_remote_copy(
        src_ref=src, dst_ref=dst, send_sem=ss, recv_sem=rs, device_id=dev, device_id_type=MESH
    )


def pieces(c, u):
    at, end = u * c, (u + 1) * c
    found = []
    while at < end:
        size = min(128 - at % 128, end - at)
        found.append((at // 128, at % 128, size))
        at += size
    return found


def columns_of(z, flat):
    rows = [flat[pl.ds(i, z.R // z.per, stride=z.span)].T for i in range(z.span)]
    tokens = []
    for u in range(z.per):
        tokens.append(jnp.concatenate([rows[i][at : at + n] for i, at, n in pieces(z.C, u)], axis=0))
    return jnp.concatenate(tokens, axis=1)


def put_rows(z, value, put):
    n = z.R // z.per
    parts = [[] for _ in range(z.span)]
    for u in range(z.per):
        c = 0
        for i, _, size in pieces(z.C, u):
            parts[i].append(value[c : c + size, u * n : (u + 1) * n])
            c += size
    for i in range(z.span):
        put(i, jnp.concatenate(parts[i], axis=0).T)


class Sizes:
    def __init__(self, mesh, tokens, query_weight, up_weight, doc_lengths):
        self.nb, self.nd, self.nh = mesh.shape["blk"], mesh.shape["dp"], mesh.shape["head"]
        self.W = self.nb * self.nd
        self.C, self.F = query_weight.shape[2], up_weight.shape[2]
        self.MB = tokens.shape[0]
        self.R = tokens.shape[3] // self.C
        self.S = self.nb // self.MB
        self.Q = self.MB * self.R
        self.N = self.R * self.C // 128
        self.per = 128 // math.gcd(self.C, 128)
        self.span = self.per * self.C // 128
        self.H = self.C // HEAD_DIM
        self.ND = doc_lengths.shape[2]
        self.r = query_weight.shape[1]
        self.rs = up_to(self.r, 8)
        self.r2 = up_to(2 * self.r, 8)
        self.rA = up_to(2 * self.rs, 16)
        self.L = 2 * self.C
        self.keep = self.nb * self.R * self.Q * self.H * 2 <= (8 << 20)
        assert self.F == 4 * self.C and self.F == self.nh * self.C and self.W % self.nh == 0


INPUTS = [
    "lens", "tok", "cot", "wq_in", "bq", "wk_in", "wv_in", "bv", "wo_in", "bo", "g1", "s1", "wup_in", "bu",
    "wdn_in", "bd", "g2", "s2",
]
OUTPUTS = ["o_mo", "o_tg", "o_G"]


def main_scratch(z, inputs):
    dma = pltpu.SemaphoreType.DMA
    v = pltpu.VMEM
    nb, W, L, R, C, F, Q, H, MB, rA, nh = z.nb, z.W, z.L, z.R, z.C, z.F, z.Q, z.H, z.MB, z.rA, z.nh
    dd = max(z.nd - 1, 1)
    return dict(
        in_sem=dma((len(INPUTS) - 1,)),
        flat=v((2 * MB, z.N, 128), F32),
        xs=v((MB, C, R), BF16),
        xb=v((nb, C, R), BF16),
        cs=v((MB, C, R), BF16),
        cb=v((MB, C, R), BF16),
        buf=v((4, W, rA, L), BF16),
        wob=v((nh, W // nh, rA, L), BF16),
        fst=v((rA, L), F32),
        vst=v((VECS, 128), F32),
        fkv=v((C + 8, L), F32),
        fq=v((C + 8, L), F32),
        fup=v((C + 16, F), F32),
        fod=v((F + 16, C), F32),
        wkv=v((C, L), BF16),
        wkvt=v((L, C), BF16),
        wq=v((C, C), BF16),
        wqt=v((C, C), BF16),
        wup=v((C, F), BF16),
        wupt=v((F, C + 16), BF16),
        wor=v((C, F), BF16),
        wot=v((C, F), BF16),
        wdn=v((F, C), BF16),
        wdnt=v((C, F), BF16),
        xq=v((C, Q), BF16),
        qx=v((MB, H, 128, R), BF16),
        kx=v((nb, H, HEAD_DIM, R), BF16),
        vx=v((nb, H, HEAD_DIM + 16, R), BF16),
        kt=v((nb, H, R, 128), BF16),
        vt=v((nb, H, R, 128), BF16),
        pbuf=v((nb, MB, H, R, R) if z.keep else (1, 1, 1, 16, 128), BF16),
        tops=v((MB, H, up_to(nb, 8), R), F32),
        top=v((MB, H, 8, R), F32),
        osum=v((MB, H, HEAD_DIM + 16, R), F32),
        oall=v((MB, nh, C, R), BF16),
        pall=v((MB, nh, C, R), BF16),
        stats=v((3, MB, nh, 8, 128), F32),
        n1=v((MB, C, R), F32),
        y1=v((MB, C, R), F32),
        h2=v((MB, C, R), F32),
        gel=v((MB, F, R), F32),
        dh1=v((MB, C, R), F32),
        y1b=v((C, Q), BF16),
        act=v((F, Q), BF16),
        dz=v((C, Q), BF16),
        du=v((F, Q), BF16),
        mo=v((MB, C, R), BF16),
        dox=v((nb if z.keep else 1, MB, H, 128, R), BF16),
        part=v((MB, H, HEAD_DIM, R), F32),
        delta=v((MB, H, 8, R), F32),
        dqacc=v((MB, H, HEAD_DIM, R), F32),
        dkacc=v((nb - MB if z.keep else 1, L, R), F32),
        dkv=v((L, R), F32),
        dq=v((C, Q), BF16),
        tgs=v((nb, C, R), BF16),
        tgo=v((MB, C, R), F32),
        tgr=v((MB, z.S, C, R), BF16),
        tgx=v((MB, C, R), BF16),
        gkv=v((C + 8, L), F32),
        gq=v((C + 8, L), F32),
        gup=v((C + 8, F), F32),
        gout=v((F + 16, C), F32),
        gdn=v((F + 16, C), F32),
        vg=v((VECS, C), F32),
        ug=v((8, F), F32),
        pk=v((4, W, rA, L), BF16),
        got1=v((4, dd, nb, rA, L), BF16),
        sent2=v((4, nb, rA, L), BF16),
        got2=v((4, nb, rA, L), BF16),
        x_ss=dma((MB,)),
        xf_ss=dma((MB, z.S)),
        x_rs=dma((nb,)),
        c_ss=dma((MB,)),
        c_rs=dma((MB,)),
        g1_ss=dma((4, nb)),
        g1_rs=dma((4, nb)),
        g2_ss=dma((4, dd, nb)),
        g2_rs=dma((4, dd, nb)),
        o_ss=dma((MB, nh)),
        o_rs=dma((MB, nh)),
        p_ss=dma((MB, nh)),
        p_rs=dma((MB, nh)),
        w_ss=dma((nh,)),
        w_rs=dma((nh,)),
        st_ss=dma((3, MB, nh)),
        st_rs=dma((3, MB, nh)),
        mo_ss=dma((MB,)),
        mo_rs=dma((MB,)),
        tp_ss=dma((nb,)),
        tp_rs=dma((MB, z.S)),
        t_ss=dma((MB,)),
        t_rs=dma((MB,)),
        s1_ss=dma((4, dd, nb)),
        s1_rs=dma((4, dd, nb)),
        s2_ss=dma((4, nb)),
        s2_rs=dma((4, nb)),
        **{"v_" + name: v(a.shape, a.dtype) for name, a in zip(INPUTS[1:], inputs)},
    )


def main_kernel(z, names, *refs):
    k = types.SimpleNamespace(**dict(zip(names, refs)))
    nb, nd, nh, W, MB, R, C, F, H, L, S, r, rs, rA = (
        z.nb, z.nd, z.nh, z.W, z.MB, z.R, z.C, z.F, z.H, z.L, z.S, z.r, z.rs, z.rA,
    )
    b, d, h = lax.axis_index("blk"), lax.axis_index("dp"), lax.axis_index("head")
    w_me = b * nd + d
    m_t, s_me = b // S, b % S
    D = nh * C
    half = nh // 2

    def xor(i):
        return lax.bitwise_xor(h, i)

    def later(e):
        return lax.rem(m_t + e, MB)

    def home(e):
        return later(e) * S + s_me

    def mate(e):
        return lax.rem(s_me + e, S)

    def other(n):
        return lax.rem(s_me + 1 + n // MB, S) + lax.rem(m_t + n, MB) * S

    fetch = [
        pltpu.make_async_copy(getattr(k, name), getattr(k, "v_" + name), k.in_sem.at[n])
        for n, name in enumerate(INPUTS[1:])
    ]
    for copy in fetch:
        copy.start()

    bar = pltpu.get_barrier_semaphore()
    peers = [(lax.rem(b + i, nb), d, h) for i in range(1, nb)]
    peers += [(b, lax.rem(d + i, nd), h) for i in range(1, nd)]
    peers += [(b, d, xor(i)) for i in range(1, nh)]
    for peer in peers:
        pl.semaphore_signal(bar, inc=1, device_id=peer, device_id_type=MESH)

    for copy in fetch:
        copy.wait()

    def pack(q):
        k.buf[q, w_me] = k.fst[...].astype(BF16)

    k.vst[...] = jnp.zeros_like(k.vst)
    for j, ref in enumerate((k.v_bq, k.v_bv, k.v_bo, k.v_g1, k.v_s1, k.v_bd, k.v_g2, k.v_s2)):
        k.vst[j : j + 1, 0:r] = ref[...].astype(F32)
    k.fst[...] = jnp.zeros_like(k.fst)
    k.fst[0:r, 0:C] = k.v_wk_in[0].astype(F32)
    k.fst[0:r, C:L] = k.v_wv_in[0].astype(F32)
    k.fst[rs : rs + r, 0:C] = k.v_wq_in[0].astype(F32)
    k.fst[rs : rs + r, C : C + VECS] = k.vst[...].T[0:r]
    k.fst[rs : rs + 1, C + VECS : C + VECS + 4 * r] = k.v_bu[...].astype(F32)
    pack(M_QKV)
    for q, src in ((M_OUT, k.v_wo_in[...]), (M_DOWN, k.v_wdn_in[0])):
        src = src.astype(F32)
        k.fst[0 : 2 * r, 0:C] = src[0 : 2 * r]
        k.fst[0 : 2 * r, C:L] = src[2 * r : 4 * r]
        pack(q)
    k.fst[0:r] = k.v_wup_in[0, :, 0:L].astype(F32)
    k.fst[rs : rs + r] = k.v_wup_in[0, :, L : 2 * L].astype(F32)
    pack(M_UP)

    for n, (src, dst) in enumerate(((k.v_tok, k.xs), (k.v_cot, k.cs))):
        both = src[...].astype(F32)
        for m in range(MB):
            k.flat[n * MB + m] = both[:, m]
            dst[m] = columns_of(z, k.flat.at[n * MB + m]).astype(BF16)
    k.xb[b] = k.xs[m_t]
    k.cb[0] = k.cs[m_t]

    pl.semaphore_wait(bar, len(peers))

    def g1(q, i):
        own = k.buf.at[q, w_me]
        return rcopy(own, own, k.g1_ss.at[q, i], k.g1_rs.at[q, i], (lax.rem(b + i, nb), d, h))

    def g1_wait(q, i):
        src = k.buf.at[q, lax.rem(b + nb - i, nb) * nd + d]
        rcopy(src, src, k.g1_ss.at[q, i], k.g1_rs.at[q, i], (b, d, h)).wait_recv()

    def g2(q, e, i):
        src = k.buf.at[q, lax.rem(b + nb - i, nb) * nd + d]
        return rcopy(src, src, k.g2_ss.at[q, e - 1, i], k.g2_rs.at[q, e - 1, i], (b, lax.rem(d + e, nd), h))

    def g2_wait(q, e, i):
        src = k.buf.at[q, lax.rem(b + nb - i, nb) * nd + lax.rem(d + nd - e, nd)]
        rcopy(src, src, k.g2_ss.at[q, e - 1, i], k.g2_rs.at[q, e - 1, i], (b, d, h)).wait_recv()

    def gather_start(q):
        for e in range(1, nd):
            g2(q, e, 0).start()
        loop(nb - 1, lambda i: g1(q, i + 1).start())

    def gather_forward(q):
        def one(i):
            g1_wait(q, i + 1)
            for e in range(1, nd):
                g2(q, e, i + 1).start()

        loop(nb - 1, one)

    def gather_wait(q):
        for e in range(1, nd):
            loop(nb, lambda i: g2_wait(q, e, i))

    def gather_drain(q):
        loop(nb - 1, lambda i: g1(q, i + 1).wait_send())
        for e in range(1, nd):
            loop(nb, lambda i: g2(q, e, i).wait_send())

    gather_start(M_QKV)

    def x_send(e):
        m = later(e)
        return rcopy(k.xs.at[m], k.xb.at[b], k.x_ss.at[e], k.x_rs.at[b], (m * S + s_me, d, h))

    def x_pass(e, f):
        src = k.xb.at[home(e)]
        return rcopy(src, src, k.xf_ss.at[e, f], k.x_rs.at[home(e)], (m_t * S + mate(f), d, h))

    def x_wait(j):
        rcopy(k.xb.at[j], k.xb.at[j], k.x_ss.at[0], k.x_rs.at[j], (b, d, h)).wait_recv()

    for e in range(1, MB):
        x_send(e).start()
    loop(S - 1, lambda f: x_pass(0, f + 1).start())

    gather_forward(M_QKV)

    gather_wait(M_QKV)

    for w in range(W):
        slab = k.buf[M_QKV, w].astype(F32)
        k.fkv[w * r : w * r + rs] = slab[0:rs]
        k.fq[w * r : w * r + rs] = slab[rs : 2 * rs]
    k.wkv[...] = k.fkv[0:C].astype(BF16)
    k.wkvt[...] = k.fkv[0:C].T.astype(BF16)
    k.wq[...] = k.fq[0:C, 0:C].astype(BF16)
    k.wqt[...] = k.fq[0:C, 0:C].T.astype(BF16)

    def vec(j):
        return k.fq[0:C, C + j : C + j + 1]

    row16 = lax.broadcasted_iota(jnp.int32, (16, R), 0)
    column = lax.broadcasted_iota(jnp.int32, (16, R), 1)
    step = R // z.per
    token = z.per * (column % step) + column // step
    pad = jnp.zeros((48, R), BF16)
    one_rows = jnp.where(row16 < 2, 1.0, 0.0).astype(BF16)

    def in_doc(j):
        doc = jnp.zeros((16, R), jnp.int32)
        end = jnp.int32(0)
        for n in range(z.ND):
            end = end + k.lens[m_t, 0, n]
            doc = doc + (j * R + token >= end).astype(jnp.int32)
        return row16 == doc

    def head_send(net, i, p):
        buf, ss, rs_ = net
        src, to = (h, xor(p)) if p <= half else (xor(half), xor(p - half))
        return rcopy(buf.at[i, src], buf.at[i, src], ss.at[i, p], rs_.at[i, p], (b, d, to))

    def head_wait(net, i, p):
        buf, ss, rs_ = net
        rcopy(buf.at[i, xor(p)], buf.at[i, xor(p)], ss.at[i, p], rs_.at[i, p], (b, d, h)).wait_recv()

    def head_start(net, i):
        for p in range(half, 0, -1):
            head_send(net, i, p).start()

    def head_pass(net, i):
        head_wait(net, i, half)
        for p in range(half + 1, nh):
            head_send(net, i, p).start()

    def head_end(net, i):
        for p in range(1, nh):
            if p != half:
                head_wait(net, i, p)

    o_net = (k.oall, k.o_ss, k.o_rs)
    p_net = (k.pall, k.p_ss, k.p_rs)

    def kv_block(t, j):
        kv = mm(k.wkvt[...], k.xb[j])
        kb = kv[0:C].astype(BF16)
        vb = (kv[C:L] + vec(V_BV)).astype(BF16)
        barred = jnp.logical_and(row16 < z.ND, jnp.logical_not(in_doc(j)))
        kf = jnp.where(barred, -BIG, 0.0).astype(BF16)
        for a in range(H):
            kh, vh = kb[a * HEAD_DIM : (a + 1) * HEAD_DIM], vb[a * HEAD_DIM : (a + 1) * HEAD_DIM]
            k.kx[t, a] = kh
            k.vx[t, a, 0:HEAD_DIM] = vh
            k.vx[t, a, HEAD_DIM:] = one_rows
            k.kt[t, a] = jnp.concatenate([kh, kf, pad], axis=0).T
            k.vt[t, a] = jnp.concatenate([vh, one_rows, pad], axis=0).T

    def query_block(e):
        xi = k.xb[home(e)]
        k.xq[:, e * R : (e + 1) * R] = xi
        qi = ((mm(k.wqt[...], xi) + vec(V_BQ)).astype(BF16).astype(F32) * HEAD_DIM**-0.5).astype(BF16)
        hot = jnp.where(in_doc(home(e)), 1.0, 0.0).astype(BF16)
        for a in range(H):
            k.qx[e, a] = jnp.concatenate([qi[a * HEAD_DIM : (a + 1) * HEAD_DIM], hot, pad], axis=0)

    def scores(e, a, t):
        return mm(k.kt[t, a], k.qx[e, a])

    def prob(e, a, t):
        if z.keep:
            return k.pbuf[t, e, a]
        return jnp.exp(scores(e, a, t) - k.tops[e, a, pl.ds(t, 1)]).astype(BF16)

    def attend(pairs):
        units = [(e, a, t) for e, t in pairs for a in range(H)]
        s = [scores(*u) for u in units]
        top = [jnp.max(x, axis=0, keepdims=True) for x in s]
        p = [jnp.exp(x - y).astype(BF16) for x, y in zip(s, top)]
        o = [mm(k.vx[t, a], x) for (e, a, t), x in zip(units, p)]
        for i, (e, a, t) in enumerate(units):
            if z.keep:
                k.pbuf[t, e, a] = p[i]
            k.tops[e, a, pl.ds(t, 1)] = top[i]
        for i, (e, a, t) in enumerate(units):
            if isinstance(t, int) and t == 0:
                k.top[e, a, 0:1] = top[i]
                k.osum[e, a] = o[i]
            else:
                old = k.top[e, a, 0:1]
                new = jnp.maximum(old, top[i])
                k.top[e, a, 0:1] = new
                k.osum[e, a] = k.osum[e, a] * jnp.exp(old - new) + o[i] * jnp.exp(top[i] - new)

    def factor(e, a, t):
        return jnp.exp(k.tops[e, a, pl.ds(t, 1)] - k.top[e, a, 0:1]) * k.top[e, a, 1:2]

    for e in range(1, MB):
        x_wait(home(e))
        loop(S - 1, lambda f: x_pass(e, f + 1).start())
    gather_start(M_OUT)
    for e in range(MB):
        kv_block(e, home(e))
        query_block(e)
    for t in range(MB):
        attend([(e, t) for e in range(MB)])

    def attend_other(n):
        x_wait(other(n))
        kv_block(MB + n, other(n))
        attend([(e, MB + n) for e in range(MB)])

    def heads_done(e):
        for a in range(H):
            o = k.osum[e, a]
            inv = 1.0 / o[HEAD_DIM : HEAD_DIM + 1]
            k.top[e, a, 1:2] = inv
            k.oall[e, h, a * HEAD_DIM : (a + 1) * HEAD_DIM] = (o[0:HEAD_DIM] * inv).astype(BF16)
        head_start(o_net, e)

    last = nb - MB - 1
    loop(last, attend_other)
    x_wait(other(last))
    gather_start(M_UP)
    kv_block(MB + last, other(last))
    for e in range(MB):
        attend([(e, MB + last)])
        heads_done(e)
    gather_start(M_DOWN)

    gather_forward(M_OUT)
    gather_forward(M_UP)
    for e in range(MB):
        head_pass(o_net, e)
    gather_wait(M_OUT)

    per = W // nh

    def w_send(p):
        src = k.buf.at[M_OUT, pl.ds(xor(p) * per, per)]
        return rcopy(src, k.wob.at[h], k.w_ss.at[p], k.w_rs.at[p], (b, d, xor(p)))

    for p in range(1, nh):
        w_send(p).start()

    def spread(dst, slab, row):
        slab = slab.astype(F32)
        dst[row : row + z.r2] = slab[0 : z.r2, 0:C]
        dst[row + 2 * r : row + 2 * r + z.r2] = slab[0 : z.r2, C:L]

    for w in range(W):
        spread(k.fod, k.buf[M_OUT, w], 4 * r * w)
    k.wot[...] = k.fod[0:F].T.astype(BF16)

    gather_forward(M_DOWN)

    def c_send(e):
        m = later(e)
        slot = lax.rem(m_t + MB - m, MB)
        return rcopy(k.cs.at[m], k.cb.at[slot], k.c_ss.at[e], k.c_rs.at[slot], (m * S + s_me, d, h))

    for e in range(1, MB):
        c_send(e).start()

    lane_rows = R // 128

    def st_send(e, i, p):
        own = k.stats.at[e, i, h]
        return rcopy(own, own, k.st_ss.at[e, i, p], k.st_rs.at[e, i, p], (b, d, xor(p)))

    def reduce_start(e, i, rows):
        for j, v in enumerate(rows):
            row = jnp.sum(v, axis=0, keepdims=True)
            for c in range(lane_rows):
                k.stats[e, i, h, pl.ds(j * lane_rows + c, 1)] = row[:, c * 128 : (c + 1) * 128]
        if len(rows) * lane_rows < 8:
            rest = 8 - len(rows) * lane_rows
            k.stats[e, i, h, pl.ds(8 - rest, rest)] = jnp.zeros((rest, 128), F32)
        for p in range(nh - 1, 0, -1):
            st_send(e, i, p).start()

    def reduce_end(e, i, n):
        for p in range(1, nh):
            src = k.stats.at[e, i, xor(p)]
            rcopy(src, src, k.st_ss.at[e, i, p], k.st_rs.at[e, i, p], (b, d, h)).wait_recv()
        total = k.stats[e, i, 0]
        for j in range(1, nh):
            total = total + k.stats[e, i, j]
        total = total / D
        return [
            jnp.concatenate([total[j * lane_rows + c :][0:1] for c in range(lane_rows)], axis=1)
            for j in range(n)
        ]

    def cols(ref, i):
        return ref[:, i * R : (i + 1) * R]

    for i in range(MB):
        head_end(o_net, i)
        h1 = cols(k.xq, i).astype(F32) + mm(k.wot[...], k.oall[i].reshape(D, R)) + vec(V_BO)
        k.n1[i] = h1
        reduce_start(0, i, (h1, h1 * h1))

    gather_wait(M_UP)
    for w in range(W):
        slab = k.buf[M_UP, w].astype(F32)
        k.fup[w * r : w * r + rs, 0:L] = slab[0:rs]
        k.fup[w * r : w * r + rs, L:F] = slab[rs : 2 * rs]
    k.fup[C : C + 16] = jnp.zeros((16, F), F32)
    for w in range(W):
        row = k.buf[M_QKV, w].astype(F32)[rs : rs + 1, C + VECS : C + VECS + 4 * r]
        k.fup[C : C + 1, 4 * r * w : 4 * r * (w + 1)] = row
    k.wup[...] = k.fup[0:C].astype(BF16)
    k.wupt[...] = k.fup[...].T.astype(BF16)
    gather_wait(M_DOWN)
    for w in range(W):
        spread(k.fod, k.buf[M_DOWN, w], 4 * r * w)
    k.wdn[...] = k.fod[0:F].astype(BF16)
    k.wdnt[...] = k.fod[0:F].T.astype(BF16)

    first_one = jnp.where(row16 < 1, 1.0, 0.0).astype(BF16)
    r1 = [None] * MB
    gdn = [None] * MB
    for i in range(MB):
        mean, square = reduce_end(0, i, 2)
        r1[i] = lax.rsqrt(square - mean * mean + EPS)
        n1 = (k.n1[i] - mean) * r1[i]
        k.n1[i] = n1
        y1 = n1 * vec(V_G1) + vec(V_S1)
        k.y1[i] = y1
        y1b = y1.astype(BF16)
        k.y1b[:, i * R : (i + 1) * R] = y1b
        u = mm(k.wupt[...], jnp.concatenate([y1b, first_one], axis=0))
        cdf = 0.5 * (1.0 + lax.erf(u * (0.5**0.5)))
        act = (u * cdf).astype(BF16)
        k.act[:, i * R : (i + 1) * R] = act
        h2 = y1 + mm(k.wdnt[...], act) + vec(V_BD)
        k.h2[i] = h2

        if i > 0:
            rcopy(k.cb.at[i], k.cb.at[i], k.c_ss.at[0], k.c_rs.at[i], (b, d, h)).wait_recv()
        dn2 = k.cb[i].astype(F32) * vec(V_G2)
        reduce_start(1, i, (h2, h2 * h2, dn2, dn2 * h2))
        k.gel[i] = cdf + u * jnp.exp(-0.5 * u * u) * ((2 * jnp.pi) ** -0.5)
    k.vg[...] = jnp.zeros_like(k.vg)
    ones = jnp.ones((16, R), BF16)

    def vec_grad(j, x):
        k.vg[j : j + 1] += mm_nt(ones, x)[0:1]

    def mo_send(i):
        return rcopy(k.mo.at[i], k.o_mo.at[m_t], k.mo_ss.at[i], k.mo_rs.at[m_t], (home(i), d, h))

    for i in range(MB):
        mean, square, dmean, dsquare = reduce_end(1, i, 4)
        r2 = lax.rsqrt(square - mean * mean + EPS)
        g = k.cb[i].astype(F32)
        dn2 = g * vec(V_G2)
        n2 = (k.h2[i] - mean) * r2
        dh2 = r2 * (dn2 - dmean - n2 * (r2 * (dsquare - mean * dmean)))
        dz = dh2.astype(BF16)
        k.dz[:, i * R : (i + 1) * R] = dz
        du = (mm(k.wdn[...], dz) * k.gel[i]).astype(BF16)
        k.du[:, i * R : (i + 1) * R] = du
        dy1 = dh2 + mm(k.wup[...], du)
        dn1 = dy1 * vec(V_G1)
        k.dh1[i] = dn1
        n1 = k.n1[i]
        reduce_start(2, i, (dn1, dn1 * n1))
        out = (n2 * vec(V_G2) + vec(V_S2)).astype(BF16)
        if i > 0:
            k.mo[i] = out
            mo_send(i).start()
        else:
            k.o_mo[m_t] = out
        vec_grad(V_G2, (g * n2).astype(BF16))
        vec_grad(V_S2, k.cb[i])
        vec_grad(V_BD, dz)
        vec_grad(V_G1, (dy1 * n1).astype(BF16))
        vec_grad(V_S1, dy1.astype(BF16))

    def s1_send(q, e, i):
        dt = lax.rem(d + e, nd)
        return rcopy(
            k.pk.at[q, i * nd + dt], k.got1.at[q, e - 1, i], k.s1_ss.at[q, e - 1, i], k.s1_rs.at[q, e - 1, i],
            (b, dt, h),
        )

    def s2_send(q, i):
        bt = lax.rem(b + i, nb)
        return rcopy(k.sent2.at[q, bt], k.got2.at[q, b], k.s2_ss.at[q, i], k.s2_rs.at[q, i], (bt, d, h))

    def scatter_start(q):
        for e in range(1, nd):
            loop(nb, lambda i: s1_send(q, e, i).start())

    def scatter_sum(q, bt):
        part = k.pk[q, bt * nd + d].astype(F32)
        for e in range(1, nd):
            src = k.got1.at[q, e - 1, bt]
            rcopy(src, src, k.s1_ss.at[q, e - 1, bt], k.s1_rs.at[q, e - 1, bt], (b, d, h)).wait_recv()
            part = part + src[...].astype(F32)
        return part

    def scatter_forward(q):
        def one(i):
            bt = lax.rem(b + i + 1, nb)
            k.sent2[q, bt] = scatter_sum(q, bt).astype(BF16)
            s2_send(q, i + 1).start()

        loop(nb - 1, one)
        k.o_G[q] = scatter_sum(q, b)

    def scatter_end(q):
        def one(i):
            src = k.got2.at[q, lax.rem(b + nb - i - 1, nb)]
            rcopy(src, src, k.s2_ss.at[q, i + 1], k.s2_rs.at[q, i + 1], (b, d, h)).wait_recv()
            k.o_G[q] += src[...].astype(F32)

        loop(nb - 1, one)
        loop(nb - 1, lambda i: s2_send(q, i + 1).wait_send())
        for e in range(1, nd):
            loop(nb, lambda i: s1_send(q, e, i).wait_send())

    def rows_of(parts):
        rows = jnp.concatenate(parts, axis=0)
        if rows.shape[0] < rA:
            rows = jnp.concatenate([rows, jnp.zeros((rA - rows.shape[0], L), F32)], axis=0)
        return rows.astype(BF16)

    def pack_halves(q, g):
        for w in range(W):
            at = 4 * r * w
            pair = jnp.concatenate([g[at : at + z.r2], g[at + 2 * r : at + 2 * r + z.r2]], axis=1)
            k.pk[q, w] = rows_of([pair])
        scatter_start(q)

    k.gdn[0:F] = mm_nt(k.act[...], k.dz[...])
    pack_halves(M_DOWN, k.gdn)
    k.gup[0:C] = mm_nt(k.y1b[...], k.du[...])
    for w in range(W):
        k.pk[M_UP, w] = rows_of([k.gup[w * r : w * r + rs, 0:L], k.gup[w * r : w * r + rs, L:F]])
    scatter_start(M_UP)

    for i in range(MB):
        dmean, dsquare = reduce_end(2, i, 2)
        dh1 = r1[i] * (k.dh1[i] - dmean - k.n1[i] * dsquare)
        k.dh1[i] = dh1
        dp = dh1.astype(BF16)
        k.pall[i, h] = dp
        head_start(p_net, i)

    g = None
    for i in range(MB):
        dp = k.pall[i, h]
        part = mm_nt(k.oall[i].reshape(D, R), dp)
        g = part if g is None else g + part
        vec_grad(V_BO, dp)
    k.gout[0:F] = g
    pack_halves(M_OUT, k.gout)
    ug = mm_nt(jnp.ones((16, z.Q), BF16), k.du[...])
    k.gq[...] = jnp.zeros_like(k.gq)
    for w in range(W):
        k.gq[w * r : w * r + 1, C + VECS : C + VECS + 4 * r] = ug[0:1, 4 * r * w : 4 * r * (w + 1)]
    k.gkv[...] = jnp.zeros_like(k.gkv)

    for p in range(1, nh):
        src = k.wob.at[xor(p)]
        rcopy(src, src, k.w_ss.at[p], k.w_rs.at[p], (b, d, h)).wait_recv()
    k.wob[h] = k.buf[M_OUT, pl.ds(h * per, per)]
    for j in range(nh):
        for n in range(per):
            spread(k.fod, k.wob[j, n], j * C + 4 * r * n)
    for j in range(nh):
        k.wor[:, j * C : (j + 1) * C] = k.fod[j * C : (j + 1) * C].astype(BF16)

    head_pass(p_net, 0)
    scatter_forward(M_DOWN)
    for i in range(1, MB):
        head_pass(p_net, i)

    def grad_in(e):
        head_end(p_net, e)
        do = mm(k.wor[...], k.pall[e].reshape(D, R)).astype(BF16).astype(F32)
        for a in range(H):
            part = do[a * HEAD_DIM : (a + 1) * HEAD_DIM]
            own = k.oall[e, h, a * HEAD_DIM : (a + 1) * HEAD_DIM].astype(F32)
            k.part[e, a] = part
            k.delta[e, a, 0:1] = jnp.sum(part * own, axis=0, keepdims=True)
            k.dqacc[e, a] = jnp.zeros((HEAD_DIM, R), F32)

    def scaled(e, a, t):
        f = factor(e, a, t)
        delta = k.delta[e, a, 0:1] * f
        hi = delta.astype(BF16).astype(F32)
        rest = jnp.where(row16 == 0, -hi, jnp.where(row16 == 1, hi - delta, 0.0))
        return jnp.concatenate([(k.part[e, a] * f).astype(BF16), rest.astype(BF16), pad], axis=0)

    def back(t, queries, into):
        for a in range(H):
            dk = dv = None
            for e in queries:
                slot = t if z.keep else 0
                k.dox[slot, e, a] = scaled(e, a, t)
                p = prob(e, a, t)
                ds = (p.astype(F32) * mm(k.vt[t, a], k.dox[slot, e, a])).astype(BF16)
                k.dqacc[e, a] += mm(k.kx[t, a], ds)
                dk_e = mm_nt(k.qx[e, a, 0:HEAD_DIM], ds)
                dv_e = mm_nt(k.dox[slot, e, a, 0:HEAD_DIM], p)
                dk = dk_e if dk is None else dk + dk_e
                dv = dv_e if dv is None else dv + dv_e
            into(slice(a * HEAD_DIM, (a + 1) * HEAD_DIM), dk)
            into(slice(C + a * HEAD_DIM, C + (a + 1) * HEAD_DIM), dv)

    def tokens_part(j, dkv):
        k.gkv[0:C] += mm_nt(k.xb[j], dkv)
        vec_grad(V_BV, dkv[C:L])
        return mm(k.wkv[...], dkv)

    def tp_send(n):
        dst = k.tgr.at[n % MB, s_me]
        to = lax.rem(s_me + 1 + n // MB, S)
        return rcopy(k.tgs.at[n], dst, k.tp_ss.at[n], k.tp_rs.at[n % MB, s_me], (m_t * S + to, d, h))

    def back_other(n, queries):
        slot = n if z.keep else 0

        def into(rows, v):
            if queries[0] == 0:
                k.dkacc[slot, rows] = v
            else:
                k.dkacc[slot, rows] += v

        back(MB + n, queries, into)
        if queries[-1] == MB - 1:
            k.tgs[n] = tokens_part(other(n), k.dkacc[slot].astype(BF16)).astype(BF16)
            tp_send(n).start()

    for e in range(MB):
        grad_in(e)
        if z.keep:
            loop(nb - MB, lambda n: back_other(nb - MB - 1 - n, [e]))
        if e == 0:
            scatter_forward(M_UP)
    if not z.keep:
        loop(nb - MB, lambda n: back_other(n, list(range(MB))))

    for e in range(MB - 1, -1, -1):

        def into(rows, v):
            k.dkv[rows] = v

        back(e, range(MB), into)
        k.tgo[e] = tokens_part(home(e), k.dkv[...].astype(BF16))
        if e == MB - 1:
            scatter_forward(M_OUT)

    for i in range(MB):
        for a in range(H):
            rows = slice(a * HEAD_DIM, (a + 1) * HEAD_DIM)
            k.dq[rows, i * R : (i + 1) * R] = (k.dqacc[i, a] * HEAD_DIM**-0.5).astype(BF16)
        vec_grad(V_BQ, cols(k.dq, i))
    k.gq[0:C, 0:C] = mm_nt(k.xq[...], k.dq[...])
    k.gq[0:C, C : C + VECS] = k.vg[...].T

    for w in range(W):
        k.pk[M_QKV, w] = rows_of([k.gkv[w * r : w * r + rs], k.gq[w * r : w * r + rs]])
    scatter_start(M_QKV)

    def t_send(e):
        return rcopy(k.tgx.at[e], k.o_tg.at[m_t], k.t_ss.at[e], k.t_rs.at[m_t], (home(e), d, h))

    def tokens_total(e):
        k.tgo[e] += k.dh1[e] + mm(k.wq[...], cols(k.dq, e))

        def add(f):
            src = k.tgr.at[e, mate(f + 1)]
            rcopy(src, src, k.tp_ss.at[0], k.tp_rs.at[e, mate(f + 1)], (b, d, h)).wait_recv()
            k.tgo[e] += src[...].astype(F32)

        loop(S - 1, add)
        return k.tgo[e].astype(BF16)

    for e in range(1, MB):
        k.tgx[e] = tokens_total(e)
        t_send(e).start()

    scatter_forward(M_QKV)

    k.o_tg[m_t] = tokens_total(0)
    for q in (M_DOWN, M_UP, M_OUT, M_QKV):
        scatter_end(q)
    for e in range(1, MB):
        m = later(e)
        for out, ss, rs_ in ((k.o_tg, k.t_ss, k.t_rs), (k.o_mo, k.mo_ss, k.mo_rs)):
            rcopy(out.at[m], out.at[m], ss.at[e], rs_.at[m], (b, d, h)).wait_recv()
        for send in (c_send, x_send, mo_send, t_send):
            send(e).wait_send()
    for e in range(MB):
        loop(S - 1, lambda f: x_pass(e, f + 1).wait_send())
    loop(nb - MB, lambda n: tp_send(n).wait_send())
    for q in range(4):
        gather_drain(q)
    for p in range(1, nh):
        w_send(p).wait_send()
        for i in range(MB):
            head_send(o_net, i, p).wait_send()
            head_send(p_net, i, p).wait_send()
            for e in range(3):
                st_send(e, i, p).wait_send()


def finish_kernel(z, mo, tg, G, *outs):
    (mixed, dtok, dwq, dbq, dwk, dwv, dbv, dwo, dbo, dg1, ds1, dwup, dbu, dwdn, dbd, dg2, ds2, both) = outs
    r, rs, C, L = z.r, z.rs, z.C, z.L
    for m in range(z.MB):


        def put_mixed(i, rows):
            both[pl.ds(i, z.R // z.per, stride=z.span), m] = rows

        def put_grad(i, rows):
            dtok[m, pl.ds(i, z.R // z.per, stride=z.span)] = rows

        put_rows(z, mo[m].astype(F32), put_mixed)
        put_rows(z, tg[m].astype(F32), put_grad)
    mixed[...] = both[...].astype(BF16)
    dwk[0] = G[M_QKV, 0:r, 0:C]
    dwv[0] = G[M_QKV, 0:r, C:L]
    dwq[0] = G[M_QKV, rs : rs + r, 0:C]
    dwup[0, :, 0:L] = G[M_UP, 0:r]
    dwup[0, :, L : 2 * L] = G[M_UP, rs : rs + r]
    for q, ref in ((M_OUT, dwo), (M_DOWN, dwdn.at[0])):
        ref[0 : 2 * r] = G[q, 0 : 2 * r, 0:C]
        ref[2 * r : 4 * r] = G[q, 0 : 2 * r, C:L]
    vecs = G[M_QKV, rs : 2 * rs, C : C + VECS].T
    for j, ref in enumerate((dbq, dbv, dbo, dg1, ds1, dbd, dg2, ds2)):
        ref[...] = vecs[j : j + 1, 0:r]
    dbu[...] = G[M_QKV, rs : rs + 1, C + VECS : C + VECS + 4 * r]


def solution(mesh):
    vec_spec = P("head", ("blk", "dp"))
    mat_spec = P("head", ("blk", "dp"), None)
    tok_spec = P(None, "dp", "head", "blk")
    out_spec = P(("blk", "dp"), "head")

    def body(
        tokens, doc_lengths, cotangent, query_weight, query_bias, key_weight, value_weight, value_bias,
        out_weight, out_bias, first_gain, first_shift, up_weight, up_bias, down_weight, down_bias,
        second_gain, second_shift,
    ):
        z = Sizes(mesh, tokens, query_weight, up_weight, doc_lengths)

        def as_rows(a):
            return a.reshape(z.MB, z.N, 128).transpose(1, 0, 2)

        operands = (
            as_rows(tokens), as_rows(cotangent), query_weight, query_bias, key_weight, value_weight, value_bias,
            out_weight, out_bias, first_gain, first_shift, up_weight, up_bias, down_weight, down_bias, second_gain,
            second_shift,
        )
        scratch = main_scratch(z, operands)
        vmem = pl.BlockSpec(memory_space=pltpu.VMEM)
        smem = pl.BlockSpec(memory_space=pltpu.SMEM)
        hbm = pl.BlockSpec(memory_space=pltpu.HBM)
        names = INPUTS + OUTPUTS + list(scratch)
        sds = jax.ShapeDtypeStruct
        parts = pl.pallas_call(
            lambda *refs: main_kernel(z, names, *refs),
            out_shape=[
                sds((z.MB, z.C, z.R), BF16),
                sds((z.MB, z.C, z.R), BF16),
                sds((4, z.rA, z.L), F32),
            ],
            in_specs=[smem] + [hbm] * len(operands),
            out_specs=[vmem] * len(OUTPUTS),
            scratch_shapes=list(scratch.values()),
            compiler_params=pltpu.CompilerParams(
                collective_id=0, has_side_effects=True, vmem_limit_bytes=63 << 20
            ),
            name="layer",
        )(doc_lengths, *operands)
        mat, vec = sds((1, z.r, z.C), F32), sds((1, z.r), F32)
        outs = pl.pallas_call(
            lambda *refs: finish_kernel(z, *refs),
            out_shape=[
                sds((z.N, z.MB, 128), BF16), sds((z.MB, z.N, 128), F32), mat, vec, mat, mat, vec,
                sds((4 * z.r, z.C), F32), vec, vec, vec, sds((1, z.r, z.F), F32), sds((1, 4 * z.r), F32),
                sds((1, 4 * z.r, z.C), F32), vec, vec, vec,
            ],
            in_specs=[vmem] * len(OUTPUTS),
            out_specs=[vmem] * 17,
            scratch_shapes=[pltpu.VMEM((z.N, z.MB, 128), F32)],
            name="finish",
        )(*parts)
        shape = tokens.shape
        return (outs[0].transpose(1, 0, 2).reshape(shape), outs[1].reshape(shape), *outs[2:])

    return jax.shard_map(
        body,
        mesh=mesh,
        in_specs=(
            tok_spec, P(None, "dp", None), tok_spec, mat_spec, vec_spec, mat_spec, mat_spec, vec_spec,
            out_spec, vec_spec, vec_spec, vec_spec, mat_spec, vec_spec, mat_spec, vec_spec, vec_spec, vec_spec,
        ),
        out_specs=(
            tok_spec, tok_spec, mat_spec, vec_spec, mat_spec, mat_spec, vec_spec, out_spec, vec_spec, vec_spec,
            vec_spec, mat_spec, vec_spec, mat_spec, vec_spec, vec_spec, vec_spec,
        ),
        check_vma=False,
    )
```

```python
import math
import types

import jax
import jax.numpy as jnp
from jax import lax
from jax.experimental import pallas as pl
from jax.experimental.pallas import tpu as pltpu
from jax.sharding import PartitionSpec as P

HEAD_DIM = 64
EPS = 1e-05
BIG = 1e30
MESH = pl.DeviceIdType.MESH
F32 = jnp.float32
BF16 = jnp.bfloat16
V_BQ, V_BV, V_BO, V_G1, V_S1, V_BD, V_G2, V_S2 = range(8)
VECS = 16
M_QKV, M_OUT, M_UP, M_DOWN = range(4)


def up_to(n, m):
    return (n + m - 1) // m * m


def mm(a, b):
    return lax.dot_general(a, b, (((1,), (0,)), ((), ())), preferred_element_type=F32)


def mm_nt(a, b):
    return lax.dot_general(a, b, (((1,), (1,)), ((), ())), preferred_element_type=F32)


def loop(n, fn):
    if n <= 8:
        for i in range(n):
            fn(i)
    else:
        lax.fori_loop(0, n, lambda i, c: (fn(i), c)[1], 0)


def rcopy(src, dst, ss, rs, dev):
    return pltpu.make_async_remote_copy(
        src_ref=src, dst_ref=dst, send_sem=ss, recv_sem=rs, device_id=dev, device_id_type=MESH
    )


def pieces(c, u):
    at, end = u * c, (u + 1) * c
    found = []
    while at < end:
        size = min(128 - at % 128, end - at)
        found.append((at // 128, at % 128, size))
        at += size
    return found


def columns_of(z, flat):
    rows = [flat[pl.ds(i, z.R // z.per, stride=z.span)].T for i in range(z.span)]
    tokens = []
    for u in range(z.per):
        tokens.append(jnp.concatenate([rows[i][at : at + n] for i, at, n in pieces(z.C, u)], axis=0))
    return jnp.concatenate(tokens, axis=1)


def put_rows(z, value, put):
    n = z.R // z.per
    parts = [[] for _ in range(z.span)]
    for u in range(z.per):
        c = 0
        for i, _, size in pieces(z.C, u):
            parts[i].append(value[c : c + size, u * n : (u + 1) * n])
            c += size
    for i in range(z.span):
        put(i, jnp.concatenate(parts[i], axis=0).T)


class Sizes:
    def __init__(self, mesh, tokens, query_weight, up_weight, doc_lengths):
        self.nb, self.nd, self.nh = mesh.shape["blk"], mesh.shape["dp"], mesh.shape["head"]
        self.W = self.nb * self.nd
        self.C, self.F = query_weight.shape[2], up_weight.shape[2]
        self.MB = tokens.shape[0]
        self.R = tokens.shape[3] // self.C
        self.S = self.nb // self.MB
        self.Q = self.MB * self.R
        self.N = self.R * self.C // 128
        self.per = 128 // math.gcd(self.C, 128)
        self.span = self.per * self.C // 128
        self.H = self.C // HEAD_DIM
        self.ND = doc_lengths.shape[2]
        self.r = query_weight.shape[1]
        self.rs = up_to(self.r, 8)
        self.r2 = up_to(2 * self.r, 8)
        self.rA = up_to(2 * self.rs, 16)
        self.L = 2 * self.C
        self.keep = self.nb * self.R * self.Q * self.H * 2 <= (8 << 20)
        assert self.F == 4 * self.C and self.F == self.nh * self.C and self.W % self.nh == 0


INPUTS = [
    "lens", "tok", "cot", "wq_in", "bq", "wk_in", "wv_in", "bv", "wo_in", "bo", "g1", "s1", "wup_in", "bu",
    "wdn_in", "bd", "g2", "s2",
]
OUTPUTS = ["o_mo", "o_tg", "o_G"]


def main_scratch(z, inputs):
    dma = pltpu.SemaphoreType.DMA
    v = pltpu.VMEM
    nb, W, L, R, C, F, Q, H, MB, rA, nh = z.nb, z.W, z.L, z.R, z.C, z.F, z.Q, z.H, z.MB, z.rA, z.nh
    dd = max(z.nd - 1, 1)
    return dict(
        in_sem=dma((len(INPUTS) - 1,)),
        flat=v((2 * MB, z.N, 128), F32),
        xs=v((MB, C, R), BF16),
        xb=v((nb, C, R), BF16),
        cs=v((MB, C, R), BF16),
        cb=v((MB, C, R), BF16),
        buf=v((4, W, rA, L), BF16),
        wob=v((nh, W // nh, rA, L), BF16),
        fst=v((rA, L), F32),
        vst=v((VECS, 128), F32),
        fkv=v((C + 8, L), F32),
        fq=v((C + 8, L), F32),
        fup=v((C + 16, F), F32),
        fod=v((F + 16, C), F32),
        wkv=v((C, L), BF16),
        wkvt=v((L, C), BF16),
        wq=v((C, C), BF16),
        wqt=v((C, C), BF16),
        wup=v((C, F), BF16),
        wupt=v((F, C + 16), BF16),
        wor=v((C, F), BF16),
        wot=v((C, F), BF16),
        wdn=v((F, C), BF16),
        wdnt=v((C, F), BF16),
        xq=v((C, Q), BF16),
        qx=v((MB, H, 128, R), BF16),
        kx=v((nb, H, HEAD_DIM, R), BF16),
        vx=v((nb, H, HEAD_DIM + 16, R), BF16),
        kt=v((nb, H, R, 128), BF16),
        vt=v((nb, H, R, 128), BF16),
        pbuf=v((nb, MB, H, R, R) if z.keep else (1, 1, 1, 16, 128), BF16),
        tops=v((MB, H, up_to(nb, 8), R), F32),
        top=v((MB, H, 8, R), F32),
        osum=v((MB, H, HEAD_DIM + 16, R), F32),
        oall=v((MB, nh, C, R), BF16),
        pall=v((MB, nh, C, R), BF16),
        stats=v((3, MB, nh, 8, 128), F32),
        n1=v((MB, C, R), F32),
        y1=v((MB, C, R), F32),
        h2=v((MB, C, R), F32),
        gel=v((MB, F, R), F32),
        up=v((MB, F, R), F32),
        dh1=v((MB, C, R), F32),
        y1b=v((C, Q), BF16),
        act=v((F, Q), BF16),
        dz=v((C, Q), BF16),
        du=v((F, Q), BF16),
        vin=v((3, MB, C, R), BF16),
        mo=v((MB, C, R), BF16),
        part=v((MB, H, HEAD_DIM, R), F32),
        delta=v((MB, H, 8, R), F32),
        dqacc=v((MB, H, HEAD_DIM, R), F32),
        dkacc=v((nb - MB if z.keep else 1, L, R), F32),
        dq=v((C, Q), BF16),
        tgs=v((nb, C, R), BF16),
        tgo=v((MB, C, R), F32),
        tgr=v((MB, z.S, C, R), BF16),
        tgx=v((MB, C, R), BF16),
        gkv=v((C + 8, L), F32),
        gq=v((C + 8, L), F32),
        gup=v((C + 8, F), F32),
        gout=v((F + 16, C), F32),
        gdn=v((F + 16, C), F32),
        vg=v((VECS, C), F32),
        ug=v((8, F), F32),
        pk=v((4, W, rA, L), BF16),
        got1=v((4, dd, nb, rA, L), BF16),
        sent2=v((4, nb, rA, L), BF16),
        got2=v((4, nb, rA, L), BF16),
        x_ss=dma((MB,)),
        xf_ss=dma((MB, z.S)),
        x_rs=dma((nb,)),
        c_ss=dma((MB,)),
        c_rs=dma((MB,)),
        g1_ss=dma((4, nb)),
        g1_rs=dma((4, nb)),
        g2_ss=dma((4, dd, nb)),
        g2_rs=dma((4, dd, nb)),
        o_ss=dma((MB, nh)),
        o_rs=dma((MB, nh)),
        p_ss=dma((MB, nh)),
        p_rs=dma((MB, nh)),
        w_ss=dma((nh,)),
        w_rs=dma((nh,)),
        st_ss=dma((3, MB, nh)),
        st_rs=dma((3, MB, nh)),
        mo_ss=dma((MB,)),
        mo_rs=dma((MB,)),
        tp_ss=dma((nb,)),
        tp_rs=dma((MB, z.S)),
        t_ss=dma((MB,)),
        t_rs=dma((MB,)),
        s1_ss=dma((4, dd, nb)),
        s1_rs=dma((4, dd, nb)),
        s2_ss=dma((4, nb)),
        s2_rs=dma((4, nb)),
        **{"v_" + name: v(a.shape, a.dtype) for name, a in zip(INPUTS[1:], inputs)},
    )


def main_kernel(z, names, *refs):
    k = types.SimpleNamespace(**dict(zip(names, refs)))
    nb, nd, nh, W, MB, R, C, F, H, L, S, r, rs, rA = (
        z.nb, z.nd, z.nh, z.W, z.MB, z.R, z.C, z.F, z.H, z.L, z.S, z.r, z.rs, z.rA,
    )
    b, d, h = lax.axis_index("blk"), lax.axis_index("dp"), lax.axis_index("head")
    w_me = b * nd + d
    m_t, s_me = b // S, b % S
    D = nh * C
    half = nh // 2

    def xor(i):
        return lax.bitwise_xor(h, i)

    def later(e):
        return lax.rem(m_t + e, MB)

    def home(e):
        return later(e) * S + s_me

    def mate(e):
        return lax.rem(s_me + e, S)

    def other(n):
        return lax.rem(s_me + 1 + n // MB, S) + lax.rem(m_t + n, MB) * S

    fetch = [
        pltpu.make_async_copy(getattr(k, name), getattr(k, "v_" + name), k.in_sem.at[n])
        for n, name in enumerate(INPUTS[1:])
    ]
    for copy in fetch:
        copy.start()

    bar = pltpu.get_barrier_semaphore()
    peers = [(lax.rem(b + i, nb), d, h) for i in range(1, nb)]
    peers += [(b, lax.rem(d + i, nd), h) for i in range(1, nd)]
    peers += [(b, d, xor(i)) for i in range(1, nh)]
    for peer in peers:
        pl.semaphore_signal(bar, inc=1, device_id=peer, device_id_type=MESH)

    for copy in fetch:
        copy.wait()

    def pack(q):
        k.buf[q, w_me] = k.fst[...].astype(BF16)

    k.vst[...] = jnp.zeros_like(k.vst)
    for j, ref in enumerate((k.v_bq, k.v_bv, k.v_bo, k.v_g1, k.v_s1, k.v_bd, k.v_g2, k.v_s2)):
        k.vst[j : j + 1, 0:r] = ref[...].astype(F32)
    k.fst[...] = jnp.zeros_like(k.fst)
    k.fst[0:r, 0:C] = k.v_wk_in[0].astype(F32)
    k.fst[0:r, C:L] = k.v_wv_in[0].astype(F32)
    k.fst[rs : rs + r, 0:C] = k.v_wq_in[0].astype(F32)
    k.fst[rs : rs + r, C : C + VECS] = k.vst[...].T[0:r]
    k.fst[rs : rs + 1, C + VECS : C + VECS + 4 * r] = k.v_bu[...].astype(F32)
    pack(M_QKV)
    for q, src in ((M_OUT, k.v_wo_in[...]), (M_DOWN, k.v_wdn_in[0])):
        src = src.astype(F32)
        k.fst[0 : 2 * r, 0:C] = src[0 : 2 * r]
        k.fst[0 : 2 * r, C:L] = src[2 * r : 4 * r]
        pack(q)
    k.fst[0:r] = k.v_wup_in[0, :, 0:L].astype(F32)
    k.fst[rs : rs + r] = k.v_wup_in[0, :, L : 2 * L].astype(F32)
    pack(M_UP)

    for n, (src, dst) in enumerate(((k.v_tok, k.xs), (k.v_cot, k.cs))):
        both = src[...].astype(F32)
        for m in range(MB):
            k.flat[n * MB + m] = both[:, m]
            dst[m] = columns_of(z, k.flat.at[n * MB + m]).astype(BF16)
    k.xb[b] = k.xs[m_t]
    k.cb[0] = k.cs[m_t]

    pl.semaphore_wait(bar, len(peers))

    def g1(q, i):
        own = k.buf.at[q, w_me]
        return rcopy(own, own, k.g1_ss.at[q, i], k.g1_rs.at[q, i], (lax.rem(b + i, nb), d, h))

    def g1_wait(q, i):
        src = k.buf.at[q, lax.rem(b + nb - i, nb) * nd + d]
        rcopy(src, src, k.g1_ss.at[q, i], k.g1_rs.at[q, i], (b, d, h)).wait_recv()

    def g2(q, e, i):
        src = k.buf.at[q, lax.rem(b + nb - i, nb) * nd + d]
        return rcopy(src, src, k.g2_ss.at[q, e - 1, i], k.g2_rs.at[q, e - 1, i], (b, lax.rem(d + e, nd), h))

    def g2_wait(q, e, i):
        src = k.buf.at[q, lax.rem(b + nb - i, nb) * nd + lax.rem(d + nd - e, nd)]
        rcopy(src, src, k.g2_ss.at[q, e - 1, i], k.g2_rs.at[q, e - 1, i], (b, d, h)).wait_recv()

    def gather_start(q):
        for e in range(1, nd):
            g2(q, e, 0).start()
        loop(nb - 1, lambda i: g1(q, i + 1).start())

    def gather_forward(q):
        def one(i):
            g1_wait(q, i + 1)
            for e in range(1, nd):
                g2(q, e, i + 1).start()

        loop(nb - 1, one)

    def gather_wait(q):
        for e in range(1, nd):
            loop(nb, lambda i: g2_wait(q, e, i))

    def gather_drain(q):
        loop(nb - 1, lambda i: g1(q, i + 1).wait_send())
        for e in range(1, nd):
            loop(nb, lambda i: g2(q, e, i).wait_send())

    gather_start(M_QKV)

    def x_send(e):
        m = later(e)
        return rcopy(k.xs.at[m], k.xb.at[b], k.x_ss.at[e], k.x_rs.at[b], (m * S + s_me, d, h))

    def x_pass(e, f):
        src = k.xb.at[home(e)]
        return rcopy(src, src, k.xf_ss.at[e, f], k.x_rs.at[home(e)], (m_t * S + mate(f), d, h))

    def x_wait(j):
        rcopy(k.xb.at[j], k.xb.at[j], k.x_ss.at[0], k.x_rs.at[j], (b, d, h)).wait_recv()

    for e in range(1, MB):
        x_send(e).start()
    loop(S - 1, lambda f: x_pass(0, f + 1).start())

    gather_forward(M_QKV)

    gather_wait(M_QKV)

    for w in range(W):
        slab = k.buf[M_QKV, w].astype(F32)
        k.fkv[w * r : w * r + rs] = slab[0:rs]
        k.fq[w * r : w * r + rs] = slab[rs : 2 * rs]
    k.wkv[...] = k.fkv[0:C].astype(BF16)
    k.wkvt[...] = k.fkv[0:C].T.astype(BF16)
    k.wq[...] = k.fq[0:C, 0:C].astype(BF16)
    k.wqt[...] = k.fq[0:C, 0:C].T.astype(BF16)

    def vec(j):
        return k.fq[0:C, C + j : C + j + 1]

    row16 = lax.broadcasted_iota(jnp.int32, (16, R), 0)
    column = lax.broadcasted_iota(jnp.int32, (16, R), 1)
    step = R // z.per
    token = z.per * (column % step) + column // step
    pad = jnp.zeros((48, R), BF16)
    one_rows = jnp.where(row16 < 2, 1.0, 0.0).astype(BF16)

    def in_doc(j):
        doc = jnp.zeros((16, R), jnp.int32)
        end = jnp.int32(0)
        for n in range(z.ND):
            end = end + k.lens[m_t, 0, n]
            doc = doc + (j * R + token >= end).astype(jnp.int32)
        return row16 == doc

    def head_send(net, i, p):
        buf, ss, rs_ = net
        src, to = (h, xor(p)) if p <= half else (xor(half), xor(p - half))
        return rcopy(buf.at[i, src], buf.at[i, src], ss.at[i, p], rs_.at[i, p], (b, d, to))

    def head_wait(net, i, p):
        buf, ss, rs_ = net
        rcopy(buf.at[i, xor(p)], buf.at[i, xor(p)], ss.at[i, p], rs_.at[i, p], (b, d, h)).wait_recv()

    def head_start(net, i):
        for p in range(half, 0, -1):
            head_send(net, i, p).start()

    def head_pass(net, i):
        head_wait(net, i, half)
        for p in range(half + 1, nh):
            head_send(net, i, p).start()

    def head_end(net, i):
        for p in range(1, nh):
            if p != half:
                head_wait(net, i, p)

    o_net = (k.oall, k.o_ss, k.o_rs)
    p_net = (k.pall, k.p_ss, k.p_rs)

    def kv_block(t, j):
        kv = mm(k.wkvt[...], k.xb[j])
        kb = kv[0:C].astype(BF16)
        vb = (kv[C:L] + vec(V_BV)).astype(BF16)
        barred = jnp.logical_and(row16 < z.ND, jnp.logical_not(in_doc(j)))
        kf = jnp.where(barred, -BIG, 0.0).astype(BF16)
        for a in range(H):
            kh, vh = kb[a * HEAD_DIM : (a + 1) * HEAD_DIM], vb[a * HEAD_DIM : (a + 1) * HEAD_DIM]
            k.kx[t, a] = kh
            k.vx[t, a, 0:HEAD_DIM] = vh
            k.vx[t, a, HEAD_DIM:] = one_rows
            k.kt[t, a] = jnp.concatenate([kh, kf, pad], axis=0).T
            k.vt[t, a] = jnp.concatenate([vh, one_rows, pad], axis=0).T

    def query_block(e):
        xi = k.xb[home(e)]
        k.xq[:, e * R : (e + 1) * R] = xi
        qi = ((mm(k.wqt[...], xi) + vec(V_BQ)).astype(BF16).astype(F32) * HEAD_DIM**-0.5).astype(BF16)
        hot = jnp.where(in_doc(home(e)), 1.0, 0.0).astype(BF16)
        for a in range(H):
            k.qx[e, a] = jnp.concatenate([qi[a * HEAD_DIM : (a + 1) * HEAD_DIM], hot, pad], axis=0)

    def scores(e, a, t):
        return mm(k.kt[t, a], k.qx[e, a])

    def prob(e, a, t):
        if z.keep:
            return k.pbuf[t, e, a]
        return jnp.exp(scores(e, a, t) - k.tops[e, a, pl.ds(t, 1)]).astype(BF16)

    def attend(pairs):
        units = [(e, a, t) for e, t in pairs for a in range(H)]
        s = [scores(*u) for u in units]
        top = [jnp.max(x, axis=0, keepdims=True) for x in s]
        p = [jnp.exp(x - y).astype(BF16) for x, y in zip(s, top)]
        o = [mm(k.vx[t, a], x) for (e, a, t), x in zip(units, p)]
        for i, (e, a, t) in enumerate(units):
            if z.keep:
                k.pbuf[t, e, a] = p[i]
            k.tops[e, a, pl.ds(t, 1)] = top[i]
        for i, (e, a, t) in enumerate(units):
            if isinstance(t, int) and t == 0:
                k.top[e, a, 0:1] = top[i]
                k.osum[e, a] = o[i]
            else:
                old = k.top[e, a, 0:1]
                new = jnp.maximum(old, top[i])
                k.top[e, a, 0:1] = new
                k.osum[e, a] = k.osum[e, a] * jnp.exp(old - new) + o[i] * jnp.exp(top[i] - new)

    def factor(e, a, t):
        return jnp.exp(k.tops[e, a, pl.ds(t, 1)] - k.top[e, a, 0:1]) * k.top[e, a, 1:2]

    for e in range(1, MB):
        x_wait(home(e))
        loop(S - 1, lambda f: x_pass(e, f + 1).start())
    gather_start(M_OUT)
    gather_start(M_UP)
    for e in range(MB):
        kv_block(e, home(e))
        query_block(e)
    for t in range(MB):
        attend([(e, t) for e in range(MB)])

    def attend_other(n):
        x_wait(other(n))
        kv_block(MB + n, other(n))
        attend([(e, MB + n) for e in range(MB)])

    def heads_done(e):
        for a in range(H):
            o = k.osum[e, a]
            inv = 1.0 / o[HEAD_DIM : HEAD_DIM + 1]
            k.top[e, a, 1:2] = inv
            k.oall[e, h, a * HEAD_DIM : (a + 1) * HEAD_DIM] = (o[0:HEAD_DIM] * inv).astype(BF16)
        head_start(o_net, e)

    last = nb - MB - 1
    loop(last, attend_other)
    x_wait(other(last))
    gather_start(M_DOWN)
    kv_block(MB + last, other(last))
    for e in range(MB):
        attend([(e, MB + last)])
        heads_done(e)

    gather_forward(M_OUT)
    gather_forward(M_UP)
    for e in range(MB):
        head_pass(o_net, e)
    gather_wait(M_OUT)

    per = W // nh

    def w_send(p):
        src = k.buf.at[M_OUT, pl.ds(xor(p) * per, per)]
        return rcopy(src, k.wob.at[h], k.w_ss.at[p], k.w_rs.at[p], (b, d, xor(p)))

    for p in range(1, nh):
        w_send(p).start()

    def spread(dst, slab, row):
        slab = slab.astype(F32)
        dst[row : row + z.r2] = slab[0 : z.r2, 0:C]
        dst[row + 2 * r : row + 2 * r + z.r2] = slab[0 : z.r2, C:L]

    for w in range(W):
        spread(k.fod, k.buf[M_OUT, w], 4 * r * w)
    k.wot[...] = k.fod[0:F].T.astype(BF16)

    gather_forward(M_DOWN)

    def c_send(e):
        m = later(e)
        slot = lax.rem(m_t + MB - m, MB)
        return rcopy(k.cs.at[m], k.cb.at[slot], k.c_ss.at[e], k.c_rs.at[slot], (m * S + s_me, d, h))

    for e in range(1, MB):
        c_send(e).start()

    lane_rows = R // 128

    def st_send(e, i, p):
        own = k.stats.at[e, i, h]
        return rcopy(own, own, k.st_ss.at[e, i, p], k.st_rs.at[e, i, p], (b, d, xor(p)))

    def reduce_start(e, i, rows):
        for j, v in enumerate(rows):
            row = jnp.sum(v, axis=0, keepdims=True)
            for c in range(lane_rows):
                k.stats[e, i, h, pl.ds(j * lane_rows + c, 1)] = row[:, c * 128 : (c + 1) * 128]
        if len(rows) * lane_rows < 8:
            rest = 8 - len(rows) * lane_rows
            k.stats[e, i, h, pl.ds(8 - rest, rest)] = jnp.zeros((rest, 128), F32)
        for p in range(nh - 1, 0, -1):
            st_send(e, i, p).start()

    def reduce_end(e, i, n):
        for p in range(1, nh):
            src = k.stats.at[e, i, xor(p)]
            rcopy(src, src, k.st_ss.at[e, i, p], k.st_rs.at[e, i, p], (b, d, h)).wait_recv()
        total = k.stats[e, i, 0]
        for j in range(1, nh):
            total = total + k.stats[e, i, j]
        total = total / D
        return [
            jnp.concatenate([total[j * lane_rows + c :][0:1] for c in range(lane_rows)], axis=1)
            for j in range(n)
        ]

    def cols(ref, i):
        return ref[:, i * R : (i + 1) * R]

    for i in range(MB):
        head_end(o_net, i)
        h1 = cols(k.xq, i).astype(F32) + mm(k.wot[...], k.oall[i].reshape(D, R)) + vec(V_BO)
        k.n1[i] = h1
        reduce_start(0, i, (h1, h1 * h1))

    gather_wait(M_UP)
    for w in range(W):
        slab = k.buf[M_UP, w].astype(F32)
        k.fup[w * r : w * r + rs, 0:L] = slab[0:rs]
        k.fup[w * r : w * r + rs, L:F] = slab[rs : 2 * rs]
    k.fup[C : C + 16] = jnp.zeros((16, F), F32)
    for w in range(W):
        row = k.buf[M_QKV, w].astype(F32)[rs : rs + 1, C + VECS : C + VECS + 4 * r]
        k.fup[C : C + 1, 4 * r * w : 4 * r * (w + 1)] = row
    k.wup[...] = k.fup[0:C].astype(BF16)
    k.wupt[...] = k.fup[...].T.astype(BF16)
    gather_wait(M_DOWN)
    for w in range(W):
        spread(k.fod, k.buf[M_DOWN, w], 4 * r * w)
    k.wdn[...] = k.fod[0:F].astype(BF16)
    k.wdnt[...] = k.fod[0:F].T.astype(BF16)

    first_one = jnp.where(row16 < 1, 1.0, 0.0).astype(BF16)
    r1 = [None] * MB
    gdn = [None] * MB
    for i in range(MB):
        mean, square = reduce_end(0, i, 2)
        r1[i] = lax.rsqrt(square - mean * mean + EPS)
        n1 = (k.n1[i] - mean) * r1[i]
        k.n1[i] = n1
        y1 = n1 * vec(V_G1) + vec(V_S1)
        k.y1[i] = y1
        y1b = y1.astype(BF16)
        k.y1b[:, i * R : (i + 1) * R] = y1b
        u = mm(k.wupt[...], jnp.concatenate([y1b, first_one], axis=0))
        cdf = 0.5 * (1.0 + lax.erf(u * (0.5**0.5)))
        act = (u * cdf).astype(BF16)
        k.act[:, i * R : (i + 1) * R] = act
        h2 = y1 + mm(k.wdnt[...], act) + vec(V_BD)
        k.h2[i] = h2

        if i > 0:
            rcopy(k.cb.at[i], k.cb.at[i], k.c_ss.at[0], k.c_rs.at[i], (b, d, h)).wait_recv()
        dn2 = k.cb[i].astype(F32) * vec(V_G2)
        reduce_start(1, i, (h2, h2 * h2, dn2, dn2 * h2))
        k.up[i], k.gel[i] = u, cdf
    for i in range(MB):
        u = k.up[i]
        k.gel[i] += u * jnp.exp(-0.5 * u * u) * ((2 * jnp.pi) ** -0.5)
    k.vg[...] = jnp.zeros_like(k.vg)
    ones = jnp.ones((16, R), BF16)

    def vec_grad(j, x):
        k.vg[j : j + 1] += mm_nt(ones, x)[0:1]

    def mo_send(i):
        return rcopy(k.mo.at[i], k.o_mo.at[m_t], k.mo_ss.at[i], k.mo_rs.at[m_t], (home(i), d, h))

    for i in range(MB):
        mean, square, dmean, dsquare = reduce_end(1, i, 4)
        r2 = lax.rsqrt(square - mean * mean + EPS)
        g = k.cb[i].astype(F32)
        dn2 = g * vec(V_G2)
        n2 = (k.h2[i] - mean) * r2
        dh2 = r2 * (dn2 - dmean - n2 * (r2 * (dsquare - mean * dmean)))
        dz = dh2.astype(BF16)
        k.dz[:, i * R : (i + 1) * R] = dz
        du = (mm(k.wdn[...], dz) * k.gel[i]).astype(BF16)
        k.du[:, i * R : (i + 1) * R] = du
        dy1 = dh2 + mm(k.wup[...], du)
        dn1 = dy1 * vec(V_G1)
        k.dh1[i] = dn1
        n1 = k.n1[i]
        reduce_start(2, i, (dn1, dn1 * n1))
        out = (n2 * vec(V_G2) + vec(V_S2)).astype(BF16)
        if i > 0:
            k.mo[i] = out
            mo_send(i).start()
        else:
            k.o_mo[m_t] = out
        k.vin[0, i] = (g * n2).astype(BF16)
        k.vin[1, i] = (dy1 * n1).astype(BF16)
        k.vin[2, i] = dy1.astype(BF16)

    def s1_send(q, e, i):
        dt = lax.rem(d + e, nd)
        return rcopy(
            k.pk.at[q, i * nd + dt], k.got1.at[q, e - 1, i], k.s1_ss.at[q, e - 1, i], k.s1_rs.at[q, e - 1, i],
            (b, dt, h),
        )

    def s2_send(q, i):
        bt = lax.rem(b + i, nb)
        return rcopy(k.sent2.at[q, bt], k.got2.at[q, b], k.s2_ss.at[q, i], k.s2_rs.at[q, i], (bt, d, h))

    def scatter_start(q):
        for e in range(1, nd):
            loop(nb, lambda i: s1_send(q, e, i).start())

    def scatter_sum(q, bt):
        part = k.pk[q, bt * nd + d].astype(F32)
        for e in range(1, nd):
            src = k.got1.at[q, e - 1, bt]
            rcopy(src, src, k.s1_ss.at[q, e - 1, bt], k.s1_rs.at[q, e - 1, bt], (b, d, h)).wait_recv()
            part = part + src[...].astype(F32)
        return part

    def scatter_forward(q):
        def one(i):
            bt = lax.rem(b + i + 1, nb)
            k.sent2[q, bt] = scatter_sum(q, bt).astype(BF16)
            s2_send(q, i + 1).start()

        loop(nb - 1, one)
        k.o_G[q] = scatter_sum(q, b)

    def scatter_end(q):
        def one(i):
            src = k.got2.at[q, lax.rem(b + nb - i - 1, nb)]
            rcopy(src, src, k.s2_ss.at[q, i + 1], k.s2_rs.at[q, i + 1], (b, d, h)).wait_recv()
            k.o_G[q] += src[...].astype(F32)

        loop(nb - 1, one)
        loop(nb - 1, lambda i: s2_send(q, i + 1).wait_send())
        for e in range(1, nd):
            loop(nb, lambda i: s1_send(q, e, i).wait_send())

    def rows_of(parts):
        rows = jnp.concatenate(parts, axis=0)
        if rows.shape[0] < rA:
            rows = jnp.concatenate([rows, jnp.zeros((rA - rows.shape[0], L), F32)], axis=0)
        return rows.astype(BF16)

    def pack_halves(q, g):
        for w in range(W):
            at = 4 * r * w
            pair = jnp.concatenate([g[at : at + z.r2], g[at + 2 * r : at + 2 * r + z.r2]], axis=1)
            k.pk[q, w] = rows_of([pair])
        scatter_start(q)

    k.gdn[0:F] = mm_nt(k.act[...], k.dz[...])
    pack_halves(M_DOWN, k.gdn)
    k.gup[0:C] = mm_nt(k.y1b[...], k.du[...])
    for w in range(W):
        k.pk[M_UP, w] = rows_of([k.gup[w * r : w * r + rs, 0:L], k.gup[w * r : w * r + rs, L:F]])
    scatter_start(M_UP)
    for i in range(MB):
        for j, x in ((V_G2, k.vin[0, i]), (V_G1, k.vin[1, i]), (V_S1, k.vin[2, i]), (V_S2, k.cb[i])):
            vec_grad(j, x)
        vec_grad(V_BD, cols(k.dz, i))

    for i in range(MB):
        dmean, dsquare = reduce_end(2, i, 2)
        dh1 = r1[i] * (k.dh1[i] - dmean - k.n1[i] * dsquare)
        k.dh1[i] = dh1
        dp = dh1.astype(BF16)
        k.pall[i, h] = dp
        head_start(p_net, i)

    g = None
    for i in range(MB):
        dp = k.pall[i, h]
        part = mm_nt(k.oall[i].reshape(D, R), dp)
        g = part if g is None else g + part
        vec_grad(V_BO, dp)
    k.gout[0:F] = g
    pack_halves(M_OUT, k.gout)
    ug = mm_nt(jnp.ones((16, z.Q), BF16), k.du[...])
    k.gq[...] = jnp.zeros_like(k.gq)
    for w in range(W):
        k.gq[w * r : w * r + 1, C + VECS : C + VECS + 4 * r] = ug[0:1, 4 * r * w : 4 * r * (w + 1)]
    k.gkv[...] = jnp.zeros_like(k.gkv)

    for p in range(1, nh):
        src = k.wob.at[xor(p)]
        rcopy(src, src, k.w_ss.at[p], k.w_rs.at[p], (b, d, h)).wait_recv()
    k.wob[h] = k.buf[M_OUT, pl.ds(h * per, per)]
    for j in range(nh):
        for n in range(per):
            spread(k.fod, k.wob[j, n], j * C + 4 * r * n)
    for j in range(nh):
        k.wor[:, j * C : (j + 1) * C] = k.fod[j * C : (j + 1) * C].astype(BF16)

    head_pass(p_net, 0)
    scatter_forward(M_DOWN)
    for i in range(1, MB):
        head_pass(p_net, i)

    def grad_in(e):
        head_end(p_net, e)
        do = mm(k.wor[...], k.pall[e].reshape(D, R)).astype(BF16).astype(F32)
        for a in range(H):
            part = do[a * HEAD_DIM : (a + 1) * HEAD_DIM]
            own = k.oall[e, h, a * HEAD_DIM : (a + 1) * HEAD_DIM].astype(F32)
            k.part[e, a] = part
            k.delta[e, a, 0:1] = jnp.sum(part * own, axis=0, keepdims=True)
            k.dqacc[e, a] = jnp.zeros((HEAD_DIM, R), F32)

    def scaled(e, a, t):
        f = factor(e, a, t)
        delta = k.delta[e, a, 0:1] * f
        hi = delta.astype(BF16).astype(F32)
        rest = jnp.where(row16 == 0, -hi, jnp.where(row16 == 1, hi - delta, 0.0))
        return jnp.concatenate([(k.part[e, a] * f).astype(BF16), rest.astype(BF16), pad], axis=0)

    def back(slots, queries):
        units = [(e, a, t) for t in slots for a in range(H) for e in queries]
        dox = [scaled(*u) for u in units]
        p = [prob(*u) for u in units]
        dp = [mm(k.vt[t, a], x) for (e, a, t), x in zip(units, dox)]
        ds = [(x.astype(F32) * y).astype(BF16) for x, y in zip(p, dp)]
        dq = [mm(k.kx[t, a], x) for (e, a, t), x in zip(units, ds)]
        dk = [mm_nt(k.qx[e, a, 0:HEAD_DIM], x) for (e, a, t), x in zip(units, ds)]
        dv = [mm_nt(x[0:HEAD_DIM], y) for x, y in zip(dox, p)]
        for e in queries:
            for a in range(H):
                mine = [x for (e2, a2, t), x in zip(units, dq) if (e2, a2) == (e, a)]
                k.dqacc[e, a] += sum(mine[1:], mine[0])
        found = []
        per_slot = H * len(queries)
        for n in range(len(slots)):
            rows = []
            for x in (dk, dv):
                for a in range(H):
                    at = n * per_slot + a * len(queries)
                    rows.append(sum(x[at + 1 : at + len(queries)], x[at]))
            found.append(jnp.concatenate(rows, axis=0))
        return found

    def tokens_part(j, dkv):
        k.gkv[0:C] += mm_nt(k.xb[j], dkv)
        vec_grad(V_BV, dkv[C:L])
        return mm(k.wkv[...], dkv)

    def tp_send(n):
        dst = k.tgr.at[n % MB, s_me]
        to = lax.rem(s_me + 1 + n // MB, S)
        return rcopy(k.tgs.at[n], dst, k.tp_ss.at[n], k.tp_rs.at[n % MB, s_me], (m_t * S + to, d, h))

    def send_part(n, dkv):
        k.tgs[n] = tokens_part(other(n), dkv.astype(BF16)).astype(BF16)
        if not z.keep or n % MB:
            tp_send(n).start()

    others = list(range(nb - MB - 1, -1, -1))
    for e in range(MB):
        grad_in(e)
        if z.keep:
            found = back([MB + n for n in others], [e])
            for n, dkv in zip(others, found):
                if e > 0:
                    dkv = dkv + k.dkacc[n]
                if e < MB - 1:
                    k.dkacc[n] = dkv
                else:
                    send_part(n, dkv)
        if e == 0:
            scatter_forward(M_UP)
    if not z.keep:
        loop(nb - MB, lambda n: send_part(n, back([MB + n], range(MB))[0]))

    for e in range(MB - 1, -1, -1):
        dkv = back([e], range(MB))[0]
        k.tgo[e] = tokens_part(home(e), dkv.astype(BF16))
        if e == MB - 1:
            scatter_forward(M_OUT)

    for i in range(MB):
        for a in range(H):
            rows = slice(a * HEAD_DIM, (a + 1) * HEAD_DIM)
            k.dq[rows, i * R : (i + 1) * R] = (k.dqacc[i, a] * HEAD_DIM**-0.5).astype(BF16)
        vec_grad(V_BQ, cols(k.dq, i))
    k.gq[0:C, 0:C] = mm_nt(k.xq[...], k.dq[...])
    k.gq[0:C, C : C + VECS] = k.vg[...].T

    for w in range(W):
        k.pk[M_QKV, w] = rows_of([k.gkv[w * r : w * r + rs], k.gq[w * r : w * r + rs]])
    scatter_start(M_QKV)

    def t_send(e):
        return rcopy(k.tgx.at[e], k.o_tg.at[m_t], k.t_ss.at[e], k.t_rs.at[m_t], (home(e), d, h))

    def tokens_total(e):
        k.tgo[e] += k.dh1[e] + mm(k.wq[...], cols(k.dq, e))

        def add(f):
            src = k.tgr.at[e, mate(f + 1)]
            rcopy(src, src, k.tp_ss.at[0], k.tp_rs.at[e, mate(f + 1)], (b, d, h)).wait_recv()
            k.tgo[e] += src[...].astype(F32)

        loop(S - 1, add)
        return k.tgo[e].astype(BF16)

    for e in range(1, MB):
        k.tgx[e] = tokens_total(e)
        t_send(e).start()
    if z.keep:
        for n in range(0, nb - MB, MB):
            tp_send(n).start()

    scatter_forward(M_QKV)

    k.o_tg[m_t] = tokens_total(0)
    for q in (M_DOWN, M_UP, M_OUT, M_QKV):
        scatter_end(q)
    for e in range(1, MB):
        m = later(e)
        for out, ss, rs_ in ((k.o_tg, k.t_ss, k.t_rs), (k.o_mo, k.mo_ss, k.mo_rs)):
            rcopy(out.at[m], out.at[m], ss.at[e], rs_.at[m], (b, d, h)).wait_recv()
        for send in (c_send, x_send, mo_send, t_send):
            send(e).wait_send()
    for e in range(MB):
        loop(S - 1, lambda f: x_pass(e, f + 1).wait_send())
    loop(nb - MB, lambda n: tp_send(n).wait_send())
    for q in range(4):
        gather_drain(q)
    for p in range(1, nh):
        w_send(p).wait_send()
        for i in range(MB):
            head_send(o_net, i, p).wait_send()
            head_send(p_net, i, p).wait_send()
            for e in range(3):
                st_send(e, i, p).wait_send()


def finish_kernel(z, mo, tg, G, *outs):
    (mixed, dtok, dwq, dbq, dwk, dwv, dbv, dwo, dbo, dg1, ds1, dwup, dbu, dwdn, dbd, dg2, ds2, both) = outs
    r, rs, C, L = z.r, z.rs, z.C, z.L
    for m in range(z.MB):


        def put_mixed(i, rows):
            both[pl.ds(i, z.R // z.per, stride=z.span), m] = rows

        def put_grad(i, rows):
            dtok[m, pl.ds(i, z.R // z.per, stride=z.span)] = rows

        put_rows(z, mo[m].astype(F32), put_mixed)
        put_rows(z, tg[m].astype(F32), put_grad)
    mixed[...] = both[...].astype(BF16)
    dwk[0] = G[M_QKV, 0:r, 0:C]
    dwv[0] = G[M_QKV, 0:r, C:L]
    dwq[0] = G[M_QKV, rs : rs + r, 0:C]
    dwup[0, :, 0:L] = G[M_UP, 0:r]
    dwup[0, :, L : 2 * L] = G[M_UP, rs : rs + r]
    for q, ref in ((M_OUT, dwo), (M_DOWN, dwdn.at[0])):
        ref[0 : 2 * r] = G[q, 0 : 2 * r, 0:C]
        ref[2 * r : 4 * r] = G[q, 0 : 2 * r, C:L]
    vecs = G[M_QKV, rs : 2 * rs, C : C + VECS].T
    for j, ref in enumerate((dbq, dbv, dbo, dg1, ds1, dbd, dg2, ds2)):
        ref[...] = vecs[j : j + 1, 0:r]
    dbu[...] = G[M_QKV, rs : rs + 1, C + VECS : C + VECS + 4 * r]


def solution(mesh):
    vec_spec = P("head", ("blk", "dp"))
    mat_spec = P("head", ("blk", "dp"), None)
    tok_spec = P(None, "dp", "head", "blk")
    out_spec = P(("blk", "dp"), "head")

    def body(
        tokens, doc_lengths, cotangent, query_weight, query_bias, key_weight, value_weight, value_bias,
        out_weight, out_bias, first_gain, first_shift, up_weight, up_bias, down_weight, down_bias,
        second_gain, second_shift,
    ):
        z = Sizes(mesh, tokens, query_weight, up_weight, doc_lengths)

        def as_rows(a):
            return a.reshape(z.MB, z.N, 128).transpose(1, 0, 2)

        operands = (
            as_rows(tokens), as_rows(cotangent), query_weight, query_bias, key_weight, value_weight, value_bias,
            out_weight, out_bias, first_gain, first_shift, up_weight, up_bias, down_weight, down_bias, second_gain,
            second_shift,
        )
        scratch = main_scratch(z, operands)
        vmem = pl.BlockSpec(memory_space=pltpu.VMEM)
        smem = pl.BlockSpec(memory_space=pltpu.SMEM)
        hbm = pl.BlockSpec(memory_space=pltpu.HBM)
        names = INPUTS + OUTPUTS + list(scratch)
        sds = jax.ShapeDtypeStruct
        parts = pl.pallas_call(
            lambda *refs: main_kernel(z, names, *refs),
            out_shape=[
                sds((z.MB, z.C, z.R), BF16),
                sds((z.MB, z.C, z.R), BF16),
                sds((4, z.rA, z.L), F32),
            ],
            in_specs=[smem] + [hbm] * len(operands),
            out_specs=[vmem] * len(OUTPUTS),
            scratch_shapes=list(scratch.values()),
            compiler_params=pltpu.CompilerParams(
                collective_id=0, has_side_effects=True, vmem_limit_bytes=63 << 20
            ),
            name="layer",
        )(doc_lengths, *operands)
        mat, vec = sds((1, z.r, z.C), F32), sds((1, z.r), F32)
        outs = pl.pallas_call(
            lambda *refs: finish_kernel(z, *refs),
            out_shape=[
                sds((z.N, z.MB, 128), BF16), sds((z.MB, z.N, 128), F32), mat, vec, mat, mat, vec,
                sds((4 * z.r, z.C), F32), vec, vec, vec, sds((1, z.r, z.F), F32), sds((1, 4 * z.r), F32),
                sds((1, 4 * z.r, z.C), F32), vec, vec, vec,
            ],
            in_specs=[vmem] * len(OUTPUTS),
            out_specs=[vmem] * 17,
            scratch_shapes=[pltpu.VMEM((z.N, z.MB, 128), F32)],
            name="finish",
        )(*parts)
        shape = tokens.shape
        return (outs[0].transpose(1, 0, 2).reshape(shape), outs[1].reshape(shape), *outs[2:])

    return jax.shard_map(
        body,
        mesh=mesh,
        in_specs=(
            tok_spec, P(None, "dp", None), tok_spec, mat_spec, vec_spec, mat_spec, mat_spec, vec_spec,
            out_spec, vec_spec, vec_spec, vec_spec, mat_spec, vec_spec, mat_spec, vec_spec, vec_spec, vec_spec,
        ),
        out_specs=(
            tok_spec, tok_spec, mat_spec, vec_spec, mat_spec, mat_spec, vec_spec, out_spec, vec_spec, vec_spec,
            vec_spec, mat_spec, vec_spec, mat_spec, vec_spec, vec_spec, vec_spec,
        ),
        check_vma=False,
    )
```

```python
import math
import types

import jax
import jax.numpy as jnp
from jax import lax
from jax.experimental import pallas as pl
from jax.experimental.pallas import tpu as pltpu
from jax.sharding import PartitionSpec as P

HEAD_DIM = 64
EPS = 1e-05
BIG = 1e30
MESH = pl.DeviceIdType.MESH
F32 = jnp.float32
BF16 = jnp.bfloat16
V_BQ, V_BV, V_BO, V_G1, V_S1, V_BD, V_G2, V_S2 = range(8)
M_OUT, M_UP, M_DOWN, M_QKV = range(4)


def up_to(n, m):
    return (n + m - 1) // m * m


def mm(a, b):
    return lax.dot_general(a, b, (((1,), (0,)), ((), ())), preferred_element_type=F32)


def mm_nt(a, b):
    return lax.dot_general(a, b, (((1,), (1,)), ((), ())), preferred_element_type=F32)


def loop(n, fn):
    if n <= 8:
        for i in range(n):
            fn(i)
    else:
        lax.fori_loop(0, n, lambda i, c: (fn(i), c)[1], 0)


def rcopy(src, dst, ss, rs, dev):
    return pltpu.make_async_remote_copy(
        src_ref=src, dst_ref=dst, send_sem=ss, recv_sem=rs, device_id=dev, device_id_type=MESH
    )


def pieces(c, u):
    at, end = u * c, (u + 1) * c
    found = []
    while at < end:
        size = min(128 - at % 128, end - at)
        found.append((at // 128, at % 128, size))
        at += size
    return found


def columns_of(z, flat):
    rows = [flat[pl.ds(i, z.R // z.per, stride=z.span)].T for i in range(z.span)]
    tokens = []
    for u in range(z.per):
        tokens.append(jnp.concatenate([rows[i][at : at + n] for i, at, n in pieces(z.C, u)], axis=0))
    return jnp.concatenate(tokens, axis=1)


def put_rows(z, value, put):
    n = z.R // z.per
    parts = [[] for _ in range(z.span)]
    for u in range(z.per):
        c = 0
        for i, _, size in pieces(z.C, u):
            parts[i].append(value[c : c + size, u * n : (u + 1) * n])
            c += size
    for i in range(z.span):
        put(i, jnp.concatenate(parts[i], axis=0).T)


class Sizes:
    def __init__(self, mesh, tokens, query_weight, up_weight, doc_lengths):
        self.nb, self.nd, self.nh = mesh.shape["blk"], mesh.shape["dp"], mesh.shape["head"]
        self.W = self.nb * self.nd
        self.C, self.F = query_weight.shape[2], up_weight.shape[2]
        self.MB = tokens.shape[0]
        self.R = tokens.shape[3] // self.C
        self.S = self.nb // self.MB
        self.Q = self.MB * self.R
        self.N = self.R * self.C // 128
        self.per = 128 // math.gcd(self.C, 128)
        self.span = self.per * self.C // 128
        self.H = self.C // HEAD_DIM
        self.ND = doc_lengths.shape[2]
        self.r = query_weight.shape[1]
        self.rs = up_to(self.r, 8)
        self.r2 = up_to(2 * self.r, 8)
        self.rA = up_to(2 * self.rs, 16)
        self.L = 2 * self.C
        self.full, left = divmod(3 * self.C, 128)
        self.left = self.full * self.rs
        fold = left == 64 and self.r % 2 == 0
        self.bits = [(0, 0, self.r // 2), (64, self.r // 2, self.r // 2)] if fold else [(0, 0, self.r)]
        self.vrow = self.left + up_to(self.bits[0][2], 4)
        self.vper = min(8, 128 // self.r)
        self.brow = self.vrow + -(-8 // self.vper)
        self.rQ = up_to(max(self.brow + 1, self.left + self.rs), 16)
        self.keep = self.nb * self.R * self.Q * self.H * 2 <= (8 << 20)
        assert self.F == 4 * self.C and self.F == self.nh * self.C and self.W % self.nh == 0


INPUTS = [
    "lens", "tok", "cot", "wq_in", "bq", "wk_in", "wv_in", "bv", "wo_in", "bo", "g1", "s1", "wup_in", "bu",
    "wdn_in", "bd", "g2", "s2",
]
OUTPUTS = ["o_mo", "o_tg", "o_G", "o_Q"]


def main_scratch(z, inputs):
    dma = pltpu.SemaphoreType.DMA
    v = pltpu.VMEM
    nb, W, L, R, C, F, Q, H, MB, rA, nh = z.nb, z.W, z.L, z.R, z.C, z.F, z.Q, z.H, z.MB, z.rA, z.nh
    dd = max(z.nd - 1, 1)
    return dict(
        in_sem=dma((len(INPUTS) - 1,)),
        flat=v((2 * MB, z.N, 128), F32),
        xs=v((MB, C, R), BF16),
        xb=v((nb, C, R), BF16),
        cs=v((MB, C, R), BF16),
        cb=v((MB, C, R), BF16),
        bufq=v((W, z.rQ, 128), BF16),
        buf=v((3, W, rA, L), BF16),
        wob=v((nh, W // nh, rA, L), BF16),
        fst=v((rA, L), F32),
        fsq=v((z.rQ, 128), F32),
        fall=v((C + 8, up_to(3 * C, 128)), F32),
        vrows=v((up_to(W * (z.brow - z.vrow), 8), 128), F32),
        vcol=v((C + 8, 8), F32),
        fup=v((C + 16, F), F32),
        fod=v((F + 16, C), F32),
        wkv=v((C, L), BF16),
        wkvt=v((L, C), BF16),
        wq=v((C, C), BF16),
        wqt=v((C, C), BF16),
        wup=v((C, F), BF16),
        wupt=v((F, C + 16), BF16),
        wor=v((C, F), BF16),
        wot=v((C, F), BF16),
        wdn=v((F, C), BF16),
        wdnt=v((C, F), BF16),
        xq=v((C, Q), BF16),
        qx=v((MB, H, 128, R), BF16),
        kx=v((nb, H, HEAD_DIM, R), BF16),
        vx=v((nb, H, HEAD_DIM + 16, R), BF16),
        kt=v((nb, H, R, 128), BF16),
        vt=v((nb, H, R, 128), BF16),
        pbuf=v((nb, MB, H, R, R) if z.keep else (1, 1, 1, 16, 128), BF16),
        tops=v((MB, H, up_to(nb, 8), R), F32),
        top=v((MB, H, 8, R), F32),
        osum=v((MB, H, HEAD_DIM + 16, R), F32),
        oall=v((MB, nh, C, R), BF16),
        pall=v((MB, nh, C, R), BF16),
        stats=v((3, MB, nh, 8, 128), F32),
        n1=v((MB, C, R), F32),
        y1=v((MB, C, R), F32),
        h2=v((MB, C, R), F32),
        gel=v((MB, F, R), F32),
        up=v((MB, F, R), F32),
        dh1=v((MB, C, R), F32),
        y1b=v((C, Q), BF16),
        act=v((F, Q), BF16),
        dz=v((C, Q), BF16),
        du=v((F, Q), BF16),
        vin=v((3, MB, C, R), BF16),
        mo=v((MB, C, R), BF16),
        part=v((MB, H, HEAD_DIM, R), F32),
        delta=v((MB, H, 8, R), F32),
        dqacc=v((MB, H, HEAD_DIM, R), F32),
        dkacc=v((nb - MB if z.keep else 1, L, R), F32),
        dq=v((C, Q), BF16),
        tgs=v((nb, C, R), BF16),
        tgo=v((MB, C, R), F32),
        tgr=v((MB, z.S, C, R), BF16),
        tgx=v((MB, C, R), BF16),
        gall=v((C + 8, up_to(3 * C, 128)), F32),
        gst=v((W, z.rQ, 128), F32),
        gup=v((C + 8, F), F32),
        gout=v((F + 16, C), F32),
        gdn=v((F + 16, C), F32),
        vg=v((8, C), F32),
        pk=v((3, W, rA, L), BF16),
        got1=v((3, dd, nb, rA, L), BF16),
        sent2=v((3, nb, rA, L), BF16),
        got2=v((3, nb, rA, L), BF16),
        pkq=v((W, z.rQ, 128), BF16),
        got1q=v((dd, nb, z.rQ, 128), BF16),
        sent2q=v((nb, z.rQ, 128), BF16),
        got2q=v((nb, z.rQ, 128), BF16),
        sync=pltpu.SemaphoreType.REGULAR((2,)),
        x_ss=dma((MB, 2)),
        xf_ss=dma((MB, z.S, 2)),
        x_rs=dma((nb, 2)),
        c_ss=dma((MB,)),
        c_rs=dma((MB,)),
        g1_ss=dma((4, nb)),
        g1_rs=dma((4, nb)),
        g2_ss=dma((4, dd, nb)),
        g2_rs=dma((4, dd, nb)),
        o_ss=dma((MB, nh)),
        o_rs=dma((MB, nh)),
        p_ss=dma((MB, nh)),
        p_rs=dma((MB, nh)),
        w_ss=dma((nh,)),
        w_rs=dma((nh,)),
        st_ss=dma((3, MB, nh)),
        st_rs=dma((3, MB, nh)),
        mo_ss=dma((MB,)),
        mo_rs=dma((MB,)),
        tp_ss=dma((nb,)),
        tp_rs=dma((MB, z.S)),
        t_ss=dma((MB,)),
        t_rs=dma((MB,)),
        s1_ss=dma((4, dd, nb)),
        s1_rs=dma((4, dd, nb)),
        s2_ss=dma((4, nb)),
        s2_rs=dma((4, nb)),
        **{"v_" + name: v(a.shape, a.dtype) for name, a in zip(INPUTS[1:], inputs)},
    )


def main_kernel(z, names, *refs):
    k = types.SimpleNamespace(**dict(zip(names, refs)))
    nb, nd, nh, W, MB, R, C, F, H, L, S, r, rs, rA = (
        z.nb, z.nd, z.nh, z.W, z.MB, z.R, z.C, z.F, z.H, z.L, z.S, z.r, z.rs, z.rA,
    )
    b, d, h = lax.axis_index("blk"), lax.axis_index("dp"), lax.axis_index("head")
    w_me = b * nd + d
    m_t, s_me = b // S, b % S
    D = nh * C
    half = nh // 2

    def xor(i):
        return lax.bitwise_xor(h, i)

    def later(e):
        return lax.rem(m_t + e, MB)

    def home(e):
        return later(e) * S + s_me

    def mate(e):
        return lax.rem(s_me + e, S)

    def other(n):
        return lax.rem(s_me + 1 + n // MB, S) + lax.rem(m_t + n, MB) * S

    fetch = [
        pltpu.make_async_copy(getattr(k, name), getattr(k, "v_" + name), k.in_sem.at[n])
        for n, name in enumerate(INPUTS[1:])
    ]
    for copy in fetch:
        copy.start()

    bar = pltpu.get_barrier_semaphore()
    peers = [(lax.rem(b + i, nb), d, h) for i in range(1, nb)]
    peers += [(b, lax.rem(d + i, nd), h) for i in range(1, nd)]
    peers += [(b, d, xor(i)) for i in range(1, nh)]
    for peer in peers:
        pl.semaphore_signal(bar, inc=1, device_id=peer, device_id_type=MESH)

    for copy in fetch:
        copy.wait()

    def pack(q):
        k.buf[q, w_me] = k.fst[...].astype(BF16)

    def place(n, put):
        column = 0
        for block, at, size in pieces(C, n):
            if block < z.full:
                put(block * rs, at, r, 0, column, size)
            else:
                for where, row, rows in z.bits:
                    put(z.left, at + where, rows, row, column, size)
            column += size

    vectors = (k.v_bq, k.v_bv, k.v_bo, k.v_g1, k.v_s1, k.v_bd, k.v_g2, k.v_s2)

    def vec_at(j):
        return z.vrow + j // z.vper, j % z.vper * r

    k.fsq[...] = jnp.zeros_like(k.fsq)
    for n, src in enumerate((k.v_wk_in[0], k.v_wv_in[0], k.v_wq_in[0])):
        src = src.astype(F32)

        def put(row, at, rows, row2, column, size):
            k.fsq[row : row + rows, at : at + size] = src[row2 : row2 + rows, column : column + size]

        place(n, put)
    for j, ref in enumerate(vectors):
        row, at = vec_at(j)
        k.fsq[row : row + 1, at : at + r] = ref[...].astype(F32)
    k.fsq[z.brow : z.brow + 1, 0 : 4 * r] = k.v_bu[...].astype(F32)
    k.bufq[w_me] = k.fsq[...].astype(BF16)
    k.fst[...] = jnp.zeros_like(k.fst)
    for q, src in ((M_OUT, k.v_wo_in[...]), (M_DOWN, k.v_wdn_in[0])):
        src = src.astype(F32)
        k.fst[0 : 2 * r, 0:C] = src[0 : 2 * r]
        k.fst[0 : 2 * r, C:L] = src[2 * r : 4 * r]
        pack(q)
    k.fst[0:r] = k.v_wup_in[0, :, 0:L].astype(F32)
    k.fst[rs : rs + r] = k.v_wup_in[0, :, L : 2 * L].astype(F32)
    pack(M_UP)

    for n, (src, dst) in enumerate(((k.v_tok, k.xs), (k.v_cot, k.cs))):
        both = src[...].astype(F32)
        for m in range(MB):
            k.flat[n * MB + m] = both[:, m]
            dst[m] = columns_of(z, k.flat.at[n * MB + m]).astype(BF16)
    k.xb[b] = k.xs[m_t]
    k.cb[0] = k.cs[m_t]

    pl.semaphore_wait(bar, len(peers))

    def shares(q):
        return k.bufq if q == M_QKV else k.buf.at[q]

    def g1(q, i):
        own = shares(q).at[w_me]
        return rcopy(own, own, k.g1_ss.at[q, i], k.g1_rs.at[q, i], (lax.rem(b + i, nb), d, h))

    def g1_wait(q, i):
        src = shares(q).at[lax.rem(b + nb - i, nb) * nd + d]
        rcopy(src, src, k.g1_ss.at[q, i], k.g1_rs.at[q, i], (b, d, h)).wait_recv()

    def g2(q, e, i):
        src = shares(q).at[lax.rem(b + nb - i, nb) * nd + d]
        return rcopy(src, src, k.g2_ss.at[q, e - 1, i], k.g2_rs.at[q, e - 1, i], (b, lax.rem(d + e, nd), h))

    def g2_wait(q, e, i):
        src = shares(q).at[lax.rem(b + nb - i, nb) * nd + lax.rem(d + nd - e, nd)]
        rcopy(src, src, k.g2_ss.at[q, e - 1, i], k.g2_rs.at[q, e - 1, i], (b, d, h)).wait_recv()

    def gather_start(q):
        for e in range(1, nd):
            g2(q, e, 0).start()
        loop(nb - 1, lambda i: g1(q, i + 1).start())

    def gather_forward(q):
        def one(i):
            g1_wait(q, i + 1)
            for e in range(1, nd):
                g2(q, e, i + 1).start()

        loop(nb - 1, one)

    def gather_wait(q):
        for e in range(1, nd):
            loop(nb, lambda i: g2_wait(q, e, i))

    def gather_drain(q):
        if q != M_QKV:
            loop(nb - 1, lambda i: g1(q, i + 1).wait_send())
        for e in range(1, nd):
            loop(nb, lambda i: g2(q, e, i).wait_send())

    def in_step(n):
        pl.semaphore_signal(k.sync.at[n], inc=1, device_id=(b, d, xor(1)), device_id_type=MESH)
        pl.semaphore_wait(k.sync.at[n], 1)

    gather_start(M_QKV)

    halves = [pl.ds(0, C // 2), pl.ds(C // 2, C // 2)]

    def x_send(e, c):
        m = later(e)
        dst = k.xb.at[b, halves[c]]
        return rcopy(k.xs.at[m, halves[c]], dst, k.x_ss.at[e, c], k.x_rs.at[b, c], (m * S + s_me, d, h))

    def x_pass(e, f, c):
        src = k.xb.at[home(e), halves[c]]
        return rcopy(src, src, k.xf_ss.at[e, f, c], k.x_rs.at[home(e), c], (m_t * S + mate(f), d, h))

    def x_wait(j, c):
        src = k.xb.at[j, halves[c]]
        rcopy(src, src, k.x_ss.at[0, c], k.x_rs.at[j, c], (b, d, h)).wait_recv()

    loop(nb - 1, lambda i: g1(M_QKV, i + 1).wait_send())
    in_step(0)
    for c in range(2):
        for e in range(1, MB):
            x_send(e, c).start()
    for c in range(2):
        loop(S - 1, lambda f: x_pass(0, f + 1, c).start())

    gather_forward(M_QKV)

    gather_wait(M_QKV)

    for w in range(W):
        slab = k.bufq[w].astype(F32)
        for block in range(z.full):
            k.fall[w * r : w * r + rs, block * 128 : (block + 1) * 128] = slab[block * rs : (block + 1) * rs]
        end = z.full * 128
        for at, row, rows in z.bits:
            rows = rows if len(z.bits) > 1 else rs
            part = slab[z.left : z.left + rows, at : at + 3 * C - end]
            k.fall[w * r + row : w * r + row + rows, end : 3 * C] = part
        per = z.brow - z.vrow
        k.vrows[w * per : (w + 1) * per] = slab[z.vrow : z.brow]
    k.wkv[...] = k.fall[0:C, 0:L].astype(BF16)
    k.wkvt[...] = k.fall[0:C, 0:L].T.astype(BF16)
    k.wq[...] = k.fall[0:C, L : 3 * C].astype(BF16)
    k.wqt[...] = k.fall[0:C, L : 3 * C].T.astype(BF16)
    columns = k.vrows[...].T
    for w in range(W):
        for j in range(8):
            row, at = vec_at(j)
            column = w * (z.brow - z.vrow) + row - z.vrow
            k.vcol[w * r : (w + 1) * r, j : j + 1] = columns[at : at + r, column : column + 1]

    def vec(j):
        return k.vcol[0:C, j : j + 1]

    row16 = lax.broadcasted_iota(jnp.int32, (16, R), 0)
    column = lax.broadcasted_iota(jnp.int32, (16, R), 1)
    step = R // z.per
    token = z.per * (column % step) + column // step
    pad = jnp.zeros((48, R), BF16)
    one_rows = jnp.where(row16 < 2, 1.0, 0.0).astype(BF16)

    def in_doc(j):
        doc = jnp.zeros((16, R), jnp.int32)
        end = jnp.int32(0)
        for n in range(z.ND):
            end = end + k.lens[m_t, 0, n]
            doc = doc + (j * R + token >= end).astype(jnp.int32)
        return row16 == doc

    def head_send(net, i, p):
        buf, ss, rs_ = net
        src, to = (h, xor(p)) if p <= half else (xor(half), xor(p - half))
        return rcopy(buf.at[i, src], buf.at[i, src], ss.at[i, p], rs_.at[i, p], (b, d, to))

    def head_wait(net, i, p):
        buf, ss, rs_ = net
        rcopy(buf.at[i, xor(p)], buf.at[i, xor(p)], ss.at[i, p], rs_.at[i, p], (b, d, h)).wait_recv()

    def head_start(net, i):
        for p in range(half, 0, -1):
            head_send(net, i, p).start()

    def head_pass(net, i):
        head_wait(net, i, half)
        for p in range(half + 1, nh):
            head_send(net, i, p).start()

    def head_end(net, i):
        for p in range(1, nh):
            if p != half:
                head_wait(net, i, p)

    o_net = (k.oall, k.o_ss, k.o_rs)
    p_net = (k.pall, k.p_ss, k.p_rs)

    def kv_block(t, j):
        kv = mm(k.wkvt[...], k.xb[j])
        kb = kv[0:C].astype(BF16)
        vb = (kv[C:L] + vec(V_BV)).astype(BF16)
        barred = jnp.logical_and(row16 < z.ND, jnp.logical_not(in_doc(j)))
        kf = jnp.where(barred, -BIG, 0.0).astype(BF16)
        for a in range(H):
            kh, vh = kb[a * HEAD_DIM : (a + 1) * HEAD_DIM], vb[a * HEAD_DIM : (a + 1) * HEAD_DIM]
            k.kx[t, a] = kh
            k.vx[t, a, 0:HEAD_DIM] = vh
            k.vx[t, a, HEAD_DIM:] = one_rows
            k.kt[t, a] = jnp.concatenate([kh, kf, pad], axis=0).T
            k.vt[t, a] = jnp.concatenate([vh, one_rows, pad], axis=0).T

    def query_block(e):
        xi = k.xb[home(e)]
        k.xq[:, e * R : (e + 1) * R] = xi
        qi = ((mm(k.wqt[...], xi) + vec(V_BQ)).astype(BF16).astype(F32) * HEAD_DIM**-0.5).astype(BF16)
        hot = jnp.where(in_doc(home(e)), 1.0, 0.0).astype(BF16)
        for a in range(H):
            k.qx[e, a] = jnp.concatenate([qi[a * HEAD_DIM : (a + 1) * HEAD_DIM], hot, pad], axis=0)

    def scores(e, a, t):
        return mm(k.kt[t, a], k.qx[e, a])

    def prob(e, a, t):
        if z.keep:
            return k.pbuf[t, e, a]
        return jnp.exp(scores(e, a, t) - k.tops[e, a, pl.ds(t, 1)]).astype(BF16)

    def attend(pairs):
        units = [(e, a, t) for e, t in pairs for a in range(H)]
        s = [scores(*u) for u in units]
        top = [jnp.max(x, axis=0, keepdims=True) for x in s]
        p = [jnp.exp(x - y).astype(BF16) for x, y in zip(s, top)]
        o = [mm(k.vx[t, a], x) for (e, a, t), x in zip(units, p)]
        for i, (e, a, t) in enumerate(units):
            if z.keep:
                k.pbuf[t, e, a] = p[i]
            k.tops[e, a, pl.ds(t, 1)] = top[i]
        for i, (e, a, t) in enumerate(units):
            if isinstance(t, int) and t == 0:
                k.top[e, a, 0:1] = top[i]
                k.osum[e, a] = o[i]
            else:
                old = k.top[e, a, 0:1]
                new = jnp.maximum(old, top[i])
                k.top[e, a, 0:1] = new
                k.osum[e, a] = k.osum[e, a] * jnp.exp(old - new) + o[i] * jnp.exp(top[i] - new)

    def factor(e, a, t):
        return jnp.exp(k.tops[e, a, pl.ds(t, 1)] - k.top[e, a, 0:1]) * k.top[e, a, 1:2]

    for c in range(2):
        for e in range(1, MB):
            x_wait(home(e), c)
            loop(S - 1, lambda f: x_pass(e, f + 1, c).start())
    gather_start(M_OUT)
    gather_start(M_UP)
    for e in range(MB):
        kv_block(e, home(e))
        query_block(e)
    for t in range(MB):
        attend([(e, t) for e in range(MB)])

    def attend_other(n):
        for c in range(2):
            x_wait(other(n), c)
        kv_block(MB + n, other(n))
        attend([(e, MB + n) for e in range(MB)])

    def heads_done(e):
        for a in range(H):
            o = k.osum[e, a]
            inv = 1.0 / o[HEAD_DIM : HEAD_DIM + 1]
            k.top[e, a, 1:2] = inv
            k.oall[e, h, a * HEAD_DIM : (a + 1) * HEAD_DIM] = (o[0:HEAD_DIM] * inv).astype(BF16)
        head_start(o_net, e)

    last = nb - MB - 1
    loop(last, attend_other)
    for c in range(2):
        x_wait(other(last), c)
    gather_start(M_DOWN)
    kv_block(MB + last, other(last))
    for e in range(MB):
        attend([(e, MB + last)])
        heads_done(e)

    gather_forward(M_OUT)
    gather_forward(M_UP)
    for e in range(MB):
        head_pass(o_net, e)
    gather_wait(M_OUT)

    per = W // nh

    def w_send(p):
        src = k.buf.at[M_OUT, pl.ds(xor(p) * per, per)]
        return rcopy(src, k.wob.at[h], k.w_ss.at[p], k.w_rs.at[p], (b, d, xor(p)))

    for p in range(1, nh):
        w_send(p).start()

    def spread(dst, slab, row):
        slab = slab.astype(F32)
        dst[row : row + z.r2] = slab[0 : z.r2, 0:C]
        dst[row + 2 * r : row + 2 * r + z.r2] = slab[0 : z.r2, C:L]

    for w in range(W):
        spread(k.fod, k.buf[M_OUT, w], 4 * r * w)
    k.wot[...] = k.fod[0:F].T.astype(BF16)

    gather_forward(M_DOWN)

    def c_send(e):
        m = later(e)
        slot = lax.rem(m_t + MB - m, MB)
        return rcopy(k.cs.at[m], k.cb.at[slot], k.c_ss.at[e], k.c_rs.at[slot], (m * S + s_me, d, h))

    for e in range(1, MB):
        c_send(e).start()

    lane_rows = R // 128

    def st_send(e, i, p):
        own = k.stats.at[e, i, h]
        return rcopy(own, own, k.st_ss.at[e, i, p], k.st_rs.at[e, i, p], (b, d, xor(p)))

    def reduce_start(e, i, rows):
        for j, v in enumerate(rows):
            row = jnp.sum(v, axis=0, keepdims=True)
            for c in range(lane_rows):
                k.stats[e, i, h, pl.ds(j * lane_rows + c, 1)] = row[:, c * 128 : (c + 1) * 128]
        if len(rows) * lane_rows < 8:
            rest = 8 - len(rows) * lane_rows
            k.stats[e, i, h, pl.ds(8 - rest, rest)] = jnp.zeros((rest, 128), F32)
        for p in range(nh - 1, 0, -1):
            st_send(e, i, p).start()

    def reduce_end(e, i, n):
        for p in range(1, nh):
            src = k.stats.at[e, i, xor(p)]
            rcopy(src, src, k.st_ss.at[e, i, p], k.st_rs.at[e, i, p], (b, d, h)).wait_recv()
        total = k.stats[e, i, 0]
        for j in range(1, nh):
            total = total + k.stats[e, i, j]
        total = total / D
        return [
            jnp.concatenate([total[j * lane_rows + c :][0:1] for c in range(lane_rows)], axis=1)
            for j in range(n)
        ]

    def cols(ref, i):
        return ref[:, i * R : (i + 1) * R]

    for i in range(MB):
        head_end(o_net, i)
        h1 = cols(k.xq, i).astype(F32) + mm(k.wot[...], k.oall[i].reshape(D, R)) + vec(V_BO)
        k.n1[i] = h1
        reduce_start(0, i, (h1, h1 * h1))

    gather_wait(M_UP)
    for w in range(W):
        slab = k.buf[M_UP, w].astype(F32)
        k.fup[w * r : w * r + rs, 0:L] = slab[0:rs]
        k.fup[w * r : w * r + rs, L:F] = slab[rs : 2 * rs]
    k.fup[C : C + 16] = jnp.zeros((16, F), F32)
    for w in range(W):
        row = k.bufq[w].astype(F32)[z.brow : z.brow + 1, 0 : 4 * r]
        k.fup[C : C + 1, 4 * r * w : 4 * r * (w + 1)] = row
    k.wup[...] = k.fup[0:C].astype(BF16)
    k.wupt[...] = k.fup[...].T.astype(BF16)
    gather_wait(M_DOWN)
    for w in range(W):
        spread(k.fod, k.buf[M_DOWN, w], 4 * r * w)
    k.wdn[...] = k.fod[0:F].astype(BF16)
    k.wdnt[...] = k.fod[0:F].T.astype(BF16)

    first_one = jnp.where(row16 < 1, 1.0, 0.0).astype(BF16)
    r1 = [None] * MB
    gdn = [None] * MB
    for i in range(MB):
        mean, square = reduce_end(0, i, 2)
        r1[i] = lax.rsqrt(square - mean * mean + EPS)
        n1 = (k.n1[i] - mean) * r1[i]
        k.n1[i] = n1
        y1 = n1 * vec(V_G1) + vec(V_S1)
        k.y1[i] = y1
        y1b = y1.astype(BF16)
        k.y1b[:, i * R : (i + 1) * R] = y1b
        u = mm(k.wupt[...], jnp.concatenate([y1b, first_one], axis=0))
        cdf = 0.5 * (1.0 + lax.erf(u * (0.5**0.5)))
        act = (u * cdf).astype(BF16)
        k.act[:, i * R : (i + 1) * R] = act
        h2 = y1 + mm(k.wdnt[...], act) + vec(V_BD)
        k.h2[i] = h2

        if i > 0:
            rcopy(k.cb.at[i], k.cb.at[i], k.c_ss.at[0], k.c_rs.at[i], (b, d, h)).wait_recv()
        dn2 = k.cb[i].astype(F32) * vec(V_G2)
        reduce_start(1, i, (h2, h2 * h2, dn2, dn2 * h2))
        k.up[i], k.gel[i] = u, cdf
    for i in range(MB):
        u = k.up[i]
        k.gel[i] += u * jnp.exp(-0.5 * u * u) * ((2 * jnp.pi) ** -0.5)
    k.vg[...] = jnp.zeros_like(k.vg)
    ones = jnp.ones((16, R), BF16)

    def vec_grad(j, x):
        k.vg[j : j + 1] += mm_nt(ones, x)[0:1]

    def mo_send(i):
        return rcopy(k.mo.at[i], k.o_mo.at[m_t], k.mo_ss.at[i], k.mo_rs.at[m_t], (home(i), d, h))

    for i in range(MB):
        mean, square, dmean, dsquare = reduce_end(1, i, 4)
        r2 = lax.rsqrt(square - mean * mean + EPS)
        g = k.cb[i].astype(F32)
        dn2 = g * vec(V_G2)
        n2 = (k.h2[i] - mean) * r2
        dh2 = r2 * (dn2 - dmean - n2 * (r2 * (dsquare - mean * dmean)))
        dz = dh2.astype(BF16)
        k.dz[:, i * R : (i + 1) * R] = dz
        du = (mm(k.wdn[...], dz) * k.gel[i]).astype(BF16)
        k.du[:, i * R : (i + 1) * R] = du
        dy1 = dh2 + mm(k.wup[...], du)
        dn1 = dy1 * vec(V_G1)
        k.dh1[i] = dn1
        n1 = k.n1[i]
        reduce_start(2, i, (dn1, dn1 * n1))
        out = (n2 * vec(V_G2) + vec(V_S2)).astype(BF16)
        if i > 0:
            k.mo[i] = out
            mo_send(i).start()
        else:
            k.o_mo[m_t] = out
        k.vin[0, i] = (g * n2).astype(BF16)
        k.vin[1, i] = (dy1 * n1).astype(BF16)
        k.vin[2, i] = dy1.astype(BF16)

    def sums(q):
        if q == M_QKV:
            return k.pkq, k.got1q, k.sent2q, k.got2q, k.o_Q
        return k.pk.at[q], k.got1.at[q], k.sent2.at[q], k.got2.at[q], k.o_G.at[q]

    def s1_send(q, e, i):
        dt = lax.rem(d + e, nd)
        return rcopy(
            sums(q)[0].at[i * nd + dt], sums(q)[1].at[e - 1, i], k.s1_ss.at[q, e - 1, i], k.s1_rs.at[q, e - 1, i],
            (b, dt, h),
        )

    def s2_send(q, i):
        bt = lax.rem(b + i, nb)
        return rcopy(sums(q)[2].at[bt], sums(q)[3].at[b], k.s2_ss.at[q, i], k.s2_rs.at[q, i], (bt, d, h))

    def scatter_start(q):
        for e in range(1, nd):
            loop(nb, lambda i: s1_send(q, e, i).start())

    def scatter_sum(q, bt):
        part = sums(q)[0][bt * nd + d].astype(F32)
        for e in range(1, nd):
            src = sums(q)[1].at[e - 1, bt]
            rcopy(src, src, k.s1_ss.at[q, e - 1, bt], k.s1_rs.at[q, e - 1, bt], (b, d, h)).wait_recv()
            part = part + src[...].astype(F32)
        return part

    def scatter_forward(q):
        def one(i):
            bt = lax.rem(b + i + 1, nb)
            sums(q)[2][bt] = scatter_sum(q, bt).astype(BF16)
            s2_send(q, i + 1).start()

        loop(nb - 1, one)
        sums(q)[4][...] = scatter_sum(q, b)

    def scatter_end(q):
        def one(i):
            src = sums(q)[3].at[lax.rem(b + nb - i - 1, nb)]
            rcopy(src, src, k.s2_ss.at[q, i + 1], k.s2_rs.at[q, i + 1], (b, d, h)).wait_recv()
            sums(q)[4][...] += src[...].astype(F32)

        loop(nb - 1, one)
        loop(nb - 1, lambda i: s2_send(q, i + 1).wait_send())
        for e in range(1, nd):
            loop(nb, lambda i: s1_send(q, e, i).wait_send())

    def rows_of(parts):
        rows = jnp.concatenate(parts, axis=0)
        if rows.shape[0] < rA:
            rows = jnp.concatenate([rows, jnp.zeros((rA - rows.shape[0], L), F32)], axis=0)
        return rows.astype(BF16)

    def pack_halves(q, g):
        for w in range(W):
            at = 4 * r * w
            pair = jnp.concatenate([g[at : at + z.r2], g[at + 2 * r : at + 2 * r + z.r2]], axis=1)
            k.pk[q, w] = rows_of([pair])
        scatter_start(q)

    k.gdn[0:F] = mm_nt(k.act[...], k.dz[...])
    pack_halves(M_DOWN, k.gdn)
    k.gup[0:C] = mm_nt(k.y1b[...], k.du[...])
    for w in range(W):
        k.pk[M_UP, w] = rows_of([k.gup[w * r : w * r + rs, 0:L], k.gup[w * r : w * r + rs, L:F]])
    scatter_start(M_UP)
    for i in range(MB):
        for j, x in ((V_G2, k.vin[0, i]), (V_G1, k.vin[1, i]), (V_S1, k.vin[2, i]), (V_S2, k.cb[i])):
            vec_grad(j, x)
        vec_grad(V_BD, cols(k.dz, i))

    for i in range(MB):
        dmean, dsquare = reduce_end(2, i, 2)
        dh1 = r1[i] * (k.dh1[i] - dmean - k.n1[i] * dsquare)
        k.dh1[i] = dh1
        dp = dh1.astype(BF16)
        k.pall[i, h] = dp
        head_start(p_net, i)

    g = None
    for i in range(MB):
        dp = k.pall[i, h]
        part = mm_nt(k.oall[i].reshape(D, R), dp)
        g = part if g is None else g + part
        vec_grad(V_BO, dp)
    k.gout[0:F] = g
    pack_halves(M_OUT, k.gout)
    ug = mm_nt(jnp.ones((16, z.Q), BF16), k.du[...])
    k.gst[...] = jnp.zeros_like(k.gst)
    for w in range(W):
        k.gst[w, z.brow : z.brow + 1, 0 : 4 * r] = ug[0:1, 4 * r * w : 4 * r * (w + 1)]

    def pack_vec(j):
        row, at = vec_at(j)
        for w in range(W):
            k.gst[w, row : row + 1, at : at + r] = k.vg[j : j + 1, w * r : (w + 1) * r]

    for j in (V_BO, V_G1, V_S1, V_BD, V_G2, V_S2):
        pack_vec(j)
    k.gall[...] = jnp.zeros_like(k.gall)

    for p in range(1, nh):
        src = k.wob.at[xor(p)]
        rcopy(src, src, k.w_ss.at[p], k.w_rs.at[p], (b, d, h)).wait_recv()
    k.wob[h] = k.buf[M_OUT, pl.ds(h * per, per)]
    for j in range(nh):
        for n in range(per):
            spread(k.fod, k.wob[j, n], j * C + 4 * r * n)
    for j in range(nh):
        k.wor[:, j * C : (j + 1) * C] = k.fod[j * C : (j + 1) * C].astype(BF16)

    scatter_forward(M_DOWN)
    head_pass(p_net, 0)
    for i in range(1, MB):
        head_pass(p_net, i)

    def grad_in(e):
        head_end(p_net, e)
        do = mm(k.wor[...], k.pall[e].reshape(D, R)).astype(BF16).astype(F32)
        for a in range(H):
            part = do[a * HEAD_DIM : (a + 1) * HEAD_DIM]
            own = k.oall[e, h, a * HEAD_DIM : (a + 1) * HEAD_DIM].astype(F32)
            k.part[e, a] = part
            k.delta[e, a, 0:1] = jnp.sum(part * own, axis=0, keepdims=True)
            k.dqacc[e, a] = jnp.zeros((HEAD_DIM, R), F32)

    def scaled(e, a, t):
        f = factor(e, a, t)
        delta = k.delta[e, a, 0:1] * f
        hi = delta.astype(BF16).astype(F32)
        rest = jnp.where(row16 == 0, -hi, jnp.where(row16 == 1, hi - delta, 0.0))
        return jnp.concatenate([(k.part[e, a] * f).astype(BF16), rest.astype(BF16), pad], axis=0)

    def back(slots, queries):
        units = [(e, a, t) for t in slots for a in range(H) for e in queries]
        dox = [scaled(*u) for u in units]
        p = [prob(*u) for u in units]
        dp = [mm(k.vt[t, a], x) for (e, a, t), x in zip(units, dox)]
        ds = [(x.astype(F32) * y).astype(BF16) for x, y in zip(p, dp)]
        dq = [mm(k.kx[t, a], x) for (e, a, t), x in zip(units, ds)]
        dk = [mm_nt(k.qx[e, a, 0:HEAD_DIM], x) for (e, a, t), x in zip(units, ds)]
        dv = [mm_nt(x[0:HEAD_DIM], y) for x, y in zip(dox, p)]
        for e in queries:
            for a in range(H):
                mine = [x for (e2, a2, t), x in zip(units, dq) if (e2, a2) == (e, a)]
                k.dqacc[e, a] += sum(mine[1:], mine[0])
        found = []
        per_slot = H * len(queries)
        for n in range(len(slots)):
            rows = []
            for x in (dk, dv):
                for a in range(H):
                    at = n * per_slot + a * len(queries)
                    rows.append(sum(x[at + 1 : at + len(queries)], x[at]))
            found.append(jnp.concatenate(rows, axis=0))
        return found

    def tokens_part(j, dkv):
        k.gall[0:C, 0:L] += mm_nt(k.xb[j], dkv)
        vec_grad(V_BV, dkv[C:L])
        return mm(k.wkv[...], dkv)

    def tp_send(n):
        dst = k.tgr.at[n % MB, s_me]
        to = lax.rem(s_me + 1 + n // MB, S)
        return rcopy(k.tgs.at[n], dst, k.tp_ss.at[n], k.tp_rs.at[n % MB, s_me], (m_t * S + to, d, h))

    def send_part(n, dkv):
        k.tgs[n] = tokens_part(other(n), dkv.astype(BF16)).astype(BF16)
        if not z.keep or n % MB:
            tp_send(n).start()

    others = list(range(nb - MB - 1, -1, -1))
    for e in range(MB):
        grad_in(e)
        if z.keep:
            found = back([MB + n for n in others], [e])
            for n, dkv in zip(others, found):
                if e > 0:
                    dkv = dkv + k.dkacc[n]
                if e < MB - 1:
                    k.dkacc[n] = dkv
                else:
                    send_part(n, dkv)
        if e == 0:
            scatter_forward(M_UP)
    if not z.keep:
        loop(nb - MB, lambda n: send_part(n, back([MB + n], range(MB))[0]))

    for e in range(MB - 1, -1, -1):
        dkv = back([e], range(MB))[0]
        k.tgo[e] = tokens_part(home(e), dkv.astype(BF16))
        if e == MB - 1:
            scatter_forward(M_OUT)

    for i in range(MB):
        for a in range(H):
            rows = slice(a * HEAD_DIM, (a + 1) * HEAD_DIM)
            k.dq[rows, i * R : (i + 1) * R] = (k.dqacc[i, a] * HEAD_DIM**-0.5).astype(BF16)
        vec_grad(V_BQ, cols(k.dq, i))
    k.gall[0:C, L : 3 * C] = mm_nt(k.xq[...], k.dq[...])
    pack_vec(V_BQ)
    pack_vec(V_BV)

    for w in range(W):
        for n in range(3):

            def put(row, at, rows, row2, column, size):
                src = k.gall[w * r + row2 : w * r + row2 + rows, n * C + column : n * C + column + size]
                k.gst[w, row : row + rows, at : at + size] = src

            place(n, put)
        k.pkq[w] = k.gst[w].astype(BF16)
    scatter_start(M_QKV)

    def t_send(e):
        return rcopy(k.tgx.at[e], k.o_tg.at[m_t], k.t_ss.at[e], k.t_rs.at[m_t], (home(e), d, h))

    def tokens_total(e):
        k.tgo[e] += k.dh1[e] + mm(k.wq[...], cols(k.dq, e))

        def add(f):
            src = k.tgr.at[e, mate(f + 1)]
            rcopy(src, src, k.tp_ss.at[0], k.tp_rs.at[e, mate(f + 1)], (b, d, h)).wait_recv()
            k.tgo[e] += src[...].astype(F32)

        loop(S - 1, add)
        return k.tgo[e].astype(BF16)

    for e in range(1, MB):
        k.tgx[e] = tokens_total(e)
        t_send(e).start()
    if z.keep:
        for n in range(0, nb - MB, MB):
            tp_send(n).start()

    scatter_forward(M_QKV)

    k.o_tg[m_t] = tokens_total(0)
    for q in (M_DOWN, M_UP, M_OUT):
        scatter_end(q)
    for q in range(4):
        gather_drain(q)
    for p in range(1, nh):
        w_send(p).wait_send()
        for i in range(MB):
            head_send(o_net, i, p).wait_send()
            head_send(p_net, i, p).wait_send()
            for e in range(3):
                st_send(e, i, p).wait_send()
    for e in range(MB):
        for c in range(2):
            loop(S - 1, lambda f: x_pass(e, f + 1, c).wait_send())
    loop(nb - MB, lambda n: tp_send(n).wait_send())
    for e in range(1, MB):
        m = later(e)
        rcopy(k.o_mo.at[m], k.o_mo.at[m], k.mo_ss.at[e], k.mo_rs.at[m], (b, d, h)).wait_recv()
        for send in (c_send, mo_send):
            send(e).wait_send()
        for c in range(2):
            x_send(e, c).wait_send()

    for e in range(1, MB):
        m = later(e)
        rcopy(k.o_tg.at[m], k.o_tg.at[m], k.t_ss.at[e], k.t_rs.at[m], (b, d, h)).wait_recv()
        t_send(e).wait_send()
    scatter_end(M_QKV)


def finish_kernel(z, mo, tg, G, GQ, *outs):
    (mixed, dtok, dwq, dbq, dwk, dwv, dbv, dwo, dbo, dg1, ds1, dwup, dbu, dwdn, dbd, dg2, ds2, both) = outs
    r, rs, C, L = z.r, z.rs, z.C, z.L
    for m in range(z.MB):


        def put_mixed(i, rows):
            both[pl.ds(i, z.R // z.per, stride=z.span), m] = rows

        def put_grad(i, rows):
            dtok[m, pl.ds(i, z.R // z.per, stride=z.span)] = rows

        put_rows(z, mo[m].astype(F32), put_mixed)
        put_rows(z, tg[m].astype(F32), put_grad)
    mixed[...] = both[...].astype(BF16)
    for n, ref in enumerate((dwk, dwv, dwq)):
        column = 0
        for block, at, size in pieces(C, n):
            if block < z.full:
                ref[0, :, column : column + size] = GQ[block * rs : block * rs + r, at : at + size]
            else:
                for where, row, rows in z.bits:
                    part = GQ[z.left : z.left + rows, at + where : at + where + size]
                    ref[0, row : row + rows, column : column + size] = part
            column += size
    dwup[0, :, 0:L] = G[M_UP, 0:r]
    dwup[0, :, L : 2 * L] = G[M_UP, rs : rs + r]
    for q, ref in ((M_OUT, dwo), (M_DOWN, dwdn.at[0])):
        ref[0 : 2 * r] = G[q, 0 : 2 * r, 0:C]
        ref[2 * r : 4 * r] = G[q, 0 : 2 * r, C:L]
    for j, ref in enumerate((dbq, dbv, dbo, dg1, ds1, dbd, dg2, ds2)):
        row, at = z.vrow + j // z.vper, j % z.vper * r
        ref[...] = GQ[row : row + 1, at : at + r]
    dbu[...] = GQ[z.brow : z.brow + 1, 0 : 4 * r]


def solution(mesh):
    vec_spec = P("head", ("blk", "dp"))
    mat_spec = P("head", ("blk", "dp"), None)
    tok_spec = P(None, "dp", "head", "blk")
    out_spec = P(("blk", "dp"), "head")

    def body(
        tokens, doc_lengths, cotangent, query_weight, query_bias, key_weight, value_weight, value_bias,
        out_weight, out_bias, first_gain, first_shift, up_weight, up_bias, down_weight, down_bias,
        second_gain, second_shift,
    ):
        z = Sizes(mesh, tokens, query_weight, up_weight, doc_lengths)

        def as_rows(a):
            return a.reshape(z.MB, z.N, 128).transpose(1, 0, 2)

        operands = (
            as_rows(tokens), as_rows(cotangent), query_weight, query_bias, key_weight, value_weight, value_bias,
            out_weight, out_bias, first_gain, first_shift, up_weight, up_bias, down_weight, down_bias, second_gain,
            second_shift,
        )
        scratch = main_scratch(z, operands)
        vmem = pl.BlockSpec(memory_space=pltpu.VMEM)
        smem = pl.BlockSpec(memory_space=pltpu.SMEM)
        hbm = pl.BlockSpec(memory_space=pltpu.HBM)
        names = INPUTS + OUTPUTS + list(scratch)
        sds = jax.ShapeDtypeStruct
        parts = pl.pallas_call(
            lambda *refs: main_kernel(z, names, *refs),
            out_shape=[
                sds((z.MB, z.C, z.R), BF16),
                sds((z.MB, z.C, z.R), BF16),
                sds((3, z.rA, z.L), F32),
                sds((z.rQ, 128), F32),
            ],
            in_specs=[smem] + [hbm] * len(operands),
            out_specs=[vmem] * len(OUTPUTS),
            scratch_shapes=list(scratch.values()),
            compiler_params=pltpu.CompilerParams(
                collective_id=0, has_side_effects=True, vmem_limit_bytes=63 << 20
            ),
            name="layer",
        )(doc_lengths, *operands)
        mat, vec = sds((1, z.r, z.C), F32), sds((1, z.r), F32)
        outs = pl.pallas_call(
            lambda *refs: finish_kernel(z, *refs),
            out_shape=[
                sds((z.N, z.MB, 128), BF16), sds((z.MB, z.N, 128), F32), mat, vec, mat, mat, vec,
                sds((4 * z.r, z.C), F32), vec, vec, vec, sds((1, z.r, z.F), F32), sds((1, 4 * z.r), F32),
                sds((1, 4 * z.r, z.C), F32), vec, vec, vec,
            ],
            in_specs=[vmem] * len(OUTPUTS),
            out_specs=[vmem] * 17,
            scratch_shapes=[pltpu.VMEM((z.N, z.MB, 128), F32)],
            name="finish",
        )(*parts)
        shape = tokens.shape
        return (outs[0].transpose(1, 0, 2).reshape(shape), outs[1].reshape(shape), *outs[2:])

    return jax.shard_map(
        body,
        mesh=mesh,
        in_specs=(
            tok_spec, P(None, "dp", None), tok_spec, mat_spec, vec_spec, mat_spec, mat_spec, vec_spec,
            out_spec, vec_spec, vec_spec, vec_spec, mat_spec, vec_spec, mat_spec, vec_spec, vec_spec, vec_spec,
        ),
        out_specs=(
            tok_spec, tok_spec, mat_spec, vec_spec, mat_spec, mat_spec, vec_spec, out_spec, vec_spec, vec_spec,
            vec_spec, mat_spec, vec_spec, mat_spec, vec_spec, vec_spec, vec_spec,
        ),
        check_vma=False,
    )
```

```python
import math
import types

import jax
import jax.numpy as jnp
from jax import lax
from jax.experimental import pallas as pl
from jax.experimental.pallas import tpu as pltpu
from jax.sharding import PartitionSpec as P

HEAD_DIM = 64
EPS = 1e-05
BIG = 1e30
MESH = pl.DeviceIdType.MESH
F32 = jnp.float32
BF16 = jnp.bfloat16
V_BQ, V_BV, V_BO, V_G1, V_S1, V_BD, V_G2, V_S2 = range(8)
M_OUT, M_UP, M_DOWN, M_QKV = range(4)


def up_to(n, m):
    return (n + m - 1) // m * m


def mm(a, b):
    return lax.dot_general(a, b, (((1,), (0,)), ((), ())), preferred_element_type=F32)


def mm_nt(a, b):
    return lax.dot_general(a, b, (((1,), (1,)), ((), ())), preferred_element_type=F32)


def loop(n, fn):
    if n <= 8:
        for i in range(n):
            fn(i)
    else:
        lax.fori_loop(0, n, lambda i, c: (fn(i), c)[1], 0)


def rcopy(src, dst, ss, rs, dev):
    return pltpu.make_async_remote_copy(
        src_ref=src, dst_ref=dst, send_sem=ss, recv_sem=rs, device_id=dev, device_id_type=MESH
    )


def pieces(c, u):
    at, end = u * c, (u + 1) * c
    found = []
    while at < end:
        size = min(128 - at % 128, end - at)
        found.append((at // 128, at % 128, size))
        at += size
    return found


def columns_of(z, flat):
    rows = [flat[pl.ds(i, z.R // z.per, stride=z.span)].T for i in range(z.span)]
    tokens = []
    for u in range(z.per):
        tokens.append(jnp.concatenate([rows[i][at : at + n] for i, at, n in pieces(z.C, u)], axis=0))
    return jnp.concatenate(tokens, axis=1)


def put_rows(z, value, put):
    n = z.R // z.per
    parts = [[] for _ in range(z.span)]
    for u in range(z.per):
        c = 0
        for i, _, size in pieces(z.C, u):
            parts[i].append(value[c : c + size, u * n : (u + 1) * n])
            c += size
    for i in range(z.span):
        put(i, jnp.concatenate(parts[i], axis=0).T)


class Sizes:
    def __init__(self, mesh, tokens, query_weight, up_weight, doc_lengths):
        self.nb, self.nd, self.nh = mesh.shape["blk"], mesh.shape["dp"], mesh.shape["head"]
        self.W = self.nb * self.nd
        self.C, self.F = query_weight.shape[2], up_weight.shape[2]
        self.MB = tokens.shape[0]
        self.R = tokens.shape[3] // self.C
        self.S = self.nb // self.MB
        self.Q = self.MB * self.R
        self.N = self.R * self.C // 128
        self.per = 128 // math.gcd(self.C, 128)
        self.span = self.per * self.C // 128
        self.H = self.C // HEAD_DIM
        self.ND = doc_lengths.shape[2]
        self.r = query_weight.shape[1]
        self.rs = up_to(self.r, 8)
        self.r2 = up_to(2 * self.r, 8)
        self.rA = up_to(2 * self.rs, 16)
        self.L = 2 * self.C
        self.full, left = divmod(3 * self.C, 128)
        self.left = self.full * self.rs
        fold = left == 64 and self.r % 2 == 0
        self.bits = [(0, 0, self.r // 2), (64, self.r // 2, self.r // 2)] if fold else [(0, 0, self.r)]
        self.vrow = self.left + up_to(self.bits[0][2], 4)
        self.vper = min(8, 128 // self.r)
        self.brow = self.vrow + -(-8 // self.vper)
        self.rQ = up_to(max(self.brow + 1, self.left + self.rs), 16)
        self.keep = self.nb * self.R * self.Q * self.H * 2 <= (8 << 20)
        assert self.F == 4 * self.C and self.F == self.nh * self.C and self.W % self.nh == 0


INPUTS = [
    "lens", "tok", "cot", "wq_in", "bq", "wk_in", "wv_in", "bv", "wo_in", "bo", "g1", "s1", "wup_in", "bu",
    "wdn_in", "bd", "g2", "s2",
]
OUTPUTS = ["o_mo", "o_tg", "o_G", "o_Q"]


def main_scratch(z, inputs):
    dma = pltpu.SemaphoreType.DMA
    v = pltpu.VMEM
    nb, W, L, R, C, F, Q, H, MB, rA, nh = z.nb, z.W, z.L, z.R, z.C, z.F, z.Q, z.H, z.MB, z.rA, z.nh
    dd = max(z.nd - 1, 1)
    return dict(
        in_sem=dma((len(INPUTS) - 1,)),
        flat=v((2 * MB, z.N, 128), F32),
        xs=v((MB, C, R), BF16),
        xb=v((nb, C, R), BF16),
        cs=v((MB, C, R), BF16),
        cb=v((MB, C, R), BF16),
        bufq=v((W, z.rQ, 128), BF16),
        buf=v((3, W, rA, L), BF16),
        wob=v((nh, W // nh, rA, L), BF16),
        fst=v((rA, L), F32),
        fsq=v((z.rQ, 128), F32),
        fall=v((C + 8, up_to(3 * C, 128)), F32),
        vrows=v((up_to(W * (z.brow - z.vrow), 8), 128), F32),
        vcol=v((C + 8, 8), F32),
        fup=v((C + 16, F), F32),
        fod=v((F + 16, C), F32),
        wkv=v((C, L), BF16),
        wkvt=v((L, C), BF16),
        wq=v((C, C), BF16),
        wqt=v((C, C), BF16),
        wup=v((C, F), BF16),
        wupt=v((F, C + 16), BF16),
        wor=v((C, F), BF16),
        wot=v((C, F), BF16),
        wdn=v((F, C), BF16),
        wdnt=v((C, F), BF16),
        xq=v((C, Q), BF16),
        qx=v((MB, H, 128, R), BF16),
        kx=v((nb, H, HEAD_DIM, R), BF16),
        vx=v((nb, H, HEAD_DIM + 16, R), BF16),
        kt=v((nb, H, R, 128), BF16),
        vt=v((nb, H, R, 128), BF16),
        pbuf=v((nb, MB, H, R, R) if z.keep else (1, 1, 1, 16, 128), BF16),
        tops=v((MB, H, up_to(nb, 8), R), F32),
        top=v((MB, H, 8, R), F32),
        osum=v((MB, H, HEAD_DIM + 16, R), F32),
        oall=v((MB, nh, C, R), BF16),
        pall=v((MB, nh, C, R), BF16),
        stats=v((3, MB, nh, 8, 128), F32),
        n1=v((MB, C, R), F32),
        y1=v((MB, C, R), F32),
        h2=v((MB, C, R), F32),
        gel=v((MB, F, R), F32),
        up=v((MB, F, R), F32),
        dh1=v((MB, C, R), F32),
        y1b=v((C, Q), BF16),
        act=v((F, Q), BF16),
        dz=v((C, Q), BF16),
        du=v((F, Q), BF16),
        vin=v((3, MB, C, R), BF16),
        mo=v((MB, C, R), BF16),
        part=v((MB, H, HEAD_DIM, R), F32),
        delta=v((MB, H, 8, R), F32),
        dqacc=v((MB, H, HEAD_DIM, R), F32),
        dkacc=v((nb - MB if z.keep else 1, L, R), F32),
        dq=v((C, Q), BF16),
        tgs=v((nb, C, R), BF16),
        tgo=v((MB, C, R), F32),
        tgr=v((MB, z.S, C, R), BF16),
        tgx=v((MB, C, R), BF16),
        gall=v((C + 8, up_to(3 * C, 128)), F32),
        gst=v((W, z.rQ, 128), F32),
        gup=v((C + 8, F), F32),
        gout=v((F + 16, C), F32),
        gdn=v((F + 16, C), F32),
        vg=v((8, C), F32),
        pk=v((3, W, rA, L), BF16),
        got1=v((3, dd, nb, rA, L), BF16),
        sent2=v((3, nb, rA, L), BF16),
        got2=v((3, nb, rA, L), BF16),
        pkq=v((W, z.rQ, 128), BF16),
        got1q=v((dd, nb, z.rQ, 128), BF16),
        sent2q=v((nb, z.rQ, 128), BF16),
        got2q=v((nb, z.rQ, 128), BF16),
        sync=pltpu.SemaphoreType.REGULAR((2,)),
        x_ss=dma((MB, 2)),
        xf_ss=dma((MB, z.S, 2)),
        x_rs=dma((nb, 2)),
        c_ss=dma((MB,)),
        c_rs=dma((MB,)),
        g1_ss=dma((4, nb)),
        g1_rs=dma((4, nb)),
        g2_ss=dma((4, dd, nb)),
        g2_rs=dma((4, dd, nb)),
        o_ss=dma((MB, nh)),
        o_rs=dma((MB, nh)),
        p_ss=dma((MB, nh)),
        p_rs=dma((MB, nh)),
        w_ss=dma((nh,)),
        w_rs=dma((nh,)),
        st_ss=dma((3, MB, nh)),
        st_rs=dma((3, MB, nh)),
        mo_ss=dma((MB,)),
        mo_rs=dma((MB,)),
        tp_ss=dma((nb,)),
        tp_rs=dma((MB, z.S)),
        t_ss=dma((MB,)),
        t_rs=dma((MB,)),
        s1_ss=dma((4, dd, nb)),
        s1_rs=dma((4, dd, nb)),
        s2_ss=dma((4, nb)),
        s2_rs=dma((4, nb)),
        **{"v_" + name: v(a.shape, a.dtype) for name, a in zip(INPUTS[1:], inputs)},
    )


def main_kernel(z, names, *refs):
    k = types.SimpleNamespace(**dict(zip(names, refs)))
    nb, nd, nh, W, MB, R, C, F, H, L, S, r, rs, rA = (
        z.nb, z.nd, z.nh, z.W, z.MB, z.R, z.C, z.F, z.H, z.L, z.S, z.r, z.rs, z.rA,
    )
    b, d, h = lax.axis_index("blk"), lax.axis_index("dp"), lax.axis_index("head")
    w_me = b * nd + d
    m_t, s_me = b // S, b % S
    D = nh * C
    half = nh // 2

    def xor(i):
        return lax.bitwise_xor(h, i)

    def later(e):
        return lax.rem(m_t + e, MB)

    def home(e):
        return later(e) * S + s_me

    def mate(e):
        return lax.rem(s_me + e, S)

    def other(n):
        return lax.rem(s_me + 1 + n // MB, S) + lax.rem(m_t + n, MB) * S

    copies = {
        name: pltpu.make_async_copy(getattr(k, name), getattr(k, "v_" + name), k.in_sem.at[n])
        for n, name in enumerate(INPUTS[1:])
    }
    rest = ["wo_in", "wdn_in", "wup_in", "cot"]
    first = [name for name in INPUTS[1:] if name not in rest and name != "tok"]
    for name in first + ["tok"] + rest:
        copies[name].start()

    bar = pltpu.get_barrier_semaphore()
    peers = [(lax.rem(b + i, nb), d, h) for i in range(1, nb)]
    peers += [(b, lax.rem(d + i, nd), h) for i in range(1, nd)]
    peers += [(b, d, xor(i)) for i in range(1, nh)]
    for peer in peers:
        pl.semaphore_signal(bar, inc=1, device_id=peer, device_id_type=MESH)

    for name in first:
        copies[name].wait()

    def place(n, put):
        column = 0
        for block, at, size in pieces(C, n):
            if block < z.full:
                put(block * rs, at, r, 0, column, size)
            else:
                for where, row, rows in z.bits:
                    put(z.left, at + where, rows, row, column, size)
            column += size

    vectors = (k.v_bq, k.v_bv, k.v_bo, k.v_g1, k.v_s1, k.v_bd, k.v_g2, k.v_s2)

    def vec_at(j):
        return z.vrow + j // z.vper, j % z.vper * r

    k.fsq[...] = jnp.zeros_like(k.fsq)
    for n, src in enumerate((k.v_wk_in[0], k.v_wv_in[0], k.v_wq_in[0])):
        src = src.astype(F32)

        def put(row, at, rows, row2, column, size):
            k.fsq[row : row + rows, at : at + size] = src[row2 : row2 + rows, column : column + size]

        place(n, put)
    for j, ref in enumerate(vectors):
        row, at = vec_at(j)
        k.fsq[row : row + 1, at : at + r] = ref[...].astype(F32)
    k.fsq[z.brow : z.brow + 1, 0 : 4 * r] = k.v_bu[...].astype(F32)
    k.bufq[w_me] = k.fsq[...].astype(BF16)
    pl.semaphore_wait(bar, len(peers))

    def shares(q):
        return k.bufq if q == M_QKV else k.buf.at[q]

    def g1(q, i):
        own = shares(q).at[w_me]
        return rcopy(own, own, k.g1_ss.at[q, i], k.g1_rs.at[q, i], (lax.rem(b + i, nb), d, h))

    def g1_wait(q, i):
        src = shares(q).at[lax.rem(b + nb - i, nb) * nd + d]
        rcopy(src, src, k.g1_ss.at[q, i], k.g1_rs.at[q, i], (b, d, h)).wait_recv()

    def g2(q, e, i):
        src = shares(q).at[lax.rem(b + nb - i, nb) * nd + d]
        return rcopy(src, src, k.g2_ss.at[q, e - 1, i], k.g2_rs.at[q, e - 1, i], (b, lax.rem(d + e, nd), h))

    def g2_wait(q, e, i):
        src = shares(q).at[lax.rem(b + nb - i, nb) * nd + lax.rem(d + nd - e, nd)]
        rcopy(src, src, k.g2_ss.at[q, e - 1, i], k.g2_rs.at[q, e - 1, i], (b, d, h)).wait_recv()

    def gather_start(q):
        for e in range(1, nd):
            g2(q, e, 0).start()
        loop(nb - 1, lambda i: g1(q, i + 1).start())

    def gather_forward(q):
        def one(i):
            g1_wait(q, i + 1)
            for e in range(1, nd):
                g2(q, e, i + 1).start()

        loop(nb - 1, one)

    def gather_wait(q):
        for e in range(1, nd):
            loop(nb, lambda i: g2_wait(q, e, i))

    def gather_drain(q):
        if q != M_QKV:
            loop(nb - 1, lambda i: g1(q, i + 1).wait_send())
        for e in range(1, nd):
            loop(nb, lambda i: g2(q, e, i).wait_send())

    def in_step(n):
        pl.semaphore_signal(k.sync.at[n], inc=1, device_id=(b, d, xor(1)), device_id_type=MESH)
        pl.semaphore_wait(k.sync.at[n], 1)

    gather_start(M_QKV)

    def load_blocks(name, n, dst):
        copies[name].wait()
        both = getattr(k, "v_" + name)[...].astype(F32)
        for m in range(MB):
            k.flat[n * MB + m] = both[:, m]
            dst[m] = columns_of(z, k.flat.at[n * MB + m]).astype(BF16)

    load_blocks("tok", 0, k.xs)
    k.xb[b] = k.xs[m_t]

    halves = [pl.ds(0, C // 2), pl.ds(C // 2, C // 2)]

    def x_send(e, c):
        m = later(e)
        dst = k.xb.at[b, halves[c]]
        return rcopy(k.xs.at[m, halves[c]], dst, k.x_ss.at[e, c], k.x_rs.at[b, c], (m * S + s_me, d, h))

    def x_pass(e, f, c):
        src = k.xb.at[home(e), halves[c]]
        return rcopy(src, src, k.xf_ss.at[e, f, c], k.x_rs.at[home(e), c], (m_t * S + mate(f), d, h))

    def x_wait(j, c):
        src = k.xb.at[j, halves[c]]
        rcopy(src, src, k.x_ss.at[0, c], k.x_rs.at[j, c], (b, d, h)).wait_recv()

    loop(nb - 1, lambda i: g1(M_QKV, i + 1).wait_send())
    in_step(0)
    for c in range(2):
        for e in range(1, MB):
            x_send(e, c).start()
    for c in range(2):
        loop(S - 1, lambda f: x_pass(0, f + 1, c).start())

    load_blocks("cot", 1, k.cs)
    k.cb[0] = k.cs[m_t]
    for name in rest[:-1]:
        copies[name].wait()

    def pack(q):
        k.buf[q, w_me] = k.fst[...].astype(BF16)

    k.fst[...] = jnp.zeros_like(k.fst)
    for q, src in ((M_OUT, k.v_wo_in[...]), (M_DOWN, k.v_wdn_in[0])):
        src = src.astype(F32)
        k.fst[0 : 2 * r, 0:C] = src[0 : 2 * r]
        k.fst[0 : 2 * r, C:L] = src[2 * r : 4 * r]
        pack(q)
    k.fst[0:r] = k.v_wup_in[0, :, 0:L].astype(F32)
    k.fst[rs : rs + r] = k.v_wup_in[0, :, L : 2 * L].astype(F32)
    pack(M_UP)

    gather_forward(M_QKV)

    gather_wait(M_QKV)

    for w in range(W):
        slab = k.bufq[w].astype(F32)
        for block in range(z.full):
            k.fall[w * r : w * r + rs, block * 128 : (block + 1) * 128] = slab[block * rs : (block + 1) * rs]
        end = z.full * 128
        for at, row, rows in z.bits:
            rows = rows if len(z.bits) > 1 else rs
            part = slab[z.left : z.left + rows, at : at + 3 * C - end]
            k.fall[w * r + row : w * r + row + rows, end : 3 * C] = part
        per = z.brow - z.vrow
        k.vrows[w * per : (w + 1) * per] = slab[z.vrow : z.brow]
    k.wkv[...] = k.fall[0:C, 0:L].astype(BF16)
    k.wkvt[...] = k.fall[0:C, 0:L].T.astype(BF16)
    k.wq[...] = k.fall[0:C, L : 3 * C].astype(BF16)
    k.wqt[...] = k.fall[0:C, L : 3 * C].T.astype(BF16)
    columns = k.vrows[...].T
    for w in range(W):
        for j in range(8):
            row, at = vec_at(j)
            column = w * (z.brow - z.vrow) + row - z.vrow
            k.vcol[w * r : (w + 1) * r, j : j + 1] = columns[at : at + r, column : column + 1]

    def vec(j):
        return k.vcol[0:C, j : j + 1]

    row16 = lax.broadcasted_iota(jnp.int32, (16, R), 0)
    column = lax.broadcasted_iota(jnp.int32, (16, R), 1)
    step = R // z.per
    token = z.per * (column % step) + column // step
    pad = jnp.zeros((48, R), BF16)
    one_rows = jnp.where(row16 < 2, 1.0, 0.0).astype(BF16)

    def in_doc(j):
        doc = jnp.zeros((16, R), jnp.int32)
        end = jnp.int32(0)
        for n in range(z.ND):
            end = end + k.lens[m_t, 0, n]
            doc = doc + (j * R + token >= end).astype(jnp.int32)
        return row16 == doc

    def head_send(net, i, p):
        buf, ss, rs_ = net
        src, to = (h, xor(p)) if p <= half else (xor(half), xor(p - half))
        return rcopy(buf.at[i, src], buf.at[i, src], ss.at[i, p], rs_.at[i, p], (b, d, to))

    def head_wait(net, i, p):
        buf, ss, rs_ = net
        rcopy(buf.at[i, xor(p)], buf.at[i, xor(p)], ss.at[i, p], rs_.at[i, p], (b, d, h)).wait_recv()

    def head_start(net, i):
        for p in range(half, 0, -1):
            head_send(net, i, p).start()

    def head_pass(net, i):
        head_wait(net, i, half)
        for p in range(half + 1, nh):
            head_send(net, i, p).start()

    def head_end(net, i):
        for p in range(1, nh):
            if p != half:
                head_wait(net, i, p)

    o_net = (k.oall, k.o_ss, k.o_rs)
    p_net = (k.pall, k.p_ss, k.p_rs)

    def kv_block(t, j):
        kv = mm(k.wkvt[...], k.xb[j])
        kb = kv[0:C].astype(BF16)
        vb = (kv[C:L] + vec(V_BV)).astype(BF16)
        barred = jnp.logical_and(row16 < z.ND, jnp.logical_not(in_doc(j)))
        kf = jnp.where(barred, -BIG, 0.0).astype(BF16)
        for a in range(H):
            kh, vh = kb[a * HEAD_DIM : (a + 1) * HEAD_DIM], vb[a * HEAD_DIM : (a + 1) * HEAD_DIM]
            k.kx[t, a] = kh
            k.vx[t, a, 0:HEAD_DIM] = vh
            k.vx[t, a, HEAD_DIM:] = one_rows
            k.kt[t, a] = jnp.concatenate([kh, kf, pad], axis=0).T
            k.vt[t, a] = jnp.concatenate([vh, one_rows, pad], axis=0).T

    def query_block(e):
        xi = k.xb[home(e)]
        k.xq[:, e * R : (e + 1) * R] = xi
        qi = ((mm(k.wqt[...], xi) + vec(V_BQ)).astype(BF16).astype(F32) * HEAD_DIM**-0.5).astype(BF16)
        hot = jnp.where(in_doc(home(e)), 1.0, 0.0).astype(BF16)
        for a in range(H):
            k.qx[e, a] = jnp.concatenate([qi[a * HEAD_DIM : (a + 1) * HEAD_DIM], hot, pad], axis=0)

    def scores(e, a, t):
        return mm(k.kt[t, a], k.qx[e, a])

    def prob(e, a, t):
        if z.keep:
            return k.pbuf[t, e, a]
        return jnp.exp(scores(e, a, t) - k.tops[e, a, pl.ds(t, 1)]).astype(BF16)

    def attend(pairs):
        units = [(e, a, t) for e, t in pairs for a in range(H)]
        s = [scores(*u) for u in units]
        top = [jnp.max(x, axis=0, keepdims=True) for x in s]
        p = [jnp.exp(x - y).astype(BF16) for x, y in zip(s, top)]
        o = [mm(k.vx[t, a], x) for (e, a, t), x in zip(units, p)]
        for i, (e, a, t) in enumerate(units):
            if z.keep:
                k.pbuf[t, e, a] = p[i]
            k.tops[e, a, pl.ds(t, 1)] = top[i]
        for i, (e, a, t) in enumerate(units):
            if isinstance(t, int) and t == 0:
                k.top[e, a, 0:1] = top[i]
                k.osum[e, a] = o[i]
            else:
                old = k.top[e, a, 0:1]
                new = jnp.maximum(old, top[i])
                k.top[e, a, 0:1] = new
                k.osum[e, a] = k.osum[e, a] * jnp.exp(old - new) + o[i] * jnp.exp(top[i] - new)

    def factor(e, a, t):
        return jnp.exp(k.tops[e, a, pl.ds(t, 1)] - k.top[e, a, 0:1]) * k.top[e, a, 1:2]

    for c in range(2):
        for e in range(1, MB):
            x_wait(home(e), c)
            loop(S - 1, lambda f: x_pass(e, f + 1, c).start())
    gather_start(M_OUT)
    gather_start(M_UP)
    for e in range(MB):
        kv_block(e, home(e))
        query_block(e)
    for t in range(MB):
        attend([(e, t) for e in range(MB)])

    def attend_other(n):
        for c in range(2):
            x_wait(other(n), c)
        kv_block(MB + n, other(n))
        attend([(e, MB + n) for e in range(MB)])

    def heads_done(e):
        for a in range(H):
            o = k.osum[e, a]
            inv = 1.0 / o[HEAD_DIM : HEAD_DIM + 1]
            k.top[e, a, 1:2] = inv
            k.oall[e, h, a * HEAD_DIM : (a + 1) * HEAD_DIM] = (o[0:HEAD_DIM] * inv).astype(BF16)
        head_start(o_net, e)

    last = nb - MB - 1
    loop(last, attend_other)
    for c in range(2):
        x_wait(other(last), c)
    gather_start(M_DOWN)
    kv_block(MB + last, other(last))
    for e in range(MB):
        attend([(e, MB + last)])
        heads_done(e)

    gather_forward(M_OUT)
    head_pass(o_net, 0)
    gather_forward(M_UP)
    for e in range(1, MB):
        head_pass(o_net, e)
    gather_wait(M_OUT)

    per = W // nh

    def w_send(p):
        src = k.buf.at[M_OUT, pl.ds(xor(p) * per, per)]
        return rcopy(src, k.wob.at[h], k.w_ss.at[p], k.w_rs.at[p], (b, d, xor(p)))

    for p in range(1, nh):
        w_send(p).start()

    def spread(dst, slab, row):
        slab = slab.astype(F32)
        dst[row : row + z.r2] = slab[0 : z.r2, 0:C]
        dst[row + 2 * r : row + 2 * r + z.r2] = slab[0 : z.r2, C:L]

    for w in range(W):
        spread(k.fod, k.buf[M_OUT, w], 4 * r * w)
    k.wot[...] = k.fod[0:F].T.astype(BF16)

    gather_forward(M_DOWN)

    def c_send(e):
        m = later(e)
        slot = lax.rem(m_t + MB - m, MB)
        return rcopy(k.cs.at[m], k.cb.at[slot], k.c_ss.at[e], k.c_rs.at[slot], (m * S + s_me, d, h))

    for e in range(1, MB):
        c_send(e).start()

    lane_rows = R // 128

    def st_send(e, i, p):
        own = k.stats.at[e, i, h]
        return rcopy(own, own, k.st_ss.at[e, i, p], k.st_rs.at[e, i, p], (b, d, xor(p)))

    def reduce_start(e, i, rows):
        for j, v in enumerate(rows):
            row = jnp.sum(v, axis=0, keepdims=True)
            for c in range(lane_rows):
                k.stats[e, i, h, pl.ds(j * lane_rows + c, 1)] = row[:, c * 128 : (c + 1) * 128]
        if len(rows) * lane_rows < 8:
            rest = 8 - len(rows) * lane_rows
            k.stats[e, i, h, pl.ds(8 - rest, rest)] = jnp.zeros((rest, 128), F32)
        for p in range(nh - 1, 0, -1):
            st_send(e, i, p).start()

    def reduce_end(e, i, n):
        for p in range(1, nh):
            src = k.stats.at[e, i, xor(p)]
            rcopy(src, src, k.st_ss.at[e, i, p], k.st_rs.at[e, i, p], (b, d, h)).wait_recv()
        total = k.stats[e, i, 0]
        for j in range(1, nh):
            total = total + k.stats[e, i, j]
        total = total / D
        return [
            jnp.concatenate([total[j * lane_rows + c :][0:1] for c in range(lane_rows)], axis=1)
            for j in range(n)
        ]

    def cols(ref, i):
        return ref[:, i * R : (i + 1) * R]

    for i in range(MB):
        head_end(o_net, i)
        h1 = cols(k.xq, i).astype(F32) + mm(k.wot[...], k.oall[i].reshape(D, R)) + vec(V_BO)
        k.n1[i] = h1
        reduce_start(0, i, (h1, h1 * h1))

    gather_wait(M_UP)
    for w in range(W):
        slab = k.buf[M_UP, w].astype(F32)
        k.fup[w * r : w * r + rs, 0:L] = slab[0:rs]
        k.fup[w * r : w * r + rs, L:F] = slab[rs : 2 * rs]
    k.fup[C : C + 16] = jnp.zeros((16, F), F32)
    for w in range(W):
        row = k.bufq[w].astype(F32)[z.brow : z.brow + 1, 0 : 4 * r]
        k.fup[C : C + 1, 4 * r * w : 4 * r * (w + 1)] = row
    k.wup[...] = k.fup[0:C].astype(BF16)
    k.wupt[...] = k.fup[...].T.astype(BF16)
    gather_wait(M_DOWN)
    for w in range(W):
        spread(k.fod, k.buf[M_DOWN, w], 4 * r * w)
    k.wdn[...] = k.fod[0:F].astype(BF16)
    k.wdnt[...] = k.fod[0:F].T.astype(BF16)

    first_one = jnp.where(row16 < 1, 1.0, 0.0).astype(BF16)
    r1 = [None] * MB
    gdn = [None] * MB
    for i in range(MB):
        mean, square = reduce_end(0, i, 2)
        r1[i] = lax.rsqrt(square - mean * mean + EPS)
        n1 = (k.n1[i] - mean) * r1[i]
        k.n1[i] = n1
        y1 = n1 * vec(V_G1) + vec(V_S1)
        k.y1[i] = y1
        y1b = y1.astype(BF16)
        k.y1b[:, i * R : (i + 1) * R] = y1b
        u = mm(k.wupt[...], jnp.concatenate([y1b, first_one], axis=0))
        cdf = 0.5 * (1.0 + lax.erf(u * (0.5**0.5)))
        act = (u * cdf).astype(BF16)
        k.act[:, i * R : (i + 1) * R] = act
        h2 = y1 + mm(k.wdnt[...], act) + vec(V_BD)
        k.h2[i] = h2

        if i > 0:
            rcopy(k.cb.at[i], k.cb.at[i], k.c_ss.at[0], k.c_rs.at[i], (b, d, h)).wait_recv()
        dn2 = k.cb[i].astype(F32) * vec(V_G2)
        reduce_start(1, i, (h2, h2 * h2, dn2, dn2 * h2))
        k.up[i], k.gel[i] = u, cdf
    for i in range(MB):
        u = k.up[i]
        k.gel[i] += u * jnp.exp(-0.5 * u * u) * ((2 * jnp.pi) ** -0.5)
    k.vg[...] = jnp.zeros_like(k.vg)
    ones = jnp.ones((16, R), BF16)

    def vec_grad(j, x):
        k.vg[j : j + 1] += mm_nt(ones, x)[0:1]

    def mo_send(i):
        return rcopy(k.mo.at[i], k.o_mo.at[m_t], k.mo_ss.at[i], k.mo_rs.at[m_t], (home(i), d, h))

    for i in range(MB):
        mean, square, dmean, dsquare = reduce_end(1, i, 4)
        r2 = lax.rsqrt(square - mean * mean + EPS)
        g = k.cb[i].astype(F32)
        dn2 = g * vec(V_G2)
        n2 = (k.h2[i] - mean) * r2
        dh2 = r2 * (dn2 - dmean - n2 * (r2 * (dsquare - mean * dmean)))
        dz = dh2.astype(BF16)
        k.dz[:, i * R : (i + 1) * R] = dz
        du = (mm(k.wdn[...], dz) * k.gel[i]).astype(BF16)
        k.du[:, i * R : (i + 1) * R] = du
        dy1 = dh2 + mm(k.wup[...], du)
        dn1 = dy1 * vec(V_G1)
        k.dh1[i] = dn1
        n1 = k.n1[i]
        reduce_start(2, i, (dn1, dn1 * n1))
        out = (n2 * vec(V_G2) + vec(V_S2)).astype(BF16)
        if i > 0:
            k.mo[i] = out
            mo_send(i).start()
        else:
            k.o_mo[m_t] = out
        k.vin[0, i] = (g * n2).astype(BF16)
        k.vin[1, i] = (dy1 * n1).astype(BF16)
        k.vin[2, i] = dy1.astype(BF16)

    def sums(q):
        if q == M_QKV:
            return k.pkq, k.got1q, k.sent2q, k.got2q, k.o_Q
        return k.pk.at[q], k.got1.at[q], k.sent2.at[q], k.got2.at[q], k.o_G.at[q]

    def s1_send(q, e, i):
        dt = lax.rem(d + e, nd)
        return rcopy(
            sums(q)[0].at[i * nd + dt], sums(q)[1].at[e - 1, i], k.s1_ss.at[q, e - 1, i], k.s1_rs.at[q, e - 1, i],
            (b, dt, h),
        )

    def s2_send(q, i):
        bt = lax.rem(b + i, nb)
        return rcopy(sums(q)[2].at[bt], sums(q)[3].at[b], k.s2_ss.at[q, i], k.s2_rs.at[q, i], (bt, d, h))

    def scatter_start(q):
        for e in range(1, nd):
            loop(nb, lambda i: s1_send(q, e, i).start())

    def scatter_sum(q, bt):
        part = sums(q)[0][bt * nd + d].astype(F32)
        for e in range(1, nd):
            src = sums(q)[1].at[e - 1, bt]
            rcopy(src, src, k.s1_ss.at[q, e - 1, bt], k.s1_rs.at[q, e - 1, bt], (b, d, h)).wait_recv()
            part = part + src[...].astype(F32)
        return part

    def scatter_forward(q):
        def one(i):
            bt = lax.rem(b + i + 1, nb)
            sums(q)[2][bt] = scatter_sum(q, bt).astype(BF16)
            s2_send(q, i + 1).start()

        loop(nb - 1, one)
        sums(q)[4][...] = scatter_sum(q, b)

    def scatter_end(q):
        def one(i):
            src = sums(q)[3].at[lax.rem(b + nb - i - 1, nb)]
            rcopy(src, src, k.s2_ss.at[q, i + 1], k.s2_rs.at[q, i + 1], (b, d, h)).wait_recv()
            sums(q)[4][...] += src[...].astype(F32)

        loop(nb - 1, one)
        loop(nb - 1, lambda i: s2_send(q, i + 1).wait_send())
        for e in range(1, nd):
            loop(nb, lambda i: s1_send(q, e, i).wait_send())

    def rows_of(parts):
        rows = jnp.concatenate(parts, axis=0)
        if rows.shape[0] < rA:
            rows = jnp.concatenate([rows, jnp.zeros((rA - rows.shape[0], L), F32)], axis=0)
        return rows.astype(BF16)

    def pack_halves(q, g):
        for w in range(W):
            at = 4 * r * w
            pair = jnp.concatenate([g[at : at + z.r2], g[at + 2 * r : at + 2 * r + z.r2]], axis=1)
            k.pk[q, w] = rows_of([pair])
        scatter_start(q)

    k.gdn[0:F] = mm_nt(k.act[...], k.dz[...])
    pack_halves(M_DOWN, k.gdn)
    k.gup[0:C] = mm_nt(k.y1b[...], k.du[...])
    for w in range(W):
        k.pk[M_UP, w] = rows_of([k.gup[w * r : w * r + rs, 0:L], k.gup[w * r : w * r + rs, L:F]])
    scatter_start(M_UP)
    for i in range(MB):
        for j, x in ((V_G2, k.vin[0, i]), (V_G1, k.vin[1, i]), (V_S1, k.vin[2, i]), (V_S2, k.cb[i])):
            vec_grad(j, x)
        vec_grad(V_BD, cols(k.dz, i))

    for i in range(MB):
        dmean, dsquare = reduce_end(2, i, 2)
        dh1 = r1[i] * (k.dh1[i] - dmean - k.n1[i] * dsquare)
        k.dh1[i] = dh1
        dp = dh1.astype(BF16)
        k.pall[i, h] = dp
        head_start(p_net, i)

    g = None
    for i in range(MB):
        dp = k.pall[i, h]
        part = mm_nt(k.oall[i].reshape(D, R), dp)
        g = part if g is None else g + part
        vec_grad(V_BO, dp)
    k.gout[0:F] = g
    pack_halves(M_OUT, k.gout)
    ug = mm_nt(jnp.ones((16, z.Q), BF16), k.du[...])
    k.gst[...] = jnp.zeros_like(k.gst)
    for w in range(W):
        k.gst[w, z.brow : z.brow + 1, 0 : 4 * r] = ug[0:1, 4 * r * w : 4 * r * (w + 1)]

    def pack_vec(j):
        row, at = vec_at(j)
        for w in range(W):
            k.gst[w, row : row + 1, at : at + r] = k.vg[j : j + 1, w * r : (w + 1) * r]

    for j in (V_BO, V_G1, V_S1, V_BD, V_G2, V_S2):
        pack_vec(j)
    k.gall[...] = jnp.zeros_like(k.gall)

    for p in range(1, nh):
        src = k.wob.at[xor(p)]
        rcopy(src, src, k.w_ss.at[p], k.w_rs.at[p], (b, d, h)).wait_recv()
    k.wob[h] = k.buf[M_OUT, pl.ds(h * per, per)]
    for j in range(nh):
        for n in range(per):
            spread(k.fod, k.wob[j, n], j * C + 4 * r * n)
    for j in range(nh):
        k.wor[:, j * C : (j + 1) * C] = k.fod[j * C : (j + 1) * C].astype(BF16)

    scatter_forward(M_DOWN)
    head_pass(p_net, 0)
    for i in range(1, MB):
        head_pass(p_net, i)

    def grad_in(e):
        head_end(p_net, e)
        do = mm(k.wor[...], k.pall[e].reshape(D, R)).astype(BF16).astype(F32)
        for a in range(H):
            part = do[a * HEAD_DIM : (a + 1) * HEAD_DIM]
            own = k.oall[e, h, a * HEAD_DIM : (a + 1) * HEAD_DIM].astype(F32)
            k.part[e, a] = part
            k.delta[e, a, 0:1] = jnp.sum(part * own, axis=0, keepdims=True)
            k.dqacc[e, a] = jnp.zeros((HEAD_DIM, R), F32)

    def scaled(e, a, t):
        f = factor(e, a, t)
        delta = k.delta[e, a, 0:1] * f
        hi = delta.astype(BF16).astype(F32)
        rest = jnp.where(row16 == 0, -hi, jnp.where(row16 == 1, hi - delta, 0.0))
        return jnp.concatenate([(k.part[e, a] * f).astype(BF16), rest.astype(BF16), pad], axis=0)

    def back(slots, queries):
        units = [(e, a, t) for t in slots for a in range(H) for e in queries]
        dox = [scaled(*u) for u in units]
        p = [prob(*u) for u in units]
        dp = [mm(k.vt[t, a], x) for (e, a, t), x in zip(units, dox)]
        ds = [(x.astype(F32) * y).astype(BF16) for x, y in zip(p, dp)]
        dq = [mm(k.kx[t, a], x) for (e, a, t), x in zip(units, ds)]
        dk = [mm_nt(k.qx[e, a, 0:HEAD_DIM], x) for (e, a, t), x in zip(units, ds)]
        dv = [mm_nt(x[0:HEAD_DIM], y) for x, y in zip(dox, p)]
        for e in queries:
            for a in range(H):
                mine = [x for (e2, a2, t), x in zip(units, dq) if (e2, a2) == (e, a)]
                k.dqacc[e, a] += sum(mine[1:], mine[0])
        found = []
        per_slot = H * len(queries)
        for n in range(len(slots)):
            rows = []
            for x in (dk, dv):
                for a in range(H):
                    at = n * per_slot + a * len(queries)
                    rows.append(sum(x[at + 1 : at + len(queries)], x[at]))
            found.append(jnp.concatenate(rows, axis=0))
        return found

    def tokens_part(j, dkv):
        k.gall[0:C, 0:L] += mm_nt(k.xb[j], dkv)
        vec_grad(V_BV, dkv[C:L])
        return mm(k.wkv[...], dkv)

    def tp_send(n):
        dst = k.tgr.at[n % MB, s_me]
        to = lax.rem(s_me + 1 + n // MB, S)
        return rcopy(k.tgs.at[n], dst, k.tp_ss.at[n], k.tp_rs.at[n % MB, s_me], (m_t * S + to, d, h))

    def send_part(n, dkv):
        k.tgs[n] = tokens_part(other(n), dkv.astype(BF16)).astype(BF16)
        if not z.keep or n % MB:
            tp_send(n).start()

    others = list(range(nb - MB - 1, -1, -1))
    for e in range(MB):
        grad_in(e)
        if z.keep:
            found = back([MB + n for n in others], [e])
            for n, dkv in zip(others, found):
                if e > 0:
                    dkv = dkv + k.dkacc[n]
                if e < MB - 1:
                    k.dkacc[n] = dkv
                else:
                    send_part(n, dkv)
        if e == 0:
            scatter_forward(M_UP)
    if not z.keep:
        loop(nb - MB, lambda n: send_part(n, back([MB + n], range(MB))[0]))

    for e in range(MB - 1, -1, -1):
        dkv = back([e], range(MB))[0]
        k.tgo[e] = tokens_part(home(e), dkv.astype(BF16))
        if e == MB - 1:
            scatter_forward(M_OUT)

    for i in range(MB):
        for a in range(H):
            rows = slice(a * HEAD_DIM, (a + 1) * HEAD_DIM)
            k.dq[rows, i * R : (i + 1) * R] = (k.dqacc[i, a] * HEAD_DIM**-0.5).astype(BF16)
        vec_grad(V_BQ, cols(k.dq, i))
    k.gall[0:C, L : 3 * C] = mm_nt(k.xq[...], k.dq[...])
    pack_vec(V_BQ)
    pack_vec(V_BV)

    for w in range(W):
        for n in range(3):

            def put(row, at, rows, row2, column, size):
                src = k.gall[w * r + row2 : w * r + row2 + rows, n * C + column : n * C + column + size]
                k.gst[w, row : row + rows, at : at + size] = src

            place(n, put)
        k.pkq[w] = k.gst[w].astype(BF16)
    scatter_start(M_QKV)

    def t_send(e):
        return rcopy(k.tgx.at[e], k.o_tg.at[m_t], k.t_ss.at[e], k.t_rs.at[m_t], (home(e), d, h))

    def tokens_total(e):
        k.tgo[e] += k.dh1[e] + mm(k.wq[...], cols(k.dq, e))

        def add(f):
            src = k.tgr.at[e, mate(f + 1)]
            rcopy(src, src, k.tp_ss.at[0], k.tp_rs.at[e, mate(f + 1)], (b, d, h)).wait_recv()
            k.tgo[e] += src[...].astype(F32)

        loop(S - 1, add)
        return k.tgo[e].astype(BF16)

    for e in range(1, MB):
        k.tgx[e] = tokens_total(e)
        t_send(e).start()
    if z.keep:
        for n in range(0, nb - MB, MB):
            tp_send(n).start()

    scatter_forward(M_QKV)

    k.o_tg[m_t] = tokens_total(0)
    for q in (M_DOWN, M_UP, M_OUT):
        scatter_end(q)
    for q in range(4):
        gather_drain(q)
    for p in range(1, nh):
        w_send(p).wait_send()
        for i in range(MB):
            head_send(o_net, i, p).wait_send()
            head_send(p_net, i, p).wait_send()
            for e in range(3):
                st_send(e, i, p).wait_send()
    for e in range(MB):
        for c in range(2):
            loop(S - 1, lambda f: x_pass(e, f + 1, c).wait_send())
    loop(nb - MB, lambda n: tp_send(n).wait_send())
    for e in range(1, MB):
        m = later(e)
        rcopy(k.o_mo.at[m], k.o_mo.at[m], k.mo_ss.at[e], k.mo_rs.at[m], (b, d, h)).wait_recv()
        for send in (c_send, mo_send):
            send(e).wait_send()
        for c in range(2):
            x_send(e, c).wait_send()

    for e in range(1, MB):
        m = later(e)
        rcopy(k.o_tg.at[m], k.o_tg.at[m], k.t_ss.at[e], k.t_rs.at[m], (b, d, h)).wait_recv()
        t_send(e).wait_send()
    scatter_end(M_QKV)


def finish_kernel(z, mo, tg, G, GQ, *outs):
    (mixed, dtok, dwq, dbq, dwk, dwv, dbv, dwo, dbo, dg1, ds1, dwup, dbu, dwdn, dbd, dg2, ds2, both) = outs
    r, rs, C, L = z.r, z.rs, z.C, z.L
    for m in range(z.MB):


        def put_mixed(i, rows):
            both[pl.ds(i, z.R // z.per, stride=z.span), m] = rows

        def put_grad(i, rows):
            dtok[m, pl.ds(i, z.R // z.per, stride=z.span)] = rows

        put_rows(z, mo[m].astype(F32), put_mixed)
        put_rows(z, tg[m].astype(F32), put_grad)
    mixed[...] = both[...].astype(BF16)
    for n, ref in enumerate((dwk, dwv, dwq)):
        column = 0
        for block, at, size in pieces(C, n):
            if block < z.full:
                ref[0, :, column : column + size] = GQ[block * rs : block * rs + r, at : at + size]
            else:
                for where, row, rows in z.bits:
                    part = GQ[z.left : z.left + rows, at + where : at + where + size]
                    ref[0, row : row + rows, column : column + size] = part
            column += size
    dwup[0, :, 0:L] = G[M_UP, 0:r]
    dwup[0, :, L : 2 * L] = G[M_UP, rs : rs + r]
    for q, ref in ((M_OUT, dwo), (M_DOWN, dwdn.at[0])):
        ref[0 : 2 * r] = G[q, 0 : 2 * r, 0:C]
        ref[2 * r : 4 * r] = G[q, 0 : 2 * r, C:L]
    for j, ref in enumerate((dbq, dbv, dbo, dg1, ds1, dbd, dg2, ds2)):
        row, at = z.vrow + j // z.vper, j % z.vper * r
        ref[...] = GQ[row : row + 1, at : at + r]
    dbu[...] = GQ[z.brow : z.brow + 1, 0 : 4 * r]


def solution(mesh):
    vec_spec = P("head", ("blk", "dp"))
    mat_spec = P("head", ("blk", "dp"), None)
    tok_spec = P(None, "dp", "head", "blk")
    out_spec = P(("blk", "dp"), "head")

    def body(
        tokens, doc_lengths, cotangent, query_weight, query_bias, key_weight, value_weight, value_bias,
        out_weight, out_bias, first_gain, first_shift, up_weight, up_bias, down_weight, down_bias,
        second_gain, second_shift,
    ):
        z = Sizes(mesh, tokens, query_weight, up_weight, doc_lengths)

        def as_rows(a):
            return a.reshape(z.MB, z.N, 128).transpose(1, 0, 2)

        operands = (
            as_rows(tokens), as_rows(cotangent), query_weight, query_bias, key_weight, value_weight, value_bias,
            out_weight, out_bias, first_gain, first_shift, up_weight, up_bias, down_weight, down_bias, second_gain,
            second_shift,
        )
        scratch = main_scratch(z, operands)
        vmem = pl.BlockSpec(memory_space=pltpu.VMEM)
        smem = pl.BlockSpec(memory_space=pltpu.SMEM)
        hbm = pl.BlockSpec(memory_space=pltpu.HBM)
        names = INPUTS + OUTPUTS + list(scratch)
        sds = jax.ShapeDtypeStruct
        parts = pl.pallas_call(
            lambda *refs: main_kernel(z, names, *refs),
            out_shape=[
                sds((z.MB, z.C, z.R), BF16),
                sds((z.MB, z.C, z.R), BF16),
                sds((3, z.rA, z.L), F32),
                sds((z.rQ, 128), F32),
            ],
            in_specs=[smem] + [hbm] * len(operands),
            out_specs=[vmem] * len(OUTPUTS),
            scratch_shapes=list(scratch.values()),
            compiler_params=pltpu.CompilerParams(
                collective_id=0, has_side_effects=True, vmem_limit_bytes=63 << 20
            ),
            name="layer",
        )(doc_lengths, *operands)
        mat, vec = sds((1, z.r, z.C), F32), sds((1, z.r), F32)
        outs = pl.pallas_call(
            lambda *refs: finish_kernel(z, *refs),
            out_shape=[
                sds((z.N, z.MB, 128), BF16), sds((z.MB, z.N, 128), F32), mat, vec, mat, mat, vec,
                sds((4 * z.r, z.C), F32), vec, vec, vec, sds((1, z.r, z.F), F32), sds((1, 4 * z.r), F32),
                sds((1, 4 * z.r, z.C), F32), vec, vec, vec,
            ],
            in_specs=[vmem] * len(OUTPUTS),
            out_specs=[vmem] * 17,
            scratch_shapes=[pltpu.VMEM((z.N, z.MB, 128), F32)],
            name="finish",
        )(*parts)
        shape = tokens.shape
        return (outs[0].transpose(1, 0, 2).reshape(shape), outs[1].reshape(shape), *outs[2:])

    return jax.shard_map(
        body,
        mesh=mesh,
        in_specs=(
            tok_spec, P(None, "dp", None), tok_spec, mat_spec, vec_spec, mat_spec, mat_spec, vec_spec,
            out_spec, vec_spec, vec_spec, vec_spec, mat_spec, vec_spec, mat_spec, vec_spec, vec_spec, vec_spec,
        ),
        out_specs=(
            tok_spec, tok_spec, mat_spec, vec_spec, mat_spec, mat_spec, vec_spec, out_spec, vec_spec, vec_spec,
            vec_spec, mat_spec, vec_spec, mat_spec, vec_spec, vec_spec, vec_spec,
        ),
        check_vma=False,
    )
```

```python
import math
import types

import jax
import jax.numpy as jnp
from jax import lax
from jax.experimental import pallas as pl
from jax.experimental.pallas import tpu as pltpu
from jax.sharding import PartitionSpec as P

HEAD_DIM = 64
EPS = 1e-05
BIG = 1e30
MESH = pl.DeviceIdType.MESH
F32 = jnp.float32
BF16 = jnp.bfloat16
V_BQ, V_BV, V_BO, V_G1, V_S1, V_BD, V_G2, V_S2 = range(8)
M_OUT, M_UP, M_DOWN, M_QKV = range(4)


def up_to(n, m):
    return (n + m - 1) // m * m


def mm(a, b):
    return lax.dot_general(a, b, (((1,), (0,)), ((), ())), preferred_element_type=F32)


def mm_nt(a, b):
    return lax.dot_general(a, b, (((1,), (1,)), ((), ())), preferred_element_type=F32)


def loop(n, fn):
    if n <= 8:
        for i in range(n):
            fn(i)
    else:
        lax.fori_loop(0, n, lambda i, c: (fn(i), c)[1], 0)


def rcopy(src, dst, ss, rs, dev):
    return pltpu.make_async_remote_copy(
        src_ref=src, dst_ref=dst, send_sem=ss, recv_sem=rs, device_id=dev, device_id_type=MESH
    )


def pieces(c, u):
    at, end = u * c, (u + 1) * c
    found = []
    while at < end:
        size = min(128 - at % 128, end - at)
        found.append((at // 128, at % 128, size))
        at += size
    return found


def columns_of(z, flat):
    rows = [flat[pl.ds(i, z.R // z.per, stride=z.span)].T for i in range(z.span)]
    tokens = []
    for u in range(z.per):
        tokens.append(jnp.concatenate([rows[i][at : at + n] for i, at, n in pieces(z.C, u)], axis=0))
    return jnp.concatenate(tokens, axis=1)


def put_rows(z, value, put):
    n = z.R // z.per
    parts = [[] for _ in range(z.span)]
    for u in range(z.per):
        c = 0
        for i, _, size in pieces(z.C, u):
            parts[i].append(value[c : c + size, u * n : (u + 1) * n])
            c += size
    for i in range(z.span):
        put(i, jnp.concatenate(parts[i], axis=0).T)


class Sizes:
    def __init__(self, mesh, tokens, query_weight, up_weight, doc_lengths):
        self.nb, self.nd, self.nh = mesh.shape["blk"], mesh.shape["dp"], mesh.shape["head"]
        self.W = self.nb * self.nd
        self.C, self.F = query_weight.shape[2], up_weight.shape[2]
        self.MB = tokens.shape[0]
        self.R = tokens.shape[3] // self.C
        self.S = self.nb // self.MB
        self.Q = self.MB * self.R
        self.N = self.R * self.C // 128
        self.per = 128 // math.gcd(self.C, 128)
        self.span = self.per * self.C // 128
        self.H = self.C // HEAD_DIM
        self.ND = doc_lengths.shape[2]
        self.r = query_weight.shape[1]
        self.rs = up_to(self.r, 8)
        self.r2 = up_to(2 * self.r, 8)
        self.rA = up_to(2 * self.rs, 16)
        self.L = 2 * self.C
        self.full, left = divmod(3 * self.C, 128)
        self.left = self.full * self.rs
        fold = left == 64 and self.r % 2 == 0
        self.bits = [(0, 0, self.r // 2), (64, self.r // 2, self.r // 2)] if fold else [(0, 0, self.r)]
        self.vrow = self.left + up_to(self.bits[0][2], 4)
        self.vper = min(8, 128 // self.r)
        self.brow = self.vrow + -(-8 // self.vper)
        self.rQ = up_to(max(self.brow + 1, self.left + self.rs), 16)
        self.keep = self.nb * self.R * self.Q * self.H * 2 <= (8 << 20)
        assert self.F == 4 * self.C and self.F == self.nh * self.C and self.W % self.nh == 0


INPUTS = [
    "lens", "tok", "cot", "wq_in", "bq", "wk_in", "wv_in", "bv", "wo_in", "bo", "g1", "s1", "wup_in", "bu",
    "wdn_in", "bd", "g2", "s2",
]
OUTPUTS = ["o_mo", "o_tg", "o_G", "o_Q"]


def main_scratch(z, inputs):
    dma = pltpu.SemaphoreType.DMA
    v = pltpu.VMEM
    nb, W, L, R, C, F, Q, H, MB, rA, nh = z.nb, z.W, z.L, z.R, z.C, z.F, z.Q, z.H, z.MB, z.rA, z.nh
    dd = max(z.nd - 1, 1)
    return dict(
        in_sem=dma((len(INPUTS) - 1,)),
        flat=v((2 * MB, z.N, 128), F32),
        xs=v((MB, C, R), BF16),
        xb=v((nb, C, R), BF16),
        cs=v((MB, C, R), BF16),
        cb=v((MB, C, R), BF16),
        bufq=v((W, z.rQ, 128), BF16),
        buf=v((3, W, rA, L), BF16),
        wob=v((nh, W // nh, rA, L), BF16),
        fst=v((rA, L), F32),
        fsq=v((z.rQ, 128), F32),
        fall=v((C + 8, up_to(3 * C, 128)), F32),
        vrows=v((up_to(W * (z.brow - z.vrow), 8), 128), F32),
        vcol=v((C + 8, 8), F32),
        fup=v((C + 16, F), F32),
        fod=v((F + 16, C), F32),
        wkv=v((C, L), BF16),
        wkvt=v((L, C), BF16),
        wq=v((C, C), BF16),
        wqt=v((C, C), BF16),
        wup=v((C, F), BF16),
        wupt=v((F, C + 16), BF16),
        wor=v((C, F), BF16),
        wot=v((C, F), BF16),
        wdn=v((F, C), BF16),
        wdnt=v((C, F), BF16),
        xq=v((C, Q), BF16),
        qx=v((MB, H, 128, R), BF16),
        kx=v((nb, H, HEAD_DIM, R), BF16),
        vx=v((nb, H, HEAD_DIM + 16, R), BF16),
        kt=v((nb, H, R, 128), BF16),
        vt=v((nb, H, R, 128), BF16),
        pbuf=v((nb, MB, H, R, R) if z.keep else (1, 1, 1, 16, 128), BF16),
        tops=v((MB, H, up_to(nb, 8), R), F32),
        top=v((MB, H, 8, R), F32),
        osum=v((MB, H, HEAD_DIM + 16, R), F32),
        oall=v((MB, nh, C, R), BF16),
        pall=v((MB, nh, C, R), BF16),
        stats=v((3, MB, nh, 8, 128), F32),
        n1=v((MB, C, R), F32),
        y1=v((MB, C, R), F32),
        h2=v((MB, C, R), F32),
        gel=v((MB, F, R), F32),
        up=v((MB, F, R), F32),
        dh1=v((MB, C, R), F32),
        y1b=v((C, Q), BF16),
        act=v((F, Q), BF16),
        dz=v((C, Q), BF16),
        du=v((F, Q), BF16),
        vin=v((3, MB, C, R), BF16),
        mo=v((MB, C, R), BF16),
        part=v((MB, H, HEAD_DIM, R), F32),
        delta=v((MB, H, 8, R), F32),
        dqacc=v((MB, H, HEAD_DIM, R), F32),
        dkacc=v((nb - MB if z.keep else 1, L, R), F32),
        dq=v((C, Q), BF16),
        tgs=v((nb, C, R), BF16),
        tgo=v((MB, C, R), F32),
        tgr=v((MB, z.S, C, R), BF16),
        tgx=v((MB, C, R), BF16),
        gall=v((C + 8, up_to(3 * C, 128)), F32),
        gst=v((W, z.rQ, 128), F32),
        gup=v((C + 8, F), F32),
        gout=v((F + 16, C), F32),
        gdn=v((F + 16, C), F32),
        vg=v((8, C), F32),
        pk=v((3, W, rA, L), BF16),
        got1=v((3, dd, nb, rA, L), BF16),
        sent2=v((3, nb, rA, L), BF16),
        got2=v((3, nb, rA, L), BF16),
        pkq=v((W, z.rQ, 128), BF16),
        got1q=v((dd, nb, z.rQ, 128), BF16),
        sent2q=v((nb, z.rQ, 128), BF16),
        got2q=v((nb, z.rQ, 128), BF16),
        sync=pltpu.SemaphoreType.REGULAR,
        x_ss=dma,
        xf_ss=dma,
        x_rs=dma((MB, 2)),
        xp_rs=dma((nb,)),
        c_ss=dma,
        c_rs=dma((MB,)),
        g1_ss=dma((4,)),
        g1_rs=dma((4, max(nb - 1, 1))),
        g2_ss=dma((4,)),
        g2_rs=dma((4,)),
        o_ss=dma,
        o_rs=dma((MB, 2)),
        w_ss=dma,
        w_rs=dma,
        st_ss=dma((3,)),
        st_rs=dma((3, MB)),
        p_ss=dma,
        p_rs=dma((MB, 2)),
        mo_ss=dma,
        mo_rs=dma((MB,)),
        tp_ss=dma,
        tp_rs=dma((MB, z.S)),
        t_ss=dma,
        t_rs=dma((MB,)),
        s_ss=dma((4,)),
        s1_rs=dma((4, dd, nb)),
        s2_rs=dma((4,)),
        **{"v_" + name: v(a.shape, a.dtype) for name, a in zip(INPUTS[1:], inputs)},
    )


def main_kernel(z, names, *refs):
    k = types.SimpleNamespace(**dict(zip(names, refs)))
    nb, nd, nh, W, MB, R, C, F, H, L, S, r, rs, rA = (
        z.nb, z.nd, z.nh, z.W, z.MB, z.R, z.C, z.F, z.H, z.L, z.S, z.r, z.rs, z.rA,
    )
    b, d, h = lax.axis_index("blk"), lax.axis_index("dp"), lax.axis_index("head")
    w_me = b * nd + d
    m_t, s_me = b // S, b % S
    D = nh * C
    half = nh // 2

    def xor(i):
        return lax.bitwise_xor(h, i)

    def later(e):
        return lax.rem(m_t + e, MB)

    def home(e):
        return later(e) * S + s_me

    def mate(e):
        return lax.rem(s_me + e, S)

    def other(n):
        return lax.rem(s_me + 1 + n // MB, S) + lax.rem(m_t + n, MB) * S

    copies = {
        name: pltpu.make_async_copy(getattr(k, name), getattr(k, "v_" + name), k.in_sem.at[n])
        for n, name in enumerate(INPUTS[1:])
    }
    rest = ["wo_in", "wdn_in", "wup_in", "cot"]
    first = [name for name in INPUTS[1:] if name not in rest and name != "tok"]
    for name in first + ["tok"] + rest:
        copies[name].start()

    bar = pltpu.get_barrier_semaphore()
    peers = [(lax.rem(b + i, nb), d, h) for i in range(1, nb)]
    peers += [(b, lax.rem(d + i, nd), h) for i in range(1, nd)]
    peers += [(b, d, xor(i)) for i in range(1, nh)]
    for peer in peers:
        pl.semaphore_signal(bar, inc=1, device_id=peer, device_id_type=MESH)

    for name in first:
        copies[name].wait()

    def place(n, put):
        column = 0
        for block, at, size in pieces(C, n):
            if block < z.full:
                put(block * rs, at, r, 0, column, size)
            else:
                for where, row, rows in z.bits:
                    put(z.left, at + where, rows, row, column, size)
            column += size

    vectors = (k.v_bq, k.v_bv, k.v_bo, k.v_g1, k.v_s1, k.v_bd, k.v_g2, k.v_s2)

    def vec_at(j):
        return z.vrow + j // z.vper, j % z.vper * r

    k.fsq[...] = jnp.zeros_like(k.fsq)
    for n, src in enumerate((k.v_wk_in[0], k.v_wv_in[0], k.v_wq_in[0])):
        src = src.astype(F32)

        def put(row, at, rows, row2, column, size):
            k.fsq[row : row + rows, at : at + size] = src[row2 : row2 + rows, column : column + size]

        place(n, put)
    for j, ref in enumerate(vectors):
        row, at = vec_at(j)
        k.fsq[row : row + 1, at : at + r] = ref[...].astype(F32)
    k.fsq[z.brow : z.brow + 1, 0 : 4 * r] = k.v_bu[...].astype(F32)
    k.bufq[w_me] = k.fsq[...].astype(BF16)
    pl.semaphore_wait(bar, len(peers))

    def shares(q):
        return k.bufq if q == M_QKV else k.buf.at[q]

    def g1(q, i):
        own = shares(q).at[w_me]
        return rcopy(own, own, k.g1_ss.at[q], k.g1_rs.at[q, i - 1], (lax.rem(b + i, nb), d, h))

    def g1_wait(q, i):
        src = shares(q).at[lax.rem(b + nb - i, nb) * nd + d]
        rcopy(src, src, k.g1_ss.at[q], k.g1_rs.at[q, i - 1], (b, d, h)).wait_recv()

    def g2(q, e, i):
        src = shares(q).at[lax.rem(b + nb - i, nb) * nd + d]
        return rcopy(src, src, k.g2_ss.at[q], k.g2_rs.at[q], (b, lax.rem(d + e, nd), h))

    def gather_start(q):
        for e in range(1, nd):
            g2(q, e, 0).start()
        loop(nb - 1, lambda i: g1(q, i + 1).start())

    def gather_forward(q):
        def one(i):
            g1_wait(q, i + 1)
            for e in range(1, nd):
                g2(q, e, i + 1).start()

        loop(nb - 1, one)

    def gather_wait(q):
        some = shares(q).at[pl.ds(0, nb * (nd - 1))]
        rcopy(some, some, k.g2_ss.at[q], k.g2_rs.at[q], (b, d, h)).wait_recv()

    def gather_sent(q):
        some = shares(q).at[pl.ds(0, nb - 1)]
        rcopy(some, some, k.g1_ss.at[q], k.g1_rs.at[q, 0], (b, d, h)).wait_send()

    def gather_drain(q):
        if q != M_QKV:
            gather_sent(q)
        some = shares(q).at[pl.ds(0, nb * (nd - 1))]
        rcopy(some, some, k.g2_ss.at[q], k.g2_rs.at[q], (b, d, h)).wait_send()

    gather_start(M_QKV)

    def load_blocks(name, n, dst):
        copies[name].wait()
        both = getattr(k, "v_" + name)[...].astype(F32)
        for m in range(MB):
            k.flat[n * MB + m] = both[:, m]
            dst[m] = columns_of(z, k.flat.at[n * MB + m]).astype(BF16)

    load_blocks("tok", 0, k.xs)
    k.xb[b] = k.xs[m_t]

    halves = [pl.ds(0, C // 2), pl.ds(C // 2, C // 2)]

    def slot_at(m):
        return lax.rem(m_t + MB - m, MB)

    def x_send(e, c):
        m = later(e)
        dst = k.xb.at[b, halves[c]]
        return rcopy(k.xs.at[m, halves[c]], dst, k.x_ss, k.x_rs.at[slot_at(m), c], (m * S + s_me, d, h))

    def x_pass(e, f, c):
        src = k.xb.at[home(e), halves[c]]
        return rcopy(src, src, k.xf_ss, k.xp_rs.at[home(e)], (m_t * S + mate(f), d, h))

    def x_wait(e, c):
        src = k.xb.at[home(e), halves[c]]
        rcopy(src, src, k.x_ss, k.x_rs.at[e, c], (b, d, h)).wait_recv()

    def xp_wait(j):
        rcopy(k.xb.at[j], k.xb.at[j], k.xf_ss, k.xp_rs.at[j], (b, d, h)).wait_recv()

    gather_sent(M_QKV)
    pl.semaphore_signal(k.sync, inc=1, device_id=(b, d, xor(1)), device_id_type=MESH)
    pl.semaphore_wait(k.sync, 1)
    for c in range(2):
        for e in range(1, MB):
            x_send(e, c).start()
    for c in range(2):
        loop(S - 1, lambda f: x_pass(0, f + 1, c).start())

    load_blocks("cot", 1, k.cs)
    k.cb[0] = k.cs[m_t]
    for name in rest[:-1]:
        copies[name].wait()

    def pack(q):
        k.buf[q, w_me] = k.fst[...].astype(BF16)

    k.fst[...] = jnp.zeros_like(k.fst)
    for q, src in ((M_OUT, k.v_wo_in[...]), (M_DOWN, k.v_wdn_in[0])):
        src = src.astype(F32)
        k.fst[0 : 2 * r, 0:C] = src[0 : 2 * r]
        k.fst[0 : 2 * r, C:L] = src[2 * r : 4 * r]
        pack(q)
    k.fst[0:r] = k.v_wup_in[0, :, 0:L].astype(F32)
    k.fst[rs : rs + r] = k.v_wup_in[0, :, L : 2 * L].astype(F32)
    pack(M_UP)

    gather_forward(M_QKV)

    gather_wait(M_QKV)

    for w in range(W):
        slab = k.bufq[w].astype(F32)
        for block in range(z.full):
            k.fall[w * r : w * r + rs, block * 128 : (block + 1) * 128] = slab[block * rs : (block + 1) * rs]
        end = z.full * 128
        for at, row, rows in z.bits:
            rows = rows if len(z.bits) > 1 else rs
            part = slab[z.left : z.left + rows, at : at + 3 * C - end]
            k.fall[w * r + row : w * r + row + rows, end : 3 * C] = part
        per = z.brow - z.vrow
        k.vrows[w * per : (w + 1) * per] = slab[z.vrow : z.brow]
    k.wkv[...] = k.fall[0:C, 0:L].astype(BF16)
    k.wkvt[...] = k.fall[0:C, 0:L].T.astype(BF16)
    k.wq[...] = k.fall[0:C, L : 3 * C].astype(BF16)
    k.wqt[...] = k.fall[0:C, L : 3 * C].T.astype(BF16)
    columns = k.vrows[...].T
    for w in range(W):
        for j in range(8):
            row, at = vec_at(j)
            column = w * (z.brow - z.vrow) + row - z.vrow
            k.vcol[w * r : (w + 1) * r, j : j + 1] = columns[at : at + r, column : column + 1]

    def vec(j):
        return k.vcol[0:C, j : j + 1]

    row16 = lax.broadcasted_iota(jnp.int32, (16, R), 0)
    column = lax.broadcasted_iota(jnp.int32, (16, R), 1)
    step = R // z.per
    token = z.per * (column % step) + column // step
    pad = jnp.zeros((48, R), BF16)
    one_rows = jnp.where(row16 < 2, 1.0, 0.0).astype(BF16)

    def in_doc(j):
        doc = jnp.zeros((16, R), jnp.int32)
        end = jnp.int32(0)
        for n in range(z.ND):
            end = end + k.lens[m_t, 0, n]
            doc = doc + (j * R + token >= end).astype(jnp.int32)
        return row16 == doc

    def head_send(net, i, p):
        buf, ss, rs_ = net
        src, to = (h, xor(p)) if p <= half else (xor(half), xor(p - half))
        return rcopy(buf.at[i, src], buf.at[i, src], ss, rs_.at[i, 0 if p == half else 1], (b, d, to))

    def head_start(net, i):
        for p in range(half, 0, -1):
            head_send(net, i, p).start()

    def head_pass(net, i):
        buf, ss, rs_ = net
        src = buf.at[i, xor(half)]
        rcopy(src, src, ss, rs_.at[i, 0], (b, d, h)).wait_recv()
        for p in range(half + 1, nh):
            head_send(net, i, p).start()

    def head_end(net, i):
        buf, ss, rs_ = net
        some = buf.at[i, pl.ds(0, nh - 2)]
        rcopy(some, some, ss, rs_.at[i, 1], (b, d, h)).wait_recv()

    def head_drain(net):
        buf, ss, rs_ = net
        some = buf.at[:, pl.ds(0, nh - 1)]
        rcopy(some, some, ss, rs_.at[0, 0], (b, d, h)).wait_send()

    o_net = (k.oall, k.o_ss, k.o_rs)
    p_net = (k.pall, k.p_ss, k.p_rs)

    def kv_block(t, j):
        kv = mm(k.wkvt[...], k.xb[j])
        kb = kv[0:C].astype(BF16)
        vb = (kv[C:L] + vec(V_BV)).astype(BF16)
        barred = jnp.logical_and(row16 < z.ND, jnp.logical_not(in_doc(j)))
        kf = jnp.where(barred, -BIG, 0.0).astype(BF16)
        for a in range(H):
            kh, vh = kb[a * HEAD_DIM : (a + 1) * HEAD_DIM], vb[a * HEAD_DIM : (a + 1) * HEAD_DIM]
            k.kx[t, a] = kh
            k.vx[t, a, 0:HEAD_DIM] = vh
            k.vx[t, a, HEAD_DIM:] = one_rows
            k.kt[t, a] = jnp.concatenate([kh, kf, pad], axis=0).T
            k.vt[t, a] = jnp.concatenate([vh, one_rows, pad], axis=0).T

    def query_block(e):
        xi = k.xb[home(e)]
        k.xq[:, e * R : (e + 1) * R] = xi
        qi = ((mm(k.wqt[...], xi) + vec(V_BQ)).astype(BF16).astype(F32) * HEAD_DIM**-0.5).astype(BF16)
        hot = jnp.where(in_doc(home(e)), 1.0, 0.0).astype(BF16)
        for a in range(H):
            k.qx[e, a] = jnp.concatenate([qi[a * HEAD_DIM : (a + 1) * HEAD_DIM], hot, pad], axis=0)

    def scores(e, a, t):
        return mm(k.kt[t, a], k.qx[e, a])

    def prob(e, a, t):
        if z.keep:
            return k.pbuf[t, e, a]
        return jnp.exp(scores(e, a, t) - k.tops[e, a, pl.ds(t, 1)]).astype(BF16)

    def attend(pairs):
        units = [(e, a, t) for e, t in pairs for a in range(H)]
        s = [scores(*u) for u in units]
        top = [jnp.max(x, axis=0, keepdims=True) for x in s]
        p = [jnp.exp(x - y).astype(BF16) for x, y in zip(s, top)]
        o = [mm(k.vx[t, a], x) for (e, a, t), x in zip(units, p)]
        for i, (e, a, t) in enumerate(units):
            if z.keep:
                k.pbuf[t, e, a] = p[i]
            k.tops[e, a, pl.ds(t, 1)] = top[i]
        for i, (e, a, t) in enumerate(units):
            if isinstance(t, int) and t == 0:
                k.top[e, a, 0:1] = top[i]
                k.osum[e, a] = o[i]
            else:
                old = k.top[e, a, 0:1]
                new = jnp.maximum(old, top[i])
                k.top[e, a, 0:1] = new
                k.osum[e, a] = k.osum[e, a] * jnp.exp(old - new) + o[i] * jnp.exp(top[i] - new)

    def factor(e, a, t):
        return jnp.exp(k.tops[e, a, pl.ds(t, 1)] - k.top[e, a, 0:1]) * k.top[e, a, 1:2]

    for c in range(2):
        for e in range(1, MB):
            x_wait(e, c)
            loop(S - 1, lambda f: x_pass(e, f + 1, c).start())
    gather_start(M_OUT)
    gather_start(M_UP)
    for e in range(MB):
        kv_block(e, home(e))
        query_block(e)
    for t in range(MB):
        attend([(e, t) for e in range(MB)])

    def attend_other(n):
        xp_wait(other(n))
        kv_block(MB + n, other(n))
        attend([(e, MB + n) for e in range(MB)])

    def heads_done(e):
        for a in range(H):
            o = k.osum[e, a]
            inv = 1.0 / o[HEAD_DIM : HEAD_DIM + 1]
            k.top[e, a, 1:2] = inv
            k.oall[e, h, a * HEAD_DIM : (a + 1) * HEAD_DIM] = (o[0:HEAD_DIM] * inv).astype(BF16)
        head_start(o_net, e)

    last = nb - MB - 1
    loop(last, attend_other)
    xp_wait(other(last))
    gather_start(M_DOWN)
    kv_block(MB + last, other(last))
    for e in range(MB):
        attend([(e, MB + last)])
        heads_done(e)

    gather_forward(M_OUT)
    head_pass(o_net, 0)
    gather_forward(M_UP)
    for e in range(1, MB):
        head_pass(o_net, e)
    gather_wait(M_OUT)

    per = W // nh

    def w_send(p):
        src = k.buf.at[M_OUT, pl.ds(xor(p) * per, per)]
        return rcopy(src, k.wob.at[h], k.w_ss, k.w_rs, (b, d, xor(p)))

    for p in range(1, nh):
        w_send(p).start()

    def spread(dst, slab, row):
        slab = slab.astype(F32)
        dst[row : row + z.r2] = slab[0 : z.r2, 0:C]
        dst[row + 2 * r : row + 2 * r + z.r2] = slab[0 : z.r2, C:L]

    for w in range(W):
        spread(k.fod, k.buf[M_OUT, w], 4 * r * w)
    k.wot[...] = k.fod[0:F].T.astype(BF16)

    gather_forward(M_DOWN)

    def c_send(e):
        m = later(e)
        slot = slot_at(m)
        return rcopy(k.cs.at[m], k.cb.at[slot], k.c_ss, k.c_rs.at[slot], (m * S + s_me, d, h))

    for e in range(1, MB):
        c_send(e).start()

    lane_rows = R // 128

    def st_send(e, i, p):
        own = k.stats.at[e, i, h]
        return rcopy(own, own, k.st_ss.at[e], k.st_rs.at[e, i], (b, d, xor(p)))

    def reduce_start(e, i, rows):
        for j, v in enumerate(rows):
            row = jnp.sum(v, axis=0, keepdims=True)
            for c in range(lane_rows):
                k.stats[e, i, h, pl.ds(j * lane_rows + c, 1)] = row[:, c * 128 : (c + 1) * 128]
        if len(rows) * lane_rows < 8:
            rest = 8 - len(rows) * lane_rows
            k.stats[e, i, h, pl.ds(8 - rest, rest)] = jnp.zeros((rest, 128), F32)
        for p in range(nh - 1, 0, -1):
            st_send(e, i, p).start()

    def reduce_end(e, i, n):
        some = k.stats.at[e, i, pl.ds(0, nh - 1)]
        rcopy(some, some, k.st_ss.at[e], k.st_rs.at[e, i], (b, d, h)).wait_recv()
        total = k.stats[e, i, 0]
        for j in range(1, nh):
            total = total + k.stats[e, i, j]
        total = total / D
        return [
            jnp.concatenate([total[j * lane_rows + c :][0:1] for c in range(lane_rows)], axis=1)
            for j in range(n)
        ]

    def cols(ref, i):
        return ref[:, i * R : (i + 1) * R]

    for i in range(MB):
        head_end(o_net, i)
        h1 = cols(k.xq, i).astype(F32) + mm(k.wot[...], k.oall[i].reshape(D, R)) + vec(V_BO)
        k.n1[i] = h1
        reduce_start(0, i, (h1, h1 * h1))

    gather_wait(M_UP)
    for w in range(W):
        slab = k.buf[M_UP, w].astype(F32)
        k.fup[w * r : w * r + rs, 0:L] = slab[0:rs]
        k.fup[w * r : w * r + rs, L:F] = slab[rs : 2 * rs]
    k.fup[C : C + 16] = jnp.zeros((16, F), F32)
    for w in range(W):
        row = k.bufq[w].astype(F32)[z.brow : z.brow + 1, 0 : 4 * r]
        k.fup[C : C + 1, 4 * r * w : 4 * r * (w + 1)] = row
    k.wup[...] = k.fup[0:C].astype(BF16)
    k.wupt[...] = k.fup[...].T.astype(BF16)
    gather_wait(M_DOWN)
    for w in range(W):
        spread(k.fod, k.buf[M_DOWN, w], 4 * r * w)
    k.wdn[...] = k.fod[0:F].astype(BF16)
    k.wdnt[...] = k.fod[0:F].T.astype(BF16)

    first_one = jnp.where(row16 < 1, 1.0, 0.0).astype(BF16)
    r1 = [None] * MB
    gdn = [None] * MB
    for i in range(MB):
        mean, square = reduce_end(0, i, 2)
        r1[i] = lax.rsqrt(square - mean * mean + EPS)
        n1 = (k.n1[i] - mean) * r1[i]
        k.n1[i] = n1
        y1 = n1 * vec(V_G1) + vec(V_S1)
        k.y1[i] = y1
        y1b = y1.astype(BF16)
        k.y1b[:, i * R : (i + 1) * R] = y1b
        u = mm(k.wupt[...], jnp.concatenate([y1b, first_one], axis=0))
        cdf = 0.5 * (1.0 + lax.erf(u * (0.5**0.5)))
        act = (u * cdf).astype(BF16)
        k.act[:, i * R : (i + 1) * R] = act
        h2 = y1 + mm(k.wdnt[...], act) + vec(V_BD)
        k.h2[i] = h2

        if i > 0:
            rcopy(k.cb.at[i], k.cb.at[i], k.c_ss, k.c_rs.at[i], (b, d, h)).wait_recv()
        dn2 = k.cb[i].astype(F32) * vec(V_G2)
        reduce_start(1, i, (h2, h2 * h2, dn2, dn2 * h2))
        k.up[i], k.gel[i] = u, cdf
    for i in range(MB):
        u = k.up[i]
        k.gel[i] += u * jnp.exp(-0.5 * u * u) * ((2 * jnp.pi) ** -0.5)
    k.vg[...] = jnp.zeros_like(k.vg)
    ones = jnp.ones((16, R), BF16)

    def vec_grad(j, x):
        k.vg[j : j + 1] += mm_nt(ones, x)[0:1]

    def mo_send(i):
        return rcopy(k.mo.at[i], k.o_mo.at[m_t], k.mo_ss, k.mo_rs.at[m_t], (home(i), d, h))

    for i in range(MB):
        mean, square, dmean, dsquare = reduce_end(1, i, 4)
        r2 = lax.rsqrt(square - mean * mean + EPS)
        g = k.cb[i].astype(F32)
        dn2 = g * vec(V_G2)
        n2 = (k.h2[i] - mean) * r2
        dh2 = r2 * (dn2 - dmean - n2 * (r2 * (dsquare - mean * dmean)))
        dz = dh2.astype(BF16)
        k.dz[:, i * R : (i + 1) * R] = dz
        du = (mm(k.wdn[...], dz) * k.gel[i]).astype(BF16)
        k.du[:, i * R : (i + 1) * R] = du
        dy1 = dh2 + mm(k.wup[...], du)
        dn1 = dy1 * vec(V_G1)
        k.dh1[i] = dn1
        n1 = k.n1[i]
        reduce_start(2, i, (dn1, dn1 * n1))
        out = (n2 * vec(V_G2) + vec(V_S2)).astype(BF16)
        if i > 0:
            k.mo[i] = out
            mo_send(i).start()
        else:
            k.o_mo[m_t] = out
        k.vin[0, i] = (g * n2).astype(BF16)
        k.vin[1, i] = (dy1 * n1).astype(BF16)
        k.vin[2, i] = dy1.astype(BF16)

    def sums(q):
        if q == M_QKV:
            return k.pkq, k.got1q, k.sent2q, k.got2q, k.o_Q
        return k.pk.at[q], k.got1.at[q], k.sent2.at[q], k.got2.at[q], k.o_G.at[q]

    def s1_send(q, e, i):
        dt = lax.rem(d + e, nd)
        return rcopy(
            sums(q)[0].at[i * nd + dt], sums(q)[1].at[e - 1, i], k.s_ss.at[q], k.s1_rs.at[q, e - 1, i],
            (b, dt, h),
        )

    def s2_send(q, i):
        bt = lax.rem(b + i, nb)
        return rcopy(sums(q)[2].at[bt], sums(q)[3].at[b], k.s_ss.at[q], k.s2_rs.at[q], (bt, d, h))

    def scatter_start(q):
        for e in range(1, nd):
            loop(nb, lambda i: s1_send(q, e, i).start())

    def scatter_sum(q, bt):
        part = sums(q)[0][bt * nd + d].astype(F32)
        for e in range(1, nd):
            src = sums(q)[1].at[e - 1, bt]
            rcopy(src, src, k.s_ss.at[q], k.s1_rs.at[q, e - 1, bt], (b, d, h)).wait_recv()
            part = part + src[...].astype(F32)
        return part

    def scatter_forward(q):
        def one(i):
            bt = lax.rem(b + i + 1, nb)
            sums(q)[2][bt] = scatter_sum(q, bt).astype(BF16)
            s2_send(q, i + 1).start()

        loop(nb - 1, one)
        sums(q)[4][...] = scatter_sum(q, b)

    def scatter_end(q):
        some = sums(q)[3].at[pl.ds(0, nb - 1)]
        rcopy(some, some, k.s_ss.at[q], k.s2_rs.at[q], (b, d, h)).wait_recv()

        def one(i):
            sums(q)[4][...] += sums(q)[3][lax.rem(b + nb - i - 1, nb)].astype(F32)

        loop(nb - 1, one)
        some = sums(q)[0].at[pl.ds(0, W - 1)]
        rcopy(some, some, k.s_ss.at[q], k.s2_rs.at[q], (b, d, h)).wait_send()

    def rows_of(parts):
        rows = jnp.concatenate(parts, axis=0)
        if rows.shape[0] < rA:
            rows = jnp.concatenate([rows, jnp.zeros((rA - rows.shape[0], L), F32)], axis=0)
        return rows.astype(BF16)

    def pack_halves(q, g):
        for w in range(W):
            at = 4 * r * w
            pair = jnp.concatenate([g[at : at + z.r2], g[at + 2 * r : at + 2 * r + z.r2]], axis=1)
            k.pk[q, w] = rows_of([pair])
        scatter_start(q)

    k.gdn[0:F] = mm_nt(k.act[...], k.dz[...])
    pack_halves(M_DOWN, k.gdn)
    k.gup[0:C] = mm_nt(k.y1b[...], k.du[...])
    for w in range(W):
        k.pk[M_UP, w] = rows_of([k.gup[w * r : w * r + rs, 0:L], k.gup[w * r : w * r + rs, L:F]])
    scatter_start(M_UP)
    for i in range(MB):
        for j, x in ((V_G2, k.vin[0, i]), (V_G1, k.vin[1, i]), (V_S1, k.vin[2, i]), (V_S2, k.cb[i])):
            vec_grad(j, x)
        vec_grad(V_BD, cols(k.dz, i))

    for i in range(MB):
        dmean, dsquare = reduce_end(2, i, 2)
        dh1 = r1[i] * (k.dh1[i] - dmean - k.n1[i] * dsquare)
        k.dh1[i] = dh1
        dp = dh1.astype(BF16)
        k.pall[i, h] = dp
        head_start(p_net, i)

    g = None
    for i in range(MB):
        dp = k.pall[i, h]
        part = mm_nt(k.oall[i].reshape(D, R), dp)
        g = part if g is None else g + part
        vec_grad(V_BO, dp)
    k.gout[0:F] = g
    pack_halves(M_OUT, k.gout)
    ug = mm_nt(jnp.ones((16, z.Q), BF16), k.du[...])
    k.gst[...] = jnp.zeros_like(k.gst)
    for w in range(W):
        k.gst[w, z.brow : z.brow + 1, 0 : 4 * r] = ug[0:1, 4 * r * w : 4 * r * (w + 1)]

    def pack_vec(j):
        row, at = vec_at(j)
        for w in range(W):
            k.gst[w, row : row + 1, at : at + r] = k.vg[j : j + 1, w * r : (w + 1) * r]

    for j in (V_BO, V_G1, V_S1, V_BD, V_G2, V_S2):
        pack_vec(j)
    k.gall[...] = jnp.zeros_like(k.gall)

    some_rows = k.wob.at[pl.ds(0, nh - 1)]
    rcopy(some_rows, some_rows, k.w_ss, k.w_rs, (b, d, h)).wait_recv()
    k.wob[h] = k.buf[M_OUT, pl.ds(h * per, per)]
    for j in range(nh):
        for n in range(per):
            spread(k.fod, k.wob[j, n], j * C + 4 * r * n)
    for j in range(nh):
        k.wor[:, j * C : (j + 1) * C] = k.fod[j * C : (j + 1) * C].astype(BF16)

    scatter_forward(M_DOWN)
    head_pass(p_net, 0)
    for i in range(1, MB):
        head_pass(p_net, i)

    def grad_in(e):
        head_end(p_net, e)
        do = mm(k.wor[...], k.pall[e].reshape(D, R)).astype(BF16).astype(F32)
        for a in range(H):
            part = do[a * HEAD_DIM : (a + 1) * HEAD_DIM]
            own = k.oall[e, h, a * HEAD_DIM : (a + 1) * HEAD_DIM].astype(F32)
            k.part[e, a] = part
            k.delta[e, a, 0:1] = jnp.sum(part * own, axis=0, keepdims=True)
            k.dqacc[e, a] = jnp.zeros((HEAD_DIM, R), F32)

    def scaled(e, a, t):
        f = factor(e, a, t)
        delta = k.delta[e, a, 0:1] * f
        hi = delta.astype(BF16).astype(F32)
        rest = jnp.where(row16 == 0, -hi, jnp.where(row16 == 1, hi - delta, 0.0))
        return jnp.concatenate([(k.part[e, a] * f).astype(BF16), rest.astype(BF16), pad], axis=0)

    def back(slots, queries):
        units = [(e, a, t) for t in slots for a in range(H) for e in queries]
        dox = [scaled(*u) for u in units]
        p = [prob(*u) for u in units]
        dp = [mm(k.vt[t, a], x) for (e, a, t), x in zip(units, dox)]
        ds = [(x.astype(F32) * y).astype(BF16) for x, y in zip(p, dp)]
        dq = [mm(k.kx[t, a], x) for (e, a, t), x in zip(units, ds)]
        dk = [mm_nt(k.qx[e, a, 0:HEAD_DIM], x) for (e, a, t), x in zip(units, ds)]
        dv = [mm_nt(x[0:HEAD_DIM], y) for x, y in zip(dox, p)]
        for e in queries:
            for a in range(H):
                mine = [x for (e2, a2, t), x in zip(units, dq) if (e2, a2) == (e, a)]
                k.dqacc[e, a] += sum(mine[1:], mine[0])
        found = []
        per_slot = H * len(queries)
        for n in range(len(slots)):
            rows = []
            for x in (dk, dv):
                for a in range(H):
                    at = n * per_slot + a * len(queries)
                    rows.append(sum(x[at + 1 : at + len(queries)], x[at]))
            found.append(jnp.concatenate(rows, axis=0))
        return found

    def tokens_part(j, dkv):
        k.gall[0:C, 0:L] += mm_nt(k.xb[j], dkv)
        vec_grad(V_BV, dkv[C:L])
        return mm(k.wkv[...], dkv)

    def tp_send(n):
        dst = k.tgr.at[n % MB, s_me]
        to = lax.rem(s_me + 1 + n // MB, S)
        return rcopy(k.tgs.at[n], dst, k.tp_ss, k.tp_rs.at[n % MB, s_me], (m_t * S + to, d, h))

    def send_part(n, dkv):
        k.tgs[n] = tokens_part(other(n), dkv.astype(BF16)).astype(BF16)
        if not z.keep or n % MB:
            tp_send(n).start()

    others = list(range(nb - MB - 1, -1, -1))
    for e in range(MB):
        grad_in(e)
        if z.keep:
            found = back([MB + n for n in others], [e])
            for n, dkv in zip(others, found):
                if e > 0:
                    dkv = dkv + k.dkacc[n]
                if e < MB - 1:
                    k.dkacc[n] = dkv
                else:
                    send_part(n, dkv)
        if e == 0:
            scatter_forward(M_UP)
    if not z.keep:
        loop(nb - MB, lambda n: send_part(n, back([MB + n], range(MB))[0]))

    for e in range(MB - 1, -1, -1):
        dkv = back([e], range(MB))[0]
        k.tgo[e] = tokens_part(home(e), dkv.astype(BF16))
        if e == MB - 1:
            scatter_forward(M_OUT)

    for i in range(MB):
        for a in range(H):
            rows = slice(a * HEAD_DIM, (a + 1) * HEAD_DIM)
            k.dq[rows, i * R : (i + 1) * R] = (k.dqacc[i, a] * HEAD_DIM**-0.5).astype(BF16)
        vec_grad(V_BQ, cols(k.dq, i))
    k.gall[0:C, L : 3 * C] = mm_nt(k.xq[...], k.dq[...])
    pack_vec(V_BQ)
    pack_vec(V_BV)

    for w in range(W):
        for n in range(3):

            def put(row, at, rows, row2, column, size):
                src = k.gall[w * r + row2 : w * r + row2 + rows, n * C + column : n * C + column + size]
                k.gst[w, row : row + rows, at : at + size] = src

            place(n, put)
        k.pkq[w] = k.gst[w].astype(BF16)
    scatter_start(M_QKV)

    def t_send(e):
        return rcopy(k.tgx.at[e], k.o_tg.at[m_t], k.t_ss, k.t_rs.at[m_t], (home(e), d, h))

    def tokens_total(e):
        k.tgo[e] += k.dh1[e] + mm(k.wq[...], cols(k.dq, e))

        def add(f):
            src = k.tgr.at[e, mate(f + 1)]
            rcopy(src, src, k.tp_ss, k.tp_rs.at[e, mate(f + 1)], (b, d, h)).wait_recv()
            k.tgo[e] += src[...].astype(F32)

        loop(S - 1, add)
        return k.tgo[e].astype(BF16)

    for e in range(1, MB):
        k.tgx[e] = tokens_total(e)
        t_send(e).start()
    if z.keep:
        for n in range(0, nb - MB, MB):
            tp_send(n).start()

    scatter_forward(M_QKV)

    k.o_tg[m_t] = tokens_total(0)
    for q in (M_DOWN, M_UP, M_OUT):
        scatter_end(q)
    for q in range(4):
        gather_drain(q)
    def drain(some, ss, rs_):
        rcopy(some, some, ss, rs_, (b, d, h)).wait_send()

    drain(some_rows, k.w_ss, k.w_rs)
    head_drain(o_net)
    head_drain(p_net)
    for e in range(3):
        drain(k.stats.at[e, :, pl.ds(0, nh - 1)], k.st_ss.at[e], k.st_rs.at[e, 0])
    drain(k.xs.at[pl.ds(0, MB - 1)], k.x_ss, k.x_rs.at[0, 0])
    drain(k.xb.at[pl.ds(0, MB * (S - 1))], k.xf_ss, k.xp_rs.at[0])
    drain(k.cs.at[pl.ds(0, MB - 1)], k.c_ss, k.c_rs.at[0])
    drain(k.mo.at[pl.ds(0, MB - 1)], k.mo_ss, k.mo_rs.at[0])
    drain(k.tgs.at[pl.ds(0, nb - MB)], k.tp_ss, k.tp_rs.at[0, 0])
    for e in range(1, MB):
        m = later(e)
        rcopy(k.o_mo.at[m], k.o_mo.at[m], k.mo_ss, k.mo_rs.at[m], (b, d, h)).wait_recv()

    for e in range(1, MB):
        m = later(e)
        rcopy(k.o_tg.at[m], k.o_tg.at[m], k.t_ss, k.t_rs.at[m], (b, d, h)).wait_recv()
    drain(k.tgx.at[pl.ds(0, MB - 1)], k.t_ss, k.t_rs.at[0])
    scatter_end(M_QKV)


def finish_kernel(z, mo, tg, G, GQ, *outs):
    (mixed, dtok, dwq, dbq, dwk, dwv, dbv, dwo, dbo, dg1, ds1, dwup, dbu, dwdn, dbd, dg2, ds2, both) = outs
    r, rs, C, L = z.r, z.rs, z.C, z.L
    for m in range(z.MB):


        def put_mixed(i, rows):
            both[pl.ds(i, z.R // z.per, stride=z.span), m] = rows

        def put_grad(i, rows):
            dtok[m, pl.ds(i, z.R // z.per, stride=z.span)] = rows

        put_rows(z, mo[m].astype(F32), put_mixed)
        put_rows(z, tg[m].astype(F32), put_grad)
    mixed[...] = both[...].astype(BF16)
    for n, ref in enumerate((dwk, dwv, dwq)):
        column = 0
        for block, at, size in pieces(C, n):
            if block < z.full:
                ref[0, :, column : column + size] = GQ[block * rs : block * rs + r, at : at + size]
            else:
                for where, row, rows in z.bits:
                    part = GQ[z.left : z.left + rows, at + where : at + where + size]
                    ref[0, row : row + rows, column : column + size] = part
            column += size
    dwup[0, :, 0:L] = G[M_UP, 0:r]
    dwup[0, :, L : 2 * L] = G[M_UP, rs : rs + r]
    for q, ref in ((M_OUT, dwo), (M_DOWN, dwdn.at[0])):
        ref[0 : 2 * r] = G[q, 0 : 2 * r, 0:C]
        ref[2 * r : 4 * r] = G[q, 0 : 2 * r, C:L]
    for j, ref in enumerate((dbq, dbv, dbo, dg1, ds1, dbd, dg2, ds2)):
        row, at = z.vrow + j // z.vper, j % z.vper * r
        ref[...] = GQ[row : row + 1, at : at + r]
    dbu[...] = GQ[z.brow : z.brow + 1, 0 : 4 * r]


def solution(mesh):
    vec_spec = P("head", ("blk", "dp"))
    mat_spec = P("head", ("blk", "dp"), None)
    tok_spec = P(None, "dp", "head", "blk")
    out_spec = P(("blk", "dp"), "head")

    def body(
        tokens, doc_lengths, cotangent, query_weight, query_bias, key_weight, value_weight, value_bias,
        out_weight, out_bias, first_gain, first_shift, up_weight, up_bias, down_weight, down_bias,
        second_gain, second_shift,
    ):
        z = Sizes(mesh, tokens, query_weight, up_weight, doc_lengths)

        def as_rows(a):
            return a.reshape(z.MB, z.N, 128).transpose(1, 0, 2)

        operands = (
            as_rows(tokens), as_rows(cotangent), query_weight, query_bias, key_weight, value_weight, value_bias,
            out_weight, out_bias, first_gain, first_shift, up_weight, up_bias, down_weight, down_bias, second_gain,
            second_shift,
        )
        scratch = main_scratch(z, operands)
        vmem = pl.BlockSpec(memory_space=pltpu.VMEM)
        smem = pl.BlockSpec(memory_space=pltpu.SMEM)
        hbm = pl.BlockSpec(memory_space=pltpu.HBM)
        names = INPUTS + OUTPUTS + list(scratch)
        sds = jax.ShapeDtypeStruct
        parts = pl.pallas_call(
            lambda *refs: main_kernel(z, names, *refs),
            out_shape=[
                sds((z.MB, z.C, z.R), BF16),
                sds((z.MB, z.C, z.R), BF16),
                sds((3, z.rA, z.L), F32),
                sds((z.rQ, 128), F32),
            ],
            in_specs=[smem] + [hbm] * len(operands),
            out_specs=[vmem] * len(OUTPUTS),
            scratch_shapes=list(scratch.values()),
            compiler_params=pltpu.CompilerParams(
                collective_id=0, has_side_effects=True, vmem_limit_bytes=63 << 20
            ),
            name="layer",
        )(doc_lengths, *operands)
        mat, vec = sds((1, z.r, z.C), F32), sds((1, z.r), F32)
        outs = pl.pallas_call(
            lambda *refs: finish_kernel(z, *refs),
            out_shape=[
                sds((z.N, z.MB, 128), BF16), sds((z.MB, z.N, 128), F32), mat, vec, mat, mat, vec,
                sds((4 * z.r, z.C), F32), vec, vec, vec, sds((1, z.r, z.F), F32), sds((1, 4 * z.r), F32),
                sds((1, 4 * z.r, z.C), F32), vec, vec, vec,
            ],
            in_specs=[vmem] * len(OUTPUTS),
            out_specs=[vmem] * 17,
            scratch_shapes=[pltpu.VMEM((z.N, z.MB, 128), F32)],
            name="finish",
        )(*parts)
        shape = tokens.shape
        return (outs[0].transpose(1, 0, 2).reshape(shape), outs[1].reshape(shape), *outs[2:])

    return jax.shard_map(
        body,
        mesh=mesh,
        in_specs=(
            tok_spec, P(None, "dp", None), tok_spec, mat_spec, vec_spec, mat_spec, mat_spec, vec_spec,
            out_spec, vec_spec, vec_spec, vec_spec, mat_spec, vec_spec, mat_spec, vec_spec, vec_spec, vec_spec,
        ),
        out_specs=(
            tok_spec, tok_spec, mat_spec, vec_spec, mat_spec, mat_spec, vec_spec, out_spec, vec_spec, vec_spec,
            vec_spec, mat_spec, vec_spec, mat_spec, vec_spec, vec_spec, vec_spec,
        ),
        check_vma=False,
    )
```

```python
import math
import types

import jax
import jax.numpy as jnp
from jax import lax
from jax.experimental import pallas as pl
from jax.experimental.pallas import tpu as pltpu
from jax.sharding import PartitionSpec as P

HEAD_DIM = 64
EPS = 1e-05
BIG = 1e30
MESH = pl.DeviceIdType.MESH
F32 = jnp.float32
BF16 = jnp.bfloat16
V_BQ, V_BV, V_BO, V_G1, V_S1, V_BD, V_G2, V_S2 = range(8)
M_OUT, M_UP, M_DOWN, M_QKV = range(4)


def up_to(n, m):
    return (n + m - 1) // m * m


def mm(a, b):
    return lax.dot_general(a, b, (((1,), (0,)), ((), ())), preferred_element_type=F32)


def mm_nt(a, b):
    return lax.dot_general(a, b, (((1,), (1,)), ((), ())), preferred_element_type=F32)


def loop(n, fn):
    if n <= 8:
        for i in range(n):
            fn(i)
    else:
        lax.fori_loop(0, n, lambda i, c: (fn(i), c)[1], 0)


def rcopy(src, dst, ss, rs, dev):
    return pltpu.make_async_remote_copy(
        src_ref=src, dst_ref=dst, send_sem=ss, recv_sem=rs, device_id=dev, device_id_type=MESH
    )


def pieces(c, u):
    at, end = u * c, (u + 1) * c
    found = []
    while at < end:
        size = min(128 - at % 128, end - at)
        found.append((at // 128, at % 128, size))
        at += size
    return found


def columns_of(z, flat):
    rows = [flat[pl.ds(i, z.R // z.per, stride=z.span)].T for i in range(z.span)]
    tokens = []
    for u in range(z.per):
        tokens.append(jnp.concatenate([rows[i][at : at + n] for i, at, n in pieces(z.C, u)], axis=0))
    return jnp.concatenate(tokens, axis=1)


def put_rows(z, value, put):
    n = z.R // z.per
    parts = [[] for _ in range(z.span)]
    for u in range(z.per):
        c = 0
        for i, _, size in pieces(z.C, u):
            parts[i].append(value[c : c + size, u * n : (u + 1) * n])
            c += size
    for i in range(z.span):
        put(i, jnp.concatenate(parts[i], axis=0).T)


class Sizes:
    def __init__(self, mesh, tokens, query_weight, up_weight, doc_lengths):
        self.nb, self.nd, self.nh = mesh.shape["blk"], mesh.shape["dp"], mesh.shape["head"]
        self.W = self.nb * self.nd
        self.C, self.F = query_weight.shape[2], up_weight.shape[2]
        self.MB = tokens.shape[0]
        self.R = tokens.shape[3] // self.C
        self.S = self.nb // self.MB
        self.Q = self.MB * self.R
        self.N = self.R * self.C // 128
        self.per = 128 // math.gcd(self.C, 128)
        self.span = self.per * self.C // 128
        self.H = self.C // HEAD_DIM
        self.ND = doc_lengths.shape[2]
        self.r = query_weight.shape[1]
        self.rs = up_to(self.r, 8)
        self.r2 = up_to(2 * self.r, 8)
        self.rA = up_to(2 * self.rs, 16)
        self.L = 2 * self.C
        self.full, left = divmod(3 * self.C, 128)
        self.left = self.full * self.rs
        fold = left == 64 and self.r % 2 == 0
        self.bits = [(0, 0, self.r // 2), (64, self.r // 2, self.r // 2)] if fold else [(0, 0, self.r)]
        self.vrow = self.left + up_to(self.bits[0][2], 4)
        self.vper = min(8, 128 // self.r)
        self.brow = self.vrow + -(-8 // self.vper)
        self.rQ = up_to(max(self.brow + 1, self.left + self.rs), 16)
        self.keep = self.nb * self.R * self.Q * self.H * 2 <= (8 << 20)
        assert self.F == 4 * self.C and self.F == self.nh * self.C and self.W % self.nh == 0


INPUTS = [
    "lens", "tok", "cot", "wq_in", "bq", "wk_in", "wv_in", "bv", "wo_in", "bo", "g1", "s1", "wup_in", "bu",
    "wdn_in", "bd", "g2", "s2",
]
OUTPUTS = ["o_mo", "o_tg", "o_G", "o_Q"]


def main_scratch(z, inputs):
    dma = pltpu.SemaphoreType.DMA
    v = pltpu.VMEM
    nb, W, L, R, C, F, Q, H, MB, rA, nh = z.nb, z.W, z.L, z.R, z.C, z.F, z.Q, z.H, z.MB, z.rA, z.nh
    dd = max(z.nd - 1, 1)
    return dict(
        in_sem=dma((len(INPUTS),)),
        flat=v((2 * MB, z.N, 128), F32),
        xs=v((MB, C, R), BF16),
        xb=v((nb, C, R), BF16),
        cs=v((MB, C, R), BF16),
        cb=v((MB, C, R), BF16),
        bufq=v((W, z.rQ, 128), BF16),
        buf=v((3, W, rA, L), BF16),
        wob=v((nh, W // nh, rA, L), BF16),
        fst=v((rA, L), F32),
        fsq=v((z.rQ, 128), F32),
        fall=v((C + 8, up_to(3 * C, 128)), F32),
        vrows=v((up_to(W * (z.brow - z.vrow), 8), 128), F32),
        vcol=v((C + 8, 8), F32),
        fup=v((C + 16, F), F32),
        fod=v((F + 16, C), F32),
        wkv=v((C, L), BF16),
        wkvt=v((L, C), BF16),
        wq=v((C, C), BF16),
        wqt=v((C, C), BF16),
        wup=v((C, F), BF16),
        wupt=v((F, C + 16), BF16),
        wor=v((C, F), BF16),
        wot=v((C, F), BF16),
        wdn=v((F, C), BF16),
        wdnt=v((C, F), BF16),
        xq=v((C, Q), BF16),
        qx=v((MB, H, 128, R), BF16),
        kx=v((nb, H, HEAD_DIM, R), BF16),
        vx=v((nb, H, HEAD_DIM + 16, R), BF16),
        kt=v((nb, H, R, 128), BF16),
        vt=v((nb, H, R, 128), BF16),
        pbuf=v((nb, MB, H, R, R) if z.keep else (1, 1, 1, 16, 128), BF16),
        tops=v((MB, H, up_to(nb, 8), R), F32),
        top=v((MB, H, 8, R), F32),
        osum=v((MB, H, HEAD_DIM + 16, R), F32),
        oall=v((MB, nh, C, R), BF16),
        pall=v((MB, nh, C, R), BF16),
        stats=v((3, MB, nh, 8, 128), F32),
        n1=v((MB, C, R), F32),
        y1=v((MB, C, R), F32),
        h2=v((MB, C, R), F32),
        gel=v((MB, F, R), F32),
        up=v((MB, F, R), F32),
        dh1=v((MB, C, R), F32),
        y1b=v((C, Q), BF16),
        act=v((F, Q), BF16),
        dz=v((C, Q), BF16),
        du=v((F, Q), BF16),
        vin=v((3, MB, C, R), BF16),
        mo=v((MB, C, R), BF16),
        part=v((MB, H, HEAD_DIM, R), F32),
        delta=v((MB, H, 8, R), F32),
        dqacc=v((MB, H, HEAD_DIM, R), F32),
        dkacc=v((nb - MB if z.keep else 1, L, R), F32),
        dq=v((C, Q), BF16),
        tgs=v((nb, C, R), BF16),
        tgo=v((MB, C, R), F32),
        tgr=v((MB, z.S, C, R), BF16),
        tgx=v((MB, C, R), BF16),
        gall=v((C + 8, up_to(3 * C, 128)), F32),
        gst=v((W, z.rQ, 128), F32),
        gup=v((C + 8, F), F32),
        gout=v((F + 16, C), F32),
        gdn=v((F + 16, C), F32),
        vg=v((8, C), F32),
        pk=v((3, W, rA, L), BF16),
        got1=v((3, dd, nb, rA, L), BF16),
        sent2=v((3, nb, rA, L), BF16),
        got2=v((3, nb, rA, L), BF16),
        pkq=v((W, z.rQ, 128), BF16),
        got1q=v((dd, nb, z.rQ, 128), BF16),
        sent2q=v((nb, z.rQ, 128), BF16),
        got2q=v((nb, z.rQ, 128), BF16),
        sync=pltpu.SemaphoreType.REGULAR,
        x_ss=dma,
        xf_ss=dma,
        x_rs=dma((MB, 2)),
        xp_rs=dma((nb,)),
        c_ss=dma,
        c_rs=dma((MB,)),
        g1_ss=dma((4,)),
        g1_rs=dma((4, max(nb - 1, 1))),
        g2_ss=dma((4,)),
        g2_rs=dma((4,)),
        o_ss=dma,
        o_rs=dma((MB, 2)),
        w_ss=dma,
        w_rs=dma,
        st_ss=dma((3,)),
        st_rs=dma((3, MB)),
        p_ss=dma,
        p_rs=dma((MB, 2)),
        mo_ss=dma,
        mo_rs=dma((MB,)),
        tp_ss=dma,
        tp_rs=dma((MB, z.S)),
        t_ss=dma,
        t_rs=dma((MB,)),
        s_ss=dma((4,)),
        s1_rs=dma((3,)),
        s1q_rs=dma((dd, nb)),
        s2_rs=dma((4,)),
        v_lens=pltpu.SMEM(inputs[0].shape, inputs[0].dtype),
        **{"v_" + name: v(a.shape, a.dtype) for name, a in zip(INPUTS[1:], inputs[1:])},
    )


def main_kernel(z, names, *refs):
    k = types.SimpleNamespace(**dict(zip(names, refs)))
    nb, nd, nh, W, MB, R, C, F, H, L, S, r, rs, rA = (
        z.nb, z.nd, z.nh, z.W, z.MB, z.R, z.C, z.F, z.H, z.L, z.S, z.r, z.rs, z.rA,
    )
    b, d, h = lax.axis_index("blk"), lax.axis_index("dp"), lax.axis_index("head")
    w_me = b * nd + d
    m_t, s_me = b // S, b % S
    D = nh * C
    half = nh // 2

    def xor(i):
        return lax.bitwise_xor(h, i)

    def later(e):
        return lax.rem(m_t + e, MB)

    def home(e):
        return later(e) * S + s_me

    def mate(e):
        return lax.rem(s_me + e, S)

    def other(n):
        return lax.rem(s_me + 1 + n // MB, S) + lax.rem(m_t + n, MB) * S

    copies = {
        name: pltpu.make_async_copy(getattr(k, name), getattr(k, "v_" + name), k.in_sem.at[n])
        for n, name in enumerate(INPUTS)
    }
    rest = ["wo_in", "wdn_in", "wup_in", "lens", "cot"]
    first = [name for name in INPUTS if name not in rest and name != "tok"]
    for name in first + ["tok"] + rest:
        copies[name].start()

    bar = pltpu.get_barrier_semaphore()
    peers = [(lax.rem(b + i, nb), d, h) for i in range(1, nb)]
    peers += [(b, lax.rem(d + i, nd), h) for i in range(1, nd)]
    peers += [(b, d, xor(i)) for i in range(1, nh)]
    for peer in peers:
        pl.semaphore_signal(bar, inc=1, device_id=peer, device_id_type=MESH)

    for name in first:
        copies[name].wait()

    def place(n, put):
        column = 0
        for block, at, size in pieces(C, n):
            if block < z.full:
                put(block * rs, at, r, 0, column, size)
            else:
                for where, row, rows in z.bits:
                    put(z.left, at + where, rows, row, column, size)
            column += size

    vectors = (k.v_bq, k.v_bv, k.v_bo, k.v_g1, k.v_s1, k.v_bd, k.v_g2, k.v_s2)

    def vec_at(j):
        return z.vrow + j // z.vper, j % z.vper * r

    k.fsq[...] = jnp.zeros_like(k.fsq)
    for n, src in enumerate((k.v_wk_in[0], k.v_wv_in[0], k.v_wq_in[0])):
        src = src.astype(F32)

        def put(row, at, rows, row2, column, size):
            k.fsq[row : row + rows, at : at + size] = src[row2 : row2 + rows, column : column + size]

        place(n, put)
    for j, ref in enumerate(vectors):
        row, at = vec_at(j)
        k.fsq[row : row + 1, at : at + r] = ref[...].astype(F32)
    k.fsq[z.brow : z.brow + 1, 0 : 4 * r] = k.v_bu[...].astype(F32)
    k.bufq[w_me] = k.fsq[...].astype(BF16)
    pl.semaphore_wait(bar, len(peers))

    def shares(q):
        return k.bufq if q == M_QKV else k.buf.at[q]

    def g1(q, i):
        own = shares(q).at[w_me]
        return rcopy(own, own, k.g1_ss.at[q], k.g1_rs.at[q, i - 1], (lax.rem(b + i, nb), d, h))

    def g1_wait(q, i):
        src = shares(q).at[lax.rem(b + nb - i, nb) * nd + d]
        rcopy(src, src, k.g1_ss.at[q], k.g1_rs.at[q, i - 1], (b, d, h)).wait_recv()

    def g2(q, e, i):
        src = shares(q).at[lax.rem(b + nb - i, nb) * nd + d]
        return rcopy(src, src, k.g2_ss.at[q], k.g2_rs.at[q], (b, lax.rem(d + e, nd), h))

    def gather_start(q):
        for e in range(1, nd):
            g2(q, e, 0).start()
        loop(nb - 1, lambda i: g1(q, i + 1).start())

    def gather_forward(q):
        def one(i):
            g1_wait(q, i + 1)
            for e in range(1, nd):
                g2(q, e, i + 1).start()

        loop(nb - 1, one)

    def gather_wait(q):
        some = shares(q).at[pl.ds(0, nb * (nd - 1))]
        rcopy(some, some, k.g2_ss.at[q], k.g2_rs.at[q], (b, d, h)).wait_recv()

    def gather_sent(q):
        some = shares(q).at[pl.ds(0, nb - 1)]
        rcopy(some, some, k.g1_ss.at[q], k.g1_rs.at[q, 0], (b, d, h)).wait_send()

    def gather_drain(q):
        if q != M_QKV:
            gather_sent(q)
        some = shares(q).at[pl.ds(0, nb * (nd - 1))]
        rcopy(some, some, k.g2_ss.at[q], k.g2_rs.at[q], (b, d, h)).wait_send()

    gather_start(M_QKV)

    def load_blocks(name, n, dst):
        copies[name].wait()
        both = getattr(k, "v_" + name)[...].astype(F32)
        for m in range(MB):
            k.flat[n * MB + m] = both[:, m]
            dst[m] = columns_of(z, k.flat.at[n * MB + m]).astype(BF16)

    load_blocks("tok", 0, k.xs)
    k.xb[b] = k.xs[m_t]

    halves = [pl.ds(0, C // 2), pl.ds(C // 2, C // 2)]

    def slot_at(m):
        return lax.rem(m_t + MB - m, MB)

    def x_send(e, c):
        m = later(e)
        dst = k.xb.at[b, halves[c]]
        return rcopy(k.xs.at[m, halves[c]], dst, k.x_ss, k.x_rs.at[slot_at(m), c], (m * S + s_me, d, h))

    def x_pass(e, f, c):
        src = k.xb.at[home(e), halves[c]]
        return rcopy(src, src, k.xf_ss, k.xp_rs.at[home(e)], (m_t * S + mate(f), d, h))

    def x_wait(e, c):
        src = k.xb.at[home(e), halves[c]]
        rcopy(src, src, k.x_ss, k.x_rs.at[e, c], (b, d, h)).wait_recv()

    def xp_wait(j):
        rcopy(k.xb.at[j], k.xb.at[j], k.xf_ss, k.xp_rs.at[j], (b, d, h)).wait_recv()

    gather_sent(M_QKV)
    pl.semaphore_signal(k.sync, inc=1, device_id=(b, d, xor(1)), device_id_type=MESH)
    pl.semaphore_wait(k.sync, 1)
    for c in range(2):
        for e in range(1, MB):
            x_send(e, c).start()
    for c in range(2):
        loop(S - 1, lambda f: x_pass(0, f + 1, c).start())

    load_blocks("cot", 1, k.cs)
    k.cb[0] = k.cs[m_t]
    for name in rest[:-1]:
        copies[name].wait()

    def pack(q):
        k.buf[q, w_me] = k.fst[...].astype(BF16)

    k.fst[...] = jnp.zeros_like(k.fst)
    for q, src in ((M_OUT, k.v_wo_in[...]), (M_DOWN, k.v_wdn_in[0])):
        src = src.astype(F32)
        k.fst[0 : 2 * r, 0:C] = src[0 : 2 * r]
        k.fst[0 : 2 * r, C:L] = src[2 * r : 4 * r]
        pack(q)
    k.fst[0:r] = k.v_wup_in[0, :, 0:L].astype(F32)
    k.fst[rs : rs + r] = k.v_wup_in[0, :, L : 2 * L].astype(F32)
    pack(M_UP)

    gather_forward(M_QKV)

    gather_wait(M_QKV)

    for w in range(W):
        slab = k.bufq[w].astype(F32)
        for block in range(z.full):
            k.fall[w * r : w * r + rs, block * 128 : (block + 1) * 128] = slab[block * rs : (block + 1) * rs]
        end = z.full * 128
        for at, row, rows in z.bits:
            rows = rows if len(z.bits) > 1 else rs
            part = slab[z.left : z.left + rows, at : at + 3 * C - end]
            k.fall[w * r + row : w * r + row + rows, end : 3 * C] = part
        per = z.brow - z.vrow
        k.vrows[w * per : (w + 1) * per] = slab[z.vrow : z.brow]
    k.wkv[...] = k.fall[0:C, 0:L].astype(BF16)
    k.wkvt[...] = k.fall[0:C, 0:L].T.astype(BF16)
    k.wq[...] = k.fall[0:C, L : 3 * C].astype(BF16)
    k.wqt[...] = k.fall[0:C, L : 3 * C].T.astype(BF16)
    columns = k.vrows[...].T
    for w in range(W):
        for j in range(8):
            row, at = vec_at(j)
            column = w * (z.brow - z.vrow) + row - z.vrow
            k.vcol[w * r : (w + 1) * r, j : j + 1] = columns[at : at + r, column : column + 1]

    def vec(j):
        return k.vcol[0:C, j : j + 1]

    row16 = lax.broadcasted_iota(jnp.int32, (16, R), 0)
    column = lax.broadcasted_iota(jnp.int32, (16, R), 1)
    step = R // z.per
    token = z.per * (column % step) + column // step
    pad = jnp.zeros((48, R), BF16)
    one_rows = jnp.where(row16 < 2, 1.0, 0.0).astype(BF16)

    def in_doc(j):
        doc = jnp.zeros((16, R), jnp.int32)
        end = jnp.int32(0)
        for n in range(z.ND):
            end = end + k.v_lens[m_t, 0, n]
            doc = doc + (j * R + token >= end).astype(jnp.int32)
        return row16 == doc

    def head_send(net, i, p):
        buf, ss, rs_ = net
        src, to = (h, xor(p)) if p <= half else (xor(half), xor(p - half))
        return rcopy(buf.at[i, src], buf.at[i, src], ss, rs_.at[i, 0 if p == half else 1], (b, d, to))

    def head_start(net, i):
        for p in range(half, 0, -1):
            head_send(net, i, p).start()

    def head_pass(net, i):
        buf, ss, rs_ = net
        src = buf.at[i, xor(half)]
        rcopy(src, src, ss, rs_.at[i, 0], (b, d, h)).wait_recv()
        for p in range(half + 1, nh):
            head_send(net, i, p).start()

    def head_end(net, i):
        buf, ss, rs_ = net
        some = buf.at[i, pl.ds(0, nh - 2)]
        rcopy(some, some, ss, rs_.at[i, 1], (b, d, h)).wait_recv()

    def head_drain(net):
        buf, ss, rs_ = net
        some = buf.at[:, pl.ds(0, nh - 1)]
        rcopy(some, some, ss, rs_.at[0, 0], (b, d, h)).wait_send()

    o_net = (k.oall, k.o_ss, k.o_rs)
    p_net = (k.pall, k.p_ss, k.p_rs)

    def kv_block(t, j):
        kv = mm(k.wkvt[...], k.xb[j])
        kb = kv[0:C].astype(BF16)
        vb = (kv[C:L] + vec(V_BV)).astype(BF16)
        barred = jnp.logical_and(row16 < z.ND, jnp.logical_not(in_doc(j)))
        kf = jnp.where(barred, -BIG, 0.0).astype(BF16)
        for a in range(H):
            kh, vh = kb[a * HEAD_DIM : (a + 1) * HEAD_DIM], vb[a * HEAD_DIM : (a + 1) * HEAD_DIM]
            k.kx[t, a] = kh
            k.vx[t, a, 0:HEAD_DIM] = vh
            k.vx[t, a, HEAD_DIM:] = one_rows
            k.kt[t, a] = jnp.concatenate([kh, kf, pad], axis=0).T
            k.vt[t, a] = jnp.concatenate([vh, one_rows, pad], axis=0).T

    def query_block(e):
        xi = k.xb[home(e)]
        k.xq[:, e * R : (e + 1) * R] = xi
        qi = ((mm(k.wqt[...], xi) + vec(V_BQ)).astype(BF16).astype(F32) * HEAD_DIM**-0.5).astype(BF16)
        hot = jnp.where(in_doc(home(e)), 1.0, 0.0).astype(BF16)
        for a in range(H):
            k.qx[e, a] = jnp.concatenate([qi[a * HEAD_DIM : (a + 1) * HEAD_DIM], hot, pad], axis=0)

    def scores(e, a, t):
        return mm(k.kt[t, a], k.qx[e, a])

    def prob(e, a, t):
        if z.keep:
            return k.pbuf[t, e, a]
        return jnp.exp(scores(e, a, t) - k.tops[e, a, pl.ds(t, 1)]).astype(BF16)

    def attend(pairs):
        units = [(e, a, t) for e, t in pairs for a in range(H)]
        s = [scores(*u) for u in units]
        top = [jnp.max(x, axis=0, keepdims=True) for x in s]
        p = [jnp.exp(x - y).astype(BF16) for x, y in zip(s, top)]
        o = [mm(k.vx[t, a], x) for (e, a, t), x in zip(units, p)]
        for i, (e, a, t) in enumerate(units):
            if z.keep:
                k.pbuf[t, e, a] = p[i]
            k.tops[e, a, pl.ds(t, 1)] = top[i]
        for i, (e, a, t) in enumerate(units):
            if isinstance(t, int) and t == 0:
                k.top[e, a, 0:1] = top[i]
                k.osum[e, a] = o[i]
            else:
                old = k.top[e, a, 0:1]
                new = jnp.maximum(old, top[i])
                k.top[e, a, 0:1] = new
                k.osum[e, a] = k.osum[e, a] * jnp.exp(old - new) + o[i] * jnp.exp(top[i] - new)

    def factor(e, a, t):
        return jnp.exp(k.tops[e, a, pl.ds(t, 1)] - k.top[e, a, 0:1]) * k.top[e, a, 1:2]

    for c in range(2):
        for e in range(1, MB):
            x_wait(e, c)
            loop(S - 1, lambda f: x_pass(e, f + 1, c).start())
    gather_start(M_OUT)
    gather_start(M_UP)
    for e in range(MB):
        kv_block(e, home(e))
        query_block(e)
    for t in range(MB):
        attend([(e, t) for e in range(MB)])

    def attend_other(n):
        xp_wait(other(n))
        kv_block(MB + n, other(n))
        attend([(e, MB + n) for e in range(MB)])

    def heads_done(e):
        for a in range(H):
            o = k.osum[e, a]
            inv = 1.0 / o[HEAD_DIM : HEAD_DIM + 1]
            k.top[e, a, 1:2] = inv
            k.oall[e, h, a * HEAD_DIM : (a + 1) * HEAD_DIM] = (o[0:HEAD_DIM] * inv).astype(BF16)
        head_start(o_net, e)

    last = nb - MB - 1
    loop(last, attend_other)
    xp_wait(other(last))
    gather_start(M_DOWN)
    kv_block(MB + last, other(last))
    for e in range(MB):
        attend([(e, MB + last)])
        heads_done(e)

    gather_forward(M_OUT)
    head_pass(o_net, 0)
    gather_forward(M_UP)
    for e in range(1, MB):
        head_pass(o_net, e)
    gather_wait(M_OUT)

    per = W // nh

    def w_send(p):
        src = k.buf.at[M_OUT, pl.ds(xor(p) * per, per)]
        return rcopy(src, k.wob.at[h], k.w_ss, k.w_rs, (b, d, xor(p)))

    for p in range(1, nh):
        w_send(p).start()

    def spread(dst, slab, row):
        slab = slab.astype(F32)
        dst[row : row + z.r2] = slab[0 : z.r2, 0:C]
        dst[row + 2 * r : row + 2 * r + z.r2] = slab[0 : z.r2, C:L]

    for w in range(W):
        spread(k.fod, k.buf[M_OUT, w], 4 * r * w)
    k.wot[...] = k.fod[0:F].T.astype(BF16)

    gather_forward(M_DOWN)

    def c_send(e):
        m = later(e)
        slot = slot_at(m)
        return rcopy(k.cs.at[m], k.cb.at[slot], k.c_ss, k.c_rs.at[slot], (m * S + s_me, d, h))

    for e in range(1, MB):
        c_send(e).start()

    lane_rows = R // 128

    def st_send(e, i, p):
        own = k.stats.at[e, i, h]
        return rcopy(own, own, k.st_ss.at[e], k.st_rs.at[e, i], (b, d, xor(p)))

    def reduce_start(e, i, rows):
        for j, v in enumerate(rows):
            row = jnp.sum(v, axis=0, keepdims=True)
            for c in range(lane_rows):
                k.stats[e, i, h, pl.ds(j * lane_rows + c, 1)] = row[:, c * 128 : (c + 1) * 128]
        if len(rows) * lane_rows < 8:
            rest = 8 - len(rows) * lane_rows
            k.stats[e, i, h, pl.ds(8 - rest, rest)] = jnp.zeros((rest, 128), F32)
        for p in range(nh - 1, 0, -1):
            st_send(e, i, p).start()

    def reduce_end(e, i, n):
        some = k.stats.at[e, i, pl.ds(0, nh - 1)]
        rcopy(some, some, k.st_ss.at[e], k.st_rs.at[e, i], (b, d, h)).wait_recv()
        total = k.stats[e, i, 0]
        for j in range(1, nh):
            total = total + k.stats[e, i, j]
        total = total / D
        return [
            jnp.concatenate([total[j * lane_rows + c :][0:1] for c in range(lane_rows)], axis=1)
            for j in range(n)
        ]

    def cols(ref, i):
        return ref[:, i * R : (i + 1) * R]

    for i in range(MB):
        head_end(o_net, i)
        h1 = cols(k.xq, i).astype(F32) + mm(k.wot[...], k.oall[i].reshape(D, R)) + vec(V_BO)
        k.n1[i] = h1
        reduce_start(0, i, (h1, h1 * h1))

    gather_wait(M_UP)
    for w in range(W):
        slab = k.buf[M_UP, w].astype(F32)
        k.fup[w * r : w * r + rs, 0:L] = slab[0:rs]
        k.fup[w * r : w * r + rs, L:F] = slab[rs : 2 * rs]
    k.fup[C : C + 16] = jnp.zeros((16, F), F32)
    for w in range(W):
        row = k.bufq[w].astype(F32)[z.brow : z.brow + 1, 0 : 4 * r]
        k.fup[C : C + 1, 4 * r * w : 4 * r * (w + 1)] = row
    k.wup[...] = k.fup[0:C].astype(BF16)
    k.wupt[...] = k.fup[...].T.astype(BF16)
    gather_wait(M_DOWN)
    for w in range(W):
        spread(k.fod, k.buf[M_DOWN, w], 4 * r * w)
    k.wdn[...] = k.fod[0:F].astype(BF16)
    k.wdnt[...] = k.fod[0:F].T.astype(BF16)

    first_one = jnp.where(row16 < 1, 1.0, 0.0).astype(BF16)
    r1 = [None] * MB
    gdn = [None] * MB
    for i in range(MB):
        mean, square = reduce_end(0, i, 2)
        r1[i] = lax.rsqrt(square - mean * mean + EPS)
        n1 = (k.n1[i] - mean) * r1[i]
        k.n1[i] = n1
        y1 = n1 * vec(V_G1) + vec(V_S1)
        k.y1[i] = y1
        y1b = y1.astype(BF16)
        k.y1b[:, i * R : (i + 1) * R] = y1b
        u = mm(k.wupt[...], jnp.concatenate([y1b, first_one], axis=0))
        cdf = 0.5 * (1.0 + lax.erf(u * (0.5**0.5)))
        act = (u * cdf).astype(BF16)
        k.act[:, i * R : (i + 1) * R] = act
        h2 = y1 + mm(k.wdnt[...], act) + vec(V_BD)
        k.h2[i] = h2

        if i > 0:
            rcopy(k.cb.at[i], k.cb.at[i], k.c_ss, k.c_rs.at[i], (b, d, h)).wait_recv()
        dn2 = k.cb[i].astype(F32) * vec(V_G2)
        reduce_start(1, i, (h2, h2 * h2, dn2, dn2 * h2))
        k.up[i], k.gel[i] = u, cdf
    for i in range(MB):
        u = k.up[i]
        k.gel[i] += u * jnp.exp(-0.5 * u * u) * ((2 * jnp.pi) ** -0.5)
    k.vg[...] = jnp.zeros_like(k.vg)
    ones = jnp.ones((16, R), BF16)

    def vec_grad(j, x):
        k.vg[j : j + 1] += mm_nt(ones, x)[0:1]

    def mo_send(i):
        return rcopy(k.mo.at[i], k.o_mo.at[m_t], k.mo_ss, k.mo_rs.at[m_t], (home(i), d, h))

    for i in range(MB):
        mean, square, dmean, dsquare = reduce_end(1, i, 4)
        r2 = lax.rsqrt(square - mean * mean + EPS)
        g = k.cb[i].astype(F32)
        dn2 = g * vec(V_G2)
        n2 = (k.h2[i] - mean) * r2
        dh2 = r2 * (dn2 - dmean - n2 * (r2 * (dsquare - mean * dmean)))
        dz = dh2.astype(BF16)
        k.dz[:, i * R : (i + 1) * R] = dz
        du = (mm(k.wdn[...], dz) * k.gel[i]).astype(BF16)
        k.du[:, i * R : (i + 1) * R] = du
        dy1 = dh2 + mm(k.wup[...], du)
        dn1 = dy1 * vec(V_G1)
        k.dh1[i] = dn1
        n1 = k.n1[i]
        reduce_start(2, i, (dn1, dn1 * n1))
        out = (n2 * vec(V_G2) + vec(V_S2)).astype(BF16)
        if i > 0:
            k.mo[i] = out
            mo_send(i).start()
        else:
            k.o_mo[m_t] = out
        k.vin[0, i] = (g * n2).astype(BF16)
        k.vin[1, i] = (dy1 * n1).astype(BF16)
        k.vin[2, i] = dy1.astype(BF16)

    def sums(q):
        if q == M_QKV:
            return k.pkq, k.got1q, k.sent2q, k.got2q, k.o_Q
        return k.pk.at[q], k.got1.at[q], k.sent2.at[q], k.got2.at[q], k.o_G.at[q]

    def s1_sem(q, e, i):
        return k.s1q_rs.at[e - 1, i] if q == M_QKV else k.s1_rs.at[q]

    def s1_send(q, e, i):
        dt = lax.rem(d + e, nd)
        return rcopy(
            sums(q)[0].at[i * nd + dt], sums(q)[1].at[e - 1, i], k.s_ss.at[q], s1_sem(q, e, i),
            (b, dt, h),
        )

    def s2_send(q, i):
        bt = lax.rem(b + i, nb)
        return rcopy(sums(q)[2].at[bt], sums(q)[3].at[b], k.s_ss.at[q], k.s2_rs.at[q], (bt, d, h))

    def scatter_start(q):
        for e in range(1, nd):
            loop(nb, lambda i: s1_send(q, e, i).start())

    def scatter_sum(q, bt):
        part = sums(q)[0][bt * nd + d].astype(F32)
        for e in range(1, nd):
            src = sums(q)[1].at[e - 1, bt]
            if q == M_QKV:
                rcopy(src, src, k.s_ss.at[q], s1_sem(q, e, bt), (b, d, h)).wait_recv()
            part = part + src[...].astype(F32)
        return part

    def scatter_forward(q):
        if q != M_QKV:
            rcopy(sums(q)[1], sums(q)[1], k.s_ss.at[q], s1_sem(q, 1, 0), (b, d, h)).wait_recv()

        def one(i):
            bt = lax.rem(b + i + 1, nb)
            sums(q)[2][bt] = scatter_sum(q, bt).astype(BF16)
            s2_send(q, i + 1).start()

        loop(nb - 1, one)
        sums(q)[4][...] = scatter_sum(q, b)

    def scatter_end(q):
        some = sums(q)[3].at[pl.ds(0, nb - 1)]
        rcopy(some, some, k.s_ss.at[q], k.s2_rs.at[q], (b, d, h)).wait_recv()

        def one(i):
            sums(q)[4][...] += sums(q)[3][lax.rem(b + nb - i - 1, nb)].astype(F32)

        loop(nb - 1, one)
        some = sums(q)[0].at[pl.ds(0, W - 1)]
        rcopy(some, some, k.s_ss.at[q], k.s2_rs.at[q], (b, d, h)).wait_send()

    def rows_of(parts):
        rows = jnp.concatenate(parts, axis=0)
        if rows.shape[0] < rA:
            rows = jnp.concatenate([rows, jnp.zeros((rA - rows.shape[0], L), F32)], axis=0)
        return rows.astype(BF16)

    def pack_halves(q, g):
        for w in range(W):
            at = 4 * r * w
            pair = jnp.concatenate([g[at : at + z.r2], g[at + 2 * r : at + 2 * r + z.r2]], axis=1)
            k.pk[q, w] = rows_of([pair])
        scatter_start(q)

    k.gdn[0:F] = mm_nt(k.act[...], k.dz[...])
    pack_halves(M_DOWN, k.gdn)
    k.gup[0:C] = mm_nt(k.y1b[...], k.du[...])
    for w in range(W):
        k.pk[M_UP, w] = rows_of([k.gup[w * r : w * r + rs, 0:L], k.gup[w * r : w * r + rs, L:F]])
    scatter_start(M_UP)
    for i in range(MB):
        for j, x in ((V_G2, k.vin[0, i]), (V_G1, k.vin[1, i]), (V_S1, k.vin[2, i]), (V_S2, k.cb[i])):
            vec_grad(j, x)
        vec_grad(V_BD, cols(k.dz, i))

    for i in range(MB):
        dmean, dsquare = reduce_end(2, i, 2)
        dh1 = r1[i] * (k.dh1[i] - dmean - k.n1[i] * dsquare)
        k.dh1[i] = dh1
        dp = dh1.astype(BF16)
        k.pall[i, h] = dp
        head_start(p_net, i)

    g = None
    for i in range(MB):
        dp = k.pall[i, h]
        part = mm_nt(k.oall[i].reshape(D, R), dp)
        g = part if g is None else g + part
        vec_grad(V_BO, dp)
    k.gout[0:F] = g
    pack_halves(M_OUT, k.gout)
    ug = mm_nt(jnp.ones((16, z.Q), BF16), k.du[...])
    k.gst[...] = jnp.zeros_like(k.gst)
    for w in range(W):
        k.gst[w, z.brow : z.brow + 1, 0 : 4 * r] = ug[0:1, 4 * r * w : 4 * r * (w + 1)]

    def pack_vec(j):
        row, at = vec_at(j)
        for w in range(W):
            k.gst[w, row : row + 1, at : at + r] = k.vg[j : j + 1, w * r : (w + 1) * r]

    for j in (V_BO, V_G1, V_S1, V_BD, V_G2, V_S2):
        pack_vec(j)
    k.gall[...] = jnp.zeros_like(k.gall)

    some_rows = k.wob.at[pl.ds(0, nh - 1)]
    rcopy(some_rows, some_rows, k.w_ss, k.w_rs, (b, d, h)).wait_recv()
    k.wob[h] = k.buf[M_OUT, pl.ds(h * per, per)]
    for j in range(nh):
        for n in range(per):
            spread(k.fod, k.wob[j, n], j * C + 4 * r * n)
    for j in range(nh):
        k.wor[:, j * C : (j + 1) * C] = k.fod[j * C : (j + 1) * C].astype(BF16)

    scatter_forward(M_DOWN)
    head_pass(p_net, 0)
    for i in range(1, MB):
        head_pass(p_net, i)

    def grad_in(e):
        head_end(p_net, e)
        do = mm(k.wor[...], k.pall[e].reshape(D, R)).astype(BF16).astype(F32)
        for a in range(H):
            part = do[a * HEAD_DIM : (a + 1) * HEAD_DIM]
            own = k.oall[e, h, a * HEAD_DIM : (a + 1) * HEAD_DIM].astype(F32)
            k.part[e, a] = part
            k.delta[e, a, 0:1] = jnp.sum(part * own, axis=0, keepdims=True)
            k.dqacc[e, a] = jnp.zeros((HEAD_DIM, R), F32)

    def scaled(e, a, t):
        f = factor(e, a, t)
        delta = k.delta[e, a, 0:1] * f
        hi = delta.astype(BF16).astype(F32)
        rest = jnp.where(row16 == 0, -hi, jnp.where(row16 == 1, hi - delta, 0.0))
        return jnp.concatenate([(k.part[e, a] * f).astype(BF16), rest.astype(BF16), pad], axis=0)

    def back(slots, queries):
        units = [(e, a, t) for t in slots for a in range(H) for e in queries]
        dox = [scaled(*u) for u in units]
        p = [prob(*u) for u in units]
        dp = [mm(k.vt[t, a], x) for (e, a, t), x in zip(units, dox)]
        ds = [(x.astype(F32) * y).astype(BF16) for x, y in zip(p, dp)]
        dq = [mm(k.kx[t, a], x) for (e, a, t), x in zip(units, ds)]
        dk = [mm_nt(k.qx[e, a, 0:HEAD_DIM], x) for (e, a, t), x in zip(units, ds)]
        dv = [mm_nt(x[0:HEAD_DIM], y) for x, y in zip(dox, p)]
        for e in queries:
            for a in range(H):
                mine = [x for (e2, a2, t), x in zip(units, dq) if (e2, a2) == (e, a)]
                k.dqacc[e, a] += sum(mine[1:], mine[0])
        found = []
        per_slot = H * len(queries)
        for n in range(len(slots)):
            rows = []
            for x in (dk, dv):
                for a in range(H):
                    at = n * per_slot + a * len(queries)
                    rows.append(sum(x[at + 1 : at + len(queries)], x[at]))
            found.append(jnp.concatenate(rows, axis=0))
        return found

    def tokens_part(j, dkv):
        k.gall[0:C, 0:L] += mm_nt(k.xb[j], dkv)
        vec_grad(V_BV, dkv[C:L])
        return mm(k.wkv[...], dkv)

    def tp_send(n):
        dst = k.tgr.at[n % MB, s_me]
        to = lax.rem(s_me + 1 + n // MB, S)
        return rcopy(k.tgs.at[n], dst, k.tp_ss, k.tp_rs.at[n % MB, s_me], (m_t * S + to, d, h))

    def send_part(n, dkv):
        k.tgs[n] = tokens_part(other(n), dkv.astype(BF16)).astype(BF16)
        if not z.keep or n % MB:
            tp_send(n).start()

    others = list(range(nb - MB - 1, -1, -1))
    for e in range(MB):
        grad_in(e)
        if z.keep:
            found = back([MB + n for n in others], [e])
            for n, dkv in zip(others, found):
                if e > 0:
                    dkv = dkv + k.dkacc[n]
                if e < MB - 1:
                    k.dkacc[n] = dkv
                else:
                    send_part(n, dkv)
        if e == 0:
            scatter_forward(M_UP)
    if not z.keep:
        loop(nb - MB, lambda n: send_part(n, back([MB + n], range(MB))[0]))

    for e in range(MB - 1, -1, -1):
        dkv = back([e], range(MB))[0]
        k.tgo[e] = tokens_part(home(e), dkv.astype(BF16))
        if e == MB - 1:
            scatter_forward(M_OUT)

    for i in range(MB):
        for a in range(H):
            rows = slice(a * HEAD_DIM, (a + 1) * HEAD_DIM)
            k.dq[rows, i * R : (i + 1) * R] = (k.dqacc[i, a] * HEAD_DIM**-0.5).astype(BF16)
        vec_grad(V_BQ, cols(k.dq, i))
    k.gall[0:C, L : 3 * C] = mm_nt(k.xq[...], k.dq[...])
    pack_vec(V_BQ)
    pack_vec(V_BV)

    for w in range(W):
        for n in range(3):

            def put(row, at, rows, row2, column, size):
                src = k.gall[w * r + row2 : w * r + row2 + rows, n * C + column : n * C + column + size]
                k.gst[w, row : row + rows, at : at + size] = src

            place(n, put)
        k.pkq[w] = k.gst[w].astype(BF16)
    scatter_start(M_QKV)

    def t_send(e):
        return rcopy(k.tgx.at[e], k.o_tg.at[m_t], k.t_ss, k.t_rs.at[m_t], (home(e), d, h))

    def tokens_total(e):
        k.tgo[e] += k.dh1[e] + mm(k.wq[...], cols(k.dq, e))

        def add(f):
            src = k.tgr.at[e, mate(f + 1)]
            rcopy(src, src, k.tp_ss, k.tp_rs.at[e, mate(f + 1)], (b, d, h)).wait_recv()
            k.tgo[e] += src[...].astype(F32)

        loop(S - 1, add)
        return k.tgo[e].astype(BF16)

    for e in range(1, MB):
        k.tgx[e] = tokens_total(e)
        t_send(e).start()
    if z.keep:
        for n in range(0, nb - MB, MB):
            tp_send(n).start()

    scatter_forward(M_QKV)

    k.o_tg[m_t] = tokens_total(0)
    for q in (M_DOWN, M_UP, M_OUT):
        scatter_end(q)
    for q in range(4):
        gather_drain(q)
    def drain(some, ss, rs_):
        rcopy(some, some, ss, rs_, (b, d, h)).wait_send()

    drain(some_rows, k.w_ss, k.w_rs)
    head_drain(o_net)
    head_drain(p_net)
    for e in range(3):
        drain(k.stats.at[e, :, pl.ds(0, nh - 1)], k.st_ss.at[e], k.st_rs.at[e, 0])
    drain(k.xs.at[pl.ds(0, MB - 1)], k.x_ss, k.x_rs.at[0, 0])
    drain(k.xb.at[pl.ds(0, MB * (S - 1))], k.xf_ss, k.xp_rs.at[0])
    drain(k.cs.at[pl.ds(0, MB - 1)], k.c_ss, k.c_rs.at[0])
    drain(k.mo.at[pl.ds(0, MB - 1)], k.mo_ss, k.mo_rs.at[0])
    drain(k.tgs.at[pl.ds(0, nb - MB)], k.tp_ss, k.tp_rs.at[0, 0])
    for e in range(1, MB):
        m = later(e)
        rcopy(k.o_mo.at[m], k.o_mo.at[m], k.mo_ss, k.mo_rs.at[m], (b, d, h)).wait_recv()

    for e in range(1, MB):
        m = later(e)
        rcopy(k.o_tg.at[m], k.o_tg.at[m], k.t_ss, k.t_rs.at[m], (b, d, h)).wait_recv()
    drain(k.tgx.at[pl.ds(0, MB - 1)], k.t_ss, k.t_rs.at[0])
    scatter_end(M_QKV)


def finish_kernel(z, mo, tg, G, GQ, *outs):
    (mixed, dtok, dwq, dbq, dwk, dwv, dbv, dwo, dbo, dg1, ds1, dwup, dbu, dwdn, dbd, dg2, ds2, both) = outs
    r, rs, C, L = z.r, z.rs, z.C, z.L
    for m in range(z.MB):


        def put_mixed(i, rows):
            both[pl.ds(i, z.R // z.per, stride=z.span), m] = rows

        def put_grad(i, rows):
            dtok[m, pl.ds(i, z.R // z.per, stride=z.span)] = rows

        put_rows(z, mo[m].astype(F32), put_mixed)
        put_rows(z, tg[m].astype(F32), put_grad)
    mixed[...] = both[...].astype(BF16)
    for n, ref in enumerate((dwk, dwv, dwq)):
        column = 0
        for block, at, size in pieces(C, n):
            if block < z.full:
                ref[0, :, column : column + size] = GQ[block * rs : block * rs + r, at : at + size]
            else:
                for where, row, rows in z.bits:
                    part = GQ[z.left : z.left + rows, at + where : at + where + size]
                    ref[0, row : row + rows, column : column + size] = part
            column += size
    dwup[0, :, 0:L] = G[M_UP, 0:r]
    dwup[0, :, L : 2 * L] = G[M_UP, rs : rs + r]
    for q, ref in ((M_OUT, dwo), (M_DOWN, dwdn.at[0])):
        ref[0 : 2 * r] = G[q, 0 : 2 * r, 0:C]
        ref[2 * r : 4 * r] = G[q, 0 : 2 * r, C:L]
    for j, ref in enumerate((dbq, dbv, dbo, dg1, ds1, dbd, dg2, ds2)):
        row, at = z.vrow + j // z.vper, j % z.vper * r
        ref[...] = GQ[row : row + 1, at : at + r]
    dbu[...] = GQ[z.brow : z.brow + 1, 0 : 4 * r]


def solution(mesh):
    vec_spec = P("head", ("blk", "dp"))
    mat_spec = P("head", ("blk", "dp"), None)
    tok_spec = P(None, "dp", "head", "blk")
    out_spec = P(("blk", "dp"), "head")

    def body(
        tokens, doc_lengths, cotangent, query_weight, query_bias, key_weight, value_weight, value_bias,
        out_weight, out_bias, first_gain, first_shift, up_weight, up_bias, down_weight, down_bias,
        second_gain, second_shift,
    ):
        z = Sizes(mesh, tokens, query_weight, up_weight, doc_lengths)

        def as_rows(a):
            return a.reshape(z.MB, z.N, 128).transpose(1, 0, 2)

        operands = (
            doc_lengths, as_rows(tokens), as_rows(cotangent), query_weight, query_bias, key_weight, value_weight, value_bias,
            out_weight, out_bias, first_gain, first_shift, up_weight, up_bias, down_weight, down_bias, second_gain,
            second_shift,
        )
        scratch = main_scratch(z, operands)
        vmem = pl.BlockSpec(memory_space=pltpu.VMEM)
        hbm = pl.BlockSpec(memory_space=pltpu.HBM)
        names = INPUTS + OUTPUTS + list(scratch)
        sds = jax.ShapeDtypeStruct
        parts = pl.pallas_call(
            lambda *refs: main_kernel(z, names, *refs),
            out_shape=[
                sds((z.MB, z.C, z.R), BF16),
                sds((z.MB, z.C, z.R), BF16),
                sds((3, z.rA, z.L), F32),
                sds((z.rQ, 128), F32),
            ],
            in_specs=[hbm] * len(operands),
            out_specs=[vmem] * len(OUTPUTS),
            scratch_shapes=list(scratch.values()),
            compiler_params=pltpu.CompilerParams(
                collective_id=0, has_side_effects=True, vmem_limit_bytes=63 << 20
            ),
            name="layer",
        )(*operands)
        mat, vec = sds((1, z.r, z.C), F32), sds((1, z.r), F32)
        outs = pl.pallas_call(
            lambda *refs: finish_kernel(z, *refs),
            out_shape=[
                sds((z.N, z.MB, 128), BF16), sds((z.MB, z.N, 128), F32), mat, vec, mat, mat, vec,
                sds((4 * z.r, z.C), F32), vec, vec, vec, sds((1, z.r, z.F), F32), sds((1, 4 * z.r), F32),
                sds((1, 4 * z.r, z.C), F32), vec, vec, vec,
            ],
            in_specs=[vmem] * len(OUTPUTS),
            out_specs=[vmem] * 17,
            scratch_shapes=[pltpu.VMEM((z.N, z.MB, 128), F32)],
            name="finish",
        )(*parts)
        shape = tokens.shape
        return (outs[0].transpose(1, 0, 2).reshape(shape), outs[1].reshape(shape), *outs[2:])

    return jax.shard_map(
        body,
        mesh=mesh,
        in_specs=(
            tok_spec, P(None, "dp", None), tok_spec, mat_spec, vec_spec, mat_spec, mat_spec, vec_spec,
            out_spec, vec_spec, vec_spec, vec_spec, mat_spec, vec_spec, mat_spec, vec_spec, vec_spec, vec_spec,
        ),
        out_specs=(
            tok_spec, tok_spec, mat_spec, vec_spec, mat_spec, mat_spec, vec_spec, out_spec, vec_spec, vec_spec,
            vec_spec, mat_spec, vec_spec, mat_spec, vec_spec, vec_spec, vec_spec,
        ),
        check_vma=False,
    )
```

```python
import math
import types

import jax
import jax.numpy as jnp
from jax import lax
from jax.experimental import pallas as pl
from jax.experimental.pallas import tpu as pltpu
from jax.sharding import PartitionSpec as P

HEAD_DIM = 64
EPS = 1e-05
BIG = 1e30
MESH = pl.DeviceIdType.MESH
F32 = jnp.float32
BF16 = jnp.bfloat16
V_BQ, V_BV, V_BO, V_G1, V_S1, V_BD, V_G2, V_S2 = range(8)
M_OUT, M_UP, M_DOWN, M_QKV = range(4)


def up_to(n, m):
    return (n + m - 1) // m * m


def mm(a, b):
    return lax.dot_general(a, b, (((1,), (0,)), ((), ())), preferred_element_type=F32)


def mm_nt(a, b):
    return lax.dot_general(a, b, (((1,), (1,)), ((), ())), preferred_element_type=F32)


def loop(n, fn):
    if n <= 8:
        for i in range(n):
            fn(i)
    else:
        lax.fori_loop(0, n, lambda i, c: (fn(i), c)[1], 0)


def rcopy(src, dst, ss, rs, dev):
    return pltpu.make_async_remote_copy(
        src_ref=src, dst_ref=dst, send_sem=ss, recv_sem=rs, device_id=dev, device_id_type=MESH
    )


def pieces(c, u):
    at, end = u * c, (u + 1) * c
    found = []
    while at < end:
        size = min(128 - at % 128, end - at)
        found.append((at // 128, at % 128, size))
        at += size
    return found


def columns_of(z, flat):
    rows = [flat[pl.ds(i, z.R // z.per, stride=z.span)].T for i in range(z.span)]
    tokens = []
    for u in range(z.per):
        tokens.append(jnp.concatenate([rows[i][at : at + n] for i, at, n in pieces(z.C, u)], axis=0))
    return jnp.concatenate(tokens, axis=1)


def put_rows(z, value, put):
    n = z.R // z.per
    parts = [[] for _ in range(z.span)]
    for u in range(z.per):
        c = 0
        for i, _, size in pieces(z.C, u):
            parts[i].append(value[c : c + size, u * n : (u + 1) * n])
            c += size
    for i in range(z.span):
        put(i, jnp.concatenate(parts[i], axis=0).T)


class Sizes:
    def __init__(self, mesh, tokens, query_weight, up_weight, doc_lengths):
        self.nb, self.nd, self.nh = mesh.shape["blk"], mesh.shape["dp"], mesh.shape["head"]
        self.W = self.nb * self.nd
        self.C, self.F = query_weight.shape[2], up_weight.shape[2]
        self.MB = tokens.shape[0]
        self.R = tokens.shape[3] // self.C
        self.S = self.nb // self.MB
        self.Q = self.MB * self.R
        self.N = self.R * self.C // 128
        self.per = 128 // math.gcd(self.C, 128)
        self.span = self.per * self.C // 128
        self.H = self.C // HEAD_DIM
        self.ND = doc_lengths.shape[2]
        self.r = query_weight.shape[1]
        self.rs = up_to(self.r, 8)
        self.r2 = up_to(2 * self.r, 8)
        self.rA = up_to(2 * self.rs, 16)
        self.L = 2 * self.C
        self.full, left = divmod(3 * self.C, 128)
        self.left = self.full * self.rs
        fold = left == 64 and self.r % 2 == 0
        self.bits = [(0, 0, self.r // 2), (64, self.r // 2, self.r // 2)] if fold else [(0, 0, self.r)]
        self.vrow = self.left + up_to(self.bits[0][2], 4)
        self.vper = min(8, 128 // self.r)
        self.brow = self.vrow + -(-8 // self.vper)
        self.rQ = up_to(max(self.brow + 1, self.left + self.rs), 16)
        self.keep = self.nb * self.R * self.Q * self.H * 2 <= (8 << 20)
        assert self.F == 4 * self.C and self.F == self.nh * self.C and self.W % self.nh == 0


INPUTS = [
    "lens", "tok", "cot", "wq_in", "bq", "wk_in", "wv_in", "bv", "wo_in", "bo", "g1", "s1", "wup_in", "bu",
    "wdn_in", "bd", "g2", "s2",
]
MATS = ["wk_in", "wv_in", "wq_in"]
VECS = ["bq", "bv", "bo", "g1", "s1", "bd", "g2", "s2"]
OUTPUTS = ["o_mo", "o_tg", "o_G", "o_Q"]


def main_scratch(z, inputs):
    dma = pltpu.SemaphoreType.DMA
    v = pltpu.VMEM
    nb, W, L, R, C, F, Q, H, MB, rA, nh = z.nb, z.W, z.L, z.R, z.C, z.F, z.Q, z.H, z.MB, z.rA, z.nh
    dd = max(z.nd - 1, 1)
    return dict(
        in_sem=dma((len(INPUTS) - len(MATS) - len(VECS) + 2,)),
        flat=v((2 * MB, z.N, 128), F32),
        xs=v((MB, C, R), BF16),
        xb=v((nb, C, R), BF16),
        cs=v((MB, C, R), BF16),
        cb=v((MB, C, R), BF16),
        bufq=v((W, z.rQ, 128), BF16),
        buf=v((3, W, rA, L), BF16),
        wob=v((nh, W // nh, rA, L), BF16),
        fst=v((rA, L), F32),
        fsq=v((z.rQ, 128), F32),
        fall=v((C + 8, up_to(3 * C, 128)), F32),
        vrows=v((up_to(W * (z.brow - z.vrow), 8), 128), F32),
        vcol=v((C + 8, 8), F32),
        fup=v((C + 16, F), F32),
        fod=v((F + 16, C), F32),
        wkv=v((C, L), BF16),
        wkvt=v((L, C), BF16),
        wq=v((C, C), BF16),
        wqt=v((C, C), BF16),
        wup=v((C, F), BF16),
        wupt=v((F, C + 16), BF16),
        wor=v((C, F), BF16),
        wot=v((C, F), BF16),
        wdn=v((F, C), BF16),
        wdnt=v((C, F), BF16),
        xq=v((C, Q), BF16),
        qx=v((MB, H, 128, R), BF16),
        kx=v((nb, H, HEAD_DIM, R), BF16),
        vx=v((nb, H, HEAD_DIM + 16, R), BF16),
        kt=v((nb, H, R, 128), BF16),
        vt=v((nb, H, R, 128), BF16),
        pbuf=v((nb, MB, H, R, R) if z.keep else (1, 1, 1, 16, 128), BF16),
        tops=v((MB, H, up_to(nb, 8), R), F32),
        top=v((MB, H, 8, R), F32),
        osum=v((MB, H, HEAD_DIM + 16, R), F32),
        oall=v((MB, nh, C, R), BF16),
        pall=v((MB, nh, C, R), BF16),
        stats=v((3, MB, nh, 8, 128), F32),
        n1=v((MB, C, R), F32),
        y1=v((MB, C, R), F32),
        h2=v((MB, C, R), F32),
        gel=v((MB, F, R), F32),
        up=v((MB, F, R), F32),
        dh1=v((MB, C, R), F32),
        y1b=v((C, Q), BF16),
        act=v((F, Q), BF16),
        dz=v((C, Q), BF16),
        du=v((F, Q), BF16),
        vin=v((3, MB, C, R), BF16),
        mo=v((MB, C, R), BF16),
        part=v((MB, H, HEAD_DIM, R), F32),
        delta=v((MB, H, 8, R), F32),
        dqacc=v((MB, H, HEAD_DIM, R), F32),
        dkacc=v((nb - MB if z.keep else 1, L, R), F32),
        dq=v((C, Q), BF16),
        tgs=v((nb, C, R), BF16),
        tgo=v((MB, C, R), F32),
        tgr=v((MB, z.S, C, R), BF16),
        tgx=v((MB, C, R), BF16),
        gall=v((C + 8, up_to(3 * C, 128)), F32),
        gst=v((W, z.rQ, 128), F32),
        gup=v((C + 8, F), F32),
        gout=v((F + 16, C), F32),
        gdn=v((F + 16, C), F32),
        vg=v((8, C), F32),
        pk=v((3, W, rA, L), BF16),
        got1=v((3, dd, nb, rA, L), BF16),
        sent2=v((3, nb, rA, L), BF16),
        got2=v((3, nb, rA, L), BF16),
        pkq=v((W, z.rQ, 128), BF16),
        got1q=v((dd, nb, z.rQ, 128), BF16),
        sent2q=v((nb, z.rQ, 128), BF16),
        got2q=v((nb, z.rQ, 128), BF16),
        sync=pltpu.SemaphoreType.REGULAR,
        x_ss=dma,
        xf_ss=dma,
        x_rs=dma((MB, 2)),
        xp_rs=dma((nb,)),
        c_ss=dma,
        c_rs=dma((MB,)),
        g1_ss=dma((4,)),
        g1_rs=dma((4, max(nb - 1, 1))),
        g2_ss=dma((4,)),
        g2_rs=dma((4,)),
        o_ss=dma,
        o_rs=dma((MB, 2)),
        w_ss=dma,
        w_rs=dma,
        st_ss=dma((3,)),
        st_rs=dma((3, MB)),
        p_ss=dma,
        p_rs=dma((MB, 2)),
        mo_ss=dma,
        mo_rs=dma((MB,)),
        tp_ss=dma,
        tp_rs=dma((MB, z.S)),
        t_ss=dma,
        t_rs=dma((MB,)),
        s_ss=dma((4,)),
        s1_rs=dma((3,)),
        s1q_rs=dma((dd, nb)),
        s2_rs=dma((4,)),
        v_lens=pltpu.SMEM(inputs[0].shape, inputs[0].dtype),
        v_mats=v((len(MATS), 1, z.r, C), BF16),
        v_vecs=v((len(VECS), 1, z.r), BF16),
        **{"v_" + x: v(a.shape, a.dtype) for x, a in zip(INPUTS[1:], inputs[1:]) if x not in MATS + VECS},
    )


def main_kernel(z, names, *refs):
    k = types.SimpleNamespace(**dict(zip(names, refs)))
    nb, nd, nh, W, MB, R, C, F, H, L, S, r, rs, rA = (
        z.nb, z.nd, z.nh, z.W, z.MB, z.R, z.C, z.F, z.H, z.L, z.S, z.r, z.rs, z.rA,
    )
    b, d, h = lax.axis_index("blk"), lax.axis_index("dp"), lax.axis_index("head")
    w_me = b * nd + d
    m_t, s_me = b // S, b % S
    D = nh * C
    half = nh // 2

    def xor(i):
        return lax.bitwise_xor(h, i)

    def later(e):
        return lax.rem(m_t + e, MB)

    def home(e):
        return later(e) * S + s_me

    def mate(e):
        return lax.rem(s_me + e, S)

    def other(n):
        return lax.rem(s_me + 1 + n // MB, S) + lax.rem(m_t + n, MB) * S

    single = [name for name in INPUTS if name not in MATS + VECS]
    copies = {
        name: pltpu.make_async_copy(getattr(k, name), getattr(k, "v_" + name), k.in_sem.at[n + 2])
        for n, name in enumerate(single)
    }
    rest = ["wo_in", "wdn_in", "wup_in", "lens", "cot"]
    for n, (names_, dst) in enumerate(((MATS, k.v_mats), (VECS, k.v_vecs))):
        for i, name in enumerate(names_):
            pltpu.make_async_copy(getattr(k, name), dst.at[i], k.in_sem.at[n]).start()
    for name in ["bu", "tok"] + rest:
        copies[name].start()

    bar = pltpu.get_barrier_semaphore()
    peers = [(lax.rem(b + i, nb), d, h) for i in range(1, nb)]
    peers += [(b, lax.rem(d + i, nd), h) for i in range(1, nd)]
    peers += [(b, d, xor(i)) for i in range(1, nh)]
    for peer in peers:
        pl.semaphore_signal(bar, inc=1, device_id=peer, device_id_type=MESH)

    for n, dst in enumerate((k.v_mats, k.v_vecs)):
        pltpu.make_async_copy(dst, dst, k.in_sem.at[n]).wait()
    copies["bu"].wait()

    def place(n, put):
        column = 0
        for block, at, size in pieces(C, n):
            if block < z.full:
                put(block * rs, at, r, 0, column, size)
            else:
                for where, row, rows in z.bits:
                    put(z.left, at + where, rows, row, column, size)
            column += size

    def vec_at(j):
        return z.vrow + j // z.vper, j % z.vper * r

    k.fsq[...] = jnp.zeros_like(k.fsq)
    for n in range(len(MATS)):
        src = k.v_mats[n, 0].astype(F32)

        def put(row, at, rows, row2, column, size):
            k.fsq[row : row + rows, at : at + size] = src[row2 : row2 + rows, column : column + size]

        place(n, put)
    for j in range(len(VECS)):
        row, at = vec_at(j)
        k.fsq[row : row + 1, at : at + r] = k.v_vecs[j].astype(F32)
    k.fsq[z.brow : z.brow + 1, 0 : 4 * r] = k.v_bu[...].astype(F32)
    k.bufq[w_me] = k.fsq[...].astype(BF16)
    pl.semaphore_wait(bar, len(peers))

    def shares(q):
        return k.bufq if q == M_QKV else k.buf.at[q]

    def g1(q, i):
        own = shares(q).at[w_me]
        return rcopy(own, own, k.g1_ss.at[q], k.g1_rs.at[q, i - 1], (lax.rem(b + i, nb), d, h))

    def g1_wait(q, i):
        src = shares(q).at[lax.rem(b + nb - i, nb) * nd + d]
        rcopy(src, src, k.g1_ss.at[q], k.g1_rs.at[q, i - 1], (b, d, h)).wait_recv()

    def g2(q, e, i):
        src = shares(q).at[lax.rem(b + nb - i, nb) * nd + d]
        return rcopy(src, src, k.g2_ss.at[q], k.g2_rs.at[q], (b, lax.rem(d + e, nd), h))

    def gather_start(q):
        loop(nb - 1, lambda i: g1(q, i + 1).start())
        for e in range(1, nd):
            g2(q, e, 0).start()

    def gather_forward(q):
        def one(i):
            g1_wait(q, i + 1)
            for e in range(1, nd):
                g2(q, e, i + 1).start()

        loop(nb - 1, one)

    def gather_wait(q):
        some = shares(q).at[pl.ds(0, nb * (nd - 1))]
        rcopy(some, some, k.g2_ss.at[q], k.g2_rs.at[q], (b, d, h)).wait_recv()

    def gather_sent(q):
        some = shares(q).at[pl.ds(0, nb - 1)]
        rcopy(some, some, k.g1_ss.at[q], k.g1_rs.at[q, 0], (b, d, h)).wait_send()

    def gather_drain(q):
        if q != M_QKV:
            gather_sent(q)
        some = shares(q).at[pl.ds(0, nb * (nd - 1))]
        rcopy(some, some, k.g2_ss.at[q], k.g2_rs.at[q], (b, d, h)).wait_send()

    gather_start(M_QKV)

    def load_blocks(name, n, dst):
        copies[name].wait()
        both = getattr(k, "v_" + name)[...].astype(F32)
        for m in range(MB):
            k.flat[n * MB + m] = both[:, m]
            dst[m] = columns_of(z, k.flat.at[n * MB + m]).astype(BF16)

    load_blocks("tok", 0, k.xs)
    k.xb[b] = k.xs[m_t]

    halves = [pl.ds(0, C // 2), pl.ds(C // 2, C // 2)]

    def slot_at(m):
        return lax.rem(m_t + MB - m, MB)

    def x_send(e, c):
        m = later(e)
        dst = k.xb.at[b, halves[c]]
        return rcopy(k.xs.at[m, halves[c]], dst, k.x_ss, k.x_rs.at[slot_at(m), c], (m * S + s_me, d, h))

    def x_pass(e, f, c):
        src = k.xb.at[home(e), halves[c]]
        return rcopy(src, src, k.xf_ss, k.xp_rs.at[home(e)], (m_t * S + mate(f), d, h))

    def x_wait(e, c):
        src = k.xb.at[home(e), halves[c]]
        rcopy(src, src, k.x_ss, k.x_rs.at[e, c], (b, d, h)).wait_recv()

    def xp_wait(j):
        rcopy(k.xb.at[j], k.xb.at[j], k.xf_ss, k.xp_rs.at[j], (b, d, h)).wait_recv()

    gather_sent(M_QKV)
    pl.semaphore_signal(k.sync, inc=1, device_id=(b, d, xor(1)), device_id_type=MESH)
    pl.semaphore_wait(k.sync, 1)
    for c in range(2):
        for e in range(1, MB):
            x_send(e, c).start()
    for c in range(2):
        loop(S - 1, lambda f: x_pass(0, f + 1, c).start())

    load_blocks("cot", 1, k.cs)
    k.cb[0] = k.cs[m_t]
    for name in rest[:-1]:
        copies[name].wait()

    def pack(q):
        k.buf[q, w_me] = k.fst[...].astype(BF16)

    k.fst[...] = jnp.zeros_like(k.fst)
    for q, src in ((M_OUT, k.v_wo_in[...]), (M_DOWN, k.v_wdn_in[0])):
        src = src.astype(F32)
        k.fst[0 : 2 * r, 0:C] = src[0 : 2 * r]
        k.fst[0 : 2 * r, C:L] = src[2 * r : 4 * r]
        pack(q)
    k.fst[0:r] = k.v_wup_in[0, :, 0:L].astype(F32)
    k.fst[rs : rs + r] = k.v_wup_in[0, :, L : 2 * L].astype(F32)
    pack(M_UP)

    gather_forward(M_QKV)

    gather_wait(M_QKV)

    for w in range(W):
        slab = k.bufq[w].astype(F32)
        for block in range(z.full):
            k.fall[w * r : w * r + rs, block * 128 : (block + 1) * 128] = slab[block * rs : (block + 1) * rs]
        end = z.full * 128
        for at, row, rows in z.bits:
            rows = rows if len(z.bits) > 1 else rs
            part = slab[z.left : z.left + rows, at : at + 3 * C - end]
            k.fall[w * r + row : w * r + row + rows, end : 3 * C] = part
        per = z.brow - z.vrow
        k.vrows[w * per : (w + 1) * per] = slab[z.vrow : z.brow]
    k.wkv[...] = k.fall[0:C, 0:L].astype(BF16)
    k.wkvt[...] = k.fall[0:C, 0:L].T.astype(BF16)
    k.wq[...] = k.fall[0:C, L : 3 * C].astype(BF16)
    k.wqt[...] = k.fall[0:C, L : 3 * C].T.astype(BF16)
    columns = k.vrows[...].T
    for w in range(W):
        for j in range(8):
            row, at = vec_at(j)
            column = w * (z.brow - z.vrow) + row - z.vrow
            k.vcol[w * r : (w + 1) * r, j : j + 1] = columns[at : at + r, column : column + 1]

    def vec(j):
        return k.vcol[0:C, j : j + 1]

    row16 = lax.broadcasted_iota(jnp.int32, (16, R), 0)
    column = lax.broadcasted_iota(jnp.int32, (16, R), 1)
    step = R // z.per
    token = z.per * (column % step) + column // step
    pad = jnp.zeros((48, R), BF16)
    one_rows = jnp.where(row16 < 2, 1.0, 0.0).astype(BF16)

    def in_doc(j):
        doc = jnp.zeros((16, R), jnp.int32)
        end = jnp.int32(0)
        for n in range(z.ND):
            end = end + k.v_lens[m_t, 0, n]
            doc = doc + (j * R + token >= end).astype(jnp.int32)
        return row16 == doc

    def head_send(net, i, p):
        buf, ss, rs_ = net
        src, to = (h, xor(p)) if p <= half else (xor(half), xor(p - half))
        return rcopy(buf.at[i, src], buf.at[i, src], ss, rs_.at[i, 0 if p == half else 1], (b, d, to))

    def head_start(net, i):
        for p in range(half, 0, -1):
            head_send(net, i, p).start()

    def head_pass(net, i):
        buf, ss, rs_ = net
        src = buf.at[i, xor(half)]
        rcopy(src, src, ss, rs_.at[i, 0], (b, d, h)).wait_recv()
        for p in range(half + 1, nh):
            head_send(net, i, p).start()

    def head_end(net, i):
        buf, ss, rs_ = net
        some = buf.at[i, pl.ds(0, nh - 2)]
        rcopy(some, some, ss, rs_.at[i, 1], (b, d, h)).wait_recv()

    def head_drain(net):
        buf, ss, rs_ = net
        some = buf.at[:, pl.ds(0, nh - 1)]
        rcopy(some, some, ss, rs_.at[0, 0], (b, d, h)).wait_send()

    o_net = (k.oall, k.o_ss, k.o_rs)
    p_net = (k.pall, k.p_ss, k.p_rs)

    def kv_block(t, j):
        kv = mm(k.wkvt[...], k.xb[j])
        kb = kv[0:C].astype(BF16)
        vb = (kv[C:L] + vec(V_BV)).astype(BF16)
        barred = jnp.logical_and(row16 < z.ND, jnp.logical_not(in_doc(j)))
        kf = jnp.where(barred, -BIG, 0.0).astype(BF16)
        for a in range(H):
            kh, vh = kb[a * HEAD_DIM : (a + 1) * HEAD_DIM], vb[a * HEAD_DIM : (a + 1) * HEAD_DIM]
            k.kx[t, a] = kh
            k.vx[t, a, 0:HEAD_DIM] = vh
            k.vx[t, a, HEAD_DIM:] = one_rows
            k.kt[t, a] = jnp.concatenate([kh, kf, pad], axis=0).T
            k.vt[t, a] = jnp.concatenate([vh, one_rows, pad], axis=0).T

    def query_block(e):
        xi = k.xb[home(e)]
        k.xq[:, e * R : (e + 1) * R] = xi
        qi = ((mm(k.wqt[...], xi) + vec(V_BQ)).astype(BF16).astype(F32) * HEAD_DIM**-0.5).astype(BF16)
        hot = jnp.where(in_doc(home(e)), 1.0, 0.0).astype(BF16)
        for a in range(H):
            k.qx[e, a] = jnp.concatenate([qi[a * HEAD_DIM : (a + 1) * HEAD_DIM], hot, pad], axis=0)

    def scores(e, a, t):
        return mm(k.kt[t, a], k.qx[e, a])

    def prob(e, a, t):
        if z.keep:
            return k.pbuf[t, e, a]
        return jnp.exp(scores(e, a, t) - k.tops[e, a, pl.ds(t, 1)]).astype(BF16)

    def attend(pairs):
        units = [(e, a, t) for e, t in pairs for a in range(H)]
        s = [scores(*u) for u in units]
        top = [jnp.max(x, axis=0, keepdims=True) for x in s]
        p = [jnp.exp(x - y).astype(BF16) for x, y in zip(s, top)]
        o = [mm(k.vx[t, a], x) for (e, a, t), x in zip(units, p)]
        for i, (e, a, t) in enumerate(units):
            if z.keep:
                k.pbuf[t, e, a] = p[i]
            k.tops[e, a, pl.ds(t, 1)] = top[i]
        for i, (e, a, t) in enumerate(units):
            if isinstance(t, int) and t == 0:
                k.top[e, a, 0:1] = top[i]
                k.osum[e, a] = o[i]
            else:
                old = k.top[e, a, 0:1]
                new = jnp.maximum(old, top[i])
                k.top[e, a, 0:1] = new
                k.osum[e, a] = k.osum[e, a] * jnp.exp(old - new) + o[i] * jnp.exp(top[i] - new)

    def factor(e, a, t):
        return jnp.exp(k.tops[e, a, pl.ds(t, 1)] - k.top[e, a, 0:1]) * k.top[e, a, 1:2]

    for c in range(2):
        for e in range(1, MB):
            x_wait(e, c)
            loop(S - 1, lambda f: x_pass(e, f + 1, c).start())
    gather_start(M_OUT)
    gather_start(M_UP)
    for e in range(MB):
        kv_block(e, home(e))
        query_block(e)
    for t in range(MB):
        attend([(e, t) for e in range(MB)])

    def attend_other(n):
        xp_wait(other(n))
        kv_block(MB + n, other(n))
        attend([(e, MB + n) for e in range(MB)])

    def heads_done(e):
        for a in range(H):
            o = k.osum[e, a]
            inv = 1.0 / o[HEAD_DIM : HEAD_DIM + 1]
            k.top[e, a, 1:2] = inv
            k.oall[e, h, a * HEAD_DIM : (a + 1) * HEAD_DIM] = (o[0:HEAD_DIM] * inv).astype(BF16)
        head_start(o_net, e)

    last = nb - MB - 1
    loop(last, attend_other)
    xp_wait(other(last))
    gather_start(M_DOWN)
    kv_block(MB + last, other(last))
    for e in range(MB):
        attend([(e, MB + last)])
        heads_done(e)

    gather_forward(M_OUT)
    head_pass(o_net, 0)
    gather_forward(M_UP)
    for e in range(1, MB):
        head_pass(o_net, e)
    gather_wait(M_OUT)

    per = W // nh

    def w_send(p):
        src = k.buf.at[M_OUT, pl.ds(xor(p) * per, per)]
        return rcopy(src, k.wob.at[h], k.w_ss, k.w_rs, (b, d, xor(p)))

    for p in range(1, nh):
        w_send(p).start()

    def spread(dst, slab, row):
        slab = slab.astype(F32)
        dst[row : row + z.r2] = slab[0 : z.r2, 0:C]
        dst[row + 2 * r : row + 2 * r + z.r2] = slab[0 : z.r2, C:L]

    for w in range(W):
        spread(k.fod, k.buf[M_OUT, w], 4 * r * w)
    k.wot[...] = k.fod[0:F].T.astype(BF16)

    gather_forward(M_DOWN)

    def c_send(e):
        m = later(e)
        slot = slot_at(m)
        return rcopy(k.cs.at[m], k.cb.at[slot], k.c_ss, k.c_rs.at[slot], (m * S + s_me, d, h))

    for e in range(1, MB):
        c_send(e).start()

    lane_rows = R // 128

    def st_send(e, i, p):
        own = k.stats.at[e, i, h]
        return rcopy(own, own, k.st_ss.at[e], k.st_rs.at[e, i], (b, d, xor(p)))

    def reduce_start(e, i, rows):
        for j, v in enumerate(rows):
            row = jnp.sum(v, axis=0, keepdims=True)
            for c in range(lane_rows):
                k.stats[e, i, h, pl.ds(j * lane_rows + c, 1)] = row[:, c * 128 : (c + 1) * 128]
        if len(rows) * lane_rows < 8:
            rest = 8 - len(rows) * lane_rows
            k.stats[e, i, h, pl.ds(8 - rest, rest)] = jnp.zeros((rest, 128), F32)
        for p in range(nh - 1, 0, -1):
            st_send(e, i, p).start()

    def reduce_end(e, i, n):
        some = k.stats.at[e, i, pl.ds(0, nh - 1)]
        rcopy(some, some, k.st_ss.at[e], k.st_rs.at[e, i], (b, d, h)).wait_recv()
        total = k.stats[e, i, 0]
        for j in range(1, nh):
            total = total + k.stats[e, i, j]
        total = total / D
        return [
            jnp.concatenate([total[j * lane_rows + c :][0:1] for c in range(lane_rows)], axis=1)
            for j in range(n)
        ]

    def cols(ref, i):
        return ref[:, i * R : (i + 1) * R]

    for i in range(MB):
        head_end(o_net, i)
        h1 = cols(k.xq, i).astype(F32) + mm(k.wot[...], k.oall[i].reshape(D, R)) + vec(V_BO)
        k.n1[i] = h1
        reduce_start(0, i, (h1, h1 * h1))

    gather_wait(M_UP)
    for w in range(W):
        slab = k.buf[M_UP, w].astype(F32)
        k.fup[w * r : w * r + rs, 0:L] = slab[0:rs]
        k.fup[w * r : w * r + rs, L:F] = slab[rs : 2 * rs]
    k.fup[C : C + 16] = jnp.zeros((16, F), F32)
    for w in range(W):
        row = k.bufq[w].astype(F32)[z.brow : z.brow + 1, 0 : 4 * r]
        k.fup[C : C + 1, 4 * r * w : 4 * r * (w + 1)] = row
    k.wup[...] = k.fup[0:C].astype(BF16)
    k.wupt[...] = k.fup[...].T.astype(BF16)
    gather_wait(M_DOWN)
    for w in range(W):
        spread(k.fod, k.buf[M_DOWN, w], 4 * r * w)
    k.wdn[...] = k.fod[0:F].astype(BF16)
    k.wdnt[...] = k.fod[0:F].T.astype(BF16)

    first_one = jnp.where(row16 < 1, 1.0, 0.0).astype(BF16)
    r1 = [None] * MB
    gdn = [None] * MB
    for i in range(MB):
        mean, square = reduce_end(0, i, 2)
        r1[i] = lax.rsqrt(square - mean * mean + EPS)
        n1 = (k.n1[i] - mean) * r1[i]
        k.n1[i] = n1
        y1 = n1 * vec(V_G1) + vec(V_S1)
        k.y1[i] = y1
        y1b = y1.astype(BF16)
        k.y1b[:, i * R : (i + 1) * R] = y1b
        u = mm(k.wupt[...], jnp.concatenate([y1b, first_one], axis=0))
        cdf = 0.5 * (1.0 + lax.erf(u * (0.5**0.5)))
        act = (u * cdf).astype(BF16)
        k.act[:, i * R : (i + 1) * R] = act
        h2 = y1 + mm(k.wdnt[...], act) + vec(V_BD)
        k.h2[i] = h2

        if i > 0:
            rcopy(k.cb.at[i], k.cb.at[i], k.c_ss, k.c_rs.at[i], (b, d, h)).wait_recv()
        dn2 = k.cb[i].astype(F32) * vec(V_G2)
        reduce_start(1, i, (h2, h2 * h2, dn2, dn2 * h2))
        k.up[i], k.gel[i] = u, cdf
    for i in range(MB):
        u = k.up[i]
        k.gel[i] += u * jnp.exp(-0.5 * u * u) * ((2 * jnp.pi) ** -0.5)
    k.vg[...] = jnp.zeros_like(k.vg)
    ones = jnp.ones((16, R), BF16)

    def vec_grad(j, x):
        k.vg[j : j + 1] += mm_nt(ones, x)[0:1]

    def mo_send(i):
        return rcopy(k.mo.at[i], k.o_mo.at[m_t], k.mo_ss, k.mo_rs.at[m_t], (home(i), d, h))

    for i in range(MB):
        mean, square, dmean, dsquare = reduce_end(1, i, 4)
        r2 = lax.rsqrt(square - mean * mean + EPS)
        g = k.cb[i].astype(F32)
        dn2 = g * vec(V_G2)
        n2 = (k.h2[i] - mean) * r2
        dh2 = r2 * (dn2 - dmean - n2 * (r2 * (dsquare - mean * dmean)))
        dz = dh2.astype(BF16)
        k.dz[:, i * R : (i + 1) * R] = dz
        du = (mm(k.wdn[...], dz) * k.gel[i]).astype(BF16)
        k.du[:, i * R : (i + 1) * R] = du
        dy1 = dh2 + mm(k.wup[...], du)
        dn1 = dy1 * vec(V_G1)
        k.dh1[i] = dn1
        n1 = k.n1[i]
        reduce_start(2, i, (dn1, dn1 * n1))
        out = (n2 * vec(V_G2) + vec(V_S2)).astype(BF16)
        if i > 0:
            k.mo[i] = out
            mo_send(i).start()
        else:
            k.o_mo[m_t] = out
        k.vin[0, i] = (g * n2).astype(BF16)
        k.vin[1, i] = (dy1 * n1).astype(BF16)
        k.vin[2, i] = dy1.astype(BF16)

    def sums(q):
        if q == M_QKV:
            return k.pkq, k.got1q, k.sent2q, k.got2q, k.o_Q
        return k.pk.at[q], k.got1.at[q], k.sent2.at[q], k.got2.at[q], k.o_G.at[q]

    def s1_sem(q, e, i):
        return k.s1q_rs.at[e - 1, i] if q == M_QKV else k.s1_rs.at[q]

    def s1_send(q, e, i):
        dt = lax.rem(d + e, nd)
        return rcopy(
            sums(q)[0].at[i * nd + dt], sums(q)[1].at[e - 1, i], k.s_ss.at[q], s1_sem(q, e, i),
            (b, dt, h),
        )

    def s2_send(q, i):
        bt = lax.rem(b + i, nb)
        return rcopy(sums(q)[2].at[bt], sums(q)[3].at[b], k.s_ss.at[q], k.s2_rs.at[q], (bt, d, h))

    def scatter_start(q):
        for e in range(1, nd):
            loop(nb, lambda i: s1_send(q, e, i).start())

    def scatter_sum(q, bt):
        part = sums(q)[0][bt * nd + d].astype(F32)
        for e in range(1, nd):
            src = sums(q)[1].at[e - 1, bt]
            if q == M_QKV:
                rcopy(src, src, k.s_ss.at[q], s1_sem(q, e, bt), (b, d, h)).wait_recv()
            part = part + src[...].astype(F32)
        return part

    def scatter_forward(q):
        if q != M_QKV:
            rcopy(sums(q)[1], sums(q)[1], k.s_ss.at[q], s1_sem(q, 1, 0), (b, d, h)).wait_recv()

        def one(i):
            bt = lax.rem(b + i + 1, nb)
            sums(q)[2][bt] = scatter_sum(q, bt).astype(BF16)
            s2_send(q, i + 1).start()

        loop(nb - 1, one)
        sums(q)[4][...] = scatter_sum(q, b)

    def scatter_end(q):
        some = sums(q)[3].at[pl.ds(0, nb - 1)]
        rcopy(some, some, k.s_ss.at[q], k.s2_rs.at[q], (b, d, h)).wait_recv()

        def one(i):
            sums(q)[4][...] += sums(q)[3][lax.rem(b + nb - i - 1, nb)].astype(F32)

        loop(nb - 1, one)
        some = sums(q)[0].at[pl.ds(0, W - 1)]
        rcopy(some, some, k.s_ss.at[q], k.s2_rs.at[q], (b, d, h)).wait_send()

    def rows_of(parts):
        rows = jnp.concatenate(parts, axis=0)
        if rows.shape[0] < rA:
            rows = jnp.concatenate([rows, jnp.zeros((rA - rows.shape[0], L), F32)], axis=0)
        return rows.astype(BF16)

    def pack_halves(q, g):
        for w in range(W):
            at = 4 * r * w
            pair = jnp.concatenate([g[at : at + z.r2], g[at + 2 * r : at + 2 * r + z.r2]], axis=1)
            k.pk[q, w] = rows_of([pair])
        scatter_start(q)

    k.gdn[0:F] = mm_nt(k.act[...], k.dz[...])
    pack_halves(M_DOWN, k.gdn)
    k.gup[0:C] = mm_nt(k.y1b[...], k.du[...])
    for w in range(W):
        k.pk[M_UP, w] = rows_of([k.gup[w * r : w * r + rs, 0:L], k.gup[w * r : w * r + rs, L:F]])
    scatter_start(M_UP)
    for i in range(MB):
        for j, x in ((V_G2, k.vin[0, i]), (V_G1, k.vin[1, i]), (V_S1, k.vin[2, i]), (V_S2, k.cb[i])):
            vec_grad(j, x)
        vec_grad(V_BD, cols(k.dz, i))

    for i in range(MB):
        dmean, dsquare = reduce_end(2, i, 2)
        dh1 = r1[i] * (k.dh1[i] - dmean - k.n1[i] * dsquare)
        k.dh1[i] = dh1
        dp = dh1.astype(BF16)
        k.pall[i, h] = dp
        head_start(p_net, i)

    g = None
    for i in range(MB):
        dp = k.pall[i, h]
        part = mm_nt(k.oall[i].reshape(D, R), dp)
        g = part if g is None else g + part
        vec_grad(V_BO, dp)
    k.gout[0:F] = g
    pack_halves(M_OUT, k.gout)
    ug = mm_nt(jnp.ones((16, z.Q), BF16), k.du[...])
    k.gst[...] = jnp.zeros_like(k.gst)
    for w in range(W):
        k.gst[w, z.brow : z.brow + 1, 0 : 4 * r] = ug[0:1, 4 * r * w : 4 * r * (w + 1)]

    def pack_vec(j):
        row, at = vec_at(j)
        for w in range(W):
            k.gst[w, row : row + 1, at : at + r] = k.vg[j : j + 1, w * r : (w + 1) * r]

    for j in (V_BO, V_G1, V_S1, V_BD, V_G2, V_S2):
        pack_vec(j)
    k.gall[...] = jnp.zeros_like(k.gall)

    some_rows = k.wob.at[pl.ds(0, nh - 1)]
    rcopy(some_rows, some_rows, k.w_ss, k.w_rs, (b, d, h)).wait_recv()
    k.wob[h] = k.buf[M_OUT, pl.ds(h * per, per)]
    for j in range(nh):
        for n in range(per):
            spread(k.fod, k.wob[j, n], j * C + 4 * r * n)
    for j in range(nh):
        k.wor[:, j * C : (j + 1) * C] = k.fod[j * C : (j + 1) * C].astype(BF16)

    scatter_forward(M_DOWN)
    head_pass(p_net, 0)
    for i in range(1, MB):
        head_pass(p_net, i)

    def grad_in(e):
        head_end(p_net, e)
        do = mm(k.wor[...], k.pall[e].reshape(D, R)).astype(BF16).astype(F32)
        for a in range(H):
            part = do[a * HEAD_DIM : (a + 1) * HEAD_DIM]
            own = k.oall[e, h, a * HEAD_DIM : (a + 1) * HEAD_DIM].astype(F32)
            k.part[e, a] = part
            k.delta[e, a, 0:1] = jnp.sum(part * own, axis=0, keepdims=True)
            k.dqacc[e, a] = jnp.zeros((HEAD_DIM, R), F32)

    def scaled(e, a, t):
        f = factor(e, a, t)
        delta = k.delta[e, a, 0:1] * f
        hi = delta.astype(BF16).astype(F32)
        rest = jnp.where(row16 == 0, -hi, jnp.where(row16 == 1, hi - delta, 0.0))
        return jnp.concatenate([(k.part[e, a] * f).astype(BF16), rest.astype(BF16), pad], axis=0)

    def back(slots, queries):
        units = [(e, a, t) for t in slots for a in range(H) for e in queries]
        dox = [scaled(*u) for u in units]
        p = [prob(*u) for u in units]
        dp = [mm(k.vt[t, a], x) for (e, a, t), x in zip(units, dox)]
        ds = [(x.astype(F32) * y).astype(BF16) for x, y in zip(p, dp)]
        dq = [mm(k.kx[t, a], x) for (e, a, t), x in zip(units, ds)]
        dk = [mm_nt(k.qx[e, a, 0:HEAD_DIM], x) for (e, a, t), x in zip(units, ds)]
        dv = [mm_nt(x[0:HEAD_DIM], y) for x, y in zip(dox, p)]
        for e in queries:
            for a in range(H):
                mine = [x for (e2, a2, t), x in zip(units, dq) if (e2, a2) == (e, a)]
                k.dqacc[e, a] += sum(mine[1:], mine[0])
        found = []
        per_slot = H * len(queries)
        for n in range(len(slots)):
            rows = []
            for x in (dk, dv):
                for a in range(H):
                    at = n * per_slot + a * len(queries)
                    rows.append(sum(x[at + 1 : at + len(queries)], x[at]))
            found.append(jnp.concatenate(rows, axis=0))
        return found

    def tokens_part(j, dkv):
        k.gall[0:C, 0:L] += mm_nt(k.xb[j], dkv)
        vec_grad(V_BV, dkv[C:L])
        return mm(k.wkv[...], dkv)

    def tp_send(n):
        dst = k.tgr.at[n % MB, s_me]
        to = lax.rem(s_me + 1 + n // MB, S)
        return rcopy(k.tgs.at[n], dst, k.tp_ss, k.tp_rs.at[n % MB, s_me], (m_t * S + to, d, h))

    def send_part(n, dkv):
        k.tgs[n] = tokens_part(other(n), dkv.astype(BF16)).astype(BF16)
        if not z.keep or n % MB:
            tp_send(n).start()

    others = list(range(nb - MB - 1, -1, -1))
    for e in range(MB):
        grad_in(e)
        if z.keep:
            found = back([MB + n for n in others], [e])
            for n, dkv in zip(others, found):
                if e > 0:
                    dkv = dkv + k.dkacc[n]
                if e < MB - 1:
                    k.dkacc[n] = dkv
                else:
                    send_part(n, dkv)
        if e == 0:
            scatter_forward(M_UP)
    if not z.keep:
        loop(nb - MB, lambda n: send_part(n, back([MB + n], range(MB))[0]))

    for e in range(MB - 1, -1, -1):
        dkv = back([e], range(MB))[0]
        k.tgo[e] = tokens_part(home(e), dkv.astype(BF16))
        if e == MB - 1:
            scatter_forward(M_OUT)

    for i in range(MB):
        for a in range(H):
            rows = slice(a * HEAD_DIM, (a + 1) * HEAD_DIM)
            k.dq[rows, i * R : (i + 1) * R] = (k.dqacc[i, a] * HEAD_DIM**-0.5).astype(BF16)
        vec_grad(V_BQ, cols(k.dq, i))
    k.gall[0:C, L : 3 * C] = mm_nt(k.xq[...], k.dq[...])
    pack_vec(V_BQ)
    pack_vec(V_BV)

    for w in range(W):
        for n in range(3):

            def put(row, at, rows, row2, column, size):
                src = k.gall[w * r + row2 : w * r + row2 + rows, n * C + column : n * C + column + size]
                k.gst[w, row : row + rows, at : at + size] = src

            place(n, put)
        k.pkq[w] = k.gst[w].astype(BF16)
    scatter_start(M_QKV)

    def t_send(e):
        return rcopy(k.tgx.at[e], k.o_tg.at[m_t], k.t_ss, k.t_rs.at[m_t], (home(e), d, h))

    def tokens_total(e):
        k.tgo[e] += k.dh1[e] + mm(k.wq[...], cols(k.dq, e))

        def add(f):
            src = k.tgr.at[e, mate(f + 1)]
            rcopy(src, src, k.tp_ss, k.tp_rs.at[e, mate(f + 1)], (b, d, h)).wait_recv()
            k.tgo[e] += src[...].astype(F32)

        loop(S - 1, add)
        return k.tgo[e].astype(BF16)

    for e in range(1, MB):
        k.tgx[e] = tokens_total(e)
        t_send(e).start()
    if z.keep:
        for n in range(0, nb - MB, MB):
            tp_send(n).start()

    scatter_forward(M_QKV)

    k.o_tg[m_t] = tokens_total(0)
    for q in (M_DOWN, M_UP, M_OUT):
        scatter_end(q)
    for q in range(4):
        gather_drain(q)
    def drain(some, ss, rs_):
        rcopy(some, some, ss, rs_, (b, d, h)).wait_send()

    drain(some_rows, k.w_ss, k.w_rs)
    head_drain(o_net)
    head_drain(p_net)
    for e in range(3):
        drain(k.stats.at[e, :, pl.ds(0, nh - 1)], k.st_ss.at[e], k.st_rs.at[e, 0])
    drain(k.xs.at[pl.ds(0, MB - 1)], k.x_ss, k.x_rs.at[0, 0])
    drain(k.xb.at[pl.ds(0, MB * (S - 1))], k.xf_ss, k.xp_rs.at[0])
    drain(k.cs.at[pl.ds(0, MB - 1)], k.c_ss, k.c_rs.at[0])
    drain(k.mo.at[pl.ds(0, MB - 1)], k.mo_ss, k.mo_rs.at[0])
    drain(k.tgs.at[pl.ds(0, nb - MB)], k.tp_ss, k.tp_rs.at[0, 0])
    for e in range(1, MB):
        m = later(e)
        rcopy(k.o_mo.at[m], k.o_mo.at[m], k.mo_ss, k.mo_rs.at[m], (b, d, h)).wait_recv()

    for e in range(1, MB):
        m = later(e)
        rcopy(k.o_tg.at[m], k.o_tg.at[m], k.t_ss, k.t_rs.at[m], (b, d, h)).wait_recv()
    drain(k.tgx.at[pl.ds(0, MB - 1)], k.t_ss, k.t_rs.at[0])
    scatter_end(M_QKV)


def finish_kernel(z, mo, tg, G, GQ, *outs):
    (mixed, dtok, dwq, dbq, dwk, dwv, dbv, dwo, dbo, dg1, ds1, dwup, dbu, dwdn, dbd, dg2, ds2, both) = outs
    r, rs, C, L = z.r, z.rs, z.C, z.L
    for m in range(z.MB):


        def put_mixed(i, rows):
            both[pl.ds(i, z.R // z.per, stride=z.span), m] = rows

        def put_grad(i, rows):
            dtok[m, pl.ds(i, z.R // z.per, stride=z.span)] = rows

        put_rows(z, mo[m].astype(F32), put_mixed)
        put_rows(z, tg[m].astype(F32), put_grad)
    mixed[...] = both[...].astype(BF16)
    for n, ref in enumerate((dwk, dwv, dwq)):
        column = 0
        for block, at, size in pieces(C, n):
            if block < z.full:
                ref[0, :, column : column + size] = GQ[block * rs : block * rs + r, at : at + size]
            else:
                for where, row, rows in z.bits:
                    part = GQ[z.left : z.left + rows, at + where : at + where + size]
                    ref[0, row : row + rows, column : column + size] = part
            column += size
    dwup[0, :, 0:L] = G[M_UP, 0:r]
    dwup[0, :, L : 2 * L] = G[M_UP, rs : rs + r]
    for q, ref in ((M_OUT, dwo), (M_DOWN, dwdn.at[0])):
        ref[0 : 2 * r] = G[q, 0 : 2 * r, 0:C]
        ref[2 * r : 4 * r] = G[q, 0 : 2 * r, C:L]
    for j, ref in enumerate((dbq, dbv, dbo, dg1, ds1, dbd, dg2, ds2)):
        row, at = z.vrow + j // z.vper, j % z.vper * r
        ref[...] = GQ[row : row + 1, at : at + r]
    dbu[...] = GQ[z.brow : z.brow + 1, 0 : 4 * r]


def solution(mesh):
    vec_spec = P("head", ("blk", "dp"))
    mat_spec = P("head", ("blk", "dp"), None)
    tok_spec = P(None, "dp", "head", "blk")
    out_spec = P(("blk", "dp"), "head")

    def body(
        tokens, doc_lengths, cotangent, query_weight, query_bias, key_weight, value_weight, value_bias,
        out_weight, out_bias, first_gain, first_shift, up_weight, up_bias, down_weight, down_bias,
        second_gain, second_shift,
    ):
        z = Sizes(mesh, tokens, query_weight, up_weight, doc_lengths)

        def as_rows(a):
            return a.reshape(z.MB, z.N, 128).transpose(1, 0, 2)

        operands = (
            doc_lengths, as_rows(tokens), as_rows(cotangent), query_weight, query_bias, key_weight, value_weight, value_bias,
            out_weight, out_bias, first_gain, first_shift, up_weight, up_bias, down_weight, down_bias, second_gain,
            second_shift,
        )
        scratch = main_scratch(z, operands)
        vmem = pl.BlockSpec(memory_space=pltpu.VMEM)
        hbm = pl.BlockSpec(memory_space=pltpu.HBM)
        names = INPUTS + OUTPUTS + list(scratch)
        sds = jax.ShapeDtypeStruct
        parts = pl.pallas_call(
            lambda *refs: main_kernel(z, names, *refs),
            out_shape=[
                sds((z.MB, z.C, z.R), BF16),
                sds((z.MB, z.C, z.R), BF16),
                sds((3, z.rA, z.L), F32),
                sds((z.rQ, 128), F32),
            ],
            in_specs=[hbm] * len(operands),
            out_specs=[vmem] * len(OUTPUTS),
            scratch_shapes=list(scratch.values()),
            compiler_params=pltpu.CompilerParams(
                collective_id=0, has_side_effects=True, vmem_limit_bytes=63 << 20
            ),
            name="layer",
        )(*operands)
        mat, vec = sds((1, z.r, z.C), F32), sds((1, z.r), F32)
        outs = pl.pallas_call(
            lambda *refs: finish_kernel(z, *refs),
            out_shape=[
                sds((z.N, z.MB, 128), BF16), sds((z.MB, z.N, 128), F32), mat, vec, mat, mat, vec,
                sds((4 * z.r, z.C), F32), vec, vec, vec, sds((1, z.r, z.F), F32), sds((1, 4 * z.r), F32),
                sds((1, 4 * z.r, z.C), F32), vec, vec, vec,
            ],
            in_specs=[vmem] * len(OUTPUTS),
            out_specs=[vmem] * 17,
            scratch_shapes=[pltpu.VMEM((z.N, z.MB, 128), F32)],
            name="finish",
        )(*parts)
        shape = tokens.shape
        return (outs[0].transpose(1, 0, 2).reshape(shape), outs[1].reshape(shape), *outs[2:])

    return jax.shard_map(
        body,
        mesh=mesh,
        in_specs=(
            tok_spec, P(None, "dp", None), tok_spec, mat_spec, vec_spec, mat_spec, mat_spec, vec_spec,
            out_spec, vec_spec, vec_spec, vec_spec, mat_spec, vec_spec, mat_spec, vec_spec, vec_spec, vec_spec,
        ),
        out_specs=(
            tok_spec, tok_spec, mat_spec, vec_spec, mat_spec, mat_spec, vec_spec, out_spec, vec_spec, vec_spec,
            vec_spec, mat_spec, vec_spec, mat_spec, vec_spec, vec_spec, vec_spec,
        ),
        check_vma=False,
    )
```
